32 devices in a mesh: dp: 4 (over y, x), ctx: 8 (over z, core).
Axes of the slice: x: 2, y: 2, z: 4, core: 2. Of those that a mesh axis runs over, the one named last changes fastest.
Arguments:
- tokens_in: bfloat16 [4, 2048, 1024], P('dp', 'ctx'), may hold values from -6 to 6
- positions: int32 [4, 2048], P('dp', 'ctx'), may hold values from 0 to 1023, as said below
- out_grad: bfloat16 [4, 2048, 1024], P('dp', 'ctx'), may hold values from -6 to 6
- w_qkv: float32 [1024, 2048], P(('dp', 'ctx')), may hold values from -0.1875 to 0.1875
- w_output: float32 [1024, 1024], P(('dp', 'ctx')), may hold values from -2 to 2
- w_gate_up: float32 [1024, 9216], P(('dp', 'ctx')), may hold values from -0.1875 to 0.1875
- w_down: float32 [1024, 4608], P(('dp', 'ctx')), may hold values from -0.09375 to 0.09375
- norm_gains: float32 [2176], P(('dp', 'ctx')), may hold values from -0.3 to 0.3
- first_qkv: float32 [1024, 2048], P(('dp', 'ctx')), may hold values from -16 to 16
- first_output: float32 [1024, 1024], P(('dp', 'ctx')), may hold values from -24 to 24
- first_gate_up: float32 [1024, 9216], P(('dp', 'ctx')), may hold values from -40 to 40
- first_down: float32 [1024, 4608], P(('dp', 'ctx')), may hold values from -96 to 96
- first_gains: float32 [2176], P(('dp', 'ctx')), may hold values from -80 to 80
- second_qkv: float32 [1024, 2048], P(('dp', 'ctx')), may hold values from 1556.48 to 6225.92
- second_output: float32 [1024, 1024], P(('dp', 'ctx')), may hold values from 62.2592 to 249.0368
- second_gate_up: float32 [1024, 9216], P(('dp', 'ctx')), may hold values from 194.56 to 778.24
- second_down: float32 [1024, 4608], P(('dp', 'ctx')), may hold values from 700.416 to 2801.664
- second_gains: float32 [2176], P(('dp', 'ctx')), may hold values from 778.24 to 3112.96
Outputs:
- block_out: bfloat16 [4, 2048, 1024], P('dp', 'ctx')
- input_grad: float32 [4, 2048, 1024], P('dp', 'ctx')
- grad_qkv: float32 [1024, 2048], P(('dp', 'ctx'))
- grad_output: float32 [1024, 1024], P(('dp', 'ctx'))
- grad_gate_up: float32 [1024, 9216], P(('dp', 'ctx'))
- grad_down: float32 [1024, 4608], P(('dp', 'ctx'))
- grad_gains: float32 [2176], P(('dp', 'ctx'))
- new_qkv: float32 [1024, 2048], P(('dp', 'ctx'))
- new_output: float32 [1024, 1024], P(('dp', 'ctx'))
- new_gate_up: float32 [1024, 9216], P(('dp', 'ctx'))
- new_down: float32 [1024, 4608], P(('dp', 'ctx'))
- new_gains: float32 [2176], P(('dp', 'ctx'))
- new_first_qkv: float32 [1024, 2048], P(('dp', 'ctx'))
- new_first_output: float32 [1024, 1024], P(('dp', 'ctx'))
- new_first_gate_up: float32 [1024, 9216], P(('dp', 'ctx'))
- new_first_down: float32 [1024, 4608], P(('dp', 'ctx'))
- new_first_gains: float32 [2176], P(('dp', 'ctx'))
- new_second_qkv: float32 [1024, 2048], P(('dp', 'ctx'))
- new_second_output: float32 [1024, 1024], P(('dp', 'ctx'))
- new_second_gate_up: float32 [1024, 9216], P(('dp', 'ctx'))
- new_second_down: float32 [1024, 4608], P(('dp', 'ctx'))
- new_second_gains: float32 [2176], P(('dp', 'ctx'))
The draws below stay inside these ranges and needn't reach their ends.
Inputs may be any that keep to these rules, and one draw needn't show every extreme that they name: `positions`: each sequence holds four documents end to end and a token's position counts from its document's first token; one document of each sequence is 1024 tokens long, the other three shorter.
All inputs are finite; a program needn't handle non-finite values.
Results may differ from the reference program's by a relative error of at most 0.015.
The reference program's roundings to bfloat16 on the way count: a program that leaves them out, or rounds other values in their place, can miss the bound.
Values may be sent and summed in bfloat16 or wider, within the bound.
A program may use at most 256 MiB of HBM per device.

```python
import math
import jax
import jax.numpy as jnp
from jax import lax

D = 1024
HEADS = 16
KV_HEADS = 8
HEAD_DIM = 64
FF = 4608
STEP = 4
HQ = 1024
HK = 512
QKV = 2048
GAINS = 2176
LEN = 2048
SEQS = 4
DOC_MOST = 1024


def one_layout(row_key):
    first_key, second_key, third_key = jax.random.split(row_key, 3)
    half = DOC_MOST
    quarter = half // 2
    cut_first = jax.random.randint(first_key, (), 1, quarter)
    cut_second = jax.random.randint(second_key, (), quarter + 1, half)
    shorter = jnp.stack([cut_first, cut_second - cut_first, half - cut_second]).astype(jnp.int32)
    longest = jax.random.randint(third_key, (), 0, 4)
    order = jnp.arange(4, dtype=jnp.int32)
    rank = jnp.clip(order - (order > longest).astype(jnp.int32), 0, 2)
    picked = jnp.sum(jnp.where(rank[:, None] == jnp.arange(3, dtype=jnp.int32)[None, :], shorter[None, :], 0), axis=1)
    lengths = jnp.where(order == longest, half, picked).astype(jnp.int32)
    ends = jnp.cumsum(lengths)
    starts = ends - lengths
    index = jnp.arange(LEN, dtype=jnp.int32)
    member = (index[:, None] >= starts[None, :]) & (index[:, None] < ends[None, :])
    start_of = jnp.sum(jnp.where(member, starts[None, :], 0), axis=1)
    return (index - start_of).astype(jnp.int32)


def draw_positions(key, part):
    return jax.vmap(one_layout)(jax.random.split(key, SEQS))


def block_scale(key, dims, cuts, least, high):
    loudness, own = 1.0, jax.random.fold_in(key, 6)
    for position, blocks in cuts:
        draws = jnp.exp(jax.random.uniform(jax.random.fold_in(own, position), (blocks,), jnp.float32, least / len(cuts), high / len(cuts)))
        loudness = loudness * jnp.repeat(draws, dims[position] // blocks).reshape([-1 if axis == position else 1 for axis in range(len(dims))])
    return loudness


def gaussian(key, shape, scale, reach, cuts=(), kind=jnp.bfloat16):
    values = scale * jax.random.normal(key, shape, jnp.float32)
    if cuts:
        values = values * block_scale(key, shape, cuts, -0.22, 0.18)
    return jnp.clip(values, -reach, reach).astype(kind)


def setup_inputs(seed: int = 0) -> dict:
    key_list = jax.random.split(jax.random.key(seed), 19)
    return {
        "tokens_in": gaussian(key_list[0], (SEQS, LEN, D), 1.0, 6.0, ((0, 4), (1, 8))),
        "positions": draw_positions(jax.random.fold_in(key_list[18], 71), 0),
        "out_grad": gaussian(key_list[2], (SEQS, LEN, D), 1.0, 6.0, ((0, 4), (1, 8))),
        "w_qkv": gaussian(key_list[3], (D, QKV), D ** -0.5, 0.1875, ((0, 32),), jnp.float32),
        "w_output": gaussian(key_list[4], (HQ, D), (HEAD_DIM // 8) ** -0.5, 2.0, ((0, 32),), jnp.float32),
        "w_gate_up": gaussian(key_list[5], (D, 2 * FF), D ** -0.5, 0.1875, ((0, 32),), jnp.float32),
        "w_down": gaussian(key_list[6], (D, FF), FF ** -0.5, 0.09375, ((0, 32),), jnp.float32),
        "norm_gains": jnp.clip(jax.random.uniform(key_list[7], (GAINS,), jnp.float32, -0.3, 0.3) * block_scale(key_list[7], (GAINS,), ((0, 32),), -0.4, 0.0), -0.3, 0.3),
        "first_qkv": gaussian(key_list[8], (D, QKV), (0.03 * (SEQS * LEN) ** 0.5), 16.0, ((0, 32),), jnp.float32),
        "first_output": gaussian(key_list[9], (HQ, D), (0.045 * (SEQS * LEN) ** 0.5), 24.0, ((0, 32),), jnp.float32),
        "first_gate_up": gaussian(key_list[10], (D, 2 * FF), (0.075 * (SEQS * LEN) ** 0.5), 40.0, ((0, 32),), jnp.float32),
        "first_down": gaussian(key_list[11], (D, FF), (0.18 * (SEQS * LEN) ** 0.5), 96.0, ((0, 32),), jnp.float32),
        "first_gains": gaussian(key_list[12], (GAINS,), (0.15 * (SEQS * LEN) ** 0.5), 80.0, ((0, 32),), jnp.float32),
        "second_qkv": jnp.clip(jnp.exp(math.log(6225.92) - 1.3862944 * jax.random.uniform(key_list[13], (D, QKV), jnp.float32) ** block_scale(key_list[13], (D, QKV), ((0, 32),), -0.2, 0.2)), 1556.48, 6225.92),
        "second_output": jnp.clip(jnp.exp(math.log(249.0368) - 1.3862944 * jax.random.uniform(key_list[14], (HQ, D), jnp.float32) ** block_scale(key_list[14], (HQ, D), ((0, 32),), -0.2, 0.2)), 62.2592, 249.0368),
        "second_gate_up": jnp.clip(jnp.exp(math.log(778.24) - 1.3862944 * jax.random.uniform(key_list[15], (D, 2 * FF), jnp.float32) ** block_scale(key_list[15], (D, 2 * FF), ((0, 32),), -0.2, 0.2)), 194.56, 778.24),
        "second_down": jnp.clip(jnp.exp(math.log(2801.664) - 1.3862944 * jax.random.uniform(key_list[16], (D, FF), jnp.float32) ** block_scale(key_list[16], (D, FF), ((0, 32),), -0.2, 0.2)), 700.416, 2801.664),
        "second_gains": jnp.clip(jnp.exp(math.log(3112.96) - 1.3862944 * jax.random.uniform(key_list[17], (GAINS,), jnp.float32) ** block_scale(key_list[17], (GAINS,), ((0, 32),), -0.2, 0.2)), 778.24, 3112.96),
    }


EPS = 1e-05
THETA = 1000000.0
NEG_BIG = -1e+30
BETA_ONE = 0.9
BETA_TWO = 0.95
ADAM_EPS = 1e-08
CONTRACT_LAST = (((1,), (1,)), ((), ()))
CONTRACT_ROWS = (((0,), (0,)), ((), ()))

def widen(values):
    return lax.optimization_barrier(values).astype(jnp.float32)

def norm_forward(values, gain):
    recip = lax.rsqrt(lax.optimization_barrier(jnp.mean(values * values, axis=-1, keepdims=True)) + EPS)
    unit = values * recip
    return (unit * gain, unit, recip)

def norm_backward(grad, gain, unit, recip):
    scaled = grad * gain
    inner = lax.optimization_barrier(jnp.mean(scaled * unit, axis=-1, keepdims=True))
    grad_in = recip * (scaled - unit * inner)
    grad_gain = lax.optimization_barrier(jnp.sum((grad * unit).reshape(-1, unit.shape[-1]), axis=0))
    return (grad_in, grad_gain)

def rope_tables(places):
    half = HEAD_DIM // 2
    freqs = jnp.exp(-math.log(THETA) * (2.0 * jnp.arange(half, dtype=jnp.float32) / HEAD_DIM))
    angles = places.astype(jnp.float32)[:, None] * freqs[None, :]
    return (jnp.cos(angles)[:, None, :], jnp.sin(angles)[:, None, :])

def rotate(values, cosine, sine):
    half = HEAD_DIM // 2
    first_half = values[..., :half]
    second_half = values[..., half:]
    return jnp.concatenate([first_half * cosine - second_half * sine, second_half * cosine + first_half * sine], axis=-1)

def unrotate(grad, cosine, sine):
    half = HEAD_DIM // 2
    first_half = grad[..., :half]
    second_half = grad[..., half:]
    return jnp.concatenate([first_half * cosine + second_half * sine, second_half * cosine - first_half * sine], axis=-1)

def split_gains(gains_used):
    return (gains_used[:D], gains_used[D:2 * D], gains_used[2 * D:2 * D + HEAD_DIM], gains_used[2 * D + HEAD_DIM:])

def front_pass(tokens_f, places, weight_qkv, gains_used):
    gain_attn, gain_ffn, gain_query, gain_key = split_gains(gains_used)
    normed, unit_in, recip_in = norm_forward(tokens_f, gain_attn)
    attn_in = normed.astype(jnp.bfloat16)
    projected = jnp.dot(attn_in, weight_qkv, preferred_element_type=jnp.float32)
    count = tokens_f.shape[0]
    query = projected[:, :HQ].reshape(count, HEADS, HEAD_DIM)
    key_raw = projected[:, HQ:HQ + HK].reshape(count, KV_HEADS, HEAD_DIM)
    value_b = projected[:, HQ + HK:].astype(jnp.bfloat16).reshape(count, KV_HEADS, HEAD_DIM)
    cosine, sine = rope_tables(places)
    query_n, unit_q, recip_q = norm_forward(query, gain_query)
    key_n, unit_k, recip_k = norm_forward(key_raw, gain_key)
    query_b = rotate(query_n, cosine, sine).astype(jnp.bfloat16)
    key_b = rotate(key_n, cosine, sine).astype(jnp.bfloat16)
    saved = (attn_in, unit_in, recip_in, unit_q, recip_q, unit_k, recip_k, cosine, sine)
    return (query_b, key_b, value_b, saved)

def ffn_forward(tokens_f, attn_out, weight_output, weight_gate_up, weight_down, gain_ffn):
    mixed = tokens_f + jnp.dot(attn_out, weight_output, preferred_element_type=jnp.float32)
    normed, unit_f, recip_f = norm_forward(mixed, gain_ffn)
    ffn_in = normed.astype(jnp.bfloat16)
    gate_up = jnp.dot(ffn_in, weight_gate_up, preferred_element_type=jnp.float32)
    width = gate_up.shape[1] // 2
    gate = gate_up[:, :width]
    upper = gate_up[:, width:]
    sigma = jax.nn.sigmoid(gate)
    active = gate * sigma
    middle = (active * upper).astype(jnp.bfloat16)
    block_out = (mixed + lax.dot_general(middle, weight_down, CONTRACT_LAST, preferred_element_type=jnp.float32)).astype(jnp.bfloat16)
    return (block_out, (unit_f, recip_f, ffn_in, gate, upper, sigma, active, middle))

def ffn_backward(cotangent, attn_out, weight_output, weight_gate_up, weight_down, gain_ffn, kept):
    unit_f, recip_f, ffn_in, gate, upper, sigma, active, middle = kept
    grad_down = lax.dot_general(cotangent, middle, CONTRACT_ROWS, preferred_element_type=jnp.float32)
    grad_middle = jnp.dot(cotangent, weight_down, preferred_element_type=jnp.float32)
    grad_gate = grad_middle * upper * sigma * (1.0 + gate * (1.0 - sigma))
    grad_upper = grad_middle * active
    grad_pair = jnp.concatenate([grad_gate, grad_upper], axis=1).astype(jnp.bfloat16)
    grad_gate_up = lax.dot_general(ffn_in, grad_pair, CONTRACT_ROWS, preferred_element_type=jnp.float32)
    grad_normed = lax.dot_general(grad_pair, weight_gate_up, CONTRACT_LAST, preferred_element_type=jnp.float32)
    grad_from_norm, grad_gain_ffn = norm_backward(grad_normed, gain_ffn, unit_f, recip_f)
    grad_mixed = cotangent.astype(jnp.float32) + grad_from_norm
    grad_mixed_b = grad_mixed.astype(jnp.bfloat16)
    grad_output = lax.dot_general(attn_out, grad_mixed_b, CONTRACT_ROWS, preferred_element_type=jnp.float32)
    grad_attn = lax.dot_general(grad_mixed_b, weight_output, CONTRACT_LAST, preferred_element_type=jnp.float32).astype(jnp.bfloat16)
    return (grad_mixed, grad_output, grad_gate_up, grad_down, grad_gain_ffn, grad_attn)

def tail_pass(grad_query, grad_key, grad_value, saved, gains_used, weight_qkv, grad_mixed):
    gain_attn, gain_ffn, gain_query, gain_key = split_gains(gains_used)
    attn_in, unit_in, recip_in, unit_q, recip_q, unit_k, recip_k, cosine, sine = saved
    count = attn_in.shape[0]
    grad_q, grad_gain_q = norm_backward(unrotate(grad_query, cosine, sine), gain_query, unit_q, recip_q)
    grad_k, grad_gain_k = norm_backward(unrotate(grad_key, cosine, sine), gain_key, unit_k, recip_k)
    grad_proj = jnp.concatenate([grad_q.reshape(count, HQ), grad_k.reshape(count, HK), grad_value.reshape(count, HK)], axis=1).astype(jnp.bfloat16)
    grad_qkv = lax.dot_general(attn_in, grad_proj, CONTRACT_ROWS, preferred_element_type=jnp.float32)
    grad_normed = lax.dot_general(grad_proj, weight_qkv, CONTRACT_LAST, preferred_element_type=jnp.float32)
    grad_in, grad_gain_attn = norm_backward(grad_normed, gain_attn, unit_in, recip_in)
    return (grad_mixed + grad_in, grad_qkv, grad_gain_attn, grad_gain_q, grad_gain_k)

def adam_step(weight, grad, first, second, rate, decay):
    first_new = BETA_ONE * first + (1.0 - BETA_ONE) * grad
    second_new = BETA_TWO * second + (1.0 - BETA_TWO) * grad * grad
    first_hat = first_new / (1.0 - BETA_ONE ** STEP)
    second_hat = second_new / (1.0 - BETA_TWO ** STEP)
    weight_new = weight - rate * (first_hat / (jnp.sqrt(second_hat) + ADAM_EPS) + decay * weight)
    return (weight_new, first_new, second_new)

def allowed_mask(query_index, lower, key_index):
    return (key_index[None, :] <= query_index[:, None]) & (key_index[None, :] >= lower[:, None])

def attend_forward(query_g, keys, values, places):
    length = query_g.shape[0]
    block = min(512, length)
    scale = HEAD_DIM ** (-0.5)
    key_index = jnp.arange(length, dtype=jnp.int32)

    def one_block(number):
        start = number * block
        query_part = lax.dynamic_slice_in_dim(query_g, start, block, 0)
        query_index = start + jnp.arange(block, dtype=jnp.int32)
        lower = query_index - lax.dynamic_slice_in_dim(places, start, block, 0)
        scores = jnp.einsum('qkgd,tkd->kgqt', widen(query_part), widen(keys)) * scale
        allowed = allowed_mask(query_index, lower, key_index)
        peak = lax.optimization_barrier(jnp.max(jnp.where(allowed, scores, NEG_BIG), axis=-1))
        weights = jnp.where(allowed, jnp.exp(scores - peak[..., None]), 0.0)
        totals = lax.optimization_barrier(jnp.sum(weights, axis=-1))
        accum = jnp.einsum('kgqt,tkd->kgqd', widen(weights.astype(jnp.bfloat16)), widen(values))
        result = (accum / totals[..., None]).transpose(2, 0, 1, 3).astype(jnp.bfloat16)
        return (result, peak + jnp.log(totals))
    results, sums = lax.map(one_block, jnp.arange(length // block, dtype=jnp.int32))
    attn_out = results.reshape(length, KV_HEADS, HEADS // KV_HEADS, HEAD_DIM)
    logsum = sums.transpose(1, 2, 0, 3).reshape(KV_HEADS, HEADS // KV_HEADS, length)
    return (attn_out, logsum)

def attend_backward(query_g, keys, values, places, grad_attn, delta, logsum):
    length = query_g.shape[0]
    block = min(512, length)
    scale = HEAD_DIM ** (-0.5)
    key_index = jnp.arange(length, dtype=jnp.int32)

    def one_block(carry, number):
        grad_keys, grad_values = carry
        start = number * block
        query_part = lax.dynamic_slice_in_dim(query_g, start, block, 0)
        grad_part = lax.dynamic_slice_in_dim(grad_attn, start, block, 0)
        delta_part = lax.dynamic_slice_in_dim(delta, start, block, 2)
        logsum_part = lax.dynamic_slice_in_dim(logsum, start, block, 2)
        query_index = start + jnp.arange(block, dtype=jnp.int32)
        lower = query_index - lax.dynamic_slice_in_dim(places, start, block, 0)
        scores = jnp.einsum('qkgd,tkd->kgqt', widen(query_part), widen(keys)) * scale
        allowed = allowed_mask(query_index, lower, key_index)
        probs = jnp.where(allowed, jnp.exp(scores - logsum_part[..., None]), 0.0)
        grad_values = grad_values + jnp.einsum('kgqt,qkgd->tkd', widen(probs.astype(jnp.bfloat16)), widen(grad_part))
        grad_probs = jnp.einsum('qkgd,tkd->kgqt', widen(grad_part), widen(values))
        grad_scores = widen((scale * probs * (grad_probs - delta_part[..., None])).astype(jnp.bfloat16))
        grad_query = jnp.einsum('kgqt,tkd->qkgd', grad_scores, widen(keys))
        grad_keys = grad_keys + jnp.einsum('kgqt,qkgd->tkd', grad_scores, widen(query_part))
        return ((grad_keys, grad_values), grad_query)
    zeros = jnp.zeros(keys.shape, jnp.float32)
    (grad_keys, grad_values), grad_query = lax.scan(one_block, (zeros, zeros), jnp.arange(length // block, dtype=jnp.int32))
    return (grad_query.reshape(length, HEADS, HEAD_DIM), grad_keys, grad_values)

def reference(tokens_in, positions, out_grad, w_qkv, w_output, w_gate_up, w_down, norm_gains, first_qkv, first_output, first_gate_up, first_down, first_gains, second_qkv, second_output, second_gate_up, second_down, second_gains):
    qkv_b = w_qkv.astype(jnp.bfloat16)
    output_b = w_output.astype(jnp.bfloat16)
    gate_up_b = w_gate_up.astype(jnp.bfloat16)
    down_b = w_down.astype(jnp.bfloat16)
    gains_used = 1.0 + widen(norm_gains.astype(jnp.bfloat16))
    gain_ffn = split_gains(gains_used)[1]

    def per_sequence(carry, inputs):
        tokens, places, cotangent = inputs
        length = tokens.shape[0]
        tokens_f = tokens.astype(jnp.float32)
        query_b, key_b, value_b, saved = front_pass(tokens_f, places, qkv_b, gains_used)
        query_g = query_b.reshape(length, KV_HEADS, HEADS // KV_HEADS, HEAD_DIM)
        attn_out4, logsum = attend_forward(query_g, key_b, value_b, places)
        attn_out = attn_out4.reshape(length, HQ)
        block_out, kept = ffn_forward(tokens_f, attn_out, output_b, gate_up_b, down_b, gain_ffn)
        grad_mixed, grad_output, grad_gate_up, grad_down, grad_gain_ffn, grad_attn = ffn_backward(cotangent, attn_out, output_b, gate_up_b, down_b, gain_ffn, kept)
        grad_attn4 = grad_attn.reshape(length, KV_HEADS, HEADS // KV_HEADS, HEAD_DIM)
        delta = jnp.einsum('qkgd,qkgd->kgq', widen(grad_attn4), widen(attn_out4))
        grad_query, grad_key, grad_value = attend_backward(query_g, key_b, value_b, places, grad_attn4, delta, logsum)
        input_grad, grad_qkv, grad_gain_attn, grad_gain_q, grad_gain_k = tail_pass(grad_query, grad_key, grad_value, saved, gains_used, qkv_b, grad_mixed)
        grad_gains = jnp.concatenate([grad_gain_attn, grad_gain_ffn, grad_gain_q, grad_gain_k])
        added = (grad_qkv, grad_output, grad_gate_up, grad_down, grad_gains)
        carry = tuple((total + term for total, term in zip(carry, added)))
        return (carry, (block_out, input_grad))
    start = (jnp.zeros(w_qkv.shape, jnp.float32), jnp.zeros(w_output.shape, jnp.float32), jnp.zeros(w_gate_up.shape, jnp.float32), jnp.zeros(w_down.shape, jnp.float32), jnp.zeros(norm_gains.shape, jnp.float32))
    grads, (block_out, input_grad) = lax.scan(per_sequence, start, (tokens_in, positions, out_grad))
    grad_qkv, grad_output, grad_gate_up, grad_down, grad_gains = grads
    new_qkv, new_first_qkv, new_second_qkv = adam_step(w_qkv, grad_qkv, first_qkv, second_qkv, 0.02, 0.1)
    new_output, new_first_output, new_second_output = adam_step(w_output, grad_output, first_output, second_output, 0.2, 0.1)
    new_gate_up, new_first_gate_up, new_second_gate_up = adam_step(w_gate_up, grad_gate_up, first_gate_up, second_gate_up, 0.02, 0.1)
    new_down, new_first_down, new_second_down = adam_step(w_down, grad_down, first_down, second_down, 0.02, 0.1)
    new_gains, new_first_gains, new_second_gains = adam_step(norm_gains, grad_gains, first_gains, second_gains, 0.1, 0.0)
    return (block_out, input_grad, grad_qkv, grad_output, grad_gate_up, grad_down, grad_gains, new_qkv, new_output, new_gate_up, new_down, new_gains, new_first_qkv, new_first_output, new_first_gate_up, new_first_down, new_first_gains, new_second_qkv, new_second_output, new_second_gate_up, new_second_down, new_second_gains)
```

```python
import functools
import math

import jax
import jax.numpy as jnp
from jax import lax
from jax.experimental import pallas as pl
from jax.experimental.pallas import tpu as pltpu
from jax.sharding import PartitionSpec as P

D = 1024
HEADS = 16
KV_HEADS = 8
HEAD_DIM = 64
STEP = 4
HQ = 1024
HK = 512


EPS = 1e-05
THETA = 1000000.0
NEG_BIG = -1e30
BETA_ONE = 0.9
BETA_TWO = 0.95
ADAM_EPS = 1e-08
CONTRACT_LAST = (((1,), (1,)), ((), ()))
CONTRACT_ROWS = (((0,), (0,)), ((), ()))


def norm_forward(values, gain):
    recip = lax.rsqrt(jnp.mean(values * values, axis=-1, keepdims=True) + EPS)
    unit = values * recip
    return (unit * gain, unit, recip)


def norm_backward(grad, gain, unit, recip):
    scaled = grad * gain
    inner = jnp.mean(scaled * unit, axis=-1, keepdims=True)
    grad_in = recip * (scaled - unit * inner)
    grad_gain = jnp.sum((grad * unit).reshape(-1, unit.shape[-1]), axis=0)
    return (grad_in, grad_gain)


def rope_tables(places):
    half = HEAD_DIM // 2
    freqs = jnp.exp(-math.log(THETA) * (2.0 * jnp.arange(half, dtype=jnp.float32) / HEAD_DIM))
    angles = places.astype(jnp.float32)[:, None] * freqs[None, :]
    return (jnp.cos(angles)[:, None, :], jnp.sin(angles)[:, None, :])


def rotate(values, cosine, sine):
    half = HEAD_DIM // 2
    first_half = values[..., :half]
    second_half = values[..., half:]
    return jnp.concatenate(
        [first_half * cosine - second_half * sine, second_half * cosine + first_half * sine],
        axis=-1,
    )


def unrotate(grad, cosine, sine):
    half = HEAD_DIM // 2
    first_half = grad[..., :half]
    second_half = grad[..., half:]
    return jnp.concatenate(
        [first_half * cosine + second_half * sine, second_half * cosine - first_half * sine],
        axis=-1,
    )


def split_gains(gains_used):
    return (
        gains_used[:D],
        gains_used[D : 2 * D],
        gains_used[2 * D : 2 * D + HEAD_DIM],
        gains_used[2 * D + HEAD_DIM :],
    )


def front_pass(tokens_f, places, weight_qkv, gains_used):
    gain_attn, gain_ffn, gain_query, gain_key = split_gains(gains_used)
    normed, unit_in, recip_in = norm_forward(tokens_f, gain_attn)
    attn_in = normed.astype(jnp.bfloat16)
    projected = jnp.dot(attn_in, weight_qkv, preferred_element_type=jnp.float32)
    count = tokens_f.shape[0]
    query = projected[:, :HQ].reshape(count, HEADS, HEAD_DIM)
    key_raw = projected[:, HQ : HQ + HK].reshape(count, KV_HEADS, HEAD_DIM)
    value_b = projected[:, HQ + HK :].astype(jnp.bfloat16).reshape(count, KV_HEADS, HEAD_DIM)
    cosine, sine = rope_tables(places)
    query_n, unit_q, recip_q = norm_forward(query, gain_query)
    key_n, unit_k, recip_k = norm_forward(key_raw, gain_key)
    query_b = rotate(query_n, cosine, sine).astype(jnp.bfloat16)
    key_b = rotate(key_n, cosine, sine).astype(jnp.bfloat16)
    saved = (attn_in, unit_in, recip_in, unit_q, recip_q, unit_k, recip_k, cosine, sine)
    return (query_b, key_b, value_b, saved)


def tail_pass(grad_query, grad_key, grad_value, saved, gains_used, weight_qkv, grad_mixed):
    gain_attn, gain_ffn, gain_query, gain_key = split_gains(gains_used)
    attn_in, unit_in, recip_in, unit_q, recip_q, unit_k, recip_k, cosine, sine = saved
    count = attn_in.shape[0]
    grad_q, grad_gain_q = norm_backward(
        unrotate(grad_query, cosine, sine), gain_query, unit_q, recip_q
    )
    grad_k, grad_gain_k = norm_backward(unrotate(grad_key, cosine, sine), gain_key, unit_k, recip_k)
    grad_proj = jnp.concatenate(
        [grad_q.reshape(count, HQ), grad_k.reshape(count, HK), grad_value.reshape(count, HK)],
        axis=1,
    ).astype(jnp.bfloat16)
    grad_qkv = lax.dot_general(
        attn_in, grad_proj, CONTRACT_ROWS, preferred_element_type=jnp.float32
    )
    grad_normed = lax.dot_general(
        grad_proj, weight_qkv, CONTRACT_LAST, preferred_element_type=jnp.float32
    )
    grad_in, grad_gain_attn = norm_backward(grad_normed, gain_attn, unit_in, recip_in)
    return (grad_mixed + grad_in, grad_qkv, grad_gain_attn, grad_gain_q, grad_gain_k)


def adam_step(weight, grad, first, second, rate, decay):
    first_new = BETA_ONE * first + (1.0 - BETA_ONE) * grad
    second_new = BETA_TWO * second + (1.0 - BETA_TWO) * grad * grad
    first_hat = first_new / (1.0 - BETA_ONE**STEP)
    second_hat = second_new / (1.0 - BETA_TWO**STEP)
    weight_new = weight - rate * (first_hat / (jnp.sqrt(second_hat) + ADAM_EPS) + decay * weight)
    return (weight_new, first_new, second_new)


BF = jnp.bfloat16
F32 = jnp.float32
MESH_ID = pl.DeviceIdType.MESH
ANY = pl.BlockSpec(memory_space=pl.ANY)
VMEM = pl.BlockSpec(memory_space=pltpu.VMEM)
DMA = pltpu.SemaphoreType.DMA
NN = (((1,), (0,)), ((), ()))
NT = (((1,), (1,)), ((), ()))
TN = (((0,), (0,)), ((), ()))
VMEM_BYTES = 60 << 20


def dot(a, b, dims):
    return lax.dot_general(a, b, dims, preferred_element_type=F32)


class Place:
    def __init__(self, planes, depth):
        self.planes, self.depth = planes, depth
        self.dp = lax.axis_index("dp")
        self.ctx = lax.axis_index("ctx")
        self.z = self.ctx // 2
        self.core = self.ctx % 2

    def sibling(self):
        return {"dp": self.dp, "ctx": self.z * 2 + 1 - self.core}

    def across(self, o):
        return {"dp": self.dp ^ o, "ctx": self.ctx}

    def behind(self, k):
        return lax.rem(self.z + self.depth - k, self.depth)

    def ahead(self, k):
        return lax.rem(self.z + k, self.depth)

    def along(self, z):
        return {"dp": self.dp, "ctx": z * 2 + self.core}


def greet(devices):
    barrier = pltpu.get_barrier_semaphore()
    for device in devices:
        pl.semaphore_signal(barrier, inc=1, device_id=device, device_id_type=MESH_ID)
    pl.semaphore_wait(barrier, len(devices))


def remote(src, dst, send, recv, device):
    return pltpu.make_async_remote_copy(
        src_ref=src, dst_ref=dst, send_sem=send, recv_sem=recv, device_id=device, device_id_type=MESH_ID
    )


def params(collective_id=None):
    if collective_id is None:
        return pltpu.CompilerParams(vmem_limit_bytes=VMEM_BYTES)
    return pltpu.CompilerParams(
        vmem_limit_bytes=VMEM_BYTES, collective_id=collective_id, has_side_effects=True
    )


def plane_exchange_kernel(planes, depth, w_ref, a_ref, send, recv, local):
    me = Place(planes, depth)
    own = pltpu.make_async_copy(w_ref.at[me.dp], a_ref.at[me.dp], local)
    own.start()
    greet([me.across(o) for o in range(1, planes)])
    copies = []
    for o in range(1, planes):
        copy = remote(
            w_ref.at[me.dp ^ o], a_ref.at[me.dp], send.at[o], recv.at[o], me.across(o)
        )
        copy.start()
        copies.append(copy)
    own.wait()
    for o in range(1, planes):
        copies[o - 1].wait_send()
        remote(
            w_ref.at[me.dp], a_ref.at[me.dp ^ o], send.at[o], recv.at[o], me.across(o)
        ).wait_recv()


def plane_exchange(blocks, planes, depth, collective_id):
    return pl.pallas_call(
        functools.partial(plane_exchange_kernel, planes, depth),
        out_shape=jax.ShapeDtypeStruct(blocks.shape, blocks.dtype),
        in_specs=[ANY],
        out_specs=ANY,
        scratch_shapes=[DMA((planes,)), DMA((planes,)), DMA(())],
        compiler_params=params(collective_id),
    )(blocks)


class Gather:
    def __init__(self, me, x_ref, g_ref, sems):
        self.me, self.x, self.g, self.sems = me, x_ref, g_ref, sems
        self.sent = []

    def push(self, src, dst, kind, o, k, device):
        copy = remote(src, dst, self.sems.at[2 * kind, o, k], self.sems.at[2 * kind + 1, o, k], device)
        copy.start()
        self.sent.append(copy)

    def expect(self, dst, kind, o, k):
        remote(dst, dst, self.sems.at[2 * kind, o, k], self.sems.at[2 * kind + 1, o, k], self.me.sibling()).wait_recv()

    def start(self):
        me = self.me
        here = self.g.at[me.dp, me.z, me.core]
        self.own = pltpu.make_async_copy(self.x, here, self.sems.at[6, 0, 0])
        self.own.start()

    def first(self):
        me = self.me
        here = self.g.at[me.dp, me.z, me.core]
        for k in range(1, me.depth):
            self.push(self.x, here, 0, 0, k, me.along(me.ahead(k)))
        for o in range(1, me.planes):
            self.push(self.x, here, 1, o, 0, me.across(o))
        self.push(self.x, here, 2, 0, 0, me.sibling())

    def second(self):
        me = self.me
        for k in range(1, me.depth):
            block = self.g.at[me.dp, me.behind(k), me.core]
            self.expect(block, 0, 0, k)
            for o in range(1, me.planes):
                self.push(block, block, 1, o, k, me.across(o))
            self.push(block, block, 2, 0, k, me.sibling())
        for k in range(me.depth):
            for o in range(1, me.planes):
                block = self.g.at[me.dp ^ o, me.behind(k), me.core]
                self.expect(block, 1, o, k)
                self.push(block, block, 2, o, k, me.sibling())

    def finish(self):
        me = self.me
        for o in range(me.planes):
            for k in range(me.depth):
                block = self.g.at[me.dp ^ o, me.behind(k), 1 - me.core]
                self.expect(block, 2, o, k)
        for copy in self.sent:
            copy.wait_send()
        self.own.wait()


def gather_kernel(planes, depth, x_ref, g_ref, sems):
    me = Place(planes, depth)
    work = Gather(me, x_ref, g_ref, sems)
    work.start()
    greet(
        [me.across(o) for o in range(1, planes)]
        + [me.along(me.ahead(k)) for k in range(1, depth)]
        + [me.sibling()]
    )
    work.first()
    work.second()
    work.finish()


def gather_all(block, planes, depth, collective_id):
    return pl.pallas_call(
        functools.partial(gather_kernel, planes, depth),
        out_shape=jax.ShapeDtypeStruct((planes, depth, 2) + block.shape, block.dtype),
        in_specs=[ANY],
        out_specs=ANY,
        scratch_shapes=[DMA((7, planes, depth))],
        compiler_params=params(collective_id),
    )(block)


def halo_kernel(planes, depth, turns, kv_ref, og_ref, wo_ref, kv_all, og_all, wo_all, local, zs, cs, ps, wsem):
    me = Place(planes, depth)
    half = turns // 2
    weights = Gather(me, wo_ref, wo_all, wsem)
    weights.start()
    own_kv = pltpu.make_async_copy(kv_ref, kv_all.at[0], local.at[0])
    own_kv.start()
    own_og = pltpu.make_async_copy(og_ref, og_all.at[0], local.at[1])
    own_og.start()
    greet(
        [me.across(o) for o in range(1, planes)]
        + [me.along(me.ahead(k)) for k in range(1, depth)]
        + [me.sibling()]
    )

    def z_copy(k):
        return remote(kv_ref, kv_all.at[2 * k], zs.at[0, k], zs.at[1, k], me.along(me.ahead(k)))

    def c_copy(i):
        return remote(
            kv_all.at[2 * i + 2 * me.core], kv_all.at[2 * i + 1], cs.at[0, i], cs.at[1, i], me.sibling()
        )

    for k in range(1, half + 1):
        @pl.when(me.z + k < depth)
        def _():
            z_copy(k).start()

    weights.first()
    shares = []
    for o in range(1, planes):
        share = remote(og_ref, og_all.at[o], ps.at[0, o], ps.at[1, o], me.across(o))
        share.start()
        shares.append(share)
    own_kv.wait()

    @pl.when(me.core == 0)
    def _():
        c_copy(0).start()

    for k in range(1, half + 1):
        there = me.z - k >= 0

        @pl.when(there)
        def _():
            z_copy(k).wait_recv()

        @pl.when(there & (me.core == 1))
        def _():
            c_copy(k - 1).start()

        if k < half:
            @pl.when(there & (me.core == 0))
            def _():
                c_copy(k).start()

        @pl.when(me.z - k < 0)
        def _():
            fill = pltpu.make_async_copy(kv_ref, kv_all.at[2 * k], local.at[2])
            fill.start()
            fill.wait()

    for i in range(half):
        @pl.when(me.z - i - 1 + me.core >= 0)
        def _():
            c_copy(i).wait_recv()

        @pl.when(me.z - i - 1 + me.core < 0)
        def _():
            fill = pltpu.make_async_copy(kv_ref, kv_all.at[2 * i + 1], local.at[2])
            fill.start()
            fill.wait()

        @pl.when(me.z - i - me.core >= 0)
        def _():
            c_copy(i).wait_send()

    for k in range(1, half + 1):
        @pl.when(me.z + k < depth)
        def _():
            z_copy(k).wait_send()

    weights.second()
    for share in shares:
        share.wait()
    weights.finish()
    own_og.wait()


def halo(kv, cotangent, w_output_b, planes, depth, turns, collective_id):
    half = turns // 2
    return pl.pallas_call(
        functools.partial(halo_kernel, planes, depth, turns),
        out_shape=(
            jax.ShapeDtypeStruct((turns + 1,) + kv.shape, kv.dtype),
            jax.ShapeDtypeStruct((planes,) + cotangent.shape, cotangent.dtype),
            jax.ShapeDtypeStruct((planes, depth, 2) + w_output_b.shape, w_output_b.dtype),
        ),
        in_specs=[ANY, ANY, ANY],
        out_specs=(ANY, ANY, ANY),
        scratch_shapes=[
            DMA((3,)),
            DMA((2, half + 1)),
            DMA((2, half)),
            DMA((2, planes)),
            DMA((7, planes, depth)),
        ],
        compiler_params=params(collective_id),
    )(kv, cotangent, w_output_b)


def fill_bias(bias, lower_ref, slots, count):
    query = lax.broadcasted_iota(jnp.int32, (count, count), 1)
    lower = lower_ref[...]
    for s in range(slots):
        key = lax.broadcasted_iota(jnp.int32, (count, count), 0) - s * count
        allowed = (key <= query) & (key >= lower)
        bias[pl.ds(s * count, count), :] = jnp.where(allowed, 0.0, NEG_BIG)


def attend_kernel(slots, count, q_ref, kv_ref, lower_ref, o_ref, lse_ref, bias):
    fill_bias(bias, lower_ref, slots, count)

    def four_heads(t, carry):
        keys = kv_ref[:, pl.ds(t * 128, 128)]
        values = kv_ref[:, pl.ds(HK + t * 128, 128)]
        queries = q_ref[:, pl.ds(t * 256, 256)]
        sums = []
        for u in range(2):
            key = keys[:, u * 64 : u * 64 + 64]
            value = values[:, u * 64 : u * 64 + 64]
            for g in range(2):
                at = u * 128 + g * 64
                query = queries[:, at : at + 64]
                scores = dot(key, query, NT) * (HEAD_DIM ** (-0.5)) + bias[...]
                weights = jnp.exp(scores)
                total = jnp.sum(weights, axis=0, keepdims=True)
                out = dot(value, weights.astype(BF), TN) / total
                o_ref[pl.ds(t * 256 + at, 64), :] = out.astype(BF)
                sums.append(jnp.log(total))
        lse_ref[t] = jnp.concatenate(sums, axis=0)
        return carry

    lax.fori_loop(0, HEADS // 4, four_heads, 0)


def attend(query, kv, lower):
    count = query.shape[0]
    slots = kv.shape[0]
    flops = 4 * HEADS * slots * count * count * HEAD_DIM
    return pl.pallas_call(
        functools.partial(attend_kernel, slots, count),
        out_shape=(
            jax.ShapeDtypeStruct((HQ, count), BF),
            jax.ShapeDtypeStruct((HEADS // 4, 4, count), F32),
        ),
        in_specs=[VMEM, VMEM, VMEM],
        out_specs=(VMEM, VMEM),
        scratch_shapes=[pltpu.VMEM((slots * count, count), F32)],
        compiler_params=params(),
        cost_estimate=pl.CostEstimate(flops=flops * 4, bytes_accessed=4 << 20, transcendentals=0),
    )(query, kv.reshape(slots * count, 2 * HK), lower)


def attend_back_kernel(slots, count, q_ref, kv_ref, lower_ref, gob_ref, lse_ref, delta_ref, gq_ref, gkv_ref, bias):
    scale = HEAD_DIM ** (-0.5)
    fill_bias(bias, lower_ref, slots, count)

    def four_heads(t, carry):
        keys = kv_ref[:, pl.ds(t * 128, 128)]
        values = kv_ref[:, pl.ds(HK + t * 128, 128)]
        queries = q_ref[:, pl.ds(t * 256, 256)]
        lse = lse_ref[t]
        delta = delta_ref[t]
        grad_keys, grad_values = [], []
        for u in range(2):
            key = keys[:, u * 64 : u * 64 + 64]
            value = values[:, u * 64 : u * 64 + 64]
            grad_key, grad_value = 0.0, 0.0
            for g in range(2):
                at, h = u * 128 + g * 64, 2 * u + g
                query = queries[:, at : at + 64]
                gob = gob_ref[pl.ds(t * 256 + at, 64), :]
                probs = jnp.exp(dot(key, query, NT) * scale + bias[...] - lse[h : h + 1, :])
                grad_value = grad_value + dot(probs.astype(BF), gob, NT)
                grad_probs = dot(value, gob, NN)
                grad_scores = (scale * probs * (grad_probs - delta[h : h + 1, :])).astype(BF)
                grad_key = grad_key + dot(grad_scores, query, NN)
                gq_ref[pl.ds(t * 256 + at, 64), :] = dot(key, grad_scores, TN)
            grad_keys.append(grad_key)
            grad_values.append(grad_value)
        gkv_ref[:, pl.ds(t * 128, 128)] = jnp.concatenate(grad_keys, axis=1).astype(BF)
        gkv_ref[:, pl.ds(HK + t * 128, 128)] = jnp.concatenate(grad_values, axis=1).astype(BF)
        return carry

    lax.fori_loop(0, HEADS // 4, four_heads, 0)


def attend_back(query, kv, lower, gob, lse, delta):
    count = query.shape[0]
    slots = kv.shape[0]
    flops = 10 * HEADS * slots * count * count * HEAD_DIM
    gq, gkv = pl.pallas_call(
        functools.partial(attend_back_kernel, slots, count),
        out_shape=(
            jax.ShapeDtypeStruct((HQ, count), F32),
            jax.ShapeDtypeStruct((slots * count, 2 * HK), BF),
        ),
        in_specs=[VMEM] * 6,
        out_specs=(VMEM, VMEM),
        scratch_shapes=[pltpu.VMEM((slots * count, count), F32)],
        compiler_params=params(),
        cost_estimate=pl.CostEstimate(flops=flops * 4, bytes_accessed=8 << 20, transcendentals=0),
    )(query, kv.reshape(slots * count, 2 * HK), lower, gob, lse, delta)
    return gq, gkv.reshape(slots, count, 2 * HK)


def ffn_kernel(
    planes, depth, hn_ref, og_ref, w_any, gn_out, parts_out, grads_out,
    w, hns, hnt, ogt, mid, pair, send_gn, recv_gn, own_gn, stage, wsem, hsem, gsem, osem,
):
    me = Place(planes, depth)
    count, width = hn_ref.shape
    full = w.shape[2]
    ctxs, dps, rows = w_any.shape[0], w_any.shape[1], w_any.shape[3]
    chunk = 384 if full % 384 == 0 else full

    def load(i, carry):
        c, d = i // dps, i % dps
        for m in range(3):
            pltpu.make_async_copy(
                w_any.at[c, d, m], w.at[m, pl.ds((d * ctxs + c) * rows, rows), :], wsem.at[m, i]
            ).start()
        return carry

    lax.fori_loop(0, ctxs * dps, load, 0)
    greet([me.across(o) for o in range(1, planes)])

    def hn_copy(o):
        return remote(hn_ref, hns.at[o], hsem.at[0, o], hsem.at[1, o], {"dp": me.dp ^ o, "ctx": me.ctx})

    def gn_copy(o):
        return remote(send_gn.at[o], recv_gn.at[o], gsem.at[0, o], gsem.at[1, o], {"dp": me.dp ^ o, "ctx": me.ctx})

    for o in range(1, planes):
        hn_copy(o).start()
    hns[0] = hn_ref[...]

    def loaded(i, carry):
        c, d = i // dps, i % dps
        for m in range(3):
            pltpu.make_async_copy(
                w_any.at[c, d, m], w.at[m, pl.ds((d * ctxs + c) * rows, rows), :], wsem.at[m, i]
            ).wait()
        return carry

    lax.fori_loop(0, ctxs * dps, loaded, 0)

    def block(o, carry):
        @pl.when(o > 0)
        def _():
            hn_copy(o).wait_recv()

        hn = hns[o]
        og = og_ref[o]
        hnt[:, pl.ds(pl.multiple_of(o * count, 128), count)] = hn.T
        ogt[:, pl.ds(pl.multiple_of(o * count, 128), count)] = og.T
        own_gn[0] = jnp.zeros((count, width), F32)
        own_gn[1] = jnp.zeros((count, width), F32)
        at = pl.ds(pl.multiple_of(o * count, 128), count)

        def part(j, inner):
            cols = pl.ds(pl.multiple_of(j * chunk, 128), chunk)
            w_gate, w_up, w_down = w[0, :, cols], w[1, :, cols], w[2, :, cols]
            gate = dot(hn, w_gate, NN)
            upper = dot(hn, w_up, NN)
            sigma = 1.0 / (1.0 + jnp.exp(-gate))
            active = gate * sigma
            middle = (active * upper).astype(BF)
            gmid = dot(og, w_down, NN)
            ggate = (gmid * upper * sigma * (1.0 + gate * (1.0 - sigma))).astype(BF)
            gupper = (gmid * active).astype(BF)
            mid[at, cols] = middle
            pair[0, at, cols] = ggate
            pair[1, at, cols] = gupper
            own_gn[0] += dot(ggate, w_gate, NT) + dot(gupper, w_up, NT)
            own_gn[1] += dot(middle, w_down, NT)
            return inner

        lax.fori_loop(0, full // chunk, part, 0)
        parts_out[o] = own_gn[1].astype(BF)

        @pl.when(o > 0)
        def _():
            send_gn[o] = own_gn[0].astype(BF)
            gn_copy(o).start()

        @pl.when(o == 0)
        def _():
            gn_out[...] = own_gn[0]

        return carry

    lax.fori_loop(0, planes, block, 0)

    strip = ctxs * rows

    def out_copy(m, d):
        return pltpu.make_async_copy(stage.at[m], grads_out.at[d, m], osem.at[m])

    def weight_grads(d, carry):
        left = pl.ds(pl.multiple_of(d * strip, 128), strip)
        for m in range(3):
            @pl.when(d > 0)
            def _():
                out_copy(m, d - 1).wait()

            if m == 2:
                total = dot(ogt[left, :], mid[...], NN)
            else:
                total = dot(hnt[left, :], pair[m], NN)
            stage[m] = total.astype(BF)
            out_copy(m, d).start()
        return carry

    lax.fori_loop(0, dps, weight_grads, 0)
    for m in range(3):
        out_copy(m, dps - 1).wait()
    total = gn_out[...]
    for o in range(1, planes):
        gn_copy(o).wait_recv()
        total = total + recv_gn[o].astype(F32)
    gn_out[...] = total
    for o in range(1, planes):
        gn_copy(o).wait_send()
        hn_copy(o).wait_send()


def ffn(hn, og_all, w_all, planes, depth, collective_id):
    count, width = hn.shape
    ctxs, dps, _, rows, full = w_all.shape
    tokens = planes * count
    strip = ctxs * rows
    flops = 18 * tokens * width * full
    return pl.pallas_call(
        functools.partial(ffn_kernel, planes, depth),
        out_shape=(
            jax.ShapeDtypeStruct((count, width), F32),
            jax.ShapeDtypeStruct((planes, count, width), BF),
            jax.ShapeDtypeStruct((dps, 3, strip, full), BF),
        ),
        in_specs=[VMEM, VMEM, ANY],
        out_specs=(VMEM, VMEM, ANY),
        scratch_shapes=[
            pltpu.VMEM((3, width, full), BF),
            pltpu.VMEM((planes, count, width), BF),
            pltpu.VMEM((width, tokens), BF),
            pltpu.VMEM((width, tokens), BF),
            pltpu.VMEM((tokens, full), BF),
            pltpu.VMEM((2, tokens, full), BF),
            pltpu.VMEM((planes, count, width), BF),
            pltpu.VMEM((planes, count, width), BF),
            pltpu.VMEM((2, count, width), F32),
            pltpu.VMEM((3, strip, full), BF),
            DMA((3, ctxs * dps)),
            DMA((2, planes)),
            DMA((2, planes)),
            DMA((3,)),
        ],
        compiler_params=params(collective_id),
        cost_estimate=pl.CostEstimate(flops=flops, bytes_accessed=20 << 20, transcendentals=0),
    )(hn, og_all, w_all)


def give_back_kernel(
    planes, depth, turns, d_ref, parts_ref, mixed_ref, kv_out, block_out, dsum, from_core, from_z, from_plane, cs, zs, ps
):
    me = Place(planes, depth)
    half = turns // 2
    greet(
        [me.across(o) for o in range(1, planes)]
        + [me.along(me.ahead(k)) for k in range(1, depth)]
        + [me.sibling()]
    )

    def c_copy(i):
        return remote(d_ref.at[2 * i + 1], from_core.at[i], cs.at[0, i], cs.at[1, i], me.sibling())

    def z_copy(k):
        return remote(dsum.at[k], from_z.at[k], zs.at[0, k], zs.at[1, k], me.along(me.behind(k)))

    def p_copy(o):
        return remote(parts_ref.at[o], from_plane.at[o], ps.at[0, o], ps.at[1, o], me.across(o))

    for i in range(half):
        @pl.when(me.z - i - 1 + me.core >= 0)
        def _():
            c_copy(i).start()

    for o in range(1, planes):
        p_copy(o).start()

    for k in range(half, 0, -1):
        @pl.when(me.z - k >= 0)
        def _():
            @pl.when(me.core == 0)
            def _():
                if k < half:
                    c_copy(k).wait_recv()
                    dsum[k] = (d_ref[2 * k].astype(F32) + from_core[min(k, half - 1)].astype(F32)).astype(BF)
                else:
                    dsum[k] = d_ref[2 * k]

            @pl.when(me.core == 1)
            def _():
                c_copy(k - 1).wait_recv()
                dsum[k] = (d_ref[2 * k].astype(F32) + from_core[k - 1].astype(F32)).astype(BF)

            z_copy(k).start()

    kv_out[...] = d_ref[0].astype(F32)

    @pl.when(me.core == 0)
    def _():
        c_copy(0).wait_recv()
        kv_out[...] += from_core[0].astype(F32)

    for k in range(1, half + 1):
        @pl.when(me.z + k < depth)
        def _():
            z_copy(k).wait_recv()
            kv_out[...] += from_z[k].astype(F32)

    total = mixed_ref[...] + parts_ref[0].astype(F32)
    for o in range(1, planes):
        p_copy(o).wait_recv()
        total = total + from_plane[o].astype(F32)
    block_out[...] = total.astype(BF)

    for o in range(1, planes):
        p_copy(o).wait_send()
    for i in range(half):
        @pl.when(me.z - i - 1 + me.core >= 0)
        def _():
            c_copy(i).wait_send()
    for k in range(1, half + 1):
        @pl.when(me.z - k >= 0)
        def _():
            z_copy(k).wait_send()


def give_back(gkv, parts, mixed, planes, depth, collective_id):
    slots, count, width = gkv.shape
    half = (slots - 1) // 2
    return pl.pallas_call(
        functools.partial(give_back_kernel, planes, depth, slots - 1),
        out_shape=(
            jax.ShapeDtypeStruct((count, width), F32),
            jax.ShapeDtypeStruct((count, D), BF),
        ),
        in_specs=[VMEM, VMEM, VMEM],
        out_specs=(VMEM, VMEM),
        scratch_shapes=[
            pltpu.VMEM((half + 1, count, width), BF),
            pltpu.VMEM((half, count, width), BF),
            pltpu.VMEM((half + 1, count, width), BF),
            pltpu.VMEM((planes, count, D), BF),
            DMA((2, half)),
            DMA((2, half + 1)),
            DMA((2, planes)),
        ],
        compiler_params=params(collective_id),
    )(gkv, parts, mixed)


def scatter_kernel(planes, depth, p_ref, out_ref, from_core, sums, from_plane, total, from_z, cs, ps, zs):
    me = Place(planes, depth)
    greet(
        [me.across(o) for o in range(1, planes)]
        + [me.along(me.ahead(k)) for k in range(1, depth)]
        + [me.sibling()]
    )

    def c_copy(o):
        return remote(
            p_ref.at[me.dp ^ o, 1 - me.core], from_core.at[o], cs.at[0, o], cs.at[1, o], me.sibling()
        )

    def p_copy(o):
        return remote(sums.at[o], from_plane.at[o], ps.at[0, o], ps.at[1, o], me.across(o))

    def z_copy(k):
        return remote(total.at[me.ahead(k)], from_z.at[k], zs.at[0, k], zs.at[1, k], me.along(me.ahead(k)))

    order = list(range(1, planes)) + [0]
    for o in order:
        c_copy(o).start()
    for o in order:
        c_copy(o).wait_recv()
        sums[o] = (p_ref[me.dp ^ o, me.core].astype(F32) + from_core[o].astype(F32)).astype(BF)
        if o > 0:
            p_copy(o).start()
    for o in range(1, planes):
        p_copy(o).wait_recv()
    for k in range(depth):
        z = me.ahead(k)
        value = sums[0, z].astype(F32)
        for o in range(1, planes):
            value = value + from_plane[o, z].astype(F32)
        total[z] = value.astype(BF)
        if k > 0:
            z_copy(k).start()
        else:
            out_ref[...] = value
    for k in range(1, depth):
        z_copy(k).wait_recv()
        out_ref[...] += from_z[k].astype(F32)
    for o in range(planes):
        c_copy(o).wait_send()
    for o in range(1, planes):
        p_copy(o).wait_send()
    for k in range(1, depth):
        z_copy(k).wait_send()


def scatter_all(partial, planes, depth, collective_id):
    rows, columns = partial.shape[3:]
    return pl.pallas_call(
        functools.partial(scatter_kernel, planes, depth),
        out_shape=jax.ShapeDtypeStruct((rows, columns), F32),
        in_specs=[VMEM],
        out_specs=VMEM,
        scratch_shapes=[
            pltpu.VMEM((planes, depth, rows, columns), BF),
            pltpu.VMEM((planes, depth, rows, columns), BF),
            pltpu.VMEM((planes, depth, rows, columns), BF),
            pltpu.VMEM((depth, rows, columns), BF),
            pltpu.VMEM((depth, rows, columns), BF),
            DMA((2, planes)),
            DMA((2, planes)),
            DMA((2, depth)),
        ],
        compiler_params=params(collective_id),
    )(partial)


def per_device(
    tokens_in,
    positions,
    out_grad,
    w_qkv,
    w_output,
    w_gate_up,
    w_down,
    norm_gains,
    first_qkv,
    first_output,
    first_gate_up,
    first_down,
    first_gains,
    second_qkv,
    second_output,
    second_gate_up,
    second_down,
    second_gains,
):
    planes, ctxs = lax.axis_size("dp"), lax.axis_size("ctx")
    depth = ctxs // 2
    turns = ctxs // 2
    rows = w_qkv.shape[0]
    full = w_down.shape[1] // planes
    n_gains = norm_gains.shape[0]
    count = tokens_in.shape[0] * tokens_in.shape[1]

    w_blocks = jnp.concatenate(
        [
            w_gate_up.astype(BF).reshape(rows, 2, planes, full).transpose(2, 1, 0, 3),
            w_down.astype(BF).reshape(rows, 1, planes, full).transpose(2, 1, 0, 3),
        ],
        axis=1,
    )
    w_mine = plane_exchange(w_blocks, planes, depth, 0)
    w_all = lax.all_gather(w_mine, "ctx", axis=0, tiled=False)

    gains_row = jnp.pad(norm_gains.astype(BF)[None, :], ((0, rows - 1), (0, 128 - n_gains)))
    front = gather_all(
        jnp.concatenate([w_qkv.astype(BF), gains_row], axis=1), planes, depth, 1
    )
    qkv_b = front.reshape(D, 2 * HQ + 128)[:, : 2 * HQ]
    gains_b = front[:, :, :, 0, 2 * HQ : 2 * HQ + n_gains].reshape(-1)
    gains_used = 1.0 + gains_b.astype(F32)
    gain_ffn = split_gains(gains_used)[1]
    tokens_f = tokens_in.reshape(count, D).astype(F32)
    places = positions.reshape(count)
    cotangent = out_grad.reshape(count, D)
    query_b, key_b, value_b, saved = front_pass(tokens_f, places, qkv_b, gains_used)
    query = query_b.reshape(count, HQ)
    kv = jnp.concatenate([key_b.reshape(count, HK), value_b.reshape(count, HK)], axis=1)
    kv_all, og_all, wo_all = halo(kv, cotangent, w_output.astype(BF), planes, depth, turns, 2)
    output_b = wo_all.reshape(HQ, D)
    lower = (jnp.arange(count, dtype=jnp.int32) - places)[None, :]
    attn_t, lse = attend(query, kv_all, lower)
    mixed = tokens_f + dot(attn_t, output_b, TN)
    normed, unit_f, recip_f = norm_forward(mixed, gain_ffn)
    ffn_in = normed.astype(BF)
    if rows % 16 == 0:
        w_used = w_all
    else:
        w_used = w_all.transpose(2, 1, 0, 3, 4).reshape(1, 1, 3, D, full)
    grad_normed, parts, grads = ffn(ffn_in, og_all, w_used, planes, depth, 3)
    grads = grads.reshape(planes, 3, ctxs, rows, full) if rows % 16 == 0 else grads.reshape(3, planes, ctxs, rows, full).transpose(1, 0, 2, 3, 4)
    grads_mine = lax.psum_scatter(
        grads.transpose(2, 0, 1, 3, 4), "ctx", scatter_dimension=0, tiled=False
    )

    grad_from_norm, grad_gain_ffn = norm_backward(grad_normed, gain_ffn, unit_f, recip_f)
    grad_mixed = cotangent.astype(F32) + grad_from_norm
    grad_mixed_b = grad_mixed.astype(BF)
    grad_output = dot(attn_t, grad_mixed_b, NN)
    gob_t = dot(output_b, grad_mixed_b, NT).astype(BF)
    delta = jnp.sum(
        (gob_t.astype(F32) * attn_t.astype(F32)).reshape(HEADS // 4, 4, HEAD_DIM, count), axis=2
    )
    gq_t, gkv_all = attend_back(query, kv_all, lower, gob_t, lse, delta)
    grad_kv, block_out = give_back(gkv_all, parts, mixed, planes, depth, 4)
    input_grad, grad_qkv, grad_gain_attn, grad_gain_q, grad_gain_k = tail_pass(
        gq_t.T.reshape(count, HEADS, HEAD_DIM),
        grad_kv[:, :HK].reshape(count, KV_HEADS, HEAD_DIM),
        grad_kv[:, HK:].reshape(count, KV_HEADS, HEAD_DIM),
        saved,
        gains_used,
        qkv_b,
        grad_mixed,
    )
    grad_gains = jnp.concatenate([grad_gain_attn, grad_gain_ffn, grad_gain_q, grad_gain_k])
    gains_block = jnp.pad(
        grad_gains.astype(BF).reshape(planes * ctxs, 1, n_gains), ((0, 0), (0, rows - 1), (0, 128 - n_gains))
    ).reshape(D, 128)
    partial = jnp.concatenate([grad_qkv.astype(BF), grad_output.astype(BF), gains_block], axis=1)
    partial = partial.reshape(planes, depth, 2, rows, 3 * D + 128).transpose(0, 2, 1, 3, 4)
    mine = scatter_all(partial, planes, depth, 5)
    shard_qkv = mine[:, : 2 * D]
    shard_output = mine[:, 2 * D : 3 * D]
    shard_gains = mine[0, 3 * D : 3 * D + n_gains]

    ffn_shards = plane_exchange(grads_mine, planes, depth, 6).astype(F32)
    shard_gate_up = ffn_shards[:, :2].transpose(2, 1, 0, 3).reshape(rows, 2 * planes * full)
    shard_down = ffn_shards[:, 2].transpose(1, 0, 2).reshape(rows, planes * full)

    new_qkv, new_first_qkv, new_second_qkv = adam_step(
        w_qkv, shard_qkv, first_qkv, second_qkv, 0.02, 0.1
    )
    new_output, new_first_output, new_second_output = adam_step(
        w_output, shard_output, first_output, second_output, 0.2, 0.1
    )
    new_gate_up, new_first_gate_up, new_second_gate_up = adam_step(
        w_gate_up, shard_gate_up, first_gate_up, second_gate_up, 0.02, 0.1
    )
    new_down, new_first_down, new_second_down = adam_step(
        w_down, shard_down, first_down, second_down, 0.02, 0.1
    )
    new_gains, new_first_gains, new_second_gains = adam_step(
        norm_gains, shard_gains, first_gains, second_gains, 0.1, 0.0
    )
    return (
        block_out.reshape(tokens_in.shape),
        input_grad.reshape(tokens_in.shape),
        shard_qkv,
        shard_output,
        shard_gate_up,
        shard_down,
        shard_gains,
        new_qkv,
        new_output,
        new_gate_up,
        new_down,
        new_gains,
        new_first_qkv,
        new_first_output,
        new_first_gate_up,
        new_first_down,
        new_first_gains,
        new_second_qkv,
        new_second_output,
        new_second_gate_up,
        new_second_down,
        new_second_gains,
    )


def solution(mesh):
    in_specs = (
        P("dp", "ctx", None),
        P("dp", "ctx"),
        P("dp", "ctx", None),
        P(("dp", "ctx"), None),
        P(("dp", "ctx"), None),
        P(("dp", "ctx"), None),
        P(("dp", "ctx"), None),
        P(("dp", "ctx")),
        P(("dp", "ctx"), None),
        P(("dp", "ctx"), None),
        P(("dp", "ctx"), None),
        P(("dp", "ctx"), None),
        P(("dp", "ctx")),
        P(("dp", "ctx"), None),
        P(("dp", "ctx"), None),
        P(("dp", "ctx"), None),
        P(("dp", "ctx"), None),
        P(("dp", "ctx")),
    )
    out_specs = (
        P("dp", "ctx", None),
        P("dp", "ctx", None),
        P(("dp", "ctx"), None),
        P(("dp", "ctx"), None),
        P(("dp", "ctx"), None),
        P(("dp", "ctx"), None),
        P(("dp", "ctx")),
        P(("dp", "ctx"), None),
        P(("dp", "ctx"), None),
        P(("dp", "ctx"), None),
        P(("dp", "ctx"), None),
        P(("dp", "ctx")),
        P(("dp", "ctx"), None),
        P(("dp", "ctx"), None),
        P(("dp", "ctx"), None),
        P(("dp", "ctx"), None),
        P(("dp", "ctx")),
        P(("dp", "ctx"), None),
        P(("dp", "ctx"), None),
        P(("dp", "ctx"), None),
        P(("dp", "ctx"), None),
        P(("dp", "ctx")),
    )
    return jax.shard_map(
        per_device, mesh=mesh, in_specs=in_specs, out_specs=out_specs, check_vma=False
    )
```

```python
import functools
import math

import jax
import jax.numpy as jnp
from jax import lax
from jax.experimental import pallas as pl
from jax.experimental.pallas import tpu as pltpu
from jax.sharding import PartitionSpec as P

D = 1024
HEADS = 16
KV_HEADS = 8
HEAD_DIM = 64
STEP = 4
HQ = 1024
HK = 512


EPS = 1e-05
THETA = 1000000.0
NEG_BIG = -1e30
BETA_ONE = 0.9
BETA_TWO = 0.95
ADAM_EPS = 1e-08


def rope_tables(places):
    half = HEAD_DIM // 2
    freqs = jnp.exp(-math.log(THETA) * (2.0 * jnp.arange(half, dtype=jnp.float32) / HEAD_DIM))
    angles = freqs[:, None] * places.astype(jnp.float32)[None, :]
    return (jnp.cos(angles), jnp.sin(angles))


def adam_step(weight, grad, first, second, rate, decay):
    first_new = BETA_ONE * first + (1.0 - BETA_ONE) * grad
    second_new = BETA_TWO * second + (1.0 - BETA_TWO) * grad * grad
    first_hat = first_new / (1.0 - BETA_ONE**STEP)
    second_hat = second_new / (1.0 - BETA_TWO**STEP)
    weight_new = weight - rate * (first_hat / (jnp.sqrt(second_hat) + ADAM_EPS) + decay * weight)
    return (weight_new, first_new, second_new)


BF = jnp.bfloat16
F32 = jnp.float32
MESH_ID = pl.DeviceIdType.MESH
ANY = pl.BlockSpec(memory_space=pl.ANY)
VMEM = pl.BlockSpec(memory_space=pltpu.VMEM)
DMA = pltpu.SemaphoreType.DMA
NN = (((1,), (0,)), ((), ()))
NT = (((1,), (1,)), ((), ()))
TN = (((0,), (0,)), ((), ()))
VMEM_BYTES = 60 << 20
GROUPS = HEADS // 4


def dot(a, b, dims):
    return lax.dot_general(a, b, dims, preferred_element_type=F32)


class Place:
    def __init__(self, planes, depth):
        self.planes, self.depth = planes, depth
        self.dp = lax.axis_index("dp")
        self.ctx = lax.axis_index("ctx")
        self.z = self.ctx // 2
        self.core = self.ctx % 2

    def sibling(self):
        return {"dp": self.dp, "ctx": self.z * 2 + 1 - self.core}

    def across(self, o):
        return {"dp": self.dp ^ o, "ctx": self.ctx}

    def behind(self, k):
        return lax.rem(self.z + self.depth - k, self.depth)

    def ahead(self, k):
        return lax.rem(self.z + k, self.depth)

    def along(self, z):
        return {"dp": self.dp, "ctx": z * 2 + self.core}

    def plane(self):
        return [self.across(o) for o in range(1, self.planes)]

    def line(self):
        return [self.along(self.ahead(k)) for k in range(1, self.depth)]


def greet(devices):
    barrier = pltpu.get_barrier_semaphore()
    for device in devices:
        pl.semaphore_signal(barrier, inc=1, device_id=device, device_id_type=MESH_ID)
    pl.semaphore_wait(barrier, len(devices))


def remote(src, dst, send, recv, device):
    return pltpu.make_async_remote_copy(
        src_ref=src, dst_ref=dst, send_sem=send, recv_sem=recv, device_id=device, device_id_type=MESH_ID
    )


def params(collective_id):
    return pltpu.CompilerParams(
        vmem_limit_bytes=VMEM_BYTES, collective_id=collective_id, has_side_effects=True
    )


def exchange_kernel(planes, depth, counts, *refs):
    n_plane, n_line = counts
    n = n_plane + n_line
    ins, outs, (send, recv, local) = refs[:n], refs[n : 2 * n], refs[2 * n :]
    me = Place(planes, depth)
    owns, copies, waits = [], [], []
    for i in range(n):
        if i < n_plane:
            own = pltpu.make_async_copy(ins[i].at[me.dp], outs[i].at[me.dp], local.at[i])
        else:
            own = pltpu.make_async_copy(ins[i], outs[i].at[me.z], local.at[i])
        own.start()
        owns.append(own)
    greet(me.plane() + (me.line() if n_line else []))
    for i in range(n_plane, n):
        for k in range(1, depth):
            sems = (send.at[i, k], recv.at[i, k])
            copies.append(remote(ins[i], outs[i].at[me.z], *sems, me.along(me.ahead(k))))
            waits.append(remote(ins[i], outs[i].at[me.behind(k)], *sems, me.along(me.ahead(k))))
    for o in range(1, planes):
        for i in range(n_plane):
            sems = (send.at[i, o], recv.at[i, o])
            copies.append(remote(ins[i].at[me.dp ^ o], outs[i].at[me.dp], *sems, me.across(o)))
            waits.append(remote(ins[i].at[me.dp], outs[i].at[me.dp ^ o], *sems, me.across(o)))
    for copy in copies:
        copy.start()
    for own in owns:
        own.wait()
    for copy in copies:
        copy.wait_send()
    for wait in waits:
        wait.wait_recv()


def exchange(plane_arrays, line_arrays, planes, depth, collective_id):
    counts = (len(plane_arrays), len(line_arrays))
    n = sum(counts)
    most = max(planes, depth)
    shapes = [jax.ShapeDtypeStruct(a.shape, a.dtype) for a in plane_arrays]
    shapes += [jax.ShapeDtypeStruct((depth,) + a.shape, a.dtype) for a in line_arrays]
    return pl.pallas_call(
        functools.partial(exchange_kernel, planes, depth, counts),
        out_shape=tuple(shapes),
        in_specs=[ANY] * n,
        out_specs=(ANY,) * n,
        scratch_shapes=[DMA((n, most)), DMA((n, most)), DMA((n,))],
        compiler_params=params(collective_id),
    )(*plane_arrays, *line_arrays)


class Spread:
    def __init__(self, me, x_ref, g_ref, sems):
        self.me, self.x, self.g, self.sems = me, x_ref, g_ref, sems
        self.sent = []

    def push(self, src, dst, kind, o, device):
        copy = remote(src, dst, self.sems.at[kind, o], self.sems.at[kind + 1, o], device)
        copy.start()
        self.sent.append(copy)

    def mine(self, o, core):
        return self.g.at[self.me.dp ^ o, :, core]

    def start(self):
        me = self.me
        self.own = pltpu.make_async_copy(self.x, self.mine(0, me.core), self.sems.at[4, 0])
        self.own.start()

    def first(self):
        me = self.me
        for o in range(1, me.planes):
            self.push(self.x, self.mine(0, me.core), 0, o, me.across(o))
        self.push(self.x, self.mine(0, me.core), 2, 0, me.sibling())

    def relay(self, o):
        block = self.mine(o, self.me.core)
        remote(block, block, self.sems.at[0, o], self.sems.at[1, o], self.me.sibling()).wait_recv()
        self.push(block, block, 2, o, self.me.sibling())

    def arrive(self, o):
        block = self.mine(o, 1 - self.me.core)
        remote(block, block, self.sems.at[2, o], self.sems.at[3, o], self.me.sibling()).wait_recv()
        if o == 0:
            self.own.wait()

    def finish(self):
        for copy in self.sent:
            copy.wait_send()


def spread_sems(planes):
    return DMA((5, planes))


class Collect:
    def __init__(self, me, p_ref, scratch):
        self.me, self.p = me, p_ref
        self.from_core, self.sums, self.from_plane, self.total, self.from_z, self.cs, self.ps, self.zs = scratch

    def c_copy(self, o):
        me = self.me
        return remote(
            self.p.at[me.dp ^ o, :, 1 - me.core], self.from_core.at[o], self.cs.at[0, o], self.cs.at[1, o], me.sibling()
        )

    def p_copy(self, o):
        return remote(
            self.sums.at[o], self.from_plane.at[o], self.ps.at[0, o], self.ps.at[1, o], self.me.across(o)
        )

    def z_copy(self, k):
        me = self.me
        return remote(
            self.total.at[me.ahead(k)], self.from_z.at[k], self.zs.at[0, k], self.zs.at[1, k], me.along(me.ahead(k))
        )

    def first(self, o):
        self.c_copy(o).start()

    def second(self, o):
        me = self.me
        self.c_copy(o).wait_recv()
        own = self.p[me.dp ^ o, :, me.core].astype(F32)
        self.sums[o] = (own + self.from_core[o].astype(F32)).astype(self.sums.dtype)
        if o > 0:
            self.p_copy(o).start()

    def third(self):
        me = self.me
        for o in range(1, me.planes):
            self.p_copy(o).wait_recv()
        for k in list(range(1, me.depth)) + [0]:
            z = me.ahead(k)
            value = self.sums[0, z].astype(F32)
            for o in range(1, me.planes):
                value = value + self.from_plane[o, z].astype(F32)
            self.total[z] = value.astype(self.total.dtype)
            if k > 0:
                self.z_copy(k).start()
        return value

    def last(self, value):
        for k in range(1, self.me.depth):
            self.z_copy(k).wait_recv()
            value = value + self.from_z[k].astype(F32)
        return value

    def finish(self):
        for o in range(self.me.planes):
            self.c_copy(o).wait_send()
        for o in range(1, self.me.planes):
            self.p_copy(o).wait_send()
        for k in range(1, self.me.depth):
            self.z_copy(k).wait_send()


def collect_scratch(planes, depth, rows, columns, kind):
    return [
        pltpu.VMEM((planes, depth, rows, columns), kind),
        pltpu.VMEM((planes, depth, rows, columns), kind),
        pltpu.VMEM((planes, depth, rows, columns), kind),
        pltpu.VMEM((depth, rows, columns), kind),
        pltpu.VMEM((depth, rows, columns), kind),
        DMA((2, planes)),
        DMA((2, planes)),
        DMA((2, depth)),
    ]


COLLECT = 8


def unit_of(values, axis):
    recip = lax.rsqrt(jnp.mean(values * values, axis=axis, keepdims=True) + EPS)
    return values * recip, recip


def column_of(row, start):
    lane = lax.broadcasted_iota(jnp.int32, (HEAD_DIM, 128), 1)
    entry = lax.broadcasted_iota(jnp.int32, (HEAD_DIM, 128), 0)
    return jnp.sum(jnp.where(lane == entry + start, row, 0.0), axis=1, keepdims=True)


def turned(values, cosine, sine):
    half = HEAD_DIM // 2
    a, b = values[:half], values[half:]
    return jnp.concatenate([a * cosine - b * sine, b * cosine + a * sine], axis=0)


def front_kernel(
    planes, depth, n_gains, tok_ref, cos_ref, sin_ref, x_ref, gain_ref,
    q_out, kv_out, w_out, xat_out, unit_out, recip_out, gains_out,
    gains_g, xa, xa_plain, proj, wsem, gsem,
):
    me = Place(planes, depth)
    count = tok_ref.shape[0]
    half = D // planes
    gains = Spread(me, gain_ref, gains_g, gsem)
    weights = Spread(me, x_ref, w_out, wsem)
    gains.start()
    weights.start()
    greet(me.plane() + [me.sibling()])
    gains.first()
    weights.first()
    unit, _ = unit_of(tok_ref[...].astype(F32), 1)
    xa_plain[...] = unit
    for o in range(1, planes):
        gains.relay(o)
    for o in range(planes):
        gains.arrive(o)
    devices = planes * depth * 2
    table = gains_g[...].reshape(devices, 8, 128)[:, 0, :].astype(BF)
    entries = devices * n_gains
    index = lax.broadcasted_iota(jnp.int32, (128, entries), 1)
    pick = jnp.where(
        index % n_gains == lax.broadcasted_iota(jnp.int32, (128, entries), 0), 1.0, 0.0
    ).astype(BF)
    spread = dot(table, pick, NN)
    owner = lax.broadcasted_iota(jnp.int32, (devices, entries), 1) // n_gains
    device = lax.broadcasted_iota(jnp.int32, (devices, entries), 0)
    gains_row = 1.0 + jnp.sum(jnp.where(owner == device, spread, 0.0), axis=0, keepdims=True)
    gains_out[...] = gains_row
    normed = (xa_plain[...] * gains_row[:, :D]).astype(BF)
    xat_out[...] = normed.T
    for d in range(planes):
        xa[d] = normed[:, d * half : (d + 1) * half]
    proj[...] = jnp.zeros_like(proj)
    for o in [0] + list(range(1, planes)):
        if o > 0:
            weights.relay(o)
        weights.arrive(o)
        rows = w_out[me.dp ^ o].reshape(half, 2 * HQ)
        piece = xa[me.dp ^ o]
        proj[...] += dot(piece, rows, NN)
    tail_row = gains_row[:, 2 * D : 2 * D + 128]
    gain_q, gain_k = column_of(tail_row, 0), column_of(tail_row, HEAD_DIM)
    cosine, sine = cos_ref[...], sin_ref[...]
    for h in range(0, HEADS + KV_HEADS, 4):
        four = proj[:, h * HEAD_DIM : (h + 4) * HEAD_DIM].T
        results, recips = [], []
        for i in range(4):
            value, recip = unit_of(four[i * HEAD_DIM : (i + 1) * HEAD_DIM], 0)
            unit_out[pl.ds((h + i) * HEAD_DIM, HEAD_DIM), :] = value
            recips.append(recip)
            results.append(turned(value * (gain_q if h < HEADS else gain_k), cosine, sine))
        recip_out[h // 4] = jnp.concatenate(recips, axis=0)
        block = jnp.concatenate(results, axis=0)
        if h < HEADS:
            q_out[pl.ds(h * HEAD_DIM, 4 * HEAD_DIM), :] = (block * HEAD_DIM ** (-0.5)).astype(BF)
        else:
            kv_out[:, pl.ds((h - HEADS) * HEAD_DIM, 4 * HEAD_DIM)] = block.T.astype(BF)
    kv_out[:, pl.ds(HK, HK)] = proj[:, HQ + HK :].astype(BF)
    gains.finish()
    weights.finish()


def front(tokens, cosine, sine, x_line, gains_line, n_gains, planes, depth, collective_id):
    count = tokens.shape[0]
    rows, columns = x_line.shape[1:]
    return pl.pallas_call(
        functools.partial(front_kernel, planes, depth, n_gains),
        out_shape=(
            jax.ShapeDtypeStruct((HQ, count), BF),
            jax.ShapeDtypeStruct((count, 2 * HK), BF),
            jax.ShapeDtypeStruct((planes, depth, 2, rows, columns), BF),
            jax.ShapeDtypeStruct((D, count), BF),
            jax.ShapeDtypeStruct((HQ + HK, count), F32),
            jax.ShapeDtypeStruct(((HEADS + KV_HEADS) // 4, 4, count), F32),
            jax.ShapeDtypeStruct((1, planes * depth * 2 * n_gains), F32),
        ),
        in_specs=[VMEM] * 5,
        out_specs=(VMEM,) * 7,
        scratch_shapes=[
            pltpu.VMEM((planes, depth, 2, 8, 128), F32),
            pltpu.VMEM((planes, count, D // planes), BF),
            pltpu.VMEM((count, D), F32),
            pltpu.VMEM((count, 2 * HQ), F32),
            spread_sems(planes),
            spread_sems(planes),
        ],
        compiler_params=params(collective_id),
        cost_estimate=pl.CostEstimate(flops=40 << 30, bytes_accessed=8 << 20, transcendentals=0),
    )(tokens, cosine, sine, x_line, gains_line)


def fill_bias(bias, lower, slot):
    count = bias.shape[0]
    query = lax.broadcasted_iota(jnp.int32, (count, count), 1)
    key = lax.broadcasted_iota(jnp.int32, (count, count), 0) - slot * count
    bias[...] = jnp.where((key <= query) & (key >= lower), 0.0, NEG_BIG)


def attend_kernel(
    planes, depth, turns, kv_ref, og_ref, wo_ref, q_ref, lower_ref, tok_ref, gains_ref,
    kv_all, og_all, wo_all, o_out, lse_out, mixed_out, hn_out,
    bias, accum, sums, local, zs, cs, ps, wsem,
):
    me = Place(planes, depth)
    half = turns // 2
    count = kv_ref.shape[0]
    weights = Spread(me, wo_ref, wo_all, wsem)
    weights.start()
    own_kv = pltpu.make_async_copy(kv_ref, kv_all.at[0], local.at[0])
    own_kv.start()
    own_og = pltpu.make_async_copy(og_ref, og_all.at[0], local.at[1])
    own_og.start()
    greet(me.plane() + me.line() + [me.sibling()])

    def z_copy(k):
        return remote(kv_ref, kv_all.at[2 * k], zs.at[0, k], zs.at[1, k], me.along(me.ahead(k)))

    def c_copy(i):
        return remote(
            kv_all.at[2 * i + 2 * me.core], kv_all.at[2 * i + 1], cs.at[0, i], cs.at[1, i], me.sibling()
        )

    for k in range(1, half + 1):
        @pl.when(me.z + k < depth)
        def _():
            z_copy(k).start()

    own_kv.wait()

    @pl.when(me.core == 0)
    def _():
        c_copy(0).start()

    weights.first()
    shares = []
    for o in range(1, planes):
        share = remote(og_ref, og_all.at[o], ps.at[0, o], ps.at[1, o], me.across(o))
        share.start()
        shares.append(share)
    accum[...] = jnp.zeros_like(accum)
    sums[...] = jnp.zeros_like(sums)

    def visit(slot):
        fill_bias(bias, lower_ref[...], slot)

        def four_heads(t, carry):
            keys = kv_all[slot, :, pl.ds(pl.multiple_of(t * 128, 128), 128)]
            values = kv_all[slot, :, pl.ds(pl.multiple_of(HK + t * 128, 128), 128)]
            totals = []
            for u in range(2):
                key = keys[:, u * 64 : u * 64 + 64]
                value = values[:, u * 64 : u * 64 + 64]
                for g in range(2):
                    at = pl.ds(pl.multiple_of(t * 256 + u * 128 + g * 64, 64), 64)
                    weight = jnp.exp(dot(key, q_ref[at, :], NN) + bias[...])
                    totals.append(jnp.sum(weight, axis=0, keepdims=True))
                    accum[at, :] += dot(value, weight.astype(BF), TN)
            sums[t] += jnp.concatenate(totals, axis=0)
            return carry

        lax.fori_loop(0, GROUPS, four_heads, 0)

    visit(0)
    for k in range(1, half + 1):
        there = me.z - k >= 0

        @pl.when(there)
        def _():
            z_copy(k).wait_recv()

        @pl.when(there & (me.core == 1))
        def _():
            c_copy(k - 1).start()

        if k < half:
            @pl.when(there & (me.core == 0))
            def _():
                c_copy(k).start()

        @pl.when(there)
        def _():
            visit(2 * k)

        @pl.when(me.z - k < 0)
        def _():
            fill = pltpu.make_async_copy(kv_ref, kv_all.at[2 * k], local.at[2])
            fill.start()
            fill.wait()

    for i in range(half):
        @pl.when(me.z - i - 1 + me.core >= 0)
        def _():
            c_copy(i).wait_recv()
            visit(2 * i + 1)

        @pl.when(me.z - i - 1 + me.core < 0)
        def _():
            fill = pltpu.make_async_copy(kv_ref, kv_all.at[2 * i + 1], local.at[2])
            fill.start()
            fill.wait()

    for o in range(1, planes):
        weights.relay(o)
    for t in range(GROUPS):
        total = sums[t]
        lse_out[t] = jnp.log(total)
        for h in range(4):
            at = pl.ds(t * 256 + h * 64, 64)
            o_out[at, :] = (accum[at, :] / total[h : h + 1, :]).astype(BF)
    for o in range(planes):
        weights.arrive(o)
    mixed = tok_ref[...].astype(F32) + dot(o_out[...].T, wo_all[...].reshape(HQ, D), NN)
    mixed_out[...] = mixed
    unit, _ = unit_of(mixed, 1)
    hn_out[...] = (unit * gains_ref[:, D : 2 * D]).astype(BF)

    for i in range(half):
        @pl.when(me.z - i - me.core >= 0)
        def _():
            c_copy(i).wait_send()

    for k in range(1, half + 1):
        @pl.when(me.z + k < depth)
        def _():
            z_copy(k).wait_send()

    for share in shares:
        share.wait()
    weights.finish()
    own_og.wait()


def attend(kv, cotangent, wo_line, query, lower, tokens, gains_row, planes, depth, turns, collective_id):
    half = turns // 2
    count = kv.shape[0]
    rows, columns = wo_line.shape[1:]
    return pl.pallas_call(
        functools.partial(attend_kernel, planes, depth, turns),
        out_shape=(
            jax.ShapeDtypeStruct((turns + 1,) + kv.shape, BF),
            jax.ShapeDtypeStruct((planes,) + cotangent.shape, BF),
            jax.ShapeDtypeStruct((planes, depth, 2, rows, columns), BF),
            jax.ShapeDtypeStruct((HQ, count), BF),
            jax.ShapeDtypeStruct((GROUPS, 4, count), F32),
            jax.ShapeDtypeStruct((count, D), F32),
            jax.ShapeDtypeStruct((count, D), BF),
        ),
        in_specs=[VMEM] * 7,
        out_specs=(VMEM,) * 7,
        scratch_shapes=[
            pltpu.VMEM((count, count), F32),
            pltpu.VMEM((HQ, count), F32),
            pltpu.VMEM((GROUPS, 4, count), F32),
            DMA((3,)),
            DMA((2, half + 1)),
            DMA((2, half)),
            DMA((2, planes)),
            spread_sems(planes),
        ],
        compiler_params=params(collective_id),
        cost_estimate=pl.CostEstimate(flops=40 << 30, bytes_accessed=8 << 20, transcendentals=0),
    )(kv, cotangent, wo_line, query, lower, tokens, gains_row)


def ffn_kernel(
    planes, depth, hn_ref, og_ref, w_any, gn_out, parts_out, down_out, pair_out,
    w, hns, hnt, ogt, mid, pair, send_gn, recv_gn, own_gn, stage, wsem, hsem, gsem, osem,
):
    me = Place(planes, depth)
    count, width = hn_ref.shape
    full = w.shape[2]
    ctxs, dps, rows = w_any.shape[0], w_any.shape[1], w_any.shape[3]
    chunk = 384 if full % 384 == 0 else full

    def w_copy(i, m):
        c, d = i // dps, i % dps
        return pltpu.make_async_copy(
            w_any.at[c, d, m], w.at[m, pl.ds((d * ctxs + c) * rows, rows), :], wsem.at[m, i]
        )

    def load(i, carry):
        for m in range(3):
            w_copy(i, m).start()
        return carry

    lax.fori_loop(0, ctxs * dps, load, 0)
    greet(me.plane())

    def hn_copy(o):
        return remote(hn_ref, hns.at[o], hsem.at[0, o], hsem.at[1, o], me.across(o))

    def gn_copy(o):
        return remote(send_gn.at[o], recv_gn.at[o], gsem.at[0, o], gsem.at[1, o], me.across(o))

    for o in range(1, planes):
        hn_copy(o).start()
    hns[0] = hn_ref[...]

    def loaded(i, carry):
        for m in range(3):
            w_copy(i, m).wait()
        return carry

    lax.fori_loop(0, ctxs * dps, loaded, 0)

    def block(o, carry):
        @pl.when(o > 0)
        def _():
            hn_copy(o).wait_recv()

        hn = hns[o]
        og = og_ref[o]
        at = pl.ds(pl.multiple_of(o * count, 128), count)
        hnt[:, at] = hn.T
        ogt[:, at] = og.T
        own_gn[0] = jnp.zeros((count, width), F32)
        own_gn[1] = jnp.zeros((count, width), F32)

        def part(j, inner):
            cols = pl.ds(pl.multiple_of(j * chunk, 128), chunk)
            w_gate, w_up, w_down = w[0, :, cols], w[1, :, cols], w[2, :, cols]
            gate = dot(hn, w_gate, NN)
            upper = dot(hn, w_up, NN)
            sigma = 1.0 / (1.0 + jnp.exp(-gate))
            active = gate * sigma
            middle = (active * upper).astype(BF)
            gmid = dot(og, w_down, NN)
            ggate = (gmid * upper * sigma * (1.0 + gate * (1.0 - sigma))).astype(BF)
            gupper = (gmid * active).astype(BF)
            mid[at, cols] = middle
            pair[0, at, cols] = ggate
            pair[1, at, cols] = gupper
            own_gn[0] += dot(ggate, w_gate, NT) + dot(gupper, w_up, NT)
            own_gn[1] += dot(middle, w_down, NT)
            return inner

        lax.fori_loop(0, full // chunk, part, 0)
        parts_out[o] = own_gn[1].astype(BF)

        @pl.when(o > 0)
        def _():
            send_gn[o] = own_gn[0].astype(BF)
            gn_copy(o).start()

        @pl.when(o == 0)
        def _():
            gn_out[...] = own_gn[0]

        return carry

    lax.fori_loop(0, planes, block, 0)

    strip = ctxs * rows

    def out_copy(m, d):
        into = down_out.at[:, d] if m == 2 else pair_out.at[:, d, m]
        return pltpu.make_async_copy(stage.at[m], into, osem.at[m])

    def weight_grads(d, carry):
        left = pl.ds(pl.multiple_of(d * strip, 128), strip)
        for m in (2, 0, 1):
            @pl.when(d > 0)
            def _():
                out_copy(m, d - 1).wait()

            if m == 2:
                total = dot(ogt[left, :], mid[...], NN)
            else:
                total = dot(hnt[left, :], pair[m], NN)
            stage[m] = total.astype(BF).reshape(ctxs, rows, full)
            out_copy(m, d).start()
        return carry

    lax.fori_loop(0, dps, weight_grads, 0)
    for m in range(3):
        out_copy(m, dps - 1).wait()
    total = gn_out[...]
    for o in range(1, planes):
        gn_copy(o).wait_recv()
        total = total + recv_gn[o].astype(F32)
    gn_out[...] = total
    for o in range(1, planes):
        gn_copy(o).wait_send()
        hn_copy(o).wait_send()


def ffn(hn, og_all, w_all, planes, depth, collective_id):
    count, width = hn.shape
    ctxs, dps, _, rows, full = w_all.shape
    tokens = planes * count
    flops = 18 * tokens * width * full
    return pl.pallas_call(
        functools.partial(ffn_kernel, planes, depth),
        out_shape=(
            jax.ShapeDtypeStruct((count, width), F32),
            jax.ShapeDtypeStruct((planes, count, width), BF),
            jax.ShapeDtypeStruct((ctxs, dps, rows, full), BF),
            jax.ShapeDtypeStruct((ctxs, dps, 2, rows, full), BF),
        ),
        in_specs=[VMEM, VMEM, ANY],
        out_specs=(VMEM, VMEM, ANY, ANY),
        scratch_shapes=[
            pltpu.VMEM((3, width, full), BF),
            pltpu.VMEM((planes, count, width), BF),
            pltpu.VMEM((width, tokens), BF),
            pltpu.VMEM((width, tokens), BF),
            pltpu.VMEM((tokens, full), BF),
            pltpu.VMEM((2, tokens, full), BF),
            pltpu.VMEM((planes, count, width), BF),
            pltpu.VMEM((planes, count, width), BF),
            pltpu.VMEM((2, count, width), F32),
            pltpu.VMEM((3, ctxs, rows, full), BF),
            DMA((3, ctxs * dps)),
            DMA((2, planes)),
            DMA((2, planes)),
            DMA((3,)),
        ],
        compiler_params=params(collective_id),
        cost_estimate=pl.CostEstimate(flops=flops, bytes_accessed=20 << 20, transcendentals=0),
    )(hn, og_all, w_all)


def back_kernel(
    planes, depth, turns, gn_ref, mixed_ref, og_ref, gains_ref, wo_ref, o_ref, lse_ref, q_ref, kv_ref, lower_ref, parts_ref,
    gq_out, kv_out, gmixed_out, dgain_out, block_out, shard_out,
    bias, gob, delta, gkv, dsum, from_core, from_z, from_plane, partial, *rest,
):
    collect = Collect(Place(planes, depth), partial, rest[:COLLECT])
    cs, zs, ps = rest[COLLECT:]
    me = collect.me
    half = turns // 2
    count = gn_ref.shape[0]
    greet(me.plane() + me.line() + [me.sibling()])

    def c_copy(i):
        return remote(gkv.at[2 * i + 1], from_core.at[i], cs.at[0, i], cs.at[1, i], me.sibling())

    def z_copy(k):
        return remote(dsum.at[k], from_z.at[k], zs.at[0, k], zs.at[1, k], me.along(me.behind(k)))

    def p_copy(o):
        return remote(parts_ref.at[o], from_plane.at[o], ps.at[0, o], ps.at[1, o], me.across(o))

    unit, recip = unit_of(mixed_ref[...], 1)
    grad = gn_ref[...]
    scaled = grad * gains_ref[:, D : 2 * D]
    inner = jnp.mean(scaled * unit, axis=1, keepdims=True)
    gmixed = og_ref[...].astype(F32) + recip * (scaled - unit * inner)
    gmixed_out[...] = gmixed
    dgain_out[...] = jnp.sum(grad * unit, axis=0, keepdims=True)
    gmixed_b = gmixed.astype(BF)
    gob[...] = dot(wo_ref[...].reshape(HQ, D), gmixed_b, NT).astype(BF)
    for t in range(GROUPS):
        rows = []
        for h in range(4):
            at = pl.ds(t * 256 + h * 64, 64)
            rows.append(
                jnp.sum(gob[at, :].astype(F32) * o_ref[at, :].astype(F32), axis=0, keepdims=True)
            )
        delta[t] = jnp.concatenate(rows, axis=0)
    gq_out[...] = jnp.zeros_like(gq_out)

    def visit(slot):
        fill_bias(bias, lower_ref[...], slot)

        def four_heads(t, carry):
            key_at = pl.ds(pl.multiple_of(t * 128, 128), 128)
            value_at = pl.ds(pl.multiple_of(HK + t * 128, 128), 128)
            keys, values = kv_ref[slot, :, key_at], kv_ref[slot, :, value_at]
            lse_t, delta_t = lse_ref[t], delta[t]
            grad_keys, grad_values = [], []
            for u in range(2):
                key = keys[:, u * 64 : u * 64 + 64]
                value = values[:, u * 64 : u * 64 + 64]
                grad_key, grad_value = 0.0, 0.0
                for g in range(2):
                    h = 2 * u + g
                    at = pl.ds(pl.multiple_of(t * 256 + h * 64, 64), 64)
                    query, gob_h = q_ref[at, :], gob[at, :]
                    probs = jnp.exp(dot(key, query, NN) + bias[...] - lse_t[h : h + 1, :])
                    grad_value = grad_value + dot(probs.astype(BF), gob_h, NT)
                    grad_scores = (probs * (dot(value, gob_h, NN) - delta_t[h : h + 1, :])).astype(BF)
                    grad_key = grad_key + dot(grad_scores, query, NT)
                    gq_out[at, :] += dot(key, grad_scores, TN)
                grad_keys.append(grad_key)
                grad_values.append(grad_value)
            gkv[slot, :, key_at] = jnp.concatenate(grad_keys, axis=1).astype(BF)
            gkv[slot, :, value_at] = jnp.concatenate(grad_values, axis=1).astype(BF)
            return carry

        lax.fori_loop(0, GROUPS, four_heads, 0)

    for i in range(half - 1, -1, -1):
        @pl.when(me.z - i - 1 + me.core >= 0)
        def _():
            visit(2 * i + 1)
            c_copy(i).start()

    for k in range(half, 0, -1):
        @pl.when(me.z - k >= 0)
        def _():
            visit(2 * k)

            @pl.when(me.core == 0)
            def _():
                if k < half:
                    c_copy(k).wait_recv()
                    dsum[k] = (gkv[2 * k].astype(F32) + from_core[min(k, half - 1)].astype(F32)).astype(BF)
                else:
                    dsum[k] = gkv[2 * k]

            @pl.when(me.core == 1)
            def _():
                c_copy(k - 1).wait_recv()
                dsum[k] = (gkv[2 * k].astype(F32) + from_core[k - 1].astype(F32)).astype(BF)

            z_copy(k).start()

    visit(0)
    gq_out[...] *= HEAD_DIM ** (-0.5)
    half_rows = D // planes
    shape = partial.shape[1:]
    order = list(range(1, planes)) + [0]
    for o in order:
        d = me.dp ^ o
        rows = o_ref[pl.ds(pl.multiple_of(d * half_rows, 128), half_rows), :]
        partial[d] = dot(rows, gmixed_b, NN).astype(BF).reshape(shape)
        collect.first(o)
    for o in order:
        collect.second(o)
    for o in range(1, planes):
        p_copy(o).start()
    value = collect.third()
    shard_out[...] = collect.last(value)

    kv_out[...] = gkv[0].astype(F32)

    @pl.when(me.core == 0)
    def _():
        c_copy(0).wait_recv()
        kv_out[...] += from_core[0].astype(F32)

    for k in range(1, half + 1):
        @pl.when(me.z + k < depth)
        def _():
            z_copy(k).wait_recv()
            kv_out[...] += from_z[k].astype(F32)

    total = mixed_ref[...] + parts_ref[0].astype(F32)
    for o in range(1, planes):
        p_copy(o).wait_recv()
        total = total + from_plane[o].astype(F32)
    block_out[...] = total.astype(BF)

    for o in range(1, planes):
        p_copy(o).wait_send()
    for i in range(half):
        @pl.when(me.z - i - 1 + me.core >= 0)
        def _():
            c_copy(i).wait_send()
    for k in range(1, half + 1):
        @pl.when(me.z - k >= 0)
        def _():
            z_copy(k).wait_send()
    collect.finish()


def back(gn, mixed, cotangent, gains_row, wo_all, o_t, lse, query, kv_all, lower, parts, planes, depth, turns, collective_id):
    half = turns // 2
    count = gn.shape[0]
    rows = wo_all.shape[3]
    return pl.pallas_call(
        functools.partial(back_kernel, planes, depth, turns),
        out_shape=(
            jax.ShapeDtypeStruct((HQ, count), F32),
            jax.ShapeDtypeStruct((count, 2 * HK), F32),
            jax.ShapeDtypeStruct((count, D), F32),
            jax.ShapeDtypeStruct((1, D), F32),
            jax.ShapeDtypeStruct((count, D), BF),
            jax.ShapeDtypeStruct((rows, D), F32),
        ),
        in_specs=[VMEM] * 11,
        out_specs=(VMEM,) * 6,
        scratch_shapes=[
            pltpu.VMEM((count, count), F32),
            pltpu.VMEM((HQ, count), BF),
            pltpu.VMEM((GROUPS, 4, count), F32),
            pltpu.VMEM((turns + 1, count, 2 * HK), BF),
            pltpu.VMEM((half + 1, count, 2 * HK), BF),
            pltpu.VMEM((half, count, 2 * HK), BF),
            pltpu.VMEM((half + 1, count, 2 * HK), BF),
            pltpu.VMEM((planes, count, D), BF),
            pltpu.VMEM((planes, depth, 2, rows, D), BF),
        ]
        + collect_scratch(planes, depth, rows, D, BF)
        + [DMA((2, half)), DMA((2, half + 1)), DMA((2, planes))],
        compiler_params=params(collective_id),
        cost_estimate=pl.CostEstimate(flops=60 << 30, bytes_accessed=8 << 20, transcendentals=0),
    )(gn, mixed, cotangent, gains_row, wo_all, o_t, lse, query, kv_all, lower, parts)


def tail_kernel(
    planes, depth, n_gains, gq_ref, gkv_ref, unit_ref, recip_ref, cos_ref, sin_ref, gains_ref, w_ref, xat_ref, tok_ref, gmixed_ref, dgf_ref,
    grad_out, shard_out, gains_out, gproj, partial, gains_p, *rest,
):
    me = Place(planes, depth)
    collect = Collect(me, partial, rest[:COLLECT])
    small = Collect(me, gains_p, rest[COLLECT:])
    count = tok_ref.shape[0]
    tail_row = gains_ref[:, 2 * D : 2 * D + 128]
    gain_q, gain_k = column_of(tail_row, 0), column_of(tail_row, HEAD_DIM)
    cosine, sine = cos_ref[...], -sin_ref[...]
    gained = [0.0, 0.0]
    for h in range(0, HEADS + KV_HEADS, 4):
        kind = 0 if h < HEADS else 1
        if kind == 0:
            four = gq_ref[pl.ds(h * HEAD_DIM, 4 * HEAD_DIM), :]
        else:
            four = gkv_ref[:, pl.ds((h - HEADS) * HEAD_DIM, 4 * HEAD_DIM)].T
        recips = recip_ref[h // 4]
        results = []
        for i in range(4):
            unit = unit_ref[pl.ds((h + i) * HEAD_DIM, HEAD_DIM), :]
            grad = turned(four[i * HEAD_DIM : (i + 1) * HEAD_DIM], cosine, sine)
            scaled = grad * (gain_k if kind else gain_q)
            inner = jnp.mean(scaled * unit, axis=0, keepdims=True)
            results.append(recips[i : i + 1, :] * (scaled - unit * inner))
            gained[kind] = gained[kind] + grad * unit
        gproj[:, pl.ds(h * HEAD_DIM, 4 * HEAD_DIM)] = jnp.concatenate(results, axis=0).T.astype(BF)
    gproj[:, pl.ds(HQ + HK, HK)] = gkv_ref[:, pl.ds(HK, HK)].astype(BF)
    greet(me.plane() + me.line() + [me.sibling()])
    half_rows = D // planes
    shape = partial.shape[1:]
    order = list(range(1, planes)) + [0]
    for o in order:
        d = me.dp ^ o
        rows = xat_ref[pl.ds(pl.multiple_of(d * half_rows, 128), half_rows), :]
        partial[d] = dot(rows, gproj[...], NN).astype(BF).reshape(shape)
        collect.first(o)
        if o != order[0]:
            collect.second(order[order.index(o) - 1])
    collect.second(0)
    grad = dot(gproj[...], w_ref[...].reshape(D, 2 * HQ), NT)
    unit, recip = unit_of(tok_ref[...].astype(F32), 1)
    scaled = grad * gains_ref[:, :D]
    inner = jnp.mean(scaled * unit, axis=1, keepdims=True)
    grad_out[...] = gmixed_ref[...] + recip * (scaled - unit * inner)
    dga = jnp.sum(grad * unit, axis=0, keepdims=True)
    lane = lax.broadcasted_iota(jnp.int32, (HEAD_DIM, 128), 1)
    entry = lax.broadcasted_iota(jnp.int32, (HEAD_DIM, 128), 0)
    sums = [jnp.sum(g, axis=1, keepdims=True) for g in gained]
    last = jnp.sum(
        jnp.where(lane == entry, sums[0], 0.0) + jnp.where(lane == entry + HEAD_DIM, sums[1], 0.0),
        axis=0,
        keepdims=True,
    )
    whole = jnp.concatenate([dga, dgf_ref[...], last], axis=1)
    devices = planes * depth * 2
    entries = devices * n_gains
    index = lax.broadcasted_iota(jnp.int32, (devices, entries), 1)
    device = lax.broadcasted_iota(jnp.int32, (devices, entries), 0)
    apart = jnp.where(index // n_gains == device, whole, 0.0)
    pick = jnp.where(
        lax.broadcasted_iota(jnp.int32, (128, entries), 1) % n_gains
        == lax.broadcasted_iota(jnp.int32, (128, entries), 0),
        1.0,
        0.0,
    )
    table = lax.dot_general(
        apart, pick, NT, preferred_element_type=F32, precision=lax.Precision.HIGHEST
    )
    gains_p[...] = jnp.broadcast_to(table[:, None, :], (devices, 8, 128)).reshape(gains_p.shape)
    for o in order:
        small.first(o)
    for o in order:
        small.second(o)
    value = collect.third()
    little = small.third()
    shard_out[...] = collect.last(value)
    gains_out[...] = small.last(little)
    collect.finish()
    small.finish()


def tail(gq, gkv, unit, recip, cosine, sine, gains_row, w_all, xat, tokens, gmixed, dgf, n_gains, planes, depth, collective_id):
    count = tokens.shape[0]
    rows, columns = w_all.shape[3:]
    return pl.pallas_call(
        functools.partial(tail_kernel, planes, depth, n_gains),
        out_shape=(
            jax.ShapeDtypeStruct((count, D), F32),
            jax.ShapeDtypeStruct((rows, columns), F32),
            jax.ShapeDtypeStruct((8, 128), F32),
        ),
        in_specs=[VMEM] * 12,
        out_specs=(VMEM,) * 3,
        scratch_shapes=[
            pltpu.VMEM((count, columns), BF),
            pltpu.VMEM((planes, depth, 2, rows, columns), BF),
            pltpu.VMEM((planes, depth, 2, 8, 128), F32),
        ]
        + collect_scratch(planes, depth, rows, columns, BF)
        + collect_scratch(planes, depth, 8, 128, F32),
        compiler_params=params(collective_id),
        cost_estimate=pl.CostEstimate(flops=40 << 30, bytes_accessed=8 << 20, transcendentals=0),
    )(gq, gkv, unit, recip, cosine, sine, gains_row, w_all, xat, tokens, gmixed, dgf)


def per_device(
    tokens_in,
    positions,
    out_grad,
    w_qkv,
    w_output,
    w_gate_up,
    w_down,
    norm_gains,
    first_qkv,
    first_output,
    first_gate_up,
    first_down,
    first_gains,
    second_qkv,
    second_output,
    second_gate_up,
    second_down,
    second_gains,
):
    planes, ctxs = lax.axis_size("dp"), lax.axis_size("ctx")
    depth = ctxs // 2
    turns = ctxs // 2
    rows = w_qkv.shape[0]
    full = w_down.shape[1] // planes
    n_gains = norm_gains.shape[0]
    count = tokens_in.shape[0] * tokens_in.shape[1]
    tokens = tokens_in.reshape(count, D)
    places = positions.reshape(count)
    cotangent = out_grad.reshape(count, D)

    w_blocks = jnp.concatenate(
        [
            w_gate_up.astype(BF).reshape(rows, 2, planes, full).transpose(2, 1, 0, 3),
            w_down.astype(BF).reshape(rows, 1, planes, full).transpose(2, 1, 0, 3),
        ],
        axis=1,
    )
    gains_block = jnp.pad(norm_gains.astype(BF).astype(F32)[None, :], ((0, 7), (0, 128 - n_gains)))
    w_mine, qkv_line, output_line, gains_line = exchange(
        [w_blocks], [w_qkv.astype(BF), w_output.astype(BF), gains_block], planes, depth, 0
    )
    w_all = lax.all_gather(w_mine, "ctx", axis=0, tiled=False)

    cosine, sine = rope_tables(places)
    query, kv, qkv_all, xat, unit_heads, recip_heads, gains_row = front(
        tokens, cosine, sine, qkv_line, gains_line, n_gains, planes, depth, 1
    )
    lower = (jnp.arange(count, dtype=jnp.int32) - places)[None, :]
    kv_all, og_all, output_all, attn_t, lse, mixed, hn = attend(
        kv, cotangent, output_line, query, lower, tokens, gains_row, planes, depth, turns, 2
    )
    w_used = w_all if rows % 16 == 0 else w_all.transpose(2, 1, 0, 3, 4).reshape(1, 1, 3, D, full)
    grad_normed, parts, down_grads, pair_grads = ffn(hn, og_all, w_used, planes, depth, 3)
    if rows % 16 != 0:
        down_grads = down_grads.reshape(planes, ctxs, rows, full).transpose(1, 0, 2, 3)
        pair_grads = pair_grads.reshape(2, planes, ctxs, rows, full).transpose(2, 1, 0, 3, 4)
    down_mine = lax.psum_scatter(down_grads, "ctx", scatter_dimension=0, tiled=False)
    grad_query, grad_kv, grad_mixed, grad_gain_ffn, block_out, shard_output = back(
        grad_normed, mixed, cotangent, gains_row, output_all, attn_t, lse, query, kv_all, lower, parts,
        planes, depth, turns, 4,
    )
    pair_grads, grad_kv = lax.optimization_barrier((pair_grads, grad_kv))
    pair_mine = lax.psum_scatter(pair_grads, "ctx", scatter_dimension=0, tiled=False)
    input_grad, shard_qkv, gains_tile = tail(
        grad_query, grad_kv, unit_heads, recip_heads, cosine, sine, gains_row, qkv_all, xat, tokens, grad_mixed,
        grad_gain_ffn, n_gains, planes, depth, 5,
    )
    shard_gains = gains_tile[0, :n_gains]

    down_shards, pair_shards = exchange([down_mine, pair_mine], [], planes, depth, 6)
    shard_gate_up = pair_shards.transpose(2, 1, 0, 3).reshape(rows, 2 * planes * full).astype(F32)
    shard_down = down_shards.transpose(1, 0, 2).reshape(rows, planes * full).astype(F32)

    new_qkv, new_first_qkv, new_second_qkv = adam_step(
        w_qkv, shard_qkv, first_qkv, second_qkv, 0.02, 0.1
    )
    new_output, new_first_output, new_second_output = adam_step(
        w_output, shard_output, first_output, second_output, 0.2, 0.1
    )
    new_gate_up, new_first_gate_up, new_second_gate_up = adam_step(
        w_gate_up, shard_gate_up, first_gate_up, second_gate_up, 0.02, 0.1
    )
    new_down, new_first_down, new_second_down = adam_step(
        w_down, shard_down, first_down, second_down, 0.02, 0.1
    )
    new_gains, new_first_gains, new_second_gains = adam_step(
        norm_gains, shard_gains, first_gains, second_gains, 0.1, 0.0
    )
    return (
        block_out.reshape(tokens_in.shape),
        input_grad.reshape(tokens_in.shape),
        shard_qkv,
        shard_output,
        shard_gate_up,
        shard_down,
        shard_gains,
        new_qkv,
        new_output,
        new_gate_up,
        new_down,
        new_gains,
        new_first_qkv,
        new_first_output,
        new_first_gate_up,
        new_first_down,
        new_first_gains,
        new_second_qkv,
        new_second_output,
        new_second_gate_up,
        new_second_down,
        new_second_gains,
    )


def solution(mesh):
    in_specs = (
        P("dp", "ctx", None),
        P("dp", "ctx"),
        P("dp", "ctx", None),
        P(("dp", "ctx"), None),
        P(("dp", "ctx"), None),
        P(("dp", "ctx"), None),
        P(("dp", "ctx"), None),
        P(("dp", "ctx")),
        P(("dp", "ctx"), None),
        P(("dp", "ctx"), None),
        P(("dp", "ctx"), None),
        P(("dp", "ctx"), None),
        P(("dp", "ctx")),
        P(("dp", "ctx"), None),
        P(("dp", "ctx"), None),
        P(("dp", "ctx"), None),
        P(("dp", "ctx"), None),
        P(("dp", "ctx")),
    )
    out_specs = (
        P("dp", "ctx", None),
        P("dp", "ctx", None),
        P(("dp", "ctx"), None),
        P(("dp", "ctx"), None),
        P(("dp", "ctx"), None),
        P(("dp", "ctx"), None),
        P(("dp", "ctx")),
        P(("dp", "ctx"), None),
        P(("dp", "ctx"), None),
        P(("dp", "ctx"), None),
        P(("dp", "ctx"), None),
        P(("dp", "ctx")),
        P(("dp", "ctx"), None),
        P(("dp", "ctx"), None),
        P(("dp", "ctx"), None),
        P(("dp", "ctx"), None),
        P(("dp", "ctx")),
        P(("dp", "ctx"), None),
        P(("dp", "ctx"), None),
        P(("dp", "ctx"), None),
        P(("dp", "ctx"), None),
        P(("dp", "ctx")),
    )
    return jax.shard_map(
        per_device, mesh=mesh, in_specs=in_specs, out_specs=out_specs, check_vma=False
    )
```

```python
import functools
import math

import jax
import jax.numpy as jnp
from jax import lax
from jax.experimental import pallas as pl
from jax.experimental.pallas import tpu as pltpu
from jax.sharding import PartitionSpec as P

D = 1024
HEADS = 16
KV_HEADS = 8
HEAD_DIM = 64
STEP = 4
HQ = 1024
HK = 512


EPS = 1e-05
THETA = 1000000.0
NEG_BIG = -1e30
BETA_ONE = 0.9
BETA_TWO = 0.95
ADAM_EPS = 1e-08


def rope_tables(places):
    half = HEAD_DIM // 2
    freqs = jnp.exp(-math.log(THETA) * (2.0 * jnp.arange(half, dtype=jnp.float32) / HEAD_DIM))
    angles = freqs[:, None] * places.astype(jnp.float32)[None, :]
    return (jnp.cos(angles), jnp.sin(angles))


def adam_step(weight, grad, first, second, rate, decay):
    first_new = BETA_ONE * first + (1.0 - BETA_ONE) * grad
    second_new = BETA_TWO * second + (1.0 - BETA_TWO) * grad * grad
    first_hat = first_new / (1.0 - BETA_ONE**STEP)
    second_hat = second_new / (1.0 - BETA_TWO**STEP)
    weight_new = weight - rate * (first_hat / (jnp.sqrt(second_hat) + ADAM_EPS) + decay * weight)
    return (weight_new, first_new, second_new)


BF = jnp.bfloat16
F32 = jnp.float32
MESH_ID = pl.DeviceIdType.MESH
ANY = pl.BlockSpec(memory_space=pl.ANY)
VMEM = pl.BlockSpec(memory_space=pltpu.VMEM)
DMA = pltpu.SemaphoreType.DMA
NN = (((1,), (0,)), ((), ()))
NT = (((1,), (1,)), ((), ()))
TN = (((0,), (0,)), ((), ()))
VMEM_BYTES = 60 << 20
GROUPS = HEADS // 4


def dot(a, b, dims):
    return lax.dot_general(a, b, dims, preferred_element_type=F32)


class Place:
    def __init__(self, planes, depth):
        self.planes, self.depth = planes, depth
        self.dp = lax.axis_index("dp")
        self.ctx = lax.axis_index("ctx")
        self.z = self.ctx // 2
        self.core = self.ctx % 2

    def sibling(self):
        return {"dp": self.dp, "ctx": self.z * 2 + 1 - self.core}

    def across(self, o):
        return {"dp": self.dp ^ o, "ctx": self.ctx}

    def behind(self, k):
        return lax.rem(self.z + self.depth - k, self.depth)

    def ahead(self, k):
        return lax.rem(self.z + k, self.depth)

    def along(self, z):
        return {"dp": self.dp, "ctx": z * 2 + self.core}

    def plane(self):
        return [self.across(o) for o in range(1, self.planes)]

    def line(self):
        return [self.along(self.ahead(k)) for k in range(1, self.depth)]


def greet(devices):
    barrier = pltpu.get_barrier_semaphore()
    for device in devices:
        pl.semaphore_signal(barrier, inc=1, device_id=device, device_id_type=MESH_ID)
    pl.semaphore_wait(barrier, len(devices))


def remote(src, dst, send, recv, device):
    return pltpu.make_async_remote_copy(
        src_ref=src, dst_ref=dst, send_sem=send, recv_sem=recv, device_id=device, device_id_type=MESH_ID
    )


def params(collective_id):
    return pltpu.CompilerParams(
        vmem_limit_bytes=VMEM_BYTES, collective_id=collective_id, has_side_effects=True
    )


class Spread:
    def __init__(self, me, g_ref, line_sems, sems):
        self.me, self.g, self.line_sems, self.sems = me, g_ref, line_sems, sems
        self.sent = []

    def push(self, src, dst, kind, o, device):
        copy = remote(src, dst, self.sems.at[kind, o], self.sems.at[kind + 1, o], device)
        copy.start()
        self.sent.append(copy)

    def mine(self, o, core):
        return self.g.at[self.me.dp ^ o, :, core]

    def line(self):
        me = self.me
        block = self.g.at[me.dp, me.z, me.core]
        for k in range(1, me.depth):
            copy = remote(
                block, block, self.line_sems.at[0, k], self.line_sems.at[1, k], me.along(me.ahead(k))
            )
            copy.start()
            self.sent.append(copy)

    def first(self):
        me = self.me
        for k in range(1, me.depth):
            block = self.g.at[me.dp, me.behind(k), me.core]
            remote(
                block, block, self.line_sems.at[0, k], self.line_sems.at[1, k], me.along(me.ahead(k))
            ).wait_recv()
        for o in range(1, me.planes):
            self.push(self.mine(0, me.core), self.mine(0, me.core), 0, o, me.across(o))
        self.push(self.mine(0, me.core), self.mine(0, me.core), 2, 0, me.sibling())

    def relay(self, o):
        block = self.mine(o, self.me.core)
        remote(block, block, self.sems.at[0, o], self.sems.at[1, o], self.me.sibling()).wait_recv()
        self.push(block, block, 2, o, self.me.sibling())

    def arrive(self, o):
        block = self.mine(o, 1 - self.me.core)
        remote(block, block, self.sems.at[2, o], self.sems.at[3, o], self.me.sibling()).wait_recv()

    def finish(self):
        for copy in self.sent:
            copy.wait_send()


def spread_sems(planes, depth):
    return [DMA((2, depth)), DMA((4, planes))]


class Collect:
    def __init__(self, me, p_ref, scratch):
        self.me, self.p = me, p_ref
        self.sums, self.from_plane, self.total, self.from_z, self.cs, self.ps, self.zs = scratch

    def c_copy(self, o):
        me = self.me
        return remote(
            self.p.at[me.dp ^ o, :, 1 - me.core], self.sums.at[o], self.cs.at[0, o], self.cs.at[1, o], me.sibling()
        )

    def p_copy(self, o):
        return remote(
            self.sums.at[o], self.from_plane.at[o - 1], self.ps.at[0, o], self.ps.at[1, o], self.me.across(o)
        )

    def z_copy(self, k):
        me = self.me
        return remote(
            self.total.at[me.ahead(k)], self.from_z.at[k], self.zs.at[0, k], self.zs.at[1, k], me.along(me.ahead(k))
        )

    def first(self, o):
        self.c_copy(o).start()

    def second(self, o):
        me = self.me
        self.c_copy(o).wait_recv()
        own = self.p[me.dp ^ o, :, me.core].astype(F32)
        self.sums[o] = (own + self.sums[o].astype(F32)).astype(self.sums.dtype)
        if o > 0:
            self.p_copy(o).start()

    def third(self):
        me = self.me
        for o in range(1, me.planes):
            self.p_copy(o).wait_recv()
        for k in list(range(1, me.depth)) + [0]:
            z = me.ahead(k)
            value = self.sums[0, z].astype(F32)
            for o in range(1, me.planes):
                value = value + self.from_plane[o - 1, z].astype(F32)
            self.total[z] = value.astype(self.total.dtype)
            if k > 0:
                self.z_copy(k).start()
        return value

    def last(self, value):
        for k in range(1, self.me.depth):
            self.z_copy(k).wait_recv()
            value = value + self.from_z[k].astype(F32)
        return value

    def finish(self):
        for o in range(self.me.planes):
            self.c_copy(o).wait_send()
        for o in range(1, self.me.planes):
            self.p_copy(o).wait_send()
        for k in range(1, self.me.depth):
            self.z_copy(k).wait_send()


def collect_scratch(planes, depth, rows, columns, kind):
    return [
        pltpu.VMEM((planes, depth, rows, columns), kind),
        pltpu.VMEM((planes - 1, depth, rows, columns), kind),
        pltpu.VMEM((depth, rows, columns), kind),
        pltpu.VMEM((depth, rows, columns), kind),
        DMA((2, planes)),
        DMA((2, planes)),
        DMA((2, depth)),
    ]


COLLECT = 7


def unit_of(values, axis):
    recip = lax.rsqrt(jnp.mean(values * values, axis=axis, keepdims=True) + EPS)
    return values * recip, recip


def column_of(row, start):
    lane = lax.broadcasted_iota(jnp.int32, (HEAD_DIM, 128), 1)
    entry = lax.broadcasted_iota(jnp.int32, (HEAD_DIM, 128), 0)
    return jnp.sum(jnp.where(lane == entry + start, row, 0.0), axis=1, keepdims=True)


def turned(values, cosine, sine):
    half = HEAD_DIM // 2
    a, b = values[:half], values[half:]
    return jnp.concatenate([a * cosine - b * sine, b * cosine + a * sine], axis=0)


def fill_bias(bias, lower, slot):
    count = bias.shape[0]
    query = lax.broadcasted_iota(jnp.int32, (count, count), 1)
    key = lax.broadcasted_iota(jnp.int32, (count, count), 0) - slot * count
    bias[...] = jnp.where((key <= query) & (key >= lower), 0.0, NEG_BIG)


class Pass:
    def __init__(self, me, w_ref, sems):
        self.me, self.w, self.sems = me, w_ref, sems

    def copy(self, kind, s, down, core=None, device=None):
        me = self.me
        z = me.z + s - 1 if down else me.z - s + 1
        block = self.w.at[z * 2 + (me.core if core is None else core)]
        device = me.sibling() if device is None else device
        return remote(block, block, self.sems.at[kind, s], self.sems.at[kind + 1, s], device)

    def held(self, s, down):
        me = self.me
        return me.z + s - 1 < me.depth if down else me.z - s + 1 >= 0

    def on(self, s, down):
        me = self.me
        return self.held(s, down) & (me.z >= 1 if down else me.z + 1 < me.depth)

    def line_copy(self, s, down):
        me = self.me
        return self.copy(2 if down else 0, s, down, None, me.along(me.z - 1 if down else me.z + 1))

    def step(self, s):
        for down in (False, True):
            if s > 1:
                @pl.when(self.held(s, down))
                def _():
                    me = self.me
                    z = me.z + s - 1 if down else me.z - s + 1
                    block = self.w.at[z * 2 + me.core]
                    kind = 2 if down else 0
                    remote(
                        block, block, self.sems.at[kind, s - 1], self.sems.at[kind + 1, s - 1], me.sibling()
                    ).wait_recv()

            @pl.when(self.on(s, down))
            def _():
                self.line_copy(s, down).start()

            if s > 1 or not down:
                @pl.when(self.held(s, down))
                def _():
                    self.copy(6 if down else 4, s, down).start()

    def finish(self):
        for s in range(1, self.me.depth + 1):
            for down in (False, True):
                @pl.when(self.on(s, down))
                def _():
                    self.line_copy(s, down).wait_send()

                if s > 1 or not down:
                    @pl.when(self.held(s, down))
                    def _():
                        self.copy(6 if down else 4, s, down).wait_send()
                        self.copy(6 if down else 4, s, down, 1 - self.me.core).wait_recv()


def ahead_kernel(
    planes, depth, turns, n_gains,
    tok_ref, cos_ref, sin_ref, lower_ref, gain_ref, wqkv_ref, wout_ref, wpair_ref, wdown_ref, og_ref,
    q_any, kv_any, wqkv_any, xat_any, unit_any, recip_any, og_all, wo_any, w_any,
    gains_out, o_out, lse_out, mixed_out, hn_out,
    q_s, kv_all, w_all, xat, unit_s, recip_s, wo_all, blocks, gains_g, xa, xa_plain, proj, bias, accum, sums,
    own_sem, keep_sem, zs, cs, ps, a2a, pass_sem, glsem, gsem, wlsem, wsem, olsem, osem,
):
    me = Place(planes, depth)
    half = turns // 2
    count = tok_ref.shape[0]
    width = D // planes
    rows = wqkv_ref.shape[0]
    full = blocks.shape[3]
    gains = Spread(me, gains_g, glsem, gsem)
    weights = Spread(me, w_all, wlsem, wsem)
    outputs = Spread(me, wo_all, olsem, osem)
    passing = Pass(me, w_any, pass_sem)
    kept = []

    def keep(source, into):
        copy = pltpu.make_async_copy(source, into, keep_sem.at[len(kept)])
        copy.start()
        kept.append(copy)

    gains_g[me.dp, me.z, me.core] = gain_ref[...]
    w_all[me.dp, me.z, me.core] = wqkv_ref[...].astype(BF)
    wo_all[me.dp, me.z, me.core] = wout_ref[...].astype(BF)
    for d in range(planes):
        for m in range(2):
            blocks[d, m] = wpair_ref[:, (m * planes + d) * full : (m * planes + d + 1) * full].astype(BF)
        blocks[d, 2] = wdown_ref[:, d * full : (d + 1) * full].astype(BF)
    own_block = pltpu.make_async_copy(blocks.at[me.dp], w_any.at[me.ctx, me.dp], own_sem.at[0])
    own_block.start()
    own_og = pltpu.make_async_copy(og_ref, og_all.at[0], own_sem.at[1])
    own_og.start()
    greet(me.plane() + me.line() + [me.sibling()])
    gains.line()
    weights.line()

    def a2a_copy(o):
        return remote(
            blocks.at[me.dp ^ o], w_any.at[me.ctx, me.dp], a2a.at[0, o], a2a.at[1, o], me.across(o)
        )

    for o in range(1, planes):
        a2a_copy(o).start()
    outputs.line()
    unit, _ = unit_of(tok_ref[...].astype(F32), 1)
    xa_plain[...] = unit
    gains.first()
    weights.first()
    own_block.wait()
    for o in range(1, planes):
        block = w_any.at[me.ctx, me.dp ^ o]
        remote(block, block, a2a.at[0, o], a2a.at[1, o], me.across(o)).wait_recv()
    passing.step(1)
    for o in range(1, planes):
        gains.relay(o)
    for o in range(planes):
        gains.arrive(o)
    devices = planes * depth * 2
    table = gains_g[...].reshape(devices, 8, 128)[:, 0, :].astype(BF)
    entries = devices * n_gains
    index = lax.broadcasted_iota(jnp.int32, (128, entries), 1)
    pick = jnp.where(
        index % n_gains == lax.broadcasted_iota(jnp.int32, (128, entries), 0), 1.0, 0.0
    ).astype(BF)
    spread = dot(table, pick, NN)
    owner = lax.broadcasted_iota(jnp.int32, (devices, entries), 1) // n_gains
    device = lax.broadcasted_iota(jnp.int32, (devices, entries), 0)
    gains_row = 1.0 + jnp.sum(jnp.where(owner == device, spread, 0.0), axis=0, keepdims=True)
    gains_out[...] = gains_row
    normed = (xa_plain[...] * gains_row[:, :D]).astype(BF)
    xat[...] = normed.T
    keep(xat, xat_any)
    for d in range(planes):
        xa[d] = normed[:, d * width : (d + 1) * width]
    proj[...] = jnp.zeros_like(proj)
    for o in range(planes):
        if o > 0:
            weights.relay(o)
        weights.arrive(o)
        proj[...] += dot(xa[me.dp ^ o], w_all[me.dp ^ o].reshape(width, 2 * HQ), NN)
    tail_row = gains_row[:, 2 * D : 2 * D + 128]
    gain_q, gain_k = column_of(tail_row, 0), column_of(tail_row, HEAD_DIM)
    cosine, sine = cos_ref[...], sin_ref[...]

    def four_raw(h):
        four = proj[:, h * HEAD_DIM : (h + 4) * HEAD_DIM].T
        results, recips = [], []
        for i in range(4):
            value, recip = unit_of(four[i * HEAD_DIM : (i + 1) * HEAD_DIM], 0)
            unit_s[pl.ds((h + i) * HEAD_DIM, HEAD_DIM), :] = value
            recips.append(recip)
            results.append(turned(value * (gain_q if h < HEADS else gain_k), cosine, sine))
        recip_s[h // 4] = jnp.concatenate(recips, axis=0)
        return jnp.concatenate(results, axis=0)

    for h in range(HEADS, HEADS + KV_HEADS, 4):
        kv_all[0, :, pl.ds((h - HEADS) * HEAD_DIM, 4 * HEAD_DIM)] = four_raw(h).T.astype(BF)
    kv_all[0, :, pl.ds(HK, HK)] = proj[:, HQ + HK :].astype(BF)

    def z_copy(k):
        return remote(kv_all.at[0], kv_all.at[2 * k], zs.at[0, k], zs.at[1, k], me.along(me.ahead(k)))

    def c_copy(i):
        return remote(
            kv_all.at[2 * i + 2 * me.core], kv_all.at[2 * i + 1], cs.at[0, i], cs.at[1, i], me.sibling()
        )

    for k in range(1, half + 1):
        @pl.when(me.z + k < depth)
        def _():
            z_copy(k).start()

    @pl.when(me.core == 0)
    def _():
        c_copy(0).start()

    outputs.first()
    passing.step(2)
    for h in range(0, HEADS, 4):
        q_s[pl.ds(h * HEAD_DIM, 4 * HEAD_DIM), :] = (four_raw(h) * HEAD_DIM ** (-0.5)).astype(BF)
    keep(q_s, q_any)
    keep(unit_s, unit_any)
    keep(recip_s, recip_any)
    keep(w_all, wqkv_any)
    shares = []
    for o in range(1, planes):
        share = remote(og_ref, og_all.at[o], ps.at[0, o], ps.at[1, o], me.across(o))
        share.start()
        shares.append(share)
    accum[...] = jnp.zeros_like(accum)
    sums[...] = jnp.zeros_like(sums)

    def visit(slot):
        fill_bias(bias, lower_ref[...], slot)

        def four_heads(t, carry):
            keys = kv_all[slot, :, pl.ds(pl.multiple_of(t * 128, 128), 128)]
            values = kv_all[slot, :, pl.ds(pl.multiple_of(HK + t * 128, 128), 128)]
            totals = []
            for u in range(2):
                key = keys[:, u * 64 : u * 64 + 64]
                value = values[:, u * 64 : u * 64 + 64]
                for g in range(2):
                    at = pl.ds(pl.multiple_of(t * 256 + u * 128 + g * 64, 64), 64)
                    weight = jnp.exp(dot(key, q_s[at, :], NN) + bias[...])
                    totals.append(jnp.sum(weight, axis=0, keepdims=True))
                    accum[at, :] += dot(value, weight.astype(BF), TN)
            sums[t] += jnp.concatenate(totals, axis=0)
            return carry

        lax.fori_loop(0, GROUPS, four_heads, 0)

    visit(0)
    for k in range(1, half + 1):
        there = me.z - k >= 0

        @pl.when(there)
        def _():
            z_copy(k).wait_recv()

        @pl.when(there & (me.core == 1))
        def _():
            c_copy(k - 1).start()

        if k < half:
            @pl.when(there & (me.core == 0))
            def _():
                c_copy(k).start()

        @pl.when(there)
        def _():
            visit(2 * k)

    if depth > 2:
        passing.step(3)
    for i in range(half):
        @pl.when(me.z - i - 1 + me.core >= 0)
        def _():
            c_copy(i).wait_recv()
            visit(2 * i + 1)

    keep(kv_all, kv_any)
    for o in range(1, planes):
        outputs.relay(o)
    for t in range(GROUPS):
        total = sums[t]
        lse_out[t] = jnp.log(total)
        for h in range(4):
            at = pl.ds(t * 256 + h * 64, 64)
            o_out[at, :] = (accum[at, :] / total[h : h + 1, :]).astype(BF)
    for o in range(planes):
        outputs.arrive(o)
    keep(wo_all, wo_any)
    mixed = tok_ref[...].astype(F32) + dot(o_out[...].T, wo_all[...].reshape(HQ, D), NN)
    mixed_out[...] = mixed
    unit, _ = unit_of(mixed, 1)
    hn_out[...] = (unit * gains_out[:, D : 2 * D]).astype(BF)
    for s in range(4, depth + 1):
        passing.step(s)
    passing.finish()

    for i in range(half):
        @pl.when(me.z - i - me.core >= 0)
        def _():
            c_copy(i).wait_send()

    for k in range(1, half + 1):
        @pl.when(me.z + k < depth)
        def _():
            z_copy(k).wait_send()

    for o in range(1, planes):
        a2a_copy(o).wait_send()
    for share in shares:
        share.wait()
    gains.finish()
    weights.finish()
    outputs.finish()
    own_og.wait()
    for copy in kept:
        copy.wait()


def ahead(tokens, cosine, sine, lower, gains_block, w_qkv, w_output, w_gate_up, w_down, cotangent, n_gains, planes, depth, turns, collective_id):
    half = turns // 2
    count = tokens.shape[0]
    rows = w_qkv.shape[0]
    full = w_down.shape[1] // planes
    shapes = [
        ((HQ, count), BF),
        ((turns + 1, count, 2 * HK), BF),
        ((planes, depth, 2, rows, 2 * HQ), BF),
        ((D, count), BF),
        ((HQ + HK, count), F32),
        (((HEADS + KV_HEADS) // 4, 4, count), F32),
        ((planes, count, D), BF),
        ((planes, depth, 2, rows, D), BF),
        ((depth * 2, planes, 3, rows, full), BF),
        ((1, planes * depth * 2 * n_gains), F32),
        ((HQ, count), BF),
        ((GROUPS, 4, count), F32),
        ((count, D), F32),
        ((count, D), BF),
    ]
    return pl.pallas_call(
        functools.partial(ahead_kernel, planes, depth, turns, n_gains),
        out_shape=tuple(jax.ShapeDtypeStruct(s, k) for s, k in shapes),
        in_specs=[VMEM] * 9 + [ANY],
        out_specs=(ANY,) * 9 + (VMEM,) * 5,
        scratch_shapes=[pltpu.VMEM(*shapes[i]) for i in (0, 1, 2, 3, 4, 5, 7)]
        + [
            pltpu.VMEM((planes, 3, rows, full), BF),
            pltpu.VMEM((planes, depth, 2, 8, 128), F32),
            pltpu.VMEM((planes, count, D // planes), BF),
            pltpu.VMEM((count, D), F32),
            pltpu.VMEM((count, 2 * HQ), F32),
            pltpu.VMEM((count, count), F32),
            pltpu.VMEM((HQ, count), F32),
            pltpu.VMEM((GROUPS, 4, count), F32),
            DMA((2,)),
            DMA((8,)),
            DMA((2, half + 1)),
            DMA((2, half)),
            DMA((2, planes)),
            DMA((2, planes)),
            DMA((8, depth + 1)),
        ]
        + spread_sems(planes, depth) * 3,
        compiler_params=params(collective_id),
        cost_estimate=pl.CostEstimate(flops=40 << 30, bytes_accessed=8 << 20, transcendentals=0),
    )(tokens, cosine, sine, lower, gains_block, w_qkv, w_output, w_gate_up, w_down, cotangent)


def ffn_kernel(
    planes, depth, hn_ref, og_ref, w_any, gn_out, parts_out, grads_out,
    w, hns, hnt, ogt, mid, pair, send_gn, recv_gn, own_gn, stage, wsem, hsem, gsem, osem,
):
    me = Place(planes, depth)
    count, width = hn_ref.shape
    full = w.shape[2]
    ctxs, dps, rows = w_any.shape[0], w_any.shape[1], w_any.shape[3]
    chunk = 384 if full % 384 == 0 else full

    def w_copy(i, m):
        c, d = i // dps, i % dps
        return pltpu.make_async_copy(
            w_any.at[c, d, m], w.at[m, pl.ds((d * ctxs + c) * rows, rows), :], wsem.at[m, i]
        )

    def load(i, carry):
        for m in range(3):
            w_copy(i, m).start()
        return carry

    lax.fori_loop(0, ctxs * dps, load, 0)
    greet(me.plane())

    def hn_copy(o):
        return remote(hn_ref, hns.at[o], hsem.at[0, o], hsem.at[1, o], me.across(o))

    def gn_copy(o):
        return remote(send_gn.at[o], recv_gn.at[o], gsem.at[0, o], gsem.at[1, o], me.across(o))

    near = [o for o in range(1, planes) if o & (o - 1) == 0]
    far = [o for o in range(1, planes) if o & (o - 1) != 0]
    for o in near:
        hn_copy(o).start()
    hns[0] = hn_ref[...]

    def loaded(i, carry):
        for m in range(3):
            w_copy(i, m).wait()
        return carry

    lax.fori_loop(0, ctxs * dps, loaded, 0)

    def block(o, carry):
        @pl.when(o > 0)
        def _():
            hn_copy(o).wait_recv()

        hn = hns[o]
        og = og_ref[o]
        at = pl.ds(pl.multiple_of(o * count, 128), count)
        hnt[:, at] = hn.T
        ogt[:, at] = og.T
        own_gn[0] = jnp.zeros((count, width), F32)
        own_gn[1] = jnp.zeros((count, width), F32)

        def part(j, inner):
            cols = pl.ds(pl.multiple_of(j * chunk, 128), chunk)
            w_gate, w_up, w_down = w[0, :, cols], w[1, :, cols], w[2, :, cols]
            gate = dot(hn, w_gate, NN)
            upper = dot(hn, w_up, NN)
            sigma = 1.0 / (1.0 + jnp.exp(-gate))
            active = gate * sigma
            middle = (active * upper).astype(BF)
            gmid = dot(og, w_down, NN)
            ggate = (gmid * upper * sigma * (1.0 + gate * (1.0 - sigma))).astype(BF)
            gupper = (gmid * active).astype(BF)
            mid[at, cols] = middle
            pair[0, at, cols] = ggate
            pair[1, at, cols] = gupper
            own_gn[0] += dot(ggate, w_gate, NT) + dot(gupper, w_up, NT)
            own_gn[1] += dot(middle, w_down, NT)
            return inner

        lax.fori_loop(0, full // chunk, part, 0)
        parts_out[o] = own_gn[1].astype(BF)

        @pl.when(o > 0)
        def _():
            send_gn[o] = own_gn[0].astype(BF)
            gn_copy(o).start()

        @pl.when(o == 0)
        def _():
            gn_out[...] = own_gn[0]
            for other in far:
                hn_copy(other).start()

        return carry

    lax.fori_loop(0, planes, block, 0)

    strip = ctxs * rows

    def out_copy(m, d):
        return pltpu.make_async_copy(stage.at[m], grads_out.at[:, d, m], osem.at[m])

    def weight_grads(d, carry):
        left = pl.ds(pl.multiple_of(d * strip, 128), strip)
        for m in (2, 0, 1):
            @pl.when(d > 0)
            def _():
                out_copy(m, d - 1).wait()

            if m == 2:
                total = dot(ogt[left, :], mid[...], NN)
            else:
                total = dot(hnt[left, :], pair[m], NN)
            stage[m] = total.astype(BF).reshape(ctxs, rows, full)
            out_copy(m, d).start()
        return carry

    lax.fori_loop(0, dps, weight_grads, 0)
    for m in range(3):
        out_copy(m, dps - 1).wait()
    total = gn_out[...]
    for o in range(1, planes):
        gn_copy(o).wait_recv()
        total = total + recv_gn[o].astype(F32)
    gn_out[...] = total
    for o in range(1, planes):
        gn_copy(o).wait_send()
        hn_copy(o).wait_send()


def ffn(hn, og_all, w_all, planes, depth, collective_id):
    count, width = hn.shape
    ctxs, dps, _, rows, full = w_all.shape
    tokens = planes * count
    flops = 18 * tokens * width * full
    return pl.pallas_call(
        functools.partial(ffn_kernel, planes, depth),
        out_shape=(
            jax.ShapeDtypeStruct((count, width), F32),
            jax.ShapeDtypeStruct((planes, count, width), BF),
            jax.ShapeDtypeStruct((ctxs, dps, 3, rows, full), BF),
        ),
        in_specs=[VMEM, VMEM, ANY],
        out_specs=(VMEM, VMEM, ANY),
        scratch_shapes=[
            pltpu.VMEM((3, width, full), BF),
            pltpu.VMEM((planes, count, width), BF),
            pltpu.VMEM((width, tokens), BF),
            pltpu.VMEM((width, tokens), BF),
            pltpu.VMEM((tokens, full), BF),
            pltpu.VMEM((2, tokens, full), BF),
            pltpu.VMEM((planes, count, width), BF),
            pltpu.VMEM((planes, count, width), BF),
            pltpu.VMEM((2, count, width), F32),
            pltpu.VMEM((3, ctxs, rows, full), BF),
            DMA((3, ctxs * dps)),
            DMA((2, planes)),
            DMA((2, planes)),
            DMA((3,)),
        ],
        compiler_params=params(collective_id),
        cost_estimate=pl.CostEstimate(flops=flops, bytes_accessed=20 << 20, transcendentals=0),
    )(hn, og_all, w_all)


class Fold:
    def __init__(self, me, g_any, scratch):
        self.me, self.g = me, g_any
        self.mine, self.other, self.from_line, self.ready, self.landed, self.sems, self.psems = scratch

    def own_copy(self, z):
        return pltpu.make_async_copy(
            self.g.at[z * 2 + self.me.core], self.mine.at[z], self.sems.at[0, z]
        )

    def core_copy(self, z):
        me = self.me
        return remote(
            self.g.at[z * 2 + 1 - me.core], self.other.at[z], self.sems.at[1, z], self.sems.at[2, z], me.sibling()
        )

    def start(self):
        for z in range(self.me.depth):
            self.own_copy(z).start()

    def first(self):
        for z in range(self.me.depth):
            self.core_copy(z).start()

    def add(self, total, term):
        def plane(d, carry):
            total[d] = (total[d].astype(F32) + term[d].astype(F32)).astype(BF)
            return carry

        lax.fori_loop(0, self.me.planes, plane, 0)

    def second(self):
        for z in range(self.me.depth):
            self.own_copy(z).wait()
            self.core_copy(z).wait_recv()
            self.add(self.mine.at[z], self.other.at[z])

    def target(self, k, down):
        me = self.me
        return k - (me.depth - 1) + me.z if down else me.depth - 1 - k + me.z

    def sends(self, k, down):
        me = self.me
        return self.target(k, down) >= 0 if down else me.z <= k

    def copy(self, k, down):
        me = self.me
        t = self.target(k, down)
        slot = me.depth if k == me.depth - 2 and not down else t
        kind = 5 if down else 3
        return remote(
            self.mine.at[t], self.from_line.at[slot], self.sems.at[kind, k], self.sems.at[kind + 1, k],
            me.along(me.z - 1 if down else me.z + 1),
        )

    def arrived(self, k, slot, down):
        block = self.from_line.at[slot]
        kind = 5 if down else 3
        remote(block, block, self.sems.at[kind, k], self.sems.at[kind + 1, k], self.me.sibling()).wait_recv()

    def step(self, k):
        me = self.me
        for down in (False, True):
            edge = me.z == me.depth - 1 if down else me.z == 0

            @pl.when(self.sends(k, down))
            def _():
                t = self.target(k, down)
                if k > 0:
                    @pl.when(jnp.logical_not(edge))
                    def _():
                        self.arrived(k - 1, t, down)
                        self.add(self.mine.at[t], self.from_line.at[t])

                self.copy(k, down).start()

    def total(self):
        me = self.me
        k = me.depth - 2

        @pl.when(me.z < me.depth - 1)
        def _():
            self.arrived(k, me.z, True)
            self.add(self.mine.at[me.z], self.from_line.at[me.z])

        @pl.when(me.z > 0)
        def _():
            self.arrived(k, me.depth, False)
            self.add(self.mine.at[me.z], self.from_line.at[me.depth])

        self.ready[...] = self.mine[me.z]
        for o in range(1, me.planes):
            self.plane_copy(o).start()

    def plane_copy(self, o):
        me = self.me
        return remote(
            self.ready.at[me.dp ^ o], self.landed.at[me.dp], self.psems.at[0, o], self.psems.at[1, o], me.across(o)
        )

    def last(self):
        me = self.me
        self.landed[me.dp] = self.ready[me.dp]
        for o in range(1, me.planes):
            block = self.landed.at[me.dp ^ o]
            remote(block, block, self.psems.at[0, o], self.psems.at[1, o], me.across(o)).wait_recv()

    def finish(self):
        me = self.me
        for z in range(me.depth):
            self.core_copy(z).wait_send()
        for k in range(me.depth - 1):
            for down in (False, True):
                @pl.when(self.sends(k, down))
                def _():
                    self.copy(k, down).wait_send()
        for o in range(1, me.planes):
            self.plane_copy(o).wait_send()


FOLD = 7


def fold_scratch(planes, depth, rows, full):
    block = (planes, 3, rows, full)
    return [
        pltpu.VMEM((depth,) + block, BF),
        pltpu.VMEM((depth,) + block, BF),
        pltpu.VMEM((depth + 1,) + block, BF),
        pltpu.VMEM(block, BF),
        pltpu.VMEM(block, BF),
        DMA((7, depth)),
        DMA((2, planes)),
    ]


def home_kernel(
    planes, depth, turns, n_gains,
    gn_ref, mixed_ref, og_ref, gains_ref, o_ref, lse_ref, q_ref, lower_ref, cos_ref, sin_ref, tok_ref,
    wo_any, kv_any, parts_any, grads_any, unit_any, recip_any, w_any, xat_any,
    block_out, grad_out, shard_out, shard_qkv, gains_out, pair_out, down_out,
    wo, kv, unit_s, recip_s, w_all, xat, own_part, gq, grad_kv, gmixed_s,
    bias, gob, delta, gkv, from_core, from_z, from_plane, partial, gproj, partial_q, gains_p, *rest,
):
    me = Place(planes, depth)
    collect = Collect(me, partial, rest[:COLLECT])
    collect_q = Collect(me, partial_q, rest[COLLECT : 2 * COLLECT])
    small = Collect(me, gains_p, rest[2 * COLLECT : 3 * COLLECT])
    fold = Fold(me, grads_any, rest[3 * COLLECT : 3 * COLLECT + FOLD])
    cs, zs, ps, load = rest[3 * COLLECT + FOLD :]
    half = turns // 2
    count = gn_ref.shape[0]
    sources = [wo_any, kv_any, unit_any, recip_any, w_any, xat_any, parts_any.at[0]]
    places = [wo, kv, unit_s, recip_s, w_all, xat, own_part]
    loads = [pltpu.make_async_copy(a, b, load.at[i]) for i, (a, b) in enumerate(zip(sources, places))]
    for copy in loads[:2]:
        copy.start()
    fold.start()
    for copy in loads[2:]:
        copy.start()
    greet(me.plane() + me.line() + [me.sibling()])
    fold.first()

    def c_copy(i):
        return remote(gkv.at[2 * i + 1], from_core.at[i], cs.at[0, i], cs.at[1, i], me.sibling())

    def z_copy(k):
        return remote(gkv.at[2 * k], from_z.at[k - 1], zs.at[0, k], zs.at[1, k], me.along(me.behind(k)))

    def p_copy(o):
        return remote(parts_any.at[o], from_plane.at[o - 1], ps.at[0, o], ps.at[1, o], me.across(o))

    for o in range(1, planes):
        p_copy(o).start()
    unit, recip = unit_of(mixed_ref[...], 1)
    grad = gn_ref[...]
    scaled = grad * gains_ref[:, D : 2 * D]
    inner = jnp.mean(scaled * unit, axis=1, keepdims=True)
    gmixed = og_ref[...].astype(F32) + recip * (scaled - unit * inner)
    gmixed_s[...] = gmixed
    dgf = jnp.sum(grad * unit, axis=0, keepdims=True)
    gmixed_b = gmixed.astype(BF)
    loads[0].wait()
    gob[...] = dot(wo[...].reshape(HQ, D), gmixed_b, NT).astype(BF)
    for t in range(GROUPS):
        rows = []
        for h in range(4):
            at = pl.ds(t * 256 + h * 64, 64)
            rows.append(
                jnp.sum(gob[at, :].astype(F32) * o_ref[at, :].astype(F32), axis=0, keepdims=True)
            )
        delta[t] = jnp.concatenate(rows, axis=0)
    half_rows = D // planes
    order = list(range(1, planes)) + [0]
    for o in order:
        d = me.dp ^ o
        rows = o_ref[pl.ds(pl.multiple_of(d * half_rows, 128), half_rows), :]
        partial[d] = dot(rows, gmixed_b, NN).astype(BF).reshape(partial.shape[1:])
        collect.first(o)
    fold.second()
    fold.step(0)
    gq[...] = jnp.zeros_like(gq)
    loads[1].wait()

    def visit(slot):
        fill_bias(bias, lower_ref[...], slot)

        def four_heads(t, carry):
            key_at = pl.ds(pl.multiple_of(t * 128, 128), 128)
            value_at = pl.ds(pl.multiple_of(HK + t * 128, 128), 128)
            keys, values = kv[slot, :, key_at], kv[slot, :, value_at]
            lse_t, delta_t = lse_ref[t], delta[t]
            grad_keys, grad_values = [], []
            for u in range(2):
                key = keys[:, u * 64 : u * 64 + 64]
                value = values[:, u * 64 : u * 64 + 64]
                grad_key, grad_value = 0.0, 0.0
                for g in range(2):
                    h = 2 * u + g
                    at = pl.ds(pl.multiple_of(t * 256 + h * 64, 64), 64)
                    query, gob_h = q_ref[at, :], gob[at, :]
                    probs = jnp.exp(dot(key, query, NN) + bias[...] - lse_t[h : h + 1, :])
                    grad_value = grad_value + dot(probs.astype(BF), gob_h, NT)
                    grad_scores = (probs * (dot(value, gob_h, NN) - delta_t[h : h + 1, :])).astype(BF)
                    grad_key = grad_key + dot(grad_scores, query, NT)
                    gq[at, :] += dot(key, grad_scores, TN)
                grad_keys.append(grad_key)
                grad_values.append(grad_value)
            gkv[slot, :, key_at] = jnp.concatenate(grad_keys, axis=1).astype(BF)
            gkv[slot, :, value_at] = jnp.concatenate(grad_values, axis=1).astype(BF)
            return carry

        lax.fori_loop(0, GROUPS, four_heads, 0)

    for i in range(half - 1, -1, -1):
        @pl.when(me.z - i - 1 + me.core >= 0)
        def _():
            visit(2 * i + 1)
            c_copy(i).start()

    for k in range(half, 0, -1):
        @pl.when(me.z - k >= 0)
        def _():
            visit(2 * k)

            @pl.when(me.core == 0)
            def _():
                if k < half:
                    c_copy(k).wait_recv()
                    gkv[2 * k] = (gkv[2 * k].astype(F32) + from_core[k].astype(F32)).astype(BF)

            @pl.when(me.core == 1)
            def _():
                c_copy(k - 1).wait_recv()
                gkv[2 * k] = (gkv[2 * k].astype(F32) + from_core[k - 1].astype(F32)).astype(BF)

            z_copy(k).start()

    for o in order:
        collect.second(o)
    if depth > 2:
        fold.step(1)
    visit(0)
    value_o = collect.third()
    total = mixed_ref[...]
    loads[6].wait()
    total = total + own_part[...].astype(F32)
    for o in range(1, planes):
        p_copy(o).wait_recv()
        total = total + from_plane[o - 1].astype(F32)
    block_out[...] = total.astype(BF)
    shard_out[...] = collect.last(value_o)
    grad_kv[...] = gkv[0].astype(F32)

    for i in (2, 3, 5, 4):
        loads[i].wait()
    tail_row = gains_ref[:, 2 * D : 2 * D + 128]
    gain_q, gain_k = column_of(tail_row, 0), column_of(tail_row, HEAD_DIM)
    cosine, sine = cos_ref[...], -sin_ref[...]
    gained = [0.0, 0.0]

    def four_grads(h):
        kind = 0 if h < HEADS else 1
        if kind == 0:
            four = gq[pl.ds(h * HEAD_DIM, 4 * HEAD_DIM), :] * HEAD_DIM ** (-0.5)
        else:
            four = grad_kv[:, pl.ds((h - HEADS) * HEAD_DIM, 4 * HEAD_DIM)].T
        recips = recip_s[h // 4]
        results = []
        for i in range(4):
            unit = unit_s[pl.ds((h + i) * HEAD_DIM, HEAD_DIM), :]
            grad = turned(four[i * HEAD_DIM : (i + 1) * HEAD_DIM], cosine, sine)
            scaled = grad * (gain_k if kind else gain_q)
            inner = jnp.mean(scaled * unit, axis=0, keepdims=True)
            results.append(recips[i : i + 1, :] * (scaled - unit * inner))
            gained[kind] = gained[kind] + grad * unit
        gproj[:, pl.ds(h * HEAD_DIM, 4 * HEAD_DIM)] = jnp.concatenate(results, axis=0).T.astype(BF)

    for h in range(0, HEADS, 4):
        four_grads(h)

    @pl.when(me.core == 0)
    def _():
        c_copy(0).wait_recv()
        grad_kv[...] += from_core[0].astype(F32)

    for k in range(1, half + 1):
        @pl.when(me.z + k < depth)
        def _():
            z_copy(k).wait_recv()
            grad_kv[...] += from_z[k - 1].astype(F32)

    for h in range(HEADS, HEADS + KV_HEADS, 4):
        four_grads(h)
    gproj[:, pl.ds(HQ + HK, HK)] = grad_kv[:, pl.ds(HK, HK)].astype(BF)
    for o in order:
        d = me.dp ^ o
        rows = xat[pl.ds(pl.multiple_of(d * half_rows, 128), half_rows), :]
        partial_q[d] = dot(rows, gproj[...], NN).astype(BF).reshape(partial_q.shape[1:])
        collect_q.first(o)
        if o != order[0]:
            collect_q.second(order[order.index(o) - 1])
    collect_q.second(0)
    for k in range(2, depth - 1):
        fold.step(k)
    grad = dot(gproj[...], w_all[...].reshape(D, 2 * HQ), NT)
    unit, recip = unit_of(tok_ref[...].astype(F32), 1)
    scaled = grad * gains_ref[:, :D]
    inner = jnp.mean(scaled * unit, axis=1, keepdims=True)
    grad_out[...] = gmixed_s[...] + recip * (scaled - unit * inner)
    dga = jnp.sum(grad * unit, axis=0, keepdims=True)
    lane = lax.broadcasted_iota(jnp.int32, (HEAD_DIM, 128), 1)
    entry = lax.broadcasted_iota(jnp.int32, (HEAD_DIM, 128), 0)
    sums = [jnp.sum(g, axis=1, keepdims=True) for g in gained]
    last = jnp.sum(
        jnp.where(lane == entry, sums[0], 0.0) + jnp.where(lane == entry + HEAD_DIM, sums[1], 0.0),
        axis=0,
        keepdims=True,
    )
    whole = jnp.concatenate([dga, dgf, last], axis=1)
    devices = planes * depth * 2
    entries = devices * n_gains
    index = lax.broadcasted_iota(jnp.int32, (devices, entries), 1)
    device = lax.broadcasted_iota(jnp.int32, (devices, entries), 0)
    apart = jnp.where(index // n_gains == device, whole, 0.0)
    pick = jnp.where(
        lax.broadcasted_iota(jnp.int32, (128, entries), 1) % n_gains
        == lax.broadcasted_iota(jnp.int32, (128, entries), 0),
        1.0,
        0.0,
    )
    table = lax.dot_general(
        apart, pick, NT, preferred_element_type=F32, precision=lax.Precision.HIGHEST
    )
    gains_p[...] = jnp.broadcast_to(table[:, None, :], (devices, 8, 128)).reshape(gains_p.shape)
    for o in order:
        small.first(o)
    for o in order:
        small.second(o)
    value = collect_q.third()
    little = small.third()
    fold.total()
    shard_qkv[...] = collect_q.last(value)
    gains_out[...] = small.last(little)
    fold.last()
    full = fold.landed.shape[3]
    for d in range(planes):
        for m in range(2):
            pair_out[:, (m * planes + d) * full : (m * planes + d + 1) * full] = fold.landed[d, m]
        down_out[:, d * full : (d + 1) * full] = fold.landed[d, 2]

    for o in range(1, planes):
        p_copy(o).wait_send()
    for i in range(half):
        @pl.when(me.z - i - 1 + me.core >= 0)
        def _():
            c_copy(i).wait_send()
    for k in range(1, half + 1):
        @pl.when(me.z - k >= 0)
        def _():
            z_copy(k).wait_send()
    collect.finish()
    collect_q.finish()
    small.finish()
    fold.finish()


def home(near, far, n_gains, planes, depth, turns, collective_id):
    half = turns // 2
    count = near[0].shape[0]
    wo_all, kv_all, _, grads, unit, recip, w_all, xat = far
    rows = wo_all.shape[3]
    full = grads.shape[4]
    return pl.pallas_call(
        functools.partial(home_kernel, planes, depth, turns, n_gains),
        out_shape=(
            jax.ShapeDtypeStruct((count, D), BF),
            jax.ShapeDtypeStruct((count, D), F32),
            jax.ShapeDtypeStruct((rows, D), F32),
            jax.ShapeDtypeStruct((rows, 2 * HQ), F32),
            jax.ShapeDtypeStruct((8, 128), F32),
            jax.ShapeDtypeStruct((rows, 2 * planes * full), BF),
            jax.ShapeDtypeStruct((rows, planes * full), BF),
        ),
        in_specs=[VMEM] * len(near) + [ANY] * len(far),
        out_specs=(VMEM,) * 7,
        scratch_shapes=[pltpu.VMEM(a.shape, a.dtype) for a in (wo_all, kv_all, unit, recip, w_all, xat)]
        + [
            pltpu.VMEM((count, D), BF),
            pltpu.VMEM((HQ, count), F32),
            pltpu.VMEM((count, 2 * HK), F32),
            pltpu.VMEM((count, D), F32),
            pltpu.VMEM((count, count), F32),
            pltpu.VMEM((HQ, count), BF),
            pltpu.VMEM((GROUPS, 4, count), F32),
            pltpu.VMEM((turns + 1, count, 2 * HK), BF),
            pltpu.VMEM((half, count, 2 * HK), BF),
            pltpu.VMEM((half, count, 2 * HK), BF),
            pltpu.VMEM((planes - 1, count, D), BF),
            pltpu.VMEM((planes, depth, 2, rows, D), BF),
            pltpu.VMEM((count, 2 * HQ), BF),
            pltpu.VMEM((planes, depth, 2, rows, 2 * HQ), BF),
            pltpu.VMEM((planes, depth, 2, 8, 128), F32),
        ]
        + collect_scratch(planes, depth, rows, D, BF)
        + collect_scratch(planes, depth, rows, 2 * HQ, BF)
        + collect_scratch(planes, depth, 8, 128, F32)
        + fold_scratch(planes, depth, rows, full)
        + [DMA((2, half)), DMA((2, half + 1)), DMA((2, planes)), DMA((7,))],
        compiler_params=params(collective_id),
        cost_estimate=pl.CostEstimate(flops=60 << 30, bytes_accessed=8 << 20, transcendentals=0),
    )(*near, *far)


def per_device(
    tokens_in,
    positions,
    out_grad,
    w_qkv,
    w_output,
    w_gate_up,
    w_down,
    norm_gains,
    first_qkv,
    first_output,
    first_gate_up,
    first_down,
    first_gains,
    second_qkv,
    second_output,
    second_gate_up,
    second_down,
    second_gains,
):
    planes, ctxs = lax.axis_size("dp"), lax.axis_size("ctx")
    depth = ctxs // 2
    turns = ctxs // 2
    rows = w_qkv.shape[0]
    full = w_down.shape[1] // planes
    n_gains = norm_gains.shape[0]
    count = tokens_in.shape[0] * tokens_in.shape[1]
    tokens = tokens_in.reshape(count, D)
    places = positions.reshape(count)
    cotangent = out_grad.reshape(count, D)

    gains_block = jnp.pad(norm_gains.astype(BF).astype(F32)[None, :], ((0, 7), (0, 128 - n_gains)))
    cosine, sine = rope_tables(places)
    lower = (jnp.arange(count, dtype=jnp.int32) - places)[None, :]
    (
        query, kv_all, qkv_all, xat, unit_heads, recip_heads, og_all, output_all, w_all,
        gains_row, attn_t, lse, mixed, hn,
    ) = ahead(
        tokens, cosine, sine, lower, gains_block, w_qkv, w_output, w_gate_up, w_down, cotangent,
        n_gains, planes, depth, turns, 0,
    )
    w_used = w_all if rows % 16 == 0 else w_all.transpose(2, 1, 0, 3, 4).reshape(1, 1, 3, D, full)
    grad_normed, parts, grads = ffn(hn, og_all, w_used, planes, depth, 1)
    if rows % 16 != 0:
        grads = grads.reshape(3, planes, ctxs, rows, full).transpose(2, 1, 0, 3, 4)
    block_out, input_grad, shard_output, shard_qkv, gains_tile, pair_b, down_b = home(
        (grad_normed, mixed, cotangent, gains_row, attn_t, lse, query, lower, cosine, sine, tokens),
        (output_all, kv_all, parts, grads, unit_heads, recip_heads, qkv_all, xat),
        n_gains, planes, depth, turns, 2,
    )
    shard_gains = gains_tile[0, :n_gains]
    shard_gate_up = pair_b.astype(F32)
    shard_down = down_b.astype(F32)

    new_qkv, new_first_qkv, new_second_qkv = adam_step(
        w_qkv, shard_qkv, first_qkv, second_qkv, 0.02, 0.1
    )
    new_output, new_first_output, new_second_output = adam_step(
        w_output, shard_output, first_output, second_output, 0.2, 0.1
    )
    new_gate_up, new_first_gate_up, new_second_gate_up = adam_step(
        w_gate_up, shard_gate_up, first_gate_up, second_gate_up, 0.02, 0.1
    )
    new_down, new_first_down, new_second_down = adam_step(
        w_down, shard_down, first_down, second_down, 0.02, 0.1
    )
    new_gains, new_first_gains, new_second_gains = adam_step(
        norm_gains, shard_gains, first_gains, second_gains, 0.1, 0.0
    )
    return (
        block_out.reshape(tokens_in.shape),
        input_grad.reshape(tokens_in.shape),
        shard_qkv,
        shard_output,
        shard_gate_up,
        shard_down,
        shard_gains,
        new_qkv,
        new_output,
        new_gate_up,
        new_down,
        new_gains,
        new_first_qkv,
        new_first_output,
        new_first_gate_up,
        new_first_down,
        new_first_gains,
        new_second_qkv,
        new_second_output,
        new_second_gate_up,
        new_second_down,
        new_second_gains,
    )


def solution(mesh):
    in_specs = (
        P("dp", "ctx", None),
        P("dp", "ctx"),
        P("dp", "ctx", None),
        P(("dp", "ctx"), None),
        P(("dp", "ctx"), None),
        P(("dp", "ctx"), None),
        P(("dp", "ctx"), None),
        P(("dp", "ctx")),
        P(("dp", "ctx"), None),
        P(("dp", "ctx"), None),
        P(("dp", "ctx"), None),
        P(("dp", "ctx"), None),
        P(("dp", "ctx")),
        P(("dp", "ctx"), None),
        P(("dp", "ctx"), None),
        P(("dp", "ctx"), None),
        P(("dp", "ctx"), None),
        P(("dp", "ctx")),
    )
    out_specs = (
        P("dp", "ctx", None),
        P("dp", "ctx", None),
        P(("dp", "ctx"), None),
        P(("dp", "ctx"), None),
        P(("dp", "ctx"), None),
        P(("dp", "ctx"), None),
        P(("dp", "ctx")),
        P(("dp", "ctx"), None),
        P(("dp", "ctx"), None),
        P(("dp", "ctx"), None),
        P(("dp", "ctx"), None),
        P(("dp", "ctx")),
        P(("dp", "ctx"), None),
        P(("dp", "ctx"), None),
        P(("dp", "ctx"), None),
        P(("dp", "ctx"), None),
        P(("dp", "ctx")),
        P(("dp", "ctx"), None),
        P(("dp", "ctx"), None),
        P(("dp", "ctx"), None),
        P(("dp", "ctx"), None),
        P(("dp", "ctx")),
    )
    return jax.shard_map(
        per_device, mesh=mesh, in_specs=in_specs, out_specs=out_specs, check_vma=False
    )
```

```python
import functools
import math

import jax
import jax.numpy as jnp
from jax import lax
from jax.experimental import pallas as pl
from jax.experimental.pallas import tpu as pltpu
from jax.sharding import PartitionSpec as P

D = 1024
HEADS = 16
KV_HEADS = 8
HEAD_DIM = 64
STEP = 4
HQ = 1024
HK = 512


EPS = 1e-05
THETA = 1000000.0
NEG_BIG = -1e30
BETA_ONE = 0.9
BETA_TWO = 0.95
ADAM_EPS = 1e-08


def rope_tables(places):
    half = HEAD_DIM // 2
    freqs = jnp.exp(-math.log(THETA) * (2.0 * jnp.arange(half, dtype=jnp.float32) / HEAD_DIM))
    angles = freqs[:, None] * places.astype(jnp.float32)[None, :]
    return (jnp.cos(angles), jnp.sin(angles))


def adam_step(weight, grad, first, second, rate, decay):
    first_new = BETA_ONE * first + (1.0 - BETA_ONE) * grad
    second_new = BETA_TWO * second + (1.0 - BETA_TWO) * grad * grad
    first_hat = first_new / (1.0 - BETA_ONE**STEP)
    second_hat = second_new / (1.0 - BETA_TWO**STEP)
    weight_new = weight - rate * (first_hat / (jnp.sqrt(second_hat) + ADAM_EPS) + decay * weight)
    return (weight_new, first_new, second_new)


BF = jnp.bfloat16
F32 = jnp.float32
MESH_ID = pl.DeviceIdType.MESH
ANY = pl.BlockSpec(memory_space=pl.ANY)
VMEM = pl.BlockSpec(memory_space=pltpu.VMEM)
DMA = pltpu.SemaphoreType.DMA
NN = (((1,), (0,)), ((), ()))
NT = (((1,), (1,)), ((), ()))
TN = (((0,), (0,)), ((), ()))
VMEM_BYTES = 60 << 20
GROUPS = HEADS // 4


def dot(a, b, dims):
    return lax.dot_general(a, b, dims, preferred_element_type=F32)


class Place:
    def __init__(self, planes, depth):
        self.planes, self.depth = planes, depth
        self.dp = lax.axis_index("dp")
        self.ctx = lax.axis_index("ctx")
        self.z = self.ctx // 2
        self.core = self.ctx % 2

    def sibling(self):
        return {"dp": self.dp, "ctx": self.z * 2 + 1 - self.core}

    def across(self, o):
        return {"dp": self.dp ^ o, "ctx": self.ctx}

    def behind(self, k):
        return lax.rem(self.z + self.depth - k, self.depth)

    def ahead(self, k):
        return lax.rem(self.z + k, self.depth)

    def along(self, z):
        return {"dp": self.dp, "ctx": z * 2 + self.core}

    def plane(self):
        return [self.across(o) for o in range(1, self.planes)]

    def line(self):
        return [self.along(self.ahead(k)) for k in range(1, self.depth)]


def near(planes):
    return [o for o in range(1, planes) if o & (o - 1) == 0]


def far(planes):
    return [o for o in range(1, planes) if o & (o - 1) != 0]


def greet(devices):
    barrier = pltpu.get_barrier_semaphore()
    for device in devices:
        pl.semaphore_signal(barrier, inc=1, device_id=device, device_id_type=MESH_ID)
    pl.semaphore_wait(barrier, len(devices))


def remote(src, dst, send, recv, device):
    return pltpu.make_async_remote_copy(
        src_ref=src, dst_ref=dst, send_sem=send, recv_sem=recv, device_id=device, device_id_type=MESH_ID
    )


def params(collective_id):
    return pltpu.CompilerParams(
        vmem_limit_bytes=VMEM_BYTES, collective_id=collective_id, has_side_effects=True
    )


class Spread:
    def __init__(self, me, g_ref, line_sems, sems):
        self.me, self.g, self.line_sems, self.sems = me, g_ref, line_sems, sems
        self.sent = []

    def push(self, src, dst, kind, o, device):
        copy = remote(src, dst, self.sems.at[kind, o], self.sems.at[kind + 1, o], device)
        copy.start()
        self.sent.append(copy)

    def mine(self, o, core):
        return self.g.at[self.me.dp ^ o, :, core]

    def line(self):
        me = self.me
        block = self.g.at[me.dp, me.z, me.core]
        for k in range(1, me.depth):
            copy = remote(
                block, block, self.line_sems.at[0, k], self.line_sems.at[1, k], me.along(me.ahead(k))
            )
            copy.start()
            self.sent.append(copy)

    def first(self):
        me = self.me
        for k in range(1, me.depth):
            block = self.g.at[me.dp, me.behind(k), me.core]
            remote(
                block, block, self.line_sems.at[0, k], self.line_sems.at[1, k], me.along(me.ahead(k))
            ).wait_recv()
        self.push(self.mine(0, me.core), self.mine(0, me.core), 2, 0, me.sibling())
        self.plane(near(me.planes))

    def plane(self, places):
        me = self.me
        for o in places:
            self.push(self.mine(0, me.core), self.mine(0, me.core), 0, o, me.across(o))

    def relay(self, o):
        block = self.mine(o, self.me.core)
        remote(block, block, self.sems.at[0, o], self.sems.at[1, o], self.me.sibling()).wait_recv()
        self.push(block, block, 2, o, self.me.sibling())

    def arrive(self, o):
        block = self.mine(o, 1 - self.me.core)
        remote(block, block, self.sems.at[2, o], self.sems.at[3, o], self.me.sibling()).wait_recv()

    def finish(self):
        for copy in self.sent:
            copy.wait_send()


def spread_sems(planes, depth):
    return [DMA((2, depth)), DMA((4, planes))]


class Collect:
    def __init__(self, me, p_ref, scratch):
        self.me, self.p = me, p_ref
        self.sums, self.from_plane, self.total, self.from_z, self.cs, self.ps, self.zs = scratch

    def c_copy(self, o):
        me = self.me
        return remote(
            self.p.at[me.dp ^ o, :, 1 - me.core], self.sums.at[o], self.cs.at[0, o], self.cs.at[1, o], me.sibling()
        )

    def p_copy(self, o):
        return remote(
            self.sums.at[o], self.from_plane.at[o - 1], self.ps.at[0, o], self.ps.at[1, o], self.me.across(o)
        )

    def z_copy(self, k):
        me = self.me
        return remote(
            self.total.at[me.ahead(k)], self.from_z.at[k], self.zs.at[0, k], self.zs.at[1, k], me.along(me.ahead(k))
        )

    def first(self, o):
        self.c_copy(o).start()

    def second(self, o):
        me = self.me
        self.c_copy(o).wait_recv()
        own = self.p[me.dp ^ o, :, me.core].astype(F32)
        self.sums[o] = (own + self.sums[o].astype(F32)).astype(self.sums.dtype)
        if o > 0:
            self.p_copy(o).start()

    def third(self):
        me = self.me
        for o in range(1, me.planes):
            self.p_copy(o).wait_recv()
        for k in list(range(1, me.depth)) + [0]:
            z = me.ahead(k)
            value = self.sums[0, z].astype(F32)
            for o in range(1, me.planes):
                value = value + self.from_plane[o - 1, z].astype(F32)
            self.total[z] = value.astype(self.total.dtype)
            if k > 0:
                self.z_copy(k).start()
        return value

    def last(self, value):
        for k in range(1, self.me.depth):
            self.z_copy(k).wait_recv()
            value = value + self.from_z[k].astype(F32)
        return value

    def finish(self):
        for o in range(self.me.planes):
            self.c_copy(o).wait_send()
        for o in range(1, self.me.planes):
            self.p_copy(o).wait_send()
        for k in range(1, self.me.depth):
            self.z_copy(k).wait_send()


def collect_scratch(planes, depth, rows, columns, kind):
    return [
        pltpu.VMEM((planes, depth, rows, columns), kind),
        pltpu.VMEM((planes - 1, depth, rows, columns), kind),
        pltpu.VMEM((depth, rows, columns), kind),
        pltpu.VMEM((depth, rows, columns), kind),
        DMA((2, planes)),
        DMA((2, planes)),
        DMA((2, depth)),
    ]


COLLECT = 7


def unit_of(values, axis):
    recip = lax.rsqrt(jnp.mean(values * values, axis=axis, keepdims=True) + EPS)
    return values * recip, recip


def column_of(row, start):
    lane = lax.broadcasted_iota(jnp.int32, (HEAD_DIM, 128), 1)
    entry = lax.broadcasted_iota(jnp.int32, (HEAD_DIM, 128), 0)
    return jnp.sum(jnp.where(lane == entry + start, row, 0.0), axis=1, keepdims=True)


def turned(values, cosine, sine):
    half = HEAD_DIM // 2
    a, b = values[:half], values[half:]
    return jnp.concatenate([a * cosine - b * sine, b * cosine + a * sine], axis=0)


def fill_bias(bias, lower, slot):
    count = bias.shape[0]
    query = lax.broadcasted_iota(jnp.int32, (count, count), 1)
    key = lax.broadcasted_iota(jnp.int32, (count, count), 0) - slot * count
    bias[...] = jnp.where((key <= query) & (key >= lower), 0.0, NEG_BIG)


class Pass:
    def __init__(self, me, w_ref, sems):
        self.me, self.w, self.sems = me, w_ref, sems

    def copy(self, kind, s, down, core=None, device=None):
        me = self.me
        z = me.z + s - 1 if down else me.z - s + 1
        block = self.w.at[:, :, z * 2 + (me.core if core is None else core)]
        device = me.sibling() if device is None else device
        return remote(block, block, self.sems.at[kind, s], self.sems.at[kind + 1, s], device)

    def held(self, s, down):
        me = self.me
        return me.z + s - 1 < me.depth if down else me.z - s + 1 >= 0

    def on(self, s, down):
        me = self.me
        return self.held(s, down) & (me.z >= 1 if down else me.z + 1 < me.depth)

    def line_copy(self, s, down):
        me = self.me
        return self.copy(2 if down else 0, s, down, None, me.along(me.z - 1 if down else me.z + 1))

    def step(self, s):
        for down in (False, True):
            if s > 1:
                @pl.when(self.held(s, down))
                def _():
                    me = self.me
                    z = me.z + s - 1 if down else me.z - s + 1
                    block = self.w.at[:, :, z * 2 + me.core]
                    kind = 2 if down else 0
                    remote(
                        block, block, self.sems.at[kind, s - 1], self.sems.at[kind + 1, s - 1], me.sibling()
                    ).wait_recv()

            @pl.when(self.on(s, down))
            def _():
                self.line_copy(s, down).start()

            if s > 1 or not down:
                @pl.when(self.held(s, down))
                def _():
                    self.copy(6 if down else 4, s, down).start()

    def arrive(self):
        for s in range(1, self.me.depth + 1):
            for down in (False, True):
                if s > 1 or not down:
                    @pl.when(self.held(s, down))
                    def _():
                        self.copy(6 if down else 4, s, down, 1 - self.me.core).wait_recv()

    def finish(self):
        for s in range(1, self.me.depth + 1):
            for down in (False, True):
                @pl.when(self.on(s, down))
                def _():
                    self.line_copy(s, down).wait_send()

                if s > 1 or not down:
                    @pl.when(self.held(s, down))
                    def _():
                        self.copy(6 if down else 4, s, down).wait_send()


def fore_kernel(
    planes, depth, turns, n_gains,
    tok_ref, cos_ref, sin_ref, lower_ref, gain_ref, wqkv_ref, wout_ref, wpair_ref, wdown_ref, og_ref,
    q_any, kv_any, wq_any, wkv_any, xat_any, unit_any, recip_any, wo_any, parts_any, spill_any, grads_a, grads_b, mine_any,
    gains_out, o_out, lse_out, mixed_out, gn_out,
    q_s, kv_all, wq_all, wkv_all, xat, unit_s, recip_s, wo_all, blocks_a, blocks_b, gains_g, xa, proj, bias, accum, sums,
    wa, wb, hns, ogs, hnt, ogt, mid, pair, send_gn, recv_gn, part_s, stage, mine,
    own_sem, keep_sem, zs, cs, ps, a2a_a, a2a_b, pass_a, pass_b, hsem, nsem, psem, ssem, stsem,
    glsem, gsem, qlsem, qsem, wlsem, wsem, olsem, osem, *fold_rest,
):
    me = Place(planes, depth)
    half = turns // 2
    count = tok_ref.shape[0]
    width = D // planes
    rows = wqkv_ref.shape[0]
    halves = (blocks_a.shape[3], blocks_b.shape[3])
    full = sum(halves)
    gains = Spread(me, gains_g, glsem, gsem)
    queries = Spread(me, wq_all, qlsem, qsem)
    weights = Spread(me, wkv_all, wlsem, wsem)
    outputs = Spread(me, wo_all, olsem, osem)
    pass_first, pass_second = Pass(me, wa, pass_a), Pass(me, wb, pass_b)
    fold = Fold(me, grads_a, mine, fold_rest)
    kept = []

    def keep(source, into):
        copy = pltpu.make_async_copy(source, into, keep_sem.at[len(kept)])
        copy.start()
        kept.append(copy)

    gains_g[me.dp, me.z, me.core] = gain_ref[...]
    wq_all[me.dp, me.z, me.core] = wqkv_ref[:, :HQ].astype(BF)
    wkv_all[me.dp, me.z, me.core] = wqkv_ref[:, HQ:].astype(BF)
    wo_all[me.dp, me.z, me.core] = wout_ref[...].astype(BF)
    for d in range(planes):
        for m in range(3):
            source = wdown_ref if m == 2 else wpair_ref
            at = d * full if m == 2 else (m * planes + d) * full
            blocks_a[d, m] = source[:, at : at + halves[0]].astype(BF)
            blocks_b[d, m] = source[:, at + halves[0] : at + full].astype(BF)
    wa[:, me.dp, me.ctx] = blocks_a[me.dp]
    wb[:, me.dp, me.ctx] = blocks_b[me.dp]
    own_og = pltpu.make_async_copy(og_ref, ogs.at[0], own_sem.at[1])
    own_og.start()
    greet(me.plane() + me.line() + [me.sibling()])
    gains.line()
    weights.line()

    def a2a_copy(part, o):
        source, into, sems = ((blocks_a, wa, a2a_a), (blocks_b, wb, a2a_b))[part]
        return remote(
            source.at[me.dp ^ o], into.at[:, me.dp, me.ctx], sems.at[0, o], sems.at[1, o], me.across(o)
        )

    def a2a_wait(part):
        into, sems = ((wa, a2a_a), (wb, a2a_b))[part]
        for o in range(1, planes):
            block = into.at[:, me.dp ^ o, me.ctx]
            remote(block, block, sems.at[0, o], sems.at[1, o], me.across(o)).wait_recv()

    for part in range(2):
        for o in range(1, planes):
            a2a_copy(part, o).start()
    queries.line()
    outputs.line()
    unit, _ = unit_of(tok_ref[...].astype(F32), 1)
    proj[:, :D] = unit
    gains.first()
    gains.plane(far(planes))
    weights.first()
    a2a_wait(0)
    pass_first.step(1)
    queries.first()
    for o in range(1, planes):
        gains.relay(o)
    for o in range(planes):
        gains.arrive(o)
    devices = planes * depth * 2
    table = gains_g[...].reshape(devices, 8, 128)[:, 0, :].astype(BF)
    entries = devices * n_gains
    index = lax.broadcasted_iota(jnp.int32, (128, entries), 1)
    pick = jnp.where(
        index % n_gains == lax.broadcasted_iota(jnp.int32, (128, entries), 0), 1.0, 0.0
    ).astype(BF)
    spread = dot(table, pick, NN)
    owner = lax.broadcasted_iota(jnp.int32, (devices, entries), 1) // n_gains
    device = lax.broadcasted_iota(jnp.int32, (devices, entries), 0)
    gains_row = 1.0 + jnp.sum(jnp.where(owner == device, spread, 0.0), axis=0, keepdims=True)
    gains_out[...] = gains_row
    normed = (proj[:, :D] * gains_row[:, :D]).astype(BF)
    xat[...] = normed.T
    keep(xat, xat_any)
    for d in range(planes):
        xa[d] = normed[:, d * width : (d + 1) * width]

    def project(source, table, at):
        proj[:, at] = jnp.zeros((count, D), F32)
        places = [0] + near(planes) + far(planes)
        for o in places:
            if o > 0:
                source.relay(o)
            source.arrive(o)
            if o == near(planes)[-1]:
                source.plane(far(planes))
            proj[:, at] += dot(xa[me.dp ^ o], table[me.dp ^ o].reshape(width, D), NN)

    project(weights, wkv_all, pl.ds(HQ, 2 * HK))
    tail_row = gains_row[:, 2 * D : 2 * D + 128]
    gain_q, gain_k = column_of(tail_row, 0), column_of(tail_row, HEAD_DIM)
    cosine, sine = cos_ref[...], sin_ref[...]

    def four_raw(h):
        four = proj[:, h * HEAD_DIM : (h + 4) * HEAD_DIM].T
        results, recips = [], []
        for i in range(4):
            value, recip = unit_of(four[i * HEAD_DIM : (i + 1) * HEAD_DIM], 0)
            unit_s[pl.ds((h + i) * HEAD_DIM, HEAD_DIM), :] = value
            recips.append(recip)
            results.append(turned(value * (gain_q if h < HEADS else gain_k), cosine, sine))
        recip_s[h // 4] = jnp.concatenate(recips, axis=0)
        return jnp.concatenate(results, axis=0)

    for h in range(HEADS, HEADS + KV_HEADS, 4):
        kv_all[0, :, pl.ds((h - HEADS) * HEAD_DIM, 4 * HEAD_DIM)] = four_raw(h).T.astype(BF)
    kv_all[0, :, pl.ds(HK, HK)] = proj[:, HQ + HK :].astype(BF)

    def z_copy(k):
        return remote(kv_all.at[0], kv_all.at[2 * k], zs.at[0, k], zs.at[1, k], me.along(me.ahead(k)))

    def c_copy(i):
        return remote(
            kv_all.at[2 * i + 2 * me.core], kv_all.at[2 * i + 1], cs.at[0, i], cs.at[1, i], me.sibling()
        )

    for k in range(1, half + 1):
        @pl.when(me.z + k < depth)
        def _():
            z_copy(k).start()

    @pl.when(me.core == 0)
    def _():
        c_copy(0).start()

    pass_first.step(2)
    project(queries, wq_all, pl.ds(0, HQ))
    outputs.first()
    for h in range(0, HEADS, 4):
        q_s[pl.ds(h * HEAD_DIM, 4 * HEAD_DIM), :] = (four_raw(h) * HEAD_DIM ** (-0.5)).astype(BF)
    keep(q_s, q_any)
    keep(unit_s, unit_any)
    keep(recip_s, recip_any)
    keep(wq_all, wq_any)
    keep(wkv_all, wkv_any)
    outputs.plane(far(planes))
    shares = []
    for o in range(1, planes):
        share = remote(og_ref, ogs.at[o], ps.at[0, o], ps.at[1, o], me.across(o))
        share.start()
        shares.append(share)
    pass_first.step(3)
    accum[...] = jnp.zeros_like(accum)
    sums[...] = jnp.zeros_like(sums)

    def visit(slot):
        fill_bias(bias, lower_ref[...], slot)

        def four_heads(t, carry):
            keys = kv_all[slot, :, pl.ds(pl.multiple_of(t * 128, 128), 128)]
            values = kv_all[slot, :, pl.ds(pl.multiple_of(HK + t * 128, 128), 128)]
            totals = []
            for u in range(2):
                key = keys[:, u * 64 : u * 64 + 64]
                value = values[:, u * 64 : u * 64 + 64]
                for g in range(2):
                    at = pl.ds(pl.multiple_of(t * 256 + u * 128 + g * 64, 64), 64)
                    weight = jnp.exp(dot(key, q_s[at, :], NN) + bias[...])
                    totals.append(jnp.sum(weight, axis=0, keepdims=True))
                    accum[at, :] += dot(value, weight.astype(BF), TN)
            sums[t] += jnp.concatenate(totals, axis=0)
            return carry

        lax.fori_loop(0, GROUPS, four_heads, 0)

    visit(0)
    for k in range(1, half + 1):
        there = me.z - k >= 0

        @pl.when(there)
        def _():
            z_copy(k).wait_recv()

        @pl.when(there & (me.core == 1))
        def _():
            c_copy(k - 1).start()

        if k < half:
            @pl.when(there & (me.core == 0))
            def _():
                c_copy(k).start()

        @pl.when(there)
        def _():
            visit(2 * k)

    a2a_wait(1)
    pass_second.step(1)
    for i in range(half):
        @pl.when(me.z - i - 1 + me.core >= 0)
        def _():
            c_copy(i).wait_recv()
            visit(2 * i + 1)

    keep(kv_all, kv_any)
    for o in range(1, planes):
        outputs.relay(o)
    for t in range(GROUPS):
        total = sums[t]
        lse_out[t] = jnp.log(total)
        for h in range(4):
            at = pl.ds(t * 256 + h * 64, 64)
            o_out[at, :] = (accum[at, :] / total[h : h + 1, :]).astype(BF)
    for o in range(planes):
        outputs.arrive(o)
    keep(wo_all, wo_any)
    mixed = tok_ref[...].astype(F32) + dot(o_out[...].T, wo_all[...].reshape(HQ, D), NN)
    mixed_out[...] = mixed
    unit, _ = unit_of(mixed, 1)
    hns[0] = (unit * gains_out[:, D : 2 * D]).astype(BF)

    def hn_copy(o):
        return remote(hns.at[0], hns.at[o], hsem.at[0, o], hsem.at[1, o], me.across(o))

    def gn_copy(o):
        return remote(send_gn.at[o - 1], recv_gn.at[o - 1], nsem.at[0, o], nsem.at[1, o], me.across(o))

    def spill_copy(o, back):
        ends = (spill_any.at[o], proj) if back else (proj, spill_any.at[o])
        return pltpu.make_async_copy(*ends, ssem.at[0])

    def parts_copy(o):
        return pltpu.make_async_copy(part_s, parts_any.at[o], psem.at[0])

    for o in near(planes):
        hn_copy(o).start()
    for s in range(4, depth + 1):
        pass_first.step(s)
    pass_first.arrive()
    own_og.wait()

    def ffn_part(part):
        w, f = (wa, wb)[part], halves[part]

        def block(o, carry):
            if part == 0:
                @pl.when(o > 0)
                def _():
                    hn_copy(o).wait_recv()
                    remote(og_ref, ogs.at[o], ps.at[0, o], ps.at[1, o], me.across(o)).wait_recv()
            else:
                spill_copy(o, True).start()

            hn, og = hns[o], ogs[o]
            at = pl.ds(pl.multiple_of(o * count, 128), count)
            if part == 0:
                hnt[:, at] = hn.T
                ogt[:, at] = og.T
            w_gate, w_up, w_down = (w[m].reshape(D, f) for m in range(3))
            gate = dot(hn, w_gate, NN)
            upper = dot(hn, w_up, NN)
            sigma = 1.0 / (1.0 + jnp.exp(-gate))
            active = gate * sigma
            middle = (active * upper).astype(BF)
            gmid = dot(og, w_down, NN)
            ggate = (gmid * upper * sigma * (1.0 + gate * (1.0 - sigma))).astype(BF)
            gupper = (gmid * active).astype(BF)
            mid[at, :f] = middle
            pair[0, at, :f] = ggate
            pair[1, at, :f] = gupper
            gn = dot(ggate, w_gate, NT) + dot(gupper, w_up, NT)
            out = dot(middle, w_down, NT)
            if part == 0:
                @pl.when(o > 0)
                def _():
                    spill_copy(o - 1, False).wait()

                proj[:, :D] = gn
                proj[:, D:] = out
                spill_copy(o, False).start()

                @pl.when(o == 0)
                def _():
                    for other in far(planes):
                        hn_copy(other).start()
                    pass_second.step(2)

                @pl.when(o == planes // 2)
                def _():
                    pass_second.step(3)
            else:
                spill_copy(o, True).wait()
                gn = gn + proj[:, :D]
                out = out + proj[:, D:]

                @pl.when(o > 0)
                def _():
                    parts_copy(o - 1).wait()
                    send_gn[o - 1] = gn.astype(BF)
                    gn_copy(o).start()

                @pl.when(o == 0)
                def _():
                    gn_out[...] = gn
                    fold.second()
                    fold.step(0)

                @pl.when(o == planes // 2)
                def _():
                    fold.step(1)

                part_s[...] = out.astype(BF)
                parts_copy(o).start()
            return carry

        lax.fori_loop(0, planes, block, 0)
        if part == 0:
            spill_copy(planes - 1, False).wait()
        else:
            parts_copy(planes - 1).wait()
        strip = D // planes
        grads = (grads_a, grads_b)[part]

        def out_copy(m, d):
            return pltpu.make_async_copy(stage.at[m, :, :, :f], grads.at[:, d, m], stsem.at[m])

        def weight_grads(d, carry):
            left = pl.ds(pl.multiple_of(d * strip, 128), strip)
            for m in (2, 0, 1):
                @pl.when(d > 0)
                def _():
                    out_copy(m, d - 1).wait()

                if m == 2:
                    total = dot(ogt[left, :], mid[:, :f], NN)
                else:
                    total = dot(hnt[left, :], pair[m, :, :f], NN)
                stage[m, :, :, :f] = total.astype(BF).reshape(depth * 2, rows, f)
                out_copy(m, d).start()
            return carry

        lax.fori_loop(0, planes, weight_grads, 0)
        for m in range(3):
            out_copy(m, planes - 1).wait()

    ffn_part(0)
    fold.first()
    for s in range(4, depth + 1):
        pass_second.step(s)
    pass_second.arrive()
    ffn_part(1)
    total = gn_out[...]
    for o in range(1, planes):
        gn_copy(o).wait_recv()
        total = total + recv_gn[o - 1].astype(F32)
    gn_out[...] = total
    fold.settle(EARLY - 1)
    keep(mine, mine_any)
    pass_first.finish()
    pass_second.finish()
    fold.finish(True, range(EARLY))
    for o in range(1, planes):
        gn_copy(o).wait_send()
        hn_copy(o).wait_send()

    for i in range(half):
        @pl.when(me.z - i - me.core >= 0)
        def _():
            c_copy(i).wait_send()

    for k in range(1, half + 1):
        @pl.when(me.z + k < depth)
        def _():
            z_copy(k).wait_send()

    for o in range(1, planes):
        a2a_copy(0, o).wait_send()
        a2a_copy(1, o).wait_send()
    for share in shares:
        share.wait_send()
    gains.finish()
    queries.finish()
    weights.finish()
    outputs.finish()
    for copy in kept:
        copy.wait()


def fore(tokens, cosine, sine, lower, gains_block, w_qkv, w_output, w_gate_up, w_down, cotangent, n_gains, planes, depth, turns, collective_id):
    half = turns // 2
    count = tokens.shape[0]
    rows = w_qkv.shape[0]
    first, second = split(w_down.shape[1] // planes)
    devices = planes * depth * 2
    everyone = (planes, depth, 2, rows)
    shapes = [
        ((HQ, count), BF),
        ((turns + 1, count, 2 * HK), BF),
        (everyone + (HQ,), BF),
        (everyone + (2 * HK,), BF),
        ((D, count), BF),
        ((HQ + HK, count), F32),
        (((HEADS + KV_HEADS) // 4, 4, count), F32),
        (everyone + (D,), BF),
        ((planes, count, D), BF),
        ((planes, count, 2 * D), F32),
        ((depth * 2, planes, 3, rows, first), BF),
        ((depth * 2, planes, 3, rows, second), BF),
        ((depth, planes, 3, rows, first), BF),
        ((1, devices * n_gains), F32),
        ((HQ, count), BF),
        ((GROUPS, 4, count), F32),
        ((count, D), F32),
        ((count, D), F32),
    ]
    flops = 18 * planes * count * D * (first + second)
    return pl.pallas_call(
        functools.partial(fore_kernel, planes, depth, turns, n_gains),
        out_shape=tuple(jax.ShapeDtypeStruct(s, k) for s, k in shapes),
        in_specs=[VMEM] * 9 + [ANY],
        out_specs=(ANY,) * 13 + (VMEM,) * 5,
        scratch_shapes=[pltpu.VMEM(*shape) for shape in shapes[:8]]
        + [
            pltpu.VMEM((planes, 3, rows, first), BF),
            pltpu.VMEM((planes, 3, rows, second), BF),
            pltpu.VMEM((planes, depth, 2, 8, 128), F32),
            pltpu.VMEM((planes, count, D // planes), BF),
            pltpu.VMEM((count, 2 * HQ), F32),
            pltpu.VMEM((count, count), F32),
            pltpu.VMEM((HQ, count), F32),
            pltpu.VMEM((GROUPS, 4, count), F32),
            pltpu.VMEM((3, planes, depth * 2, rows, first), BF),
            pltpu.VMEM((3, planes, depth * 2, rows, second), BF),
            pltpu.VMEM((planes, count, D), BF),
            pltpu.VMEM((planes, count, D), BF),
            pltpu.VMEM((D, planes * count), BF),
            pltpu.VMEM((D, planes * count), BF),
            pltpu.VMEM((planes * count, max(first, second)), BF),
            pltpu.VMEM((2, planes * count, max(first, second)), BF),
            pltpu.VMEM((planes - 1, count, D), BF),
            pltpu.VMEM((planes - 1, count, D), BF),
            pltpu.VMEM((count, D), BF),
            pltpu.VMEM((3, depth * 2, rows, max(first, second)), BF),
            pltpu.VMEM((depth, planes, 3, rows, first), BF),
            DMA((2,)),
            DMA((9,)),
            DMA((2, half + 1)),
            DMA((2, half)),
            DMA((2, planes)),
            DMA((2, planes)),
            DMA((2, planes)),
            DMA((8, depth + 1)),
            DMA((8, depth + 1)),
            DMA((2, planes)),
            DMA((2, planes)),
            DMA((1,)),
            DMA((1,)),
            DMA((3,)),
        ]
        + spread_sems(planes, depth) * 4
        + fold_scratch(planes, depth, rows, first),
        compiler_params=params(collective_id),
        cost_estimate=pl.CostEstimate(flops=flops, bytes_accessed=30 << 20, transcendentals=0),
    )(tokens, cosine, sine, lower, gains_block, w_qkv, w_output, w_gate_up, w_down, cotangent)


class Fold:
    def __init__(self, me, g_any, mine, scratch):
        self.me, self.g, self.mine = me, g_any, mine
        self.other, self.from_line, self.sems = scratch

    def own_copy(self, z):
        return pltpu.make_async_copy(
            self.g.at[z * 2 + self.me.core], self.mine.at[z], self.sems.at[0, z]
        )

    def core_copy(self, z):
        me = self.me
        return remote(
            self.g.at[z * 2 + 1 - me.core], self.other.at[z], self.sems.at[1, z], self.sems.at[2, z], me.sibling()
        )

    def first(self):
        for z in range(self.me.depth):
            self.core_copy(z).start()
            self.own_copy(z).start()

    def add(self, total, term):
        def plane(d, carry):
            total[d] = (total[d].astype(F32) + term[d].astype(F32)).astype(BF)
            return carry

        lax.fori_loop(0, self.me.planes, plane, 0)

    def second(self):
        for z in range(self.me.depth):
            self.own_copy(z).wait()
            self.core_copy(z).wait_recv()
            self.add(self.mine.at[z], self.other.at[z])

    def target(self, z, k, down):
        return k - (self.me.depth - 1) + z if down else self.me.depth - 1 - k + z

    def sends(self, k, down):
        me = self.me
        return self.target(me.z, k, down) >= 0 if down else me.z <= k

    def slot(self, t, k, down):
        return self.me.depth if k == self.me.depth - 2 and not down else t

    def copy(self, k, down):
        me = self.me
        t = self.target(me.z, k, down)
        kind = 5 if down else 3
        return remote(
            self.mine.at[t], self.from_line.at[self.slot(t, k, down)], self.sems.at[kind, k], self.sems.at[kind + 1, k],
            me.along(me.z - 1 if down else me.z + 1),
        )

    def send(self, k):
        for down in (False, True):
            @pl.when(self.sends(k, down))
            def _():
                self.copy(k, down).start()

    def settle(self, k):
        me = self.me
        for down in (False, True):
            t = self.target(me.z + 1 if down else me.z - 1, k, down)
            comes = (me.z < me.depth - 1) & (t >= 0) if down else (me.z > 0) & (me.z - 1 <= k)

            @pl.when(comes)
            def _():
                block = self.from_line.at[self.slot(t, k, down)]
                kind = 5 if down else 3
                remote(
                    block, block, self.sems.at[kind, k], self.sems.at[kind + 1, k], me.sibling()
                ).wait_recv()
                self.add(self.mine.at[t], block)

    def step(self, k):
        if k > 0:
            self.settle(k - 1)
        self.send(k)

    def finish(self, first, steps):
        if first:
            for z in range(self.me.depth):
                self.core_copy(z).wait_send()
        for k in steps:
            for down in (False, True):
                @pl.when(self.sends(k, down))
                def _():
                    self.copy(k, down).wait_send()


class Swap:
    def __init__(self, me, ready, landed, sems):
        self.me, self.ready, self.landed, self.sems = me, ready, landed, sems

    def copy(self, o):
        me = self.me
        return remote(
            self.ready.at[me.dp ^ o], self.landed.at[me.dp], self.sems.at[0, o], self.sems.at[1, o], me.across(o)
        )

    def start(self, value):
        self.ready[...] = value
        for o in range(1, self.me.planes):
            self.copy(o).start()

    def last(self):
        me = self.me
        self.landed[me.dp] = self.ready[me.dp]
        for o in range(1, me.planes):
            block = self.landed.at[me.dp ^ o]
            remote(block, block, self.sems.at[0, o], self.sems.at[1, o], me.across(o)).wait_recv()

    def finish(self):
        for o in range(1, self.me.planes):
            self.copy(o).wait_send()


FOLD = 3


def fold_scratch(planes, depth, rows, full):
    block = (planes, 3, rows, full)
    return [
        pltpu.VMEM((depth,) + block, BF),
        pltpu.VMEM((depth + 1,) + block, BF),
        DMA((7, depth)),
    ]


def split(full):
    first = (full // 128 + 1) // 2 * 128
    return (first, full - first)


EARLY = 2


def home_kernel(
    planes, depth, turns, n_gains,
    gn_ref, mixed_ref, og_ref, gains_ref, o_ref, lse_ref, q_ref, lower_ref, cos_ref, sin_ref, tok_ref,
    wo_any, kv_any, parts_any, grads_b, mine_a, unit_any, recip_any, wq_any, wkv_any, xat_any,
    block_out, grad_out, shard_out, shard_qkv, gains_out, pair_out, down_out,
    wo, kv, unit_s, recip_s, wq_all, wkv_all, xat, own_part, gq, grad_kv, gmixed_s,
    bias, gob, delta, gkv, from_core, from_z, from_plane, partial, gproj, partial_q, partial_kv, gains_p, *rest,
):
    me = Place(planes, depth)
    collect = Collect(me, partial, rest[:COLLECT])
    collect_q = Collect(me, partial_q, rest[COLLECT : 2 * COLLECT])
    collect_kv = Collect(me, partial_kv, rest[2 * COLLECT : 3 * COLLECT])
    small = Collect(me, gains_p, rest[3 * COLLECT : 4 * COLLECT])
    rest = rest[4 * COLLECT :]
    mine_first, ready_first, landed_first, swap_first, mine_second, ready_second, landed_second, swap_second = rest[:8]
    folds = (
        Fold(me, None, mine_first, (None,) + rest[8:10]),
        Fold(me, grads_b, mine_second, rest[10 : 10 + FOLD]),
    )
    swaps = (
        Swap(me, ready_first, landed_first, swap_first),
        Swap(me, ready_second, landed_second, swap_second),
    )
    cs, zs, ps, load = rest[10 + FOLD :]
    half = turns // 2
    count = gn_ref.shape[0]
    sources = [wo_any, kv_any, unit_any, recip_any, xat_any, parts_any.at[0], wq_any, wkv_any, mine_a]
    places = [wo, kv, unit_s, recip_s, xat, own_part, wq_all, wkv_all, mine_first]
    loads = [pltpu.make_async_copy(a, b, load.at[i]) for i, (a, b) in enumerate(zip(sources, places))]
    for copy in loads[8:] + loads[:8]:
        copy.start()
    greet(me.plane() + me.line() + [me.sibling()])
    loads[8].wait()
    folds[0].send(EARLY)
    folds[1].first()

    def c_copy(i):
        return remote(gkv.at[2 * i + 1], from_core.at[i], cs.at[0, i], cs.at[1, i], me.sibling())

    def z_copy(k):
        return remote(gkv.at[2 * k], from_z.at[k - 1], zs.at[0, k], zs.at[1, k], me.along(me.behind(k)))

    def p_copy(o):
        return remote(parts_any.at[o], from_plane.at[o - 1], ps.at[0, o], ps.at[1, o], me.across(o))

    for o in range(1, planes):
        p_copy(o).start()
    unit, recip = unit_of(mixed_ref[...], 1)
    grad = gn_ref[...]
    scaled = grad * gains_ref[:, D : 2 * D]
    inner = jnp.mean(scaled * unit, axis=1, keepdims=True)
    gmixed = og_ref[...].astype(F32) + recip * (scaled - unit * inner)
    gmixed_s[...] = gmixed
    dgf = jnp.sum(grad * unit, axis=0, keepdims=True)
    gmixed_b = gmixed.astype(BF)
    loads[0].wait()
    gob[...] = dot(wo[...].reshape(HQ, D), gmixed_b, NT).astype(BF)
    for t in range(GROUPS):
        rows = []
        for h in range(4):
            at = pl.ds(t * 256 + h * 64, 64)
            rows.append(
                jnp.sum(gob[at, :].astype(F32) * o_ref[at, :].astype(F32), axis=0, keepdims=True)
            )
        delta[t] = jnp.concatenate(rows, axis=0)
    half_rows = D // planes
    order = list(range(1, planes)) + [0]
    for o in order:
        d = me.dp ^ o
        rows = o_ref[pl.ds(pl.multiple_of(d * half_rows, 128), half_rows), :]
        partial[d] = dot(rows, gmixed_b, NN).astype(BF).reshape(partial.shape[1:])
        collect.first(o)
    folds[1].second()
    folds[1].step(0)
    gq[...] = jnp.zeros_like(gq)
    loads[1].wait()

    def visit(slot):
        fill_bias(bias, lower_ref[...], slot)

        def four_heads(t, carry):
            key_at = pl.ds(pl.multiple_of(t * 128, 128), 128)
            value_at = pl.ds(pl.multiple_of(HK + t * 128, 128), 128)
            keys, values = kv[slot, :, key_at], kv[slot, :, value_at]
            lse_t, delta_t = lse_ref[t], delta[t]
            grad_keys, grad_values = [], []
            for u in range(2):
                key = keys[:, u * 64 : u * 64 + 64]
                value = values[:, u * 64 : u * 64 + 64]
                grad_key, grad_value = 0.0, 0.0
                for g in range(2):
                    h = 2 * u + g
                    at = pl.ds(pl.multiple_of(t * 256 + h * 64, 64), 64)
                    query, gob_h = q_ref[at, :], gob[at, :]
                    probs = jnp.exp(dot(key, query, NN) + bias[...] - lse_t[h : h + 1, :])
                    grad_value = grad_value + dot(probs.astype(BF), gob_h, NT)
                    grad_scores = (probs * (dot(value, gob_h, NN) - delta_t[h : h + 1, :])).astype(BF)
                    grad_key = grad_key + dot(grad_scores, query, NT)
                    gq[at, :] += dot(key, grad_scores, TN)
                grad_keys.append(grad_key)
                grad_values.append(grad_value)
            gkv[slot, :, key_at] = jnp.concatenate(grad_keys, axis=1).astype(BF)
            gkv[slot, :, value_at] = jnp.concatenate(grad_values, axis=1).astype(BF)
            return carry

        lax.fori_loop(0, GROUPS, four_heads, 0)

    for i in range(half - 1, -1, -1):
        @pl.when(me.z - i - 1 + me.core >= 0)
        def _():
            visit(2 * i + 1)
            c_copy(i).start()

    for k in range(half, 0, -1):
        @pl.when(me.z - k >= 0)
        def _():
            visit(2 * k)

            @pl.when(me.core == 0)
            def _():
                if k < half:
                    c_copy(k).wait_recv()
                    gkv[2 * k] = (gkv[2 * k].astype(F32) + from_core[k].astype(F32)).astype(BF)

            @pl.when(me.core == 1)
            def _():
                c_copy(k - 1).wait_recv()
                gkv[2 * k] = (gkv[2 * k].astype(F32) + from_core[k - 1].astype(F32)).astype(BF)

            z_copy(k).start()

    visit(0)
    for i in (2, 3, 4):
        loads[i].wait()
    tail_row = gains_ref[:, 2 * D : 2 * D + 128]
    gain_q, gain_k = column_of(tail_row, 0), column_of(tail_row, HEAD_DIM)
    cosine, sine = cos_ref[...], -sin_ref[...]
    gained = [0.0, 0.0]

    def four_grads(h):
        kind = 0 if h < HEADS else 1
        if kind == 0:
            four = gq[pl.ds(h * HEAD_DIM, 4 * HEAD_DIM), :] * HEAD_DIM ** (-0.5)
        else:
            four = grad_kv[:, pl.ds((h - HEADS) * HEAD_DIM, 4 * HEAD_DIM)].T
        recips = recip_s[h // 4]
        results = []
        for i in range(4):
            unit = unit_s[pl.ds((h + i) * HEAD_DIM, HEAD_DIM), :]
            grad = turned(four[i * HEAD_DIM : (i + 1) * HEAD_DIM], cosine, sine)
            scaled = grad * (gain_k if kind else gain_q)
            inner = jnp.mean(scaled * unit, axis=0, keepdims=True)
            results.append(recips[i : i + 1, :] * (scaled - unit * inner))
            gained[kind] = gained[kind] + grad * unit
        gproj[:, pl.ds(h * HEAD_DIM, 4 * HEAD_DIM)] = jnp.concatenate(results, axis=0).T.astype(BF)

    def gather_grads(columns, table, collected):
        for o in order:
            d = me.dp ^ o
            rows = xat[pl.ds(pl.multiple_of(d * half_rows, 128), half_rows), :]
            table[d] = dot(rows, gproj[:, columns], NN).astype(BF).reshape(table.shape[1:])
            collected.first(o)
            if o != order[0]:
                collected.second(order[order.index(o) - 1])
        collected.second(0)

    for o in order:
        collect.second(o)
    for h in range(0, HEADS, 4):
        four_grads(h)
    gather_grads(pl.ds(0, HQ), partial_q, collect_q)
    folds[1].step(1)
    for k in range(EARLY + 1, depth - 1):
        folds[0].step(k)
    grad_kv[...] = gkv[0].astype(F32)

    @pl.when(me.core == 0)
    def _():
        c_copy(0).wait_recv()
        grad_kv[...] += from_core[0].astype(F32)

    for k in range(1, half + 1):
        @pl.when(me.z + k < depth)
        def _():
            z_copy(k).wait_recv()
            grad_kv[...] += from_z[k - 1].astype(F32)

    for h in range(HEADS, HEADS + KV_HEADS, 4):
        four_grads(h)
    gproj[:, pl.ds(HQ + HK, HK)] = grad_kv[:, pl.ds(HK, HK)].astype(BF)
    gather_grads(pl.ds(HQ, 2 * HK), partial_kv, collect_kv)
    value_o = collect.third()
    value_q = collect_q.third()
    for i in (6, 7):
        loads[i].wait()
    grad = dot(gproj[:, :HQ], wq_all[...].reshape(D, HQ), NT)
    grad = grad + dot(gproj[:, HQ:], wkv_all[...].reshape(D, 2 * HK), NT)
    unit, recip = unit_of(tok_ref[...].astype(F32), 1)
    scaled = grad * gains_ref[:, :D]
    inner = jnp.mean(scaled * unit, axis=1, keepdims=True)
    grad_out[...] = gmixed_s[...] + recip * (scaled - unit * inner)
    dga = jnp.sum(grad * unit, axis=0, keepdims=True)
    for k in range(2, depth - 1):
        folds[1].step(k)
    folds[0].settle(depth - 2)
    swaps[0].start(mine_first[me.z])
    lane = lax.broadcasted_iota(jnp.int32, (HEAD_DIM, 128), 1)
    entry = lax.broadcasted_iota(jnp.int32, (HEAD_DIM, 128), 0)
    sums = [jnp.sum(g, axis=1, keepdims=True) for g in gained]
    last = jnp.sum(
        jnp.where(lane == entry, sums[0], 0.0) + jnp.where(lane == entry + HEAD_DIM, sums[1], 0.0),
        axis=0,
        keepdims=True,
    )
    whole = jnp.concatenate([dga, dgf, last], axis=1)
    devices = planes * depth * 2
    entries = devices * n_gains
    index = lax.broadcasted_iota(jnp.int32, (devices, entries), 1)
    device = lax.broadcasted_iota(jnp.int32, (devices, entries), 0)
    apart = jnp.where(index // n_gains == device, whole, 0.0)
    pick = jnp.where(
        lax.broadcasted_iota(jnp.int32, (128, entries), 1) % n_gains
        == lax.broadcasted_iota(jnp.int32, (128, entries), 0),
        1.0,
        0.0,
    )
    table = lax.dot_general(
        apart, pick, NT, preferred_element_type=F32, precision=lax.Precision.HIGHEST
    )
    gains_p[...] = jnp.broadcast_to(table[:, None, :], (devices, 8, 128)).reshape(gains_p.shape)
    for o in order:
        small.first(o)
    for o in order:
        small.second(o)
    value_kv = collect_kv.third()
    little = small.third()
    total = mixed_ref[...]
    loads[5].wait()
    total = total + own_part[...].astype(F32)
    for o in range(1, planes):
        p_copy(o).wait_recv()
        total = total + from_plane[o - 1].astype(F32)
    block_out[...] = total.astype(BF)
    folds[1].settle(depth - 2)
    swaps[1].start(mine_second[me.z])
    shard_out[...] = collect.last(value_o)
    shard_qkv[:, :HQ] = collect_q.last(value_q)
    shard_qkv[:, HQ:] = collect_kv.last(value_kv)
    gains_out[...] = small.last(little)
    start = 0
    full = landed_first.shape[3] + landed_second.shape[3]
    for swap in swaps:
        swap.last()
        f = swap.landed.shape[3]
        for d in range(planes):
            for m in range(2):
                at = (m * planes + d) * full + start
                pair_out[:, at : at + f] = swap.landed[d, m]
            at = d * full + start
            down_out[:, at : at + f] = swap.landed[d, 2]
        start = f

    for o in range(1, planes):
        p_copy(o).wait_send()
    for i in range(half):
        @pl.when(me.z - i - 1 + me.core >= 0)
        def _():
            c_copy(i).wait_send()
    for k in range(1, half + 1):
        @pl.when(me.z - k >= 0)
        def _():
            z_copy(k).wait_send()
    collect.finish()
    collect_q.finish()
    collect_kv.finish()
    small.finish()
    folds[0].finish(False, range(EARLY, depth - 1))
    folds[1].finish(True, range(depth - 1))
    for swap in swaps:
        swap.finish()


def home(first, second, n_gains, planes, depth, turns, collective_id):
    half = turns // 2
    count = first[0].shape[0]
    wo_all, kv_all, _, grads, mine, unit, recip, wq_all, wkv_all, xat = second
    rows = wo_all.shape[3]
    parts = (mine.shape[4], grads.shape[4])
    full = sum(parts)
    return pl.pallas_call(
        functools.partial(home_kernel, planes, depth, turns, n_gains),
        out_shape=(
            jax.ShapeDtypeStruct((count, D), BF),
            jax.ShapeDtypeStruct((count, D), F32),
            jax.ShapeDtypeStruct((rows, D), F32),
            jax.ShapeDtypeStruct((rows, 2 * HQ), F32),
            jax.ShapeDtypeStruct((8, 128), F32),
            jax.ShapeDtypeStruct((rows, 2 * planes * full), BF),
            jax.ShapeDtypeStruct((rows, planes * full), BF),
        ),
        in_specs=[VMEM] * len(first) + [ANY] * len(second),
        out_specs=(VMEM,) * 7,
        scratch_shapes=[pltpu.VMEM(a.shape, a.dtype) for a in (wo_all, kv_all, unit, recip, wq_all, wkv_all, xat)]
        + [
            pltpu.VMEM((count, D), BF),
            pltpu.VMEM((HQ, count), F32),
            pltpu.VMEM((count, 2 * HK), F32),
            pltpu.VMEM((count, D), F32),
            pltpu.VMEM((count, count), F32),
            pltpu.VMEM((HQ, count), BF),
            pltpu.VMEM((GROUPS, 4, count), F32),
            pltpu.VMEM((turns + 1, count, 2 * HK), BF),
            pltpu.VMEM((half, count, 2 * HK), BF),
            pltpu.VMEM((half, count, 2 * HK), BF),
            pltpu.VMEM((planes - 1, count, D), BF),
            pltpu.VMEM((planes, depth, 2, rows, D), BF),
            pltpu.VMEM((count, 2 * HQ), BF),
            pltpu.VMEM((planes, depth, 2, rows, HQ), BF),
            pltpu.VMEM((planes, depth, 2, rows, 2 * HK), BF),
            pltpu.VMEM((planes, depth, 2, 8, 128), F32),
        ]
        + collect_scratch(planes, depth, rows, D, BF)
        + collect_scratch(planes, depth, rows, HQ, BF)
        + collect_scratch(planes, depth, rows, 2 * HK, BF)
        + collect_scratch(planes, depth, 8, 128, F32)
        + [
            scratch
            for part in parts
            for scratch in (
                pltpu.VMEM((depth, planes, 3, rows, part), BF),
                pltpu.VMEM((planes, 3, rows, part), BF),
                pltpu.VMEM((planes, 3, rows, part), BF),
                DMA((2, planes)),
            )
        ]
        + fold_scratch(planes, depth, rows, parts[0])[1:]
        + fold_scratch(planes, depth, rows, parts[1])
        + [DMA((2, half)), DMA((2, half + 1)), DMA((2, planes)), DMA((9,))],
        compiler_params=params(collective_id),
        cost_estimate=pl.CostEstimate(flops=60 << 30, bytes_accessed=8 << 20, transcendentals=0),
    )(*first, *second)


def per_device(
    tokens_in,
    positions,
    out_grad,
    w_qkv,
    w_output,
    w_gate_up,
    w_down,
    norm_gains,
    first_qkv,
    first_output,
    first_gate_up,
    first_down,
    first_gains,
    second_qkv,
    second_output,
    second_gate_up,
    second_down,
    second_gains,
):
    planes, ctxs = lax.axis_size("dp"), lax.axis_size("ctx")
    depth = ctxs // 2
    turns = ctxs // 2
    rows = w_qkv.shape[0]
    n_gains = norm_gains.shape[0]
    count = tokens_in.shape[0] * tokens_in.shape[1]
    tokens = tokens_in.reshape(count, D)
    places = positions.reshape(count)
    cotangent = out_grad.reshape(count, D)

    gains_block = jnp.pad(norm_gains.astype(BF).astype(F32)[None, :], ((0, 7), (0, 128 - n_gains)))
    cosine, sine = rope_tables(places)
    lower = (jnp.arange(count, dtype=jnp.int32) - places)[None, :]
    (
        query, kv_all, wq_all, wkv_all, xat, unit_heads, recip_heads, output_all, parts, _, _, grads, mine,
        gains_row, attn_t, lse, mixed, grad_normed,
    ) = fore(
        tokens, cosine, sine, lower, gains_block, w_qkv, w_output, w_gate_up, w_down, cotangent,
        n_gains, planes, depth, turns, 0,
    )
    block_out, input_grad, shard_output, shard_qkv, gains_tile, pair_b, down_b = home(
        (grad_normed, mixed, cotangent, gains_row, attn_t, lse, query, lower, cosine, sine, tokens),
        (output_all, kv_all, parts, grads, mine, unit_heads, recip_heads, wq_all, wkv_all, xat),
        n_gains, planes, depth, turns, 1,
    )
    shard_gains = gains_tile[0, :n_gains]
    shard_gate_up = pair_b.astype(F32)
    shard_down = down_b.astype(F32)

    new_qkv, new_first_qkv, new_second_qkv = adam_step(
        w_qkv, shard_qkv, first_qkv, second_qkv, 0.02, 0.1
    )
    new_output, new_first_output, new_second_output = adam_step(
        w_output, shard_output, first_output, second_output, 0.2, 0.1
    )
    new_gate_up, new_first_gate_up, new_second_gate_up = adam_step(
        w_gate_up, shard_gate_up, first_gate_up, second_gate_up, 0.02, 0.1
    )
    new_down, new_first_down, new_second_down = adam_step(
        w_down, shard_down, first_down, second_down, 0.02, 0.1
    )
    new_gains, new_first_gains, new_second_gains = adam_step(
        norm_gains, shard_gains, first_gains, second_gains, 0.1, 0.0
    )
    return (
        block_out.reshape(tokens_in.shape),
        input_grad.reshape(tokens_in.shape),
        shard_qkv,
        shard_output,
        shard_gate_up,
        shard_down,
        shard_gains,
        new_qkv,
        new_output,
        new_gate_up,
        new_down,
        new_gains,
        new_first_qkv,
        new_first_output,
        new_first_gate_up,
        new_first_down,
        new_first_gains,
        new_second_qkv,
        new_second_output,
        new_second_gate_up,
        new_second_down,
        new_second_gains,
    )


def solution(mesh):
    in_specs = (
        P("dp", "ctx", None),
        P("dp", "ctx"),
        P("dp", "ctx", None),
        P(("dp", "ctx"), None),
        P(("dp", "ctx"), None),
        P(("dp", "ctx"), None),
        P(("dp", "ctx"), None),
        P(("dp", "ctx")),
        P(("dp", "ctx"), None),
        P(("dp", "ctx"), None),
        P(("dp", "ctx"), None),
        P(("dp", "ctx"), None),
        P(("dp", "ctx")),
        P(("dp", "ctx"), None),
        P(("dp", "ctx"), None),
        P(("dp", "ctx"), None),
        P(("dp", "ctx"), None),
        P(("dp", "ctx")),
    )
    out_specs = (
        P("dp", "ctx", None),
        P("dp", "ctx", None),
        P(("dp", "ctx"), None),
        P(("dp", "ctx"), None),
        P(("dp", "ctx"), None),
        P(("dp", "ctx"), None),
        P(("dp", "ctx")),
        P(("dp", "ctx"), None),
        P(("dp", "ctx"), None),
        P(("dp", "ctx"), None),
        P(("dp", "ctx"), None),
        P(("dp", "ctx")),
        P(("dp", "ctx"), None),
        P(("dp", "ctx"), None),
        P(("dp", "ctx"), None),
        P(("dp", "ctx"), None),
        P(("dp", "ctx")),
        P(("dp", "ctx"), None),
        P(("dp", "ctx"), None),
        P(("dp", "ctx"), None),
        P(("dp", "ctx"), None),
        P(("dp", "ctx")),
    )
    return jax.shard_map(
        per_device, mesh=mesh, in_specs=in_specs, out_specs=out_specs, check_vma=False
    )
```

```python
import functools
import math

import jax
import jax.numpy as jnp
from jax import lax
from jax.experimental import pallas as pl
from jax.experimental.pallas import tpu as pltpu
from jax.sharding import PartitionSpec as P

D = 1024
HEADS = 16
KV_HEADS = 8
HEAD_DIM = 64
STEP = 4
HQ = 1024
HK = 512


EPS = 1e-05
THETA = 1000000.0
NEG_BIG = -1e30
BETA_ONE = 0.9
BETA_TWO = 0.95
ADAM_EPS = 1e-08


def rope_tables(places):
    half = HEAD_DIM // 2
    freqs = jnp.exp(-math.log(THETA) * (2.0 * jnp.arange(half, dtype=jnp.float32) / HEAD_DIM))
    angles = freqs[:, None] * places.astype(jnp.float32)[None, :]
    return (jnp.cos(angles), jnp.sin(angles))


def adam_step(weight, grad, first, second, rate, decay):
    first_new = BETA_ONE * first + (1.0 - BETA_ONE) * grad
    second_new = BETA_TWO * second + (1.0 - BETA_TWO) * grad * grad
    first_hat = first_new / (1.0 - BETA_ONE**STEP)
    second_hat = second_new / (1.0 - BETA_TWO**STEP)
    weight_new = weight - rate * (first_hat / (jnp.sqrt(second_hat) + ADAM_EPS) + decay * weight)
    return (weight_new, first_new, second_new)


BF = jnp.bfloat16
F32 = jnp.float32
MESH_ID = pl.DeviceIdType.MESH
ANY = pl.BlockSpec(memory_space=pl.ANY)
VMEM = pl.BlockSpec(memory_space=pltpu.VMEM)
DMA = pltpu.SemaphoreType.DMA
NN = (((1,), (0,)), ((), ()))
NT = (((1,), (1,)), ((), ()))
TN = (((0,), (0,)), ((), ()))
VMEM_BYTES = 60 << 20
GROUPS = HEADS // 4


def dot(a, b, dims):
    return lax.dot_general(a, b, dims, preferred_element_type=F32)


class Place:
    def __init__(self, planes, depth):
        self.planes, self.depth = planes, depth
        self.dp = lax.axis_index("dp")
        self.ctx = lax.axis_index("ctx")
        self.z = self.ctx // 2
        self.core = self.ctx % 2

    def sibling(self):
        return {"dp": self.dp, "ctx": self.z * 2 + 1 - self.core}

    def across(self, o):
        return {"dp": self.dp ^ o, "ctx": self.ctx}

    def behind(self, k):
        return lax.rem(self.z + self.depth - k, self.depth)

    def ahead(self, k):
        return lax.rem(self.z + k, self.depth)

    def along(self, z):
        return {"dp": self.dp, "ctx": z * 2 + self.core}

    def plane(self):
        return [self.across(o) for o in range(1, self.planes)]

    def line(self):
        return [self.along(self.ahead(k)) for k in range(1, self.depth)]


def near(planes):
    return [o for o in range(1, planes) if o & (o - 1) == 0]


def far(planes):
    return [o for o in range(1, planes) if o & (o - 1) != 0]


def greet(devices):
    barrier = pltpu.get_barrier_semaphore()
    for device in devices:
        pl.semaphore_signal(barrier, inc=1, device_id=device, device_id_type=MESH_ID)
    pl.semaphore_wait(barrier, len(devices))


def remote(src, dst, send, recv, device):
    return pltpu.make_async_remote_copy(
        src_ref=src, dst_ref=dst, send_sem=send, recv_sem=recv, device_id=device, device_id_type=MESH_ID
    )


def params(collective_id):
    return pltpu.CompilerParams(
        vmem_limit_bytes=VMEM_BYTES, collective_id=collective_id, has_side_effects=True
    )


class Spread:
    def __init__(self, me, g_ref, line_sems, sems, halves=True):
        self.me, self.g, self.line_sems, self.sems = me, g_ref, line_sems, sems
        self.by_halves = halves and me.planes == 4
        self.sent = []

    def push(self, src, dst, kind, o, device):
        copy = remote(src, dst, self.sems.at[kind, o], self.sems.at[kind + 1, o], device)
        copy.start()
        self.sent.append(copy)

    def mine(self, o, core):
        return self.g.at[self.me.dp ^ o, :, core]

    def line(self):
        me = self.me
        block = self.g.at[me.dp, me.z, me.core]
        for k in range(1, me.depth):
            copy = remote(
                block, block, self.line_sems.at[0, k], self.line_sems.at[1, k], me.along(me.ahead(k))
            )
            copy.start()
            self.sent.append(copy)

    def first(self):
        me = self.me
        for k in range(1, me.depth):
            block = self.g.at[me.dp, me.behind(k), me.core]
            remote(
                block, block, self.line_sems.at[0, k], self.line_sems.at[1, k], me.along(me.ahead(k))
            ).wait_recv()
        self.push(self.mine(0, me.core), self.mine(0, me.core), 2, 0, me.sibling())
        self.plane(near(me.planes))

    def plane(self, places):
        me = self.me
        for o in places:
            self.push(self.mine(0, me.core), self.mine(0, me.core), 0, o, me.across(o))

    def part(self, o, number):
        half = self.me.depth // 2
        return self.g.at[self.me.dp ^ o, pl.ds(number * half, half), self.me.core]

    def relay(self, o):
        block = self.mine(o, self.me.core)
        if self.by_halves and o == 3:
            for number in range(2):
                piece = self.part(o, number)
                kind = 4 + 2 * number
                remote(
                    piece, piece, self.sems.at[kind, o], self.sems.at[kind + 1, o], self.me.sibling()
                ).wait_recv()
        else:
            remote(block, block, self.sems.at[0, o], self.sems.at[1, o], self.me.sibling()).wait_recv()
        if self.by_halves and o < 3:
            piece = self.part(o, o - 1)
            self.push(piece, piece, 2 + 2 * o, 3, self.me.across(3 - o))
        self.push(block, block, 2, o, self.me.sibling())

    def arrive(self, o):
        block = self.mine(o, 1 - self.me.core)
        remote(block, block, self.sems.at[2, o], self.sems.at[3, o], self.me.sibling()).wait_recv()

    def finish(self):
        for copy in self.sent:
            copy.wait_send()


def spread_sems(planes, depth):
    return [DMA((2, depth)), DMA((8, planes))]


class Collect:
    def __init__(self, me, p_ref, scratch):
        self.me, self.p = me, p_ref
        self.sums, self.from_plane, self.total, self.from_z, self.cs, self.ps, self.zs = scratch

    def c_copy(self, o):
        me = self.me
        return remote(
            self.p.at[me.dp ^ o, :, 1 - me.core], self.sums.at[o], self.cs.at[0, o], self.cs.at[1, o], me.sibling()
        )

    def p_copy(self, o):
        return remote(
            self.sums.at[o], self.from_plane.at[o - 1], self.ps.at[0, o], self.ps.at[1, o], self.me.across(o)
        )

    def z_copy(self, k):
        me = self.me
        return remote(
            self.total.at[me.ahead(k)], self.from_z.at[k], self.zs.at[0, k], self.zs.at[1, k], me.along(me.ahead(k))
        )

    def first(self, o):
        self.c_copy(o).start()

    def second(self, o):
        me = self.me
        self.c_copy(o).wait_recv()
        own = self.p[me.dp ^ o, :, me.core].astype(F32)
        self.sums[o] = (own + self.sums[o].astype(F32)).astype(self.sums.dtype)
        if o > 0:
            self.p_copy(o).start()

    def third(self):
        me = self.me
        for o in range(1, me.planes):
            self.p_copy(o).wait_recv()
        for k in list(range(1, me.depth)) + [0]:
            z = me.ahead(k)
            value = self.sums[0, z].astype(F32)
            for o in range(1, me.planes):
                value = value + self.from_plane[o - 1, z].astype(F32)
            self.total[z] = value.astype(self.total.dtype)
            if k > 0:
                self.z_copy(k).start()
        return value

    def last(self, value):
        for k in range(1, self.me.depth):
            self.z_copy(k).wait_recv()
            value = value + self.from_z[k].astype(F32)
        return value

    def finish(self):
        for o in range(self.me.planes):
            self.c_copy(o).wait_send()
        for o in range(1, self.me.planes):
            self.p_copy(o).wait_send()
        for k in range(1, self.me.depth):
            self.z_copy(k).wait_send()


def collect_scratch(planes, depth, rows, columns, kind):
    return [
        pltpu.VMEM((planes, depth, rows, columns), kind),
        pltpu.VMEM((planes - 1, depth, rows, columns), kind),
        pltpu.VMEM((depth, rows, columns), kind),
        pltpu.VMEM((depth, rows, columns), kind),
        DMA((2, planes)),
        DMA((2, planes)),
        DMA((2, depth)),
    ]


COLLECT = 7


def unit_of(values, axis):
    recip = lax.rsqrt(jnp.mean(values * values, axis=axis, keepdims=True) + EPS)
    return values * recip, recip


def column_of(row, start):
    lane = lax.broadcasted_iota(jnp.int32, (HEAD_DIM, 128), 1)
    entry = lax.broadcasted_iota(jnp.int32, (HEAD_DIM, 128), 0)
    return jnp.sum(jnp.where(lane == entry + start, row, 0.0), axis=1, keepdims=True)


def turned(values, cosine, sine):
    half = HEAD_DIM // 2
    a, b = values[:half], values[half:]
    return jnp.concatenate([a * cosine - b * sine, b * cosine + a * sine], axis=0)


def fill_bias(bias, lower, slot):
    count = bias.shape[0]
    query = lax.broadcasted_iota(jnp.int32, (count, count), 1)
    key = lax.broadcasted_iota(jnp.int32, (count, count), 0) - slot * count
    bias[...] = jnp.where((key <= query) & (key >= lower), 0.0, NEG_BIG)


class Pass:
    def __init__(self, me, w_ref, sems):
        self.me, self.w, self.sems = me, w_ref, sems

    def copy(self, kind, s, down, core=None, device=None):
        me = self.me
        z = me.z + s - 1 if down else me.z - s + 1
        block = self.w.at[:, :, z * 2 + (me.core if core is None else core)]
        device = me.sibling() if device is None else device
        return remote(block, block, self.sems.at[kind, s], self.sems.at[kind + 1, s], device)

    def held(self, s, down):
        me = self.me
        return me.z + s - 1 < me.depth if down else me.z - s + 1 >= 0

    def on(self, s, down):
        me = self.me
        return self.held(s, down) & (me.z >= 1 if down else me.z + 1 < me.depth)

    def line_copy(self, s, down):
        me = self.me
        return self.copy(2 if down else 0, s, down, None, me.along(me.z - 1 if down else me.z + 1))

    def step(self, s):
        for down in (False, True):
            if s > 1:
                @pl.when(self.held(s, down))
                def _():
                    me = self.me
                    z = me.z + s - 1 if down else me.z - s + 1
                    block = self.w.at[:, :, z * 2 + me.core]
                    kind = 2 if down else 0
                    remote(
                        block, block, self.sems.at[kind, s - 1], self.sems.at[kind + 1, s - 1], me.sibling()
                    ).wait_recv()

            @pl.when(self.on(s, down))
            def _():
                self.line_copy(s, down).start()

            if s > 1 or not down:
                @pl.when(self.held(s, down))
                def _():
                    self.copy(6 if down else 4, s, down).start()

    def arrive(self):
        for s in range(1, self.me.depth + 1):
            for down in (False, True):
                if s > 1 or not down:
                    @pl.when(self.held(s, down))
                    def _():
                        self.copy(6 if down else 4, s, down, 1 - self.me.core).wait_recv()

    def finish(self):
        for s in range(1, self.me.depth + 1):
            for down in (False, True):
                @pl.when(self.on(s, down))
                def _():
                    self.line_copy(s, down).wait_send()

                if s > 1 or not down:
                    @pl.when(self.held(s, down))
                    def _():
                        self.copy(6 if down else 4, s, down).wait_send()


def fore_kernel(
    planes, depth, turns, n_gains,
    tok_ref, cos_ref, sin_ref, lower_ref, gain_ref, wqkv_ref, wout_ref, wpair_ref, wdown_ref, og_ref,
    q_any, kv_any, wq_any, wkv_any, xat_any, unit_any, recip_any, wo_any, parts_any, spill_any, grads_a, grads_b, mine_any,
    gains_out, o_out, lse_out, mixed_out, gn_out,
    q_s, kv_all, wq_all, wkv_all, xat, unit_s, recip_s, wo_all, blocks_a, blocks_b, gains_g, xa, proj, bias, accum, sums,
    wa, wb, hns, ogs, hnt, ogt, mid, pair, send_gn, recv_gn, part_s, stage, mine,
    own_sem, keep_sem, zs, cs, ps, a2a_a, a2a_b, pass_a, pass_b, hsem, nsem, psem, ssem, stsem, og_halves, hn_halves, dsem,
    glsem, gsem, qlsem, qsem, wlsem, wsem, olsem, osem, *fold_rest,
):
    me = Place(planes, depth)
    half = turns // 2
    count = tok_ref.shape[0]
    width = D // planes
    rows = wqkv_ref.shape[0]
    halves = (blocks_a.shape[3], blocks_b.shape[3])
    full = sum(halves)
    gains = Spread(me, gains_g, glsem, gsem, False)
    queries = Spread(me, wq_all, qlsem, qsem)
    weights = Spread(me, wkv_all, wlsem, wsem)
    outputs = Spread(me, wo_all, olsem, osem)
    pass_first, pass_second = Pass(me, wa, pass_a), Pass(me, wb, pass_b)
    fold = Fold(me, grads_a, mine, fold_rest)
    kept = []

    def keep(source, into):
        copy = pltpu.make_async_copy(source, into, keep_sem.at[len(kept)])
        copy.start()
        kept.append(copy)

    gains_g[me.dp, me.z, me.core] = gain_ref[...]
    wq_all[me.dp, me.z, me.core] = wqkv_ref[:, :HQ].astype(BF)
    wkv_all[me.dp, me.z, me.core] = wqkv_ref[:, HQ:].astype(BF)
    wo_all[me.dp, me.z, me.core] = wout_ref[...].astype(BF)
    for d in range(planes):
        for m in range(3):
            source = wdown_ref if m == 2 else wpair_ref
            at = d * full if m == 2 else (m * planes + d) * full
            blocks_a[d, m] = source[:, at : at + halves[0]].astype(BF)
            blocks_b[d, m] = source[:, at + halves[0] : at + full].astype(BF)
    wa[:, me.dp, me.ctx] = blocks_a[me.dp]
    wb[:, me.dp, me.ctx] = blocks_b[me.dp]
    own_og = pltpu.make_async_copy(og_ref, ogs.at[0], own_sem.at[1])
    own_og.start()
    greet(me.plane() + me.line() + [me.sibling()])
    gains.line()
    weights.line()

    def a2a_copy(part, o):
        source, into, sems = ((blocks_a, wa, a2a_a), (blocks_b, wb, a2a_b))[part]
        return remote(
            source.at[me.dp ^ o], into.at[:, me.dp, me.ctx], sems.at[0, o], sems.at[1, o], me.across(o)
        )

    def a2a_wait(part):
        into, sems = ((wa, a2a_a), (wb, a2a_b))[part]
        for o in range(1, planes):
            block = into.at[:, me.dp ^ o, me.ctx]
            remote(block, block, sems.at[0, o], sems.at[1, o], me.across(o)).wait_recv()

    for part in range(2):
        for o in range(1, planes):
            a2a_copy(part, o).start()
    queries.line()
    outputs.line()
    unit, _ = unit_of(tok_ref[...].astype(F32), 1)
    proj[:, :D] = unit
    gains.first()
    gains.plane(far(planes))
    weights.first()
    a2a_wait(0)
    pass_first.step(1)
    queries.first()
    for o in range(1, planes):
        gains.relay(o)
    for o in range(planes):
        gains.arrive(o)
    devices = planes * depth * 2
    table = gains_g[...].reshape(devices, 8, 128)[:, 0, :].astype(BF)
    entries = devices * n_gains
    index = lax.broadcasted_iota(jnp.int32, (128, entries), 1)
    pick = jnp.where(
        index % n_gains == lax.broadcasted_iota(jnp.int32, (128, entries), 0), 1.0, 0.0
    ).astype(BF)
    spread = dot(table, pick, NN)
    owner = lax.broadcasted_iota(jnp.int32, (devices, entries), 1) // n_gains
    device = lax.broadcasted_iota(jnp.int32, (devices, entries), 0)
    gains_row = 1.0 + jnp.sum(jnp.where(owner == device, spread, 0.0), axis=0, keepdims=True)
    gains_out[...] = gains_row
    normed = (proj[:, :D] * gains_row[:, :D]).astype(BF)
    xat[...] = normed.T
    keep(xat, xat_any)
    for d in range(planes):
        xa[d] = normed[:, d * width : (d + 1) * width]

    def project(source, table, at):
        proj[:, at] = jnp.zeros((count, D), F32)
        places = [0] + near(planes) + far(planes)
        for o in places:
            if o > 0:
                source.relay(o)
            source.arrive(o)
            if o == near(planes)[-1] and planes != 4:
                source.plane(far(planes))
            proj[:, at] += dot(xa[me.dp ^ o], table[me.dp ^ o].reshape(width, D), NN)

    project(weights, wkv_all, pl.ds(HQ, 2 * HK))
    tail_row = gains_row[:, 2 * D : 2 * D + 128]
    gain_q, gain_k = column_of(tail_row, 0), column_of(tail_row, HEAD_DIM)
    cosine, sine = cos_ref[...], sin_ref[...]

    def four_raw(h):
        four = proj[:, h * HEAD_DIM : (h + 4) * HEAD_DIM].T
        results, recips = [], []
        for i in range(4):
            value, recip = unit_of(four[i * HEAD_DIM : (i + 1) * HEAD_DIM], 0)
            unit_s[pl.ds((h + i) * HEAD_DIM, HEAD_DIM), :] = value
            recips.append(recip)
            results.append(turned(value * (gain_q if h < HEADS else gain_k), cosine, sine))
        recip_s[h // 4] = jnp.concatenate(recips, axis=0)
        return jnp.concatenate(results, axis=0)

    for h in range(HEADS, HEADS + KV_HEADS, 4):
        kv_all[0, :, pl.ds((h - HEADS) * HEAD_DIM, 4 * HEAD_DIM)] = four_raw(h).T.astype(BF)
    kv_all[0, :, pl.ds(HK, HK)] = proj[:, HQ + HK :].astype(BF)

    def half_copy(slots, sems, o):
        rows = pl.ds((o - 1) * (count // 2), count // 2)
        return remote(
            slots.at[o, rows], slots.at[3, rows], sems.at[0, o], sems.at[1, o], me.across(3 - o)
        )

    def z_copy(k):
        return remote(kv_all.at[0], kv_all.at[2 * k], zs.at[0, k], zs.at[1, k], me.along(me.ahead(k)))

    def c_copy(i):
        return remote(
            kv_all.at[2 * i + 2 * me.core], kv_all.at[2 * i + 1], cs.at[0, i], cs.at[1, i], me.sibling()
        )

    for k in range(1, half + 1):
        @pl.when(me.z + k < depth)
        def _():
            z_copy(k).start()

    @pl.when(me.core == 0)
    def _():
        c_copy(0).start()

    project(queries, wq_all, pl.ds(0, HQ))
    outputs.first()
    for h in range(0, HEADS, 4):
        q_s[pl.ds(h * HEAD_DIM, 4 * HEAD_DIM), :] = (four_raw(h) * HEAD_DIM ** (-0.5)).astype(BF)
    keep(q_s, q_any)
    keep(unit_s, unit_any)
    keep(recip_s, recip_any)
    keep(wq_all, wq_any)
    keep(wkv_all, wkv_any)
    square = planes == 4
    if not square:
        outputs.plane(far(planes))
    shares = []
    for o in near(planes) if square else range(1, planes):
        share = remote(og_ref, ogs.at[o], ps.at[0, o], ps.at[1, o], me.across(o))
        share.start()
        shares.append(share)
    accum[...] = jnp.zeros_like(accum)
    sums[...] = jnp.zeros_like(sums)

    def visit(slot):
        fill_bias(bias, lower_ref[...], slot)

        def four_heads(t, carry):
            keys = kv_all[slot, :, pl.ds(pl.multiple_of(t * 128, 128), 128)]
            values = kv_all[slot, :, pl.ds(pl.multiple_of(HK + t * 128, 128), 128)]
            totals = []
            for u in range(2):
                key = keys[:, u * 64 : u * 64 + 64]
                value = values[:, u * 64 : u * 64 + 64]
                for g in range(2):
                    at = pl.ds(pl.multiple_of(t * 256 + u * 128 + g * 64, 64), 64)
                    weight = jnp.exp(dot(key, q_s[at, :], NN) + bias[...])
                    totals.append(jnp.sum(weight, axis=0, keepdims=True))
                    accum[at, :] += dot(value, weight.astype(BF), TN)
            sums[t] += jnp.concatenate(totals, axis=0)
            return carry

        lax.fori_loop(0, GROUPS, four_heads, 0)

    visit(0)
    for k in range(1, half + 1):
        there = me.z - k >= 0

        @pl.when(there)
        def _():
            z_copy(k).wait_recv()

        @pl.when(there & (me.core == 1))
        def _():
            c_copy(k - 1).start()

        if k < half:
            @pl.when(there & (me.core == 0))
            def _():
                c_copy(k).start()

        @pl.when(there)
        def _():
            visit(2 * k)

    pass_first.step(2)
    for i in range(half):
        @pl.when(me.z - i - 1 + me.core >= 0)
        def _():
            c_copy(i).wait_recv()
            visit(2 * i + 1)

    pass_first.step(3)
    a2a_wait(1)
    pass_second.step(1)
    keep(kv_all, kv_any)
    for o in range(1, planes):
        outputs.relay(o)
    if square:
        for o in (1, 2):
            remote(og_ref, ogs.at[o], ps.at[0, o], ps.at[1, o], me.across(o)).wait_recv()
            half_copy(ogs, og_halves, o).start()
    for t in range(GROUPS):
        total = sums[t]
        lse_out[t] = jnp.log(total)
        for h in range(4):
            at = pl.ds(t * 256 + h * 64, 64)
            o_out[at, :] = (accum[at, :] / total[h : h + 1, :]).astype(BF)
    for o in range(planes):
        outputs.arrive(o)
    keep(wo_all, wo_any)
    mixed = tok_ref[...].astype(F32) + dot(o_out[...].T, wo_all[...].reshape(HQ, D), NN)
    mixed_out[...] = mixed
    unit, _ = unit_of(mixed, 1)
    hns[0] = (unit * gains_out[:, D : 2 * D]).astype(BF)

    def hn_copy(o):
        return remote(hns.at[0], hns.at[o], hsem.at[0, o], hsem.at[1, o], me.across(o))

    def gn_copy(o):
        return remote(send_gn.at[o - 1], recv_gn.at[o - 1], nsem.at[0, o], nsem.at[1, o], me.across(o))

    def diagonal_rows(other):
        return pl.ds((other - 1) * (count // 2), count // 2)

    def diagonal_copy(other):
        rows = diagonal_rows(other)
        return remote(
            send_gn.at[2, rows], recv_gn.at[2, rows], dsem.at[0, other], dsem.at[1, other], me.across(other)
        )

    def spill_copy(o, back):
        ends = (spill_any.at[o], proj) if back else (proj, spill_any.at[o])
        return pltpu.make_async_copy(*ends, ssem.at[0])

    def parts_copy(o):
        return pltpu.make_async_copy(part_s, parts_any.at[o], psem.at[0])

    for o in near(planes):
        hn_copy(o).start()
    for s in range(4, depth + 1):
        pass_first.step(s)
    pass_first.arrive()
    own_og.wait()

    def ffn_part(part):
        w, f = (wa, wb)[part], halves[part]

        def block(i, carry):
            o = i if part == 0 else planes - 1 - i
            if part == 0:
                if square:
                    @pl.when(o == 1)
                    def _():
                        for other in (1, 2):
                            hn_copy(other).wait_recv()
                            half_copy(hns, hn_halves, other).start()

                    @pl.when(o == 3)
                    def _():
                        for other in (1, 2):
                            half_copy(ogs, og_halves, other).wait_recv()
                            half_copy(hns, hn_halves, other).wait_recv()
                else:
                    @pl.when(o > 0)
                    def _():
                        hn_copy(o).wait_recv()
                        remote(og_ref, ogs.at[o], ps.at[0, o], ps.at[1, o], me.across(o)).wait_recv()
            else:
                spill_copy(o, True).start()

            hn, og = hns[o], ogs[o]
            at = pl.ds(pl.multiple_of(o * count, 128), count)
            if part == 0:
                hnt[:, at] = hn.T
                ogt[:, at] = og.T
            w_gate, w_up, w_down = (w[m].reshape(D, f) for m in range(3))
            gate = dot(hn, w_gate, NN)
            upper = dot(hn, w_up, NN)
            sigma = 1.0 / (1.0 + jnp.exp(-gate))
            active = gate * sigma
            middle = (active * upper).astype(BF)
            gmid = dot(og, w_down, NN)
            ggate = (gmid * upper * sigma * (1.0 + gate * (1.0 - sigma))).astype(BF)
            gupper = (gmid * active).astype(BF)
            mid[at, :f] = middle
            pair[0, at, :f] = ggate
            pair[1, at, :f] = gupper
            gn = dot(ggate, w_gate, NT) + dot(gupper, w_up, NT)
            out = dot(middle, w_down, NT)
            if part == 0:
                @pl.when(o > 0)
                def _():
                    spill_copy(o - 1, False).wait()

                proj[:, :D] = gn
                proj[:, D:] = out
                spill_copy(o, False).start()

                @pl.when(o == 0)
                def _():
                    if not square:
                        for other in far(planes):
                            hn_copy(other).start()
                    pass_second.step(2)

                @pl.when(o == planes // 2)
                def _():
                    pass_second.step(3)
            else:
                spill_copy(o, True).wait()
                gn = gn + proj[:, :D]
                out = out + proj[:, D:]

                @pl.when(i > 0)
                def _():
                    parts_copy(o + 1).wait()

                if square:
                    proj[:, :D] = gn

                    @pl.when(o == 3)
                    def _():
                        send_gn[2] = gn.astype(BF)
                        for other in (1, 2):
                            diagonal_copy(other).start()

                    for other in (1, 2):
                        @pl.when(o == other)
                        def _():
                            rows = diagonal_rows(3 - other)
                            diagonal_copy(3 - other).wait_recv()
                            proj[rows, :D] += recv_gn[2, rows].astype(F32)
                            send_gn[other - 1] = proj[:, :D].astype(BF)
                            gn_copy(other).start()
                else:
                    @pl.when(o > 0)
                    def _():
                        send_gn[o - 1] = gn.astype(BF)
                        gn_copy(o).start()

                @pl.when(o == 0)
                def _():
                    gn_out[...] = gn

                @pl.when(i == 0)
                def _():
                    fold.second()
                    fold.step(0)

                @pl.when(i == planes // 2)
                def _():
                    fold.step(1)

                part_s[...] = out.astype(BF)
                parts_copy(o).start()
            return carry

        lax.fori_loop(0, planes, block, 0)
        if part == 0:
            spill_copy(planes - 1, False).wait()
        else:
            parts_copy(0).wait()
        strip = D // planes
        grads = (grads_a, grads_b)[part]

        def out_copy(m, d):
            return pltpu.make_async_copy(stage.at[m, :, :, :f], grads.at[:, d, m], stsem.at[m])

        def weight_grads(d, carry):
            left = pl.ds(pl.multiple_of(d * strip, 128), strip)
            for m in (2, 0, 1):
                @pl.when(d > 0)
                def _():
                    out_copy(m, d - 1).wait()

                if m == 2:
                    total = dot(ogt[left, :], mid[:, :f], NN)
                else:
                    total = dot(hnt[left, :], pair[m, :, :f], NN)
                stage[m, :, :, :f] = total.astype(BF).reshape(depth * 2, rows, f)
                out_copy(m, d).start()
            return carry

        lax.fori_loop(0, planes, weight_grads, 0)
        for m in range(3):
            out_copy(m, planes - 1).wait()

    ffn_part(0)
    fold.first()
    for s in range(4, depth + 1):
        pass_second.step(s)
    pass_second.arrive()
    ffn_part(1)
    total = gn_out[...]
    for o in (1, 2) if square else range(1, planes):
        gn_copy(o).wait_recv()
        total = total + recv_gn[o - 1].astype(F32)
    gn_out[...] = total
    fold.settle(EARLY - 1)
    keep(mine, mine_any)
    pass_first.finish()
    pass_second.finish()
    fold.finish(True, range(EARLY))
    for o in (1, 2) if square else range(1, planes):
        gn_copy(o).wait_send()
        hn_copy(o).wait_send()
        if square:
            diagonal_copy(o).wait_send()
            half_copy(hns, hn_halves, o).wait_send()
            half_copy(ogs, og_halves, o).wait_send()

    for i in range(half):
        @pl.when(me.z - i - me.core >= 0)
        def _():
            c_copy(i).wait_send()

    for k in range(1, half + 1):
        @pl.when(me.z + k < depth)
        def _():
            z_copy(k).wait_send()

    for o in range(1, planes):
        a2a_copy(0, o).wait_send()
        a2a_copy(1, o).wait_send()
    for share in shares:
        share.wait_send()
    gains.finish()
    queries.finish()
    weights.finish()
    outputs.finish()
    for copy in kept:
        copy.wait()


def fore(tokens, cosine, sine, lower, gains_block, w_qkv, w_output, w_gate_up, w_down, cotangent, n_gains, planes, depth, turns, collective_id):
    half = turns // 2
    count = tokens.shape[0]
    rows = w_qkv.shape[0]
    first, second = split(w_down.shape[1] // planes)
    devices = planes * depth * 2
    everyone = (planes, depth, 2, rows)
    shapes = [
        ((HQ, count), BF),
        ((turns + 1, count, 2 * HK), BF),
        (everyone + (HQ,), BF),
        (everyone + (2 * HK,), BF),
        ((D, count), BF),
        ((HQ + HK, count), F32),
        (((HEADS + KV_HEADS) // 4, 4, count), F32),
        (everyone + (D,), BF),
        ((planes, count, D), BF),
        ((planes, count, 2 * D), F32),
        ((depth * 2, planes, 3, rows, first), BF),
        ((depth * 2, planes, 3, rows, second), BF),
        ((depth, planes, 3, rows, first), BF),
        ((1, devices * n_gains), F32),
        ((HQ, count), BF),
        ((GROUPS, 4, count), F32),
        ((count, D), F32),
        ((count, D), F32),
    ]
    flops = 18 * planes * count * D * (first + second)
    return pl.pallas_call(
        functools.partial(fore_kernel, planes, depth, turns, n_gains),
        out_shape=tuple(jax.ShapeDtypeStruct(s, k) for s, k in shapes),
        in_specs=[VMEM] * 9 + [ANY],
        out_specs=(ANY,) * 13 + (VMEM,) * 5,
        scratch_shapes=[pltpu.VMEM(*shape) for shape in shapes[:8]]
        + [
            pltpu.VMEM((planes, 3, rows, first), BF),
            pltpu.VMEM((planes, 3, rows, second), BF),
            pltpu.VMEM((planes, depth, 2, 8, 128), F32),
            pltpu.VMEM((planes, count, D // planes), BF),
            pltpu.VMEM((count, 2 * HQ), F32),
            pltpu.VMEM((count, count), F32),
            pltpu.VMEM((HQ, count), F32),
            pltpu.VMEM((GROUPS, 4, count), F32),
            pltpu.VMEM((3, planes, depth * 2, rows, first), BF),
            pltpu.VMEM((3, planes, depth * 2, rows, second), BF),
            pltpu.VMEM((planes, count, D), BF),
            pltpu.VMEM((planes, count, D), BF),
            pltpu.VMEM((D, planes * count), BF),
            pltpu.VMEM((D, planes * count), BF),
            pltpu.VMEM((planes * count, max(first, second)), BF),
            pltpu.VMEM((2, planes * count, max(first, second)), BF),
            pltpu.VMEM((planes - 1, count, D), BF),
            pltpu.VMEM((planes - 1, count, D), BF),
            pltpu.VMEM((count, D), BF),
            pltpu.VMEM((3, depth * 2, rows, max(first, second)), BF),
            pltpu.VMEM((depth, planes, 3, rows, first), BF),
            DMA((2,)),
            DMA((9,)),
            DMA((2, half + 1)),
            DMA((2, half)),
            DMA((2, planes)),
            DMA((2, planes)),
            DMA((2, planes)),
            DMA((8, depth + 1)),
            DMA((8, depth + 1)),
            DMA((2, planes)),
            DMA((2, planes)),
            DMA((1,)),
            DMA((1,)),
            DMA((3,)),
            DMA((2, 3)),
            DMA((2, 3)),
            DMA((2, 3)),
        ]
        + spread_sems(planes, depth) * 4
        + fold_scratch(planes, depth, rows, first),
        compiler_params=params(collective_id),
        cost_estimate=pl.CostEstimate(flops=flops, bytes_accessed=30 << 20, transcendentals=0),
    )(tokens, cosine, sine, lower, gains_block, w_qkv, w_output, w_gate_up, w_down, cotangent)


class Fold:
    def __init__(self, me, g_any, mine, scratch):
        self.me, self.g, self.mine = me, g_any, mine
        self.other, self.from_line, self.sems = scratch

    def own_copy(self, z):
        return pltpu.make_async_copy(
            self.g.at[z * 2 + self.me.core], self.mine.at[z], self.sems.at[0, z]
        )

    def core_copy(self, z):
        me = self.me
        return remote(
            self.g.at[z * 2 + 1 - me.core], self.other.at[z], self.sems.at[1, z], self.sems.at[2, z], me.sibling()
        )

    def first(self):
        for z in range(self.me.depth):
            self.core_copy(z).start()
            self.own_copy(z).start()

    def add(self, total, term):
        def plane(d, carry):
            total[d] = (total[d].astype(F32) + term[d].astype(F32)).astype(BF)
            return carry

        lax.fori_loop(0, self.me.planes, plane, 0)

    def second(self):
        for z in range(self.me.depth):
            self.own_copy(z).wait()
            self.core_copy(z).wait_recv()
            self.add(self.mine.at[z], self.other.at[z])

    def target(self, z, k, down):
        return k - (self.me.depth - 1) + z if down else self.me.depth - 1 - k + z

    def sends(self, k, down):
        me = self.me
        return self.target(me.z, k, down) >= 0 if down else me.z <= k

    def slot(self, t, k, down):
        return self.me.depth if k == self.me.depth - 2 and not down else t

    def copy(self, k, down):
        me = self.me
        t = self.target(me.z, k, down)
        kind = 5 if down else 3
        return remote(
            self.mine.at[t], self.from_line.at[self.slot(t, k, down)], self.sems.at[kind, k], self.sems.at[kind + 1, k],
            me.along(me.z - 1 if down else me.z + 1),
        )

    def send(self, k):
        for down in (False, True):
            @pl.when(self.sends(k, down))
            def _():
                self.copy(k, down).start()

    def settle(self, k):
        me = self.me
        for down in (False, True):
            t = self.target(me.z + 1 if down else me.z - 1, k, down)
            comes = (me.z < me.depth - 1) & (t >= 0) if down else (me.z > 0) & (me.z - 1 <= k)

            @pl.when(comes)
            def _():
                block = self.from_line.at[self.slot(t, k, down)]
                kind = 5 if down else 3
                remote(
                    block, block, self.sems.at[kind, k], self.sems.at[kind + 1, k], me.sibling()
                ).wait_recv()
                self.add(self.mine.at[t], block)

    def step(self, k):
        if k > 0:
            self.settle(k - 1)
        self.send(k)

    def finish(self, first, steps):
        if first:
            for z in range(self.me.depth):
                self.core_copy(z).wait_send()
        for k in steps:
            for down in (False, True):
                @pl.when(self.sends(k, down))
                def _():
                    self.copy(k, down).wait_send()


class Swap:
    def __init__(self, me, ready, landed, sems):
        self.me, self.ready, self.landed, self.sems = me, ready, landed, sems

    def copy(self, o):
        me = self.me
        return remote(
            self.ready.at[me.dp ^ o], self.landed.at[me.dp], self.sems.at[0, o], self.sems.at[1, o], me.across(o)
        )

    def start(self, value):
        self.ready[...] = value
        for o in range(1, self.me.planes):
            self.copy(o).start()

    def last(self):
        me = self.me
        self.landed[me.dp] = self.ready[me.dp]
        for o in range(1, me.planes):
            block = self.landed.at[me.dp ^ o]
            remote(block, block, self.sems.at[0, o], self.sems.at[1, o], me.across(o)).wait_recv()

    def finish(self):
        for o in range(1, self.me.planes):
            self.copy(o).wait_send()


FOLD = 3


def fold_scratch(planes, depth, rows, full):
    block = (planes, 3, rows, full)
    return [
        pltpu.VMEM((depth,) + block, BF),
        pltpu.VMEM((depth + 1,) + block, BF),
        DMA((7, depth)),
    ]


def split(full):
    first = (full // 128 + 1) // 2 * 128
    return (first, full - first)


EARLY = 2


def home_kernel(
    planes, depth, turns, n_gains,
    gn_ref, mixed_ref, og_ref, gains_ref, o_ref, lse_ref, q_ref, lower_ref, cos_ref, sin_ref, tok_ref,
    wo_any, kv_any, parts_any, grads_b, mine_a, unit_any, recip_any, wq_any, wkv_any, xat_any,
    block_out, grad_out, shard_out, shard_qkv, gains_out, pair_out, down_out,
    wo, kv, unit_s, recip_s, wq_all, wkv_all, xat, own_part, gq, grad_kv, gmixed_s,
    bias, gob, delta, gkv, from_core, from_z, from_plane, partial, gproj, partial_q, partial_kv, gains_p, *rest,
):
    me = Place(planes, depth)
    collect = Collect(me, partial, rest[:COLLECT])
    collect_q = Collect(me, partial_q, rest[COLLECT : 2 * COLLECT])
    collect_kv = Collect(me, partial_kv, rest[2 * COLLECT : 3 * COLLECT])
    small = Collect(me, gains_p, rest[3 * COLLECT : 4 * COLLECT])
    rest = rest[4 * COLLECT :]
    mine_first, ready_first, landed_first, swap_first, mine_second, ready_second, landed_second, swap_second = rest[:8]
    folds = (
        Fold(me, None, mine_first, (None,) + rest[8:10]),
        Fold(me, grads_b, mine_second, rest[10 : 10 + FOLD]),
    )
    swaps = (
        Swap(me, ready_first, landed_first, swap_first),
        Swap(me, ready_second, landed_second, swap_second),
    )
    cs, zs, ps, load = rest[10 + FOLD :]
    half = turns // 2
    count = gn_ref.shape[0]
    sources = [wo_any, kv_any, unit_any, recip_any, xat_any, parts_any.at[0], wq_any, wkv_any, mine_a]
    places = [wo, kv, unit_s, recip_s, xat, own_part, wq_all, wkv_all, mine_first]
    loads = [pltpu.make_async_copy(a, b, load.at[i]) for i, (a, b) in enumerate(zip(sources, places))]
    for copy in loads[8:] + loads[:8]:
        copy.start()
    greet(me.plane() + me.line() + [me.sibling()])
    loads[8].wait()
    folds[0].send(EARLY)
    folds[1].first()

    def c_copy(i):
        return remote(gkv.at[2 * i + 1], from_core.at[i], cs.at[0, i], cs.at[1, i], me.sibling())

    def z_copy(k):
        return remote(gkv.at[2 * k], from_z.at[k - 1], zs.at[0, k], zs.at[1, k], me.along(me.behind(k)))

    def p_copy(o):
        return remote(parts_any.at[o], from_plane.at[o - 1], ps.at[0, o], ps.at[1, o], me.across(o))

    for o in range(1, planes):
        p_copy(o).start()
    unit, recip = unit_of(mixed_ref[...], 1)
    grad = gn_ref[...]
    scaled = grad * gains_ref[:, D : 2 * D]
    inner = jnp.mean(scaled * unit, axis=1, keepdims=True)
    gmixed = og_ref[...].astype(F32) + recip * (scaled - unit * inner)
    gmixed_s[...] = gmixed
    dgf = jnp.sum(grad * unit, axis=0, keepdims=True)
    gmixed_b = gmixed.astype(BF)
    loads[0].wait()
    gob[...] = dot(wo[...].reshape(HQ, D), gmixed_b, NT).astype(BF)
    for t in range(GROUPS):
        rows = []
        for h in range(4):
            at = pl.ds(t * 256 + h * 64, 64)
            rows.append(
                jnp.sum(gob[at, :].astype(F32) * o_ref[at, :].astype(F32), axis=0, keepdims=True)
            )
        delta[t] = jnp.concatenate(rows, axis=0)
    half_rows = D // planes
    order = list(range(1, planes)) + [0]
    for o in order:
        d = me.dp ^ o
        rows = o_ref[pl.ds(pl.multiple_of(d * half_rows, 128), half_rows), :]
        partial[d] = dot(rows, gmixed_b, NN).astype(BF).reshape(partial.shape[1:])
        collect.first(o)
    folds[1].second()
    folds[1].step(0)
    gq[...] = jnp.zeros_like(gq)
    loads[1].wait()

    def visit(slot):
        fill_bias(bias, lower_ref[...], slot)

        def four_heads(t, carry):
            key_at = pl.ds(pl.multiple_of(t * 128, 128), 128)
            value_at = pl.ds(pl.multiple_of(HK + t * 128, 128), 128)
            keys, values = kv[slot, :, key_at], kv[slot, :, value_at]
            lse_t, delta_t = lse_ref[t], delta[t]
            grad_keys, grad_values = [], []
            for u in range(2):
                key = keys[:, u * 64 : u * 64 + 64]
                value = values[:, u * 64 : u * 64 + 64]
                grad_key, grad_value = 0.0, 0.0
                for g in range(2):
                    h = 2 * u + g
                    at = pl.ds(pl.multiple_of(t * 256 + h * 64, 64), 64)
                    query, gob_h = q_ref[at, :], gob[at, :]
                    probs = jnp.exp(dot(key, query, NN) + bias[...] - lse_t[h : h + 1, :])
                    grad_value = grad_value + dot(probs.astype(BF), gob_h, NT)
                    grad_scores = (probs * (dot(value, gob_h, NN) - delta_t[h : h + 1, :])).astype(BF)
                    grad_key = grad_key + dot(grad_scores, query, NT)
                    gq[at, :] += dot(key, grad_scores, TN)
                grad_keys.append(grad_key)
                grad_values.append(grad_value)
            gkv[slot, :, key_at] = jnp.concatenate(grad_keys, axis=1).astype(BF)
            gkv[slot, :, value_at] = jnp.concatenate(grad_values, axis=1).astype(BF)
            return carry

        lax.fori_loop(0, GROUPS, four_heads, 0)

    for i in range(half - 1, -1, -1):
        @pl.when(me.z - i - 1 + me.core >= 0)
        def _():
            visit(2 * i + 1)
            c_copy(i).start()

    for k in range(half, 0, -1):
        @pl.when(me.z - k >= 0)
        def _():
            visit(2 * k)

            @pl.when(me.core == 0)
            def _():
                if k < half:
                    c_copy(k).wait_recv()
                    gkv[2 * k] = (gkv[2 * k].astype(F32) + from_core[k].astype(F32)).astype(BF)

            @pl.when(me.core == 1)
            def _():
                c_copy(k - 1).wait_recv()
                gkv[2 * k] = (gkv[2 * k].astype(F32) + from_core[k - 1].astype(F32)).astype(BF)

            z_copy(k).start()

    visit(0)
    for i in (2, 3, 4):
        loads[i].wait()
    tail_row = gains_ref[:, 2 * D : 2 * D + 128]
    gain_q, gain_k = column_of(tail_row, 0), column_of(tail_row, HEAD_DIM)
    cosine, sine = cos_ref[...], -sin_ref[...]
    gained = [0.0, 0.0]

    def four_grads(h):
        kind = 0 if h < HEADS else 1
        if kind == 0:
            four = gq[pl.ds(h * HEAD_DIM, 4 * HEAD_DIM), :] * HEAD_DIM ** (-0.5)
        else:
            four = grad_kv[:, pl.ds((h - HEADS) * HEAD_DIM, 4 * HEAD_DIM)].T
        recips = recip_s[h // 4]
        results = []
        for i in range(4):
            unit = unit_s[pl.ds((h + i) * HEAD_DIM, HEAD_DIM), :]
            grad = turned(four[i * HEAD_DIM : (i + 1) * HEAD_DIM], cosine, sine)
            scaled = grad * (gain_k if kind else gain_q)
            inner = jnp.mean(scaled * unit, axis=0, keepdims=True)
            results.append(recips[i : i + 1, :] * (scaled - unit * inner))
            gained[kind] = gained[kind] + grad * unit
        gproj[:, pl.ds(h * HEAD_DIM, 4 * HEAD_DIM)] = jnp.concatenate(results, axis=0).T.astype(BF)

    def gather_grads(columns, table, collected):
        for o in order:
            d = me.dp ^ o
            rows = xat[pl.ds(pl.multiple_of(d * half_rows, 128), half_rows), :]
            table[d] = dot(rows, gproj[:, columns], NN).astype(BF).reshape(table.shape[1:])
            collected.first(o)
            if o != order[0]:
                collected.second(order[order.index(o) - 1])
        collected.second(0)

    for o in order:
        collect.second(o)
    for h in range(0, HEADS, 4):
        four_grads(h)
    gather_grads(pl.ds(0, HQ), partial_q, collect_q)
    folds[1].step(1)
    for k in range(EARLY + 1, depth - 1):
        folds[0].step(k)
    grad_kv[...] = gkv[0].astype(F32)

    @pl.when(me.core == 0)
    def _():
        c_copy(0).wait_recv()
        grad_kv[...] += from_core[0].astype(F32)

    for k in range(1, half + 1):
        @pl.when(me.z + k < depth)
        def _():
            z_copy(k).wait_recv()
            grad_kv[...] += from_z[k - 1].astype(F32)

    for h in range(HEADS, HEADS + KV_HEADS, 4):
        four_grads(h)
    gproj[:, pl.ds(HQ + HK, HK)] = grad_kv[:, pl.ds(HK, HK)].astype(BF)
    gather_grads(pl.ds(HQ, 2 * HK), partial_kv, collect_kv)
    value_o = collect.third()
    value_q = collect_q.third()
    for i in (6, 7):
        loads[i].wait()
    grad = dot(gproj[:, :HQ], wq_all[...].reshape(D, HQ), NT)
    grad = grad + dot(gproj[:, HQ:], wkv_all[...].reshape(D, 2 * HK), NT)
    unit, recip = unit_of(tok_ref[...].astype(F32), 1)
    scaled = grad * gains_ref[:, :D]
    inner = jnp.mean(scaled * unit, axis=1, keepdims=True)
    grad_out[...] = gmixed_s[...] + recip * (scaled - unit * inner)
    dga = jnp.sum(grad * unit, axis=0, keepdims=True)
    for k in range(2, depth - 1):
        folds[1].step(k)
    folds[0].settle(depth - 2)
    swaps[0].start(mine_first[me.z])
    lane = lax.broadcasted_iota(jnp.int32, (HEAD_DIM, 128), 1)
    entry = lax.broadcasted_iota(jnp.int32, (HEAD_DIM, 128), 0)
    sums = [jnp.sum(g, axis=1, keepdims=True) for g in gained]
    last = jnp.sum(
        jnp.where(lane == entry, sums[0], 0.0) + jnp.where(lane == entry + HEAD_DIM, sums[1], 0.0),
        axis=0,
        keepdims=True,
    )
    whole = jnp.concatenate([dga, dgf, last], axis=1)
    devices = planes * depth * 2
    entries = devices * n_gains
    index = lax.broadcasted_iota(jnp.int32, (devices, entries), 1)
    device = lax.broadcasted_iota(jnp.int32, (devices, entries), 0)
    apart = jnp.where(index // n_gains == device, whole, 0.0)
    pick = jnp.where(
        lax.broadcasted_iota(jnp.int32, (128, entries), 1) % n_gains
        == lax.broadcasted_iota(jnp.int32, (128, entries), 0),
        1.0,
        0.0,
    )
    table = lax.dot_general(
        apart, pick, NT, preferred_element_type=F32, precision=lax.Precision.HIGHEST
    )
    gains_p[...] = jnp.broadcast_to(table[:, None, :], (devices, 8, 128)).reshape(gains_p.shape)
    for o in order:
        small.first(o)
    for o in order:
        small.second(o)
    value_kv = collect_kv.third()
    little = small.third()
    total = mixed_ref[...]
    loads[5].wait()
    total = total + own_part[...].astype(F32)
    for o in range(1, planes):
        p_copy(o).wait_recv()
        total = total + from_plane[o - 1].astype(F32)
    block_out[...] = total.astype(BF)
    folds[1].settle(depth - 2)
    swaps[1].start(mine_second[me.z])
    shard_out[...] = collect.last(value_o)
    shard_qkv[:, :HQ] = collect_q.last(value_q)
    shard_qkv[:, HQ:] = collect_kv.last(value_kv)
    gains_out[...] = small.last(little)
    start = 0
    full = landed_first.shape[3] + landed_second.shape[3]
    for swap in swaps:
        swap.last()
        f = swap.landed.shape[3]
        for d in range(planes):
            for m in range(2):
                at = (m * planes + d) * full + start
                pair_out[:, at : at + f] = swap.landed[d, m]
            at = d * full + start
            down_out[:, at : at + f] = swap.landed[d, 2]
        start = f

    for o in range(1, planes):
        p_copy(o).wait_send()
    for i in range(half):
        @pl.when(me.z - i - 1 + me.core >= 0)
        def _():
            c_copy(i).wait_send()
    for k in range(1, half + 1):
        @pl.when(me.z - k >= 0)
        def _():
            z_copy(k).wait_send()
    collect.finish()
    collect_q.finish()
    collect_kv.finish()
    small.finish()
    folds[0].finish(False, range(EARLY, depth - 1))
    folds[1].finish(True, range(depth - 1))
    for swap in swaps:
        swap.finish()


def home(first, second, n_gains, planes, depth, turns, collective_id):
    half = turns // 2
    count = first[0].shape[0]
    wo_all, kv_all, _, grads, mine, unit, recip, wq_all, wkv_all, xat = second
    rows = wo_all.shape[3]
    parts = (mine.shape[4], grads.shape[4])
    full = sum(parts)
    return pl.pallas_call(
        functools.partial(home_kernel, planes, depth, turns, n_gains),
        out_shape=(
            jax.ShapeDtypeStruct((count, D), BF),
            jax.ShapeDtypeStruct((count, D), F32),
            jax.ShapeDtypeStruct((rows, D), F32),
            jax.ShapeDtypeStruct((rows, 2 * HQ), F32),
            jax.ShapeDtypeStruct((8, 128), F32),
            jax.ShapeDtypeStruct((rows, 2 * planes * full), BF),
            jax.ShapeDtypeStruct((rows, planes * full), BF),
        ),
        in_specs=[VMEM] * len(first) + [ANY] * len(second),
        out_specs=(VMEM,) * 7,
        scratch_shapes=[pltpu.VMEM(a.shape, a.dtype) for a in (wo_all, kv_all, unit, recip, wq_all, wkv_all, xat)]
        + [
            pltpu.VMEM((count, D), BF),
            pltpu.VMEM((HQ, count), F32),
            pltpu.VMEM((count, 2 * HK), F32),
            pltpu.VMEM((count, D), F32),
            pltpu.VMEM((count, count), F32),
            pltpu.VMEM((HQ, count), BF),
            pltpu.VMEM((GROUPS, 4, count), F32),
            pltpu.VMEM((turns + 1, count, 2 * HK), BF),
            pltpu.VMEM((half, count, 2 * HK), BF),
            pltpu.VMEM((half, count, 2 * HK), BF),
            pltpu.VMEM((planes - 1, count, D), BF),
            pltpu.VMEM((planes, depth, 2, rows, D), BF),
            pltpu.VMEM((count, 2 * HQ), BF),
            pltpu.VMEM((planes, depth, 2, rows, HQ), BF),
            pltpu.VMEM((planes, depth, 2, rows, 2 * HK), BF),
            pltpu.VMEM((planes, depth, 2, 8, 128), F32),
        ]
        + collect_scratch(planes, depth, rows, D, BF)
        + collect_scratch(planes, depth, rows, HQ, BF)
        + collect_scratch(planes, depth, rows, 2 * HK, BF)
        + collect_scratch(planes, depth, 8, 128, F32)
        + [
            scratch
            for part in parts
            for scratch in (
                pltpu.VMEM((depth, planes, 3, rows, part), BF),
                pltpu.VMEM((planes, 3, rows, part), BF),
                pltpu.VMEM((planes, 3, rows, part), BF),
                DMA((2, planes)),
            )
        ]
        + fold_scratch(planes, depth, rows, parts[0])[1:]
        + fold_scratch(planes, depth, rows, parts[1])
        + [DMA((2, half)), DMA((2, half + 1)), DMA((2, planes)), DMA((9,))],
        compiler_params=params(collective_id),
        cost_estimate=pl.CostEstimate(flops=60 << 30, bytes_accessed=8 << 20, transcendentals=0),
    )(*first, *second)


def per_device(
    tokens_in,
    positions,
    out_grad,
    w_qkv,
    w_output,
    w_gate_up,
    w_down,
    norm_gains,
    first_qkv,
    first_output,
    first_gate_up,
    first_down,
    first_gains,
    second_qkv,
    second_output,
    second_gate_up,
    second_down,
    second_gains,
):
    planes, ctxs = lax.axis_size("dp"), lax.axis_size("ctx")
    depth = ctxs // 2
    turns = ctxs // 2
    rows = w_qkv.shape[0]
    n_gains = norm_gains.shape[0]
    count = tokens_in.shape[0] * tokens_in.shape[1]
    tokens = tokens_in.reshape(count, D)
    places = positions.reshape(count)
    cotangent = out_grad.reshape(count, D)

    gains_block = jnp.pad(norm_gains.astype(BF).astype(F32)[None, :], ((0, 7), (0, 128 - n_gains)))
    cosine, sine = rope_tables(places)
    lower = (jnp.arange(count, dtype=jnp.int32) - places)[None, :]
    (
        query, kv_all, wq_all, wkv_all, xat, unit_heads, recip_heads, output_all, parts, _, _, grads, mine,
        gains_row, attn_t, lse, mixed, grad_normed,
    ) = fore(
        tokens, cosine, sine, lower, gains_block, w_qkv, w_output, w_gate_up, w_down, cotangent,
        n_gains, planes, depth, turns, 0,
    )
    block_out, input_grad, shard_output, shard_qkv, gains_tile, pair_b, down_b = home(
        (grad_normed, mixed, cotangent, gains_row, attn_t, lse, query, lower, cosine, sine, tokens),
        (output_all, kv_all, parts, grads, mine, unit_heads, recip_heads, wq_all, wkv_all, xat),
        n_gains, planes, depth, turns, 1,
    )
    shard_gains = gains_tile[0, :n_gains]
    shard_gate_up = pair_b.astype(F32)
    shard_down = down_b.astype(F32)

    new_qkv, new_first_qkv, new_second_qkv = adam_step(
        w_qkv, shard_qkv, first_qkv, second_qkv, 0.02, 0.1
    )
    new_output, new_first_output, new_second_output = adam_step(
        w_output, shard_output, first_output, second_output, 0.2, 0.1
    )
    new_gate_up, new_first_gate_up, new_second_gate_up = adam_step(
        w_gate_up, shard_gate_up, first_gate_up, second_gate_up, 0.02, 0.1
    )
    new_down, new_first_down, new_second_down = adam_step(
        w_down, shard_down, first_down, second_down, 0.02, 0.1
    )
    new_gains, new_first_gains, new_second_gains = adam_step(
        norm_gains, shard_gains, first_gains, second_gains, 0.1, 0.0
    )
    return (
        block_out.reshape(tokens_in.shape),
        input_grad.reshape(tokens_in.shape),
        shard_qkv,
        shard_output,
        shard_gate_up,
        shard_down,
        shard_gains,
        new_qkv,
        new_output,
        new_gate_up,
        new_down,
        new_gains,
        new_first_qkv,
        new_first_output,
        new_first_gate_up,
        new_first_down,
        new_first_gains,
        new_second_qkv,
        new_second_output,
        new_second_gate_up,
        new_second_down,
        new_second_gains,
    )


def solution(mesh):
    in_specs = (
        P("dp", "ctx", None),
        P("dp", "ctx"),
        P("dp", "ctx", None),
        P(("dp", "ctx"), None),
        P(("dp", "ctx"), None),
        P(("dp", "ctx"), None),
        P(("dp", "ctx"), None),
        P(("dp", "ctx")),
        P(("dp", "ctx"), None),
        P(("dp", "ctx"), None),
        P(("dp", "ctx"), None),
        P(("dp", "ctx"), None),
        P(("dp", "ctx")),
        P(("dp", "ctx"), None),
        P(("dp", "ctx"), None),
        P(("dp", "ctx"), None),
        P(("dp", "ctx"), None),
        P(("dp", "ctx")),
    )
    out_specs = (
        P("dp", "ctx", None),
        P("dp", "ctx", None),
        P(("dp", "ctx"), None),
        P(("dp", "ctx"), None),
        P(("dp", "ctx"), None),
        P(("dp", "ctx"), None),
        P(("dp", "ctx")),
        P(("dp", "ctx"), None),
        P(("dp", "ctx"), None),
        P(("dp", "ctx"), None),
        P(("dp", "ctx"), None),
        P(("dp", "ctx")),
        P(("dp", "ctx"), None),
        P(("dp", "ctx"), None),
        P(("dp", "ctx"), None),
        P(("dp", "ctx"), None),
        P(("dp", "ctx")),
        P(("dp", "ctx"), None),
        P(("dp", "ctx"), None),
        P(("dp", "ctx"), None),
        P(("dp", "ctx"), None),
        P(("dp", "ctx")),
    )
    return jax.shard_map(
        per_device, mesh=mesh, in_specs=in_specs, out_specs=out_specs, check_vma=False
    )
```

```python
import functools
import math

import jax
import jax.numpy as jnp
from jax import lax
from jax.experimental import pallas as pl
from jax.experimental.pallas import tpu as pltpu
from jax.sharding import PartitionSpec as P

D = 1024
HEADS = 16
KV_HEADS = 8
HEAD_DIM = 64
STEP = 4
HQ = 1024
HK = 512


EPS = 1e-05
THETA = 1000000.0
NEG_BIG = -1e30
BETA_ONE = 0.9
BETA_TWO = 0.95
ADAM_EPS = 1e-08


def adam_step(weight, grad, first, second, rate, decay):
    first_new = BETA_ONE * first + (1.0 - BETA_ONE) * grad
    second_new = BETA_TWO * second + (1.0 - BETA_TWO) * grad * grad
    first_hat = first_new / (1.0 - BETA_ONE**STEP)
    second_hat = second_new / (1.0 - BETA_TWO**STEP)
    weight_new = weight - rate * (first_hat / (jnp.sqrt(second_hat) + ADAM_EPS) + decay * weight)
    return (weight_new, first_new, second_new)


BF = jnp.bfloat16
F32 = jnp.float32
MESH_ID = pl.DeviceIdType.MESH
ANY = pl.BlockSpec(memory_space=pl.ANY)
VMEM = pl.BlockSpec(memory_space=pltpu.VMEM)
DMA = pltpu.SemaphoreType.DMA
NN = (((1,), (0,)), ((), ()))
NT = (((1,), (1,)), ((), ()))
TN = (((0,), (0,)), ((), ()))
VMEM_BYTES = 60 << 20
GROUPS = HEADS // 4


def dot(a, b, dims):
    return lax.dot_general(a, b, dims, preferred_element_type=F32)


class Place:
    def __init__(self, planes, depth):
        self.planes, self.depth = planes, depth
        self.dp = lax.axis_index("dp")
        self.ctx = lax.axis_index("ctx")
        self.z = self.ctx // 2
        self.core = self.ctx % 2

    def sibling(self):
        return {"dp": self.dp, "ctx": self.z * 2 + 1 - self.core}

    def across(self, o):
        return {"dp": self.dp ^ o, "ctx": self.ctx}

    def behind(self, k):
        return lax.rem(self.z + self.depth - k, self.depth)

    def ahead(self, k):
        return lax.rem(self.z + k, self.depth)

    def along(self, z):
        return {"dp": self.dp, "ctx": z * 2 + self.core}

    def plane(self):
        return [self.across(o) for o in range(1, self.planes)]

    def line(self):
        return [self.along(self.ahead(k)) for k in range(1, self.depth)]


def near(planes):
    return [o for o in range(1, planes) if o & (o - 1) == 0]


def far(planes):
    return [o for o in range(1, planes) if o & (o - 1) != 0]


def greet(devices):
    barrier = pltpu.get_barrier_semaphore()
    for device in devices:
        pl.semaphore_signal(barrier, inc=1, device_id=device, device_id_type=MESH_ID)
    pl.semaphore_wait(barrier, len(devices))


def remote(src, dst, send, recv, device):
    return pltpu.make_async_remote_copy(
        src_ref=src, dst_ref=dst, send_sem=send, recv_sem=recv, device_id=device, device_id_type=MESH_ID
    )


def params(collective_id):
    return pltpu.CompilerParams(
        vmem_limit_bytes=VMEM_BYTES, collective_id=collective_id, has_side_effects=True
    )


class Spread:
    def __init__(self, me, g_ref, line_sems, sems, halves=True):
        self.me, self.g, self.line_sems, self.sems = me, g_ref, line_sems, sems
        self.by_halves = halves and me.planes == 4
        self.sent = []

    def push(self, src, dst, kind, o, device):
        copy = remote(src, dst, self.sems.at[kind, o], self.sems.at[kind + 1, o], device)
        copy.start()
        self.sent.append(copy)

    def mine(self, o, core):
        return self.g.at[self.me.dp ^ o, :, core]

    def line(self):
        me = self.me
        block = self.g.at[me.dp, me.z, me.core]
        for k in range(1, me.depth):
            copy = remote(
                block, block, self.line_sems.at[0, k], self.line_sems.at[1, k], me.along(me.ahead(k))
            )
            copy.start()
            self.sent.append(copy)

    def first(self):
        me = self.me
        for k in range(1, me.depth):
            block = self.g.at[me.dp, me.behind(k), me.core]
            remote(
                block, block, self.line_sems.at[0, k], self.line_sems.at[1, k], me.along(me.ahead(k))
            ).wait_recv()
        self.push(self.mine(0, me.core), self.mine(0, me.core), 2, 0, me.sibling())
        self.plane(near(me.planes))

    def plane(self, places):
        me = self.me
        for o in places:
            self.push(self.mine(0, me.core), self.mine(0, me.core), 0, o, me.across(o))

    def part(self, o, number):
        half = self.me.depth // 2
        return self.g.at[self.me.dp ^ o, pl.ds(number * half, half), self.me.core]

    def relay(self, o):
        block = self.mine(o, self.me.core)
        if self.by_halves and o == 3:
            for number in range(2):
                piece = self.part(o, number)
                kind = 4 + 2 * number
                remote(
                    piece, piece, self.sems.at[kind, o], self.sems.at[kind + 1, o], self.me.sibling()
                ).wait_recv()
        else:
            remote(block, block, self.sems.at[0, o], self.sems.at[1, o], self.me.sibling()).wait_recv()
        if self.by_halves and o < 3:
            piece = self.part(o, o - 1)
            self.push(piece, piece, 2 + 2 * o, 3, self.me.across(3 - o))
        self.push(block, block, 2, o, self.me.sibling())

    def arrive(self, o):
        block = self.mine(o, 1 - self.me.core)
        remote(block, block, self.sems.at[2, o], self.sems.at[3, o], self.me.sibling()).wait_recv()

    def finish(self):
        for copy in self.sent:
            copy.wait_send()


def spread_sems(planes, depth):
    return [DMA((2, depth)), DMA((8, planes))]


class Collect:
    def __init__(self, me, p_ref, scratch):
        self.me, self.p = me, p_ref
        self.sums, self.from_plane, self.total, self.from_z, self.cs, self.ps, self.zs = scratch

    def c_copy(self, o):
        me = self.me
        return remote(
            self.p.at[me.dp ^ o, :, 1 - me.core], self.sums.at[o], self.cs.at[0, o], self.cs.at[1, o], me.sibling()
        )

    def p_copy(self, o):
        return remote(
            self.sums.at[o], self.from_plane.at[o - 1], self.ps.at[0, o], self.ps.at[1, o], self.me.across(o)
        )

    def z_copy(self, k):
        me = self.me
        return remote(
            self.total.at[me.ahead(k)], self.from_z.at[k], self.zs.at[0, k], self.zs.at[1, k], me.along(me.ahead(k))
        )

    def first(self, o):
        self.c_copy(o).start()

    def second(self, o):
        me = self.me
        self.c_copy(o).wait_recv()
        own = self.p[me.dp ^ o, :, me.core].astype(F32)
        self.sums[o] = (own + self.sums[o].astype(F32)).astype(self.sums.dtype)
        if o > 0:
            self.p_copy(o).start()

    def third(self):
        me = self.me
        for o in range(1, me.planes):
            self.p_copy(o).wait_recv()
        for k in list(range(1, me.depth)) + [0]:
            z = me.ahead(k)
            value = self.sums[0, z].astype(F32)
            for o in range(1, me.planes):
                value = value + self.from_plane[o - 1, z].astype(F32)
            self.total[z] = value.astype(self.total.dtype)
            if k > 0:
                self.z_copy(k).start()
        return value

    def last(self, value):
        for k in range(1, self.me.depth):
            self.z_copy(k).wait_recv()
            value = value + self.from_z[k].astype(F32)
        return value

    def finish(self):
        for o in range(self.me.planes):
            self.c_copy(o).wait_send()
        for o in range(1, self.me.planes):
            self.p_copy(o).wait_send()
        for k in range(1, self.me.depth):
            self.z_copy(k).wait_send()


def collect_scratch(planes, depth, rows, columns, kind):
    return [
        pltpu.VMEM((planes, depth, rows, columns), kind),
        pltpu.VMEM((planes - 1, depth, rows, columns), kind),
        pltpu.VMEM((depth, rows, columns), kind),
        pltpu.VMEM((depth, rows, columns), kind),
        DMA((2, planes)),
        DMA((2, planes)),
        DMA((2, depth)),
    ]


COLLECT = 7


def unit_of(values, axis):
    recip = lax.rsqrt(jnp.mean(values * values, axis=axis, keepdims=True) + EPS)
    return values * recip, recip


def column_of(row, start):
    lane = lax.broadcasted_iota(jnp.int32, (HEAD_DIM, 128), 1)
    entry = lax.broadcasted_iota(jnp.int32, (HEAD_DIM, 128), 0)
    return jnp.sum(jnp.where(lane == entry + start, row, 0.0), axis=1, keepdims=True)


def turned(values, cosine, sine):
    half = HEAD_DIM // 2
    a, b = values[:half], values[half:]
    return jnp.concatenate([a * cosine - b * sine, b * cosine + a * sine], axis=0)


def fill_bias(bias, lower, slot):
    count = bias.shape[0]
    query = lax.broadcasted_iota(jnp.int32, (count, count), 1)
    key = lax.broadcasted_iota(jnp.int32, (count, count), 0) - slot * count
    bias[...] = jnp.where((key <= query) & (key >= lower), 0.0, NEG_BIG)


class Pass:
    def __init__(self, me, w_ref, sems):
        self.me, self.w, self.sems = me, w_ref, sems

    def copy(self, kind, s, down, core=None, device=None):
        me = self.me
        z = me.z + s - 1 if down else me.z - s + 1
        block = self.w.at[:, :, z * 2 + (me.core if core is None else core)]
        device = me.sibling() if device is None else device
        return remote(block, block, self.sems.at[kind, s], self.sems.at[kind + 1, s], device)

    def held(self, s, down):
        me = self.me
        return me.z + s - 1 < me.depth if down else me.z - s + 1 >= 0

    def on(self, s, down):
        me = self.me
        return self.held(s, down) & (me.z >= 1 if down else me.z + 1 < me.depth)

    def line_copy(self, s, down):
        me = self.me
        return self.copy(2 if down else 0, s, down, None, me.along(me.z - 1 if down else me.z + 1))

    def step(self, s):
        for down in (False, True):
            if s > 1:
                @pl.when(self.held(s, down))
                def _():
                    me = self.me
                    z = me.z + s - 1 if down else me.z - s + 1
                    block = self.w.at[:, :, z * 2 + me.core]
                    kind = 2 if down else 0
                    remote(
                        block, block, self.sems.at[kind, s - 1], self.sems.at[kind + 1, s - 1], me.sibling()
                    ).wait_recv()

            @pl.when(self.on(s, down))
            def _():
                self.line_copy(s, down).start()

            if s > 1 or not down:
                @pl.when(self.held(s, down))
                def _():
                    self.copy(6 if down else 4, s, down).start()

    def arrive(self):
        for s in range(1, self.me.depth + 1):
            for down in (False, True):
                if s > 1 or not down:
                    @pl.when(self.held(s, down))
                    def _():
                        self.copy(6 if down else 4, s, down, 1 - self.me.core).wait_recv()

    def finish(self):
        for s in range(1, self.me.depth + 1):
            for down in (False, True):
                @pl.when(self.on(s, down))
                def _():
                    self.line_copy(s, down).wait_send()

                if s > 1 or not down:
                    @pl.when(self.held(s, down))
                    def _():
                        self.copy(6 if down else 4, s, down).wait_send()


def fore_kernel(
    planes, depth, turns, n_gains,
    tok_ref, place_ref, gain_ref, wqkv_ref, wout_ref, wpair_ref, wdown_ref, og_ref,
    q_any, kv_any, wq_any, wkv_any, xat_any, unit_any, recip_any, wo_any, parts_any, spill_any, grads_a, grads_b, mine_any,
    gains_out, o_out, lse_out, mixed_out, gn_out, cos_ref, sin_ref, lower_ref,
    q_s, kv_all, wq_all, wkv_all, xat, unit_s, recip_s, wo_all, blocks_a, blocks_b, gains_g, xa, proj, bias, accum, sums,
    wa, wb, hns, ogs, hnt, ogt, mid, pair, send_gn, recv_gn, part_s, stage, mine,
    own_sem, keep_sem, zs, cs, ps, a2a_a, a2a_b, pass_a, pass_b, hsem, nsem, psem, ssem, stsem, og_halves, hn_halves, dsem,
    glsem, gsem, qlsem, qsem, wlsem, wsem, olsem, osem, *fold_rest,
):
    me = Place(planes, depth)
    half = turns // 2
    count = tok_ref.shape[0]
    width = D // planes
    rows = wqkv_ref.shape[0]
    halves = (blocks_a.shape[3], blocks_b.shape[3])
    full = sum(halves)
    gains = Spread(me, gains_g, glsem, gsem, False)
    queries = Spread(me, wq_all, qlsem, qsem)
    weights = Spread(me, wkv_all, wlsem, wsem)
    outputs = Spread(me, wo_all, olsem, osem)
    pass_first, pass_second = Pass(me, wa, pass_a), Pass(me, wb, pass_b)
    fold = Fold(me, grads_a, mine, fold_rest)
    kept = []

    def keep(source, into):
        copy = pltpu.make_async_copy(source, into, keep_sem.at[len(kept)])
        copy.start()
        kept.append(copy)

    here = gains_g.at[me.dp, me.z, me.core]
    here[...] = jnp.zeros((8, 128), F32)
    here[0:1, 0:n_gains] = gain_ref[...].astype(BF).astype(F32)
    wq_all[me.dp, me.z, me.core] = wqkv_ref[:, :HQ].astype(BF)
    wkv_all[me.dp, me.z, me.core] = wqkv_ref[:, HQ:].astype(BF)
    wo_all[me.dp, me.z, me.core] = wout_ref[...].astype(BF)
    for d in range(planes):
        for m in range(3):
            source = wdown_ref if m == 2 else wpair_ref
            at = d * full if m == 2 else (m * planes + d) * full
            blocks_a[d, m] = source[:, at : at + halves[0]].astype(BF)
            blocks_b[d, m] = source[:, at + halves[0] : at + full].astype(BF)
    wa[:, me.dp, me.ctx] = blocks_a[me.dp]
    wb[:, me.dp, me.ctx] = blocks_b[me.dp]
    own_og = pltpu.make_async_copy(og_ref, ogs.at[0], own_sem.at[1])
    own_og.start()
    greet(me.plane() + me.line() + [me.sibling()])
    gains.line()
    weights.line()

    def a2a_copy(part, o):
        source, into, sems = ((blocks_a, wa, a2a_a), (blocks_b, wb, a2a_b))[part]
        return remote(
            source.at[me.dp ^ o], into.at[:, me.dp, me.ctx], sems.at[0, o], sems.at[1, o], me.across(o)
        )

    def a2a_wait(part):
        into, sems = ((wa, a2a_a), (wb, a2a_b))[part]
        for o in range(1, planes):
            block = into.at[:, me.dp ^ o, me.ctx]
            remote(block, block, sems.at[0, o], sems.at[1, o], me.across(o)).wait_recv()

    for part in range(2):
        for o in range(1, planes):
            a2a_copy(part, o).start()
    unit, _ = unit_of(tok_ref[...].astype(F32), 1)
    proj[:, :D] = unit
    places = place_ref[...]
    lower_ref[...] = lax.broadcasted_iota(jnp.int32, (1, count), 1) - places
    steps = lax.broadcasted_iota(jnp.int32, (HEAD_DIM // 2, 1), 0).astype(F32)
    angles = jnp.exp(-math.log(THETA) * (2.0 * steps / HEAD_DIM)) * places.astype(F32)
    cos_ref[...] = jnp.cos(angles)
    sin_ref[...] = jnp.sin(angles)
    gains.first()
    gains.plane(far(planes))
    weights.first()
    queries.line()
    a2a_wait(0)
    pass_first.step(1)
    for o in range(1, planes):
        gains.relay(o)
    for o in range(planes):
        gains.arrive(o)
    devices = planes * depth * 2
    table = gains_g[...].reshape(devices, 8, 128)[:, 0, :].astype(BF)
    entries = devices * n_gains
    index = lax.broadcasted_iota(jnp.int32, (128, entries), 1)
    pick = jnp.where(
        index % n_gains == lax.broadcasted_iota(jnp.int32, (128, entries), 0), 1.0, 0.0
    ).astype(BF)
    spread = dot(table, pick, NN)
    owner = lax.broadcasted_iota(jnp.int32, (devices, entries), 1) // n_gains
    device = lax.broadcasted_iota(jnp.int32, (devices, entries), 0)
    gains_row = 1.0 + jnp.sum(jnp.where(owner == device, spread, 0.0), axis=0, keepdims=True)
    gains_out[...] = gains_row
    normed = (proj[:, :D] * gains_row[:, :D]).astype(BF)
    xat[...] = normed.T
    keep(xat, xat_any)
    for d in range(planes):
        xa[d] = normed[:, d * width : (d + 1) * width]

    def project(source, table, at):
        proj[:, at] = jnp.zeros((count, D), F32)
        places = [0] + near(planes) + far(planes)
        for o in places:
            if o > 0:
                source.relay(o)
            source.arrive(o)
            if o == near(planes)[-1] and planes != 4:
                source.plane(far(planes))
            proj[:, at] += dot(xa[me.dp ^ o], table[me.dp ^ o].reshape(width, D), NN)

    project(weights, wkv_all, pl.ds(HQ, 2 * HK))
    queries.first()
    outputs.line()
    tail_row = gains_row[:, 2 * D : 2 * D + 128]
    gain_q, gain_k = column_of(tail_row, 0), column_of(tail_row, HEAD_DIM)
    cosine, sine = cos_ref[...], sin_ref[...]

    def four_raw(h):
        four = proj[:, h * HEAD_DIM : (h + 4) * HEAD_DIM].T
        results, recips = [], []
        for i in range(4):
            value, recip = unit_of(four[i * HEAD_DIM : (i + 1) * HEAD_DIM], 0)
            unit_s[pl.ds((h + i) * HEAD_DIM, HEAD_DIM), :] = value
            recips.append(recip)
            results.append(turned(value * (gain_q if h < HEADS else gain_k), cosine, sine))
        recip_s[h // 4] = jnp.concatenate(recips, axis=0)
        return jnp.concatenate(results, axis=0)

    for h in range(HEADS, HEADS + KV_HEADS, 4):
        kv_all[0, :, pl.ds((h - HEADS) * HEAD_DIM, 4 * HEAD_DIM)] = four_raw(h).T.astype(BF)
    kv_all[0, :, pl.ds(HK, HK)] = proj[:, HQ + HK :].astype(BF)

    def half_copy(slots, sems, o):
        rows = pl.ds((o - 1) * (count // 2), count // 2)
        return remote(
            slots.at[o, rows], slots.at[3, rows], sems.at[0, o], sems.at[1, o], me.across(3 - o)
        )

    def z_copy(k):
        return remote(kv_all.at[2 * k - 2], kv_all.at[2 * k], zs.at[0, k], zs.at[1, k], me.along(me.ahead(1)))

    def z_sends(k):
        return (me.z + 1 < depth) & (me.z - k + 1 >= 0)

    def c_copy(i):
        return remote(
            kv_all.at[2 * i + 2 * me.core], kv_all.at[2 * i + 1], cs.at[0, i], cs.at[1, i], me.sibling()
        )

    @pl.when(z_sends(1))
    def _():
        z_copy(1).start()

    @pl.when(me.core == 0)
    def _():
        c_copy(0).start()

    project(queries, wq_all, pl.ds(0, HQ))
    outputs.first()
    for h in range(0, HEADS, 4):
        q_s[pl.ds(h * HEAD_DIM, 4 * HEAD_DIM), :] = (four_raw(h) * HEAD_DIM ** (-0.5)).astype(BF)
    keep(q_s, q_any)
    keep(unit_s, unit_any)
    keep(recip_s, recip_any)
    keep(wq_all, wq_any)
    keep(wkv_all, wkv_any)
    square = planes == 4
    if not square:
        outputs.plane(far(planes))
    shares = []
    for o in near(planes) if square else range(1, planes):
        share = remote(og_ref, ogs.at[o], ps.at[0, o], ps.at[1, o], me.across(o))
        share.start()
        shares.append(share)
    accum[...] = jnp.zeros_like(accum)
    sums[...] = jnp.zeros_like(sums)

    def visit(slot):
        fill_bias(bias, lower_ref[...], slot)

        def four_heads(t, carry):
            keys = kv_all[slot, :, pl.ds(pl.multiple_of(t * 128, 128), 128)]
            values = kv_all[slot, :, pl.ds(pl.multiple_of(HK + t * 128, 128), 128)]
            totals = []
            for u in range(2):
                key = keys[:, u * 64 : u * 64 + 64]
                value = values[:, u * 64 : u * 64 + 64]
                for g in range(2):
                    at = pl.ds(pl.multiple_of(t * 256 + u * 128 + g * 64, 64), 64)
                    weight = jnp.exp(dot(key, q_s[at, :], NN) + bias[...])
                    totals.append(jnp.sum(weight, axis=0, keepdims=True))
                    accum[at, :] += dot(value, weight.astype(BF), TN)
            sums[t] += jnp.concatenate(totals, axis=0)
            return carry

        lax.fori_loop(0, GROUPS, four_heads, 0)

    visit(0)
    for k in range(1, half + 1):
        there = me.z - k >= 0

        @pl.when(there)
        def _():
            z_copy(k).wait_recv()

        if k < half:
            @pl.when(z_sends(k + 1))
            def _():
                z_copy(k + 1).start()

        @pl.when(there & (me.core == 1))
        def _():
            c_copy(k - 1).start()

        if k < half:
            @pl.when(there & (me.core == 0))
            def _():
                c_copy(k).start()

        @pl.when(there)
        def _():
            visit(2 * k)

    pass_first.step(2)
    for i in range(half):
        @pl.when(me.z - i - 1 + me.core >= 0)
        def _():
            c_copy(i).wait_recv()
            visit(2 * i + 1)

    pass_first.step(3)
    a2a_wait(1)
    pass_second.step(1)
    keep(kv_all, kv_any)
    for o in range(1, planes):
        outputs.relay(o)
    if square:
        for o in (1, 2):
            remote(og_ref, ogs.at[o], ps.at[0, o], ps.at[1, o], me.across(o)).wait_recv()
            half_copy(ogs, og_halves, o).start()
    for t in range(GROUPS):
        total = sums[t]
        lse_out[t] = jnp.log(total)
        for h in range(4):
            at = pl.ds(t * 256 + h * 64, 64)
            o_out[at, :] = (accum[at, :] / total[h : h + 1, :]).astype(BF)
    for o in range(planes):
        outputs.arrive(o)
    keep(wo_all, wo_any)
    mixed = tok_ref[...].astype(F32) + dot(o_out[...].T, wo_all[...].reshape(HQ, D), NN)
    mixed_out[...] = mixed
    unit, _ = unit_of(mixed, 1)
    hns[0] = (unit * gains_out[:, D : 2 * D]).astype(BF)

    def hn_copy(o):
        return remote(hns.at[0], hns.at[o], hsem.at[0, o], hsem.at[1, o], me.across(o))

    def gn_copy(o):
        return remote(send_gn.at[o - 1], recv_gn.at[o - 1], nsem.at[0, o], nsem.at[1, o], me.across(o))

    def diagonal_rows(other):
        return pl.ds((other - 1) * (count // 2), count // 2)

    def diagonal_copy(other):
        rows = diagonal_rows(other)
        return remote(
            send_gn.at[2, rows], recv_gn.at[2, rows], dsem.at[0, other], dsem.at[1, other], me.across(other)
        )

    def spill_copy(o, back):
        ends = (spill_any.at[o], proj) if back else (proj, spill_any.at[o])
        return pltpu.make_async_copy(*ends, ssem.at[0])

    def parts_copy(o):
        return pltpu.make_async_copy(part_s, parts_any.at[o], psem.at[0])

    for o in near(planes):
        hn_copy(o).start()
    for s in range(4, depth + 1):
        pass_first.step(s)
    pass_first.arrive()
    own_og.wait()

    def ffn_part(part):
        w, f = (wa, wb)[part], halves[part]

        def block(i, carry):
            o = i if part == 0 else planes - 1 - i
            if part == 0:
                if square:
                    @pl.when(o == 1)
                    def _():
                        for other in (1, 2):
                            hn_copy(other).wait_recv()
                            half_copy(hns, hn_halves, other).start()

                    @pl.when(o == 3)
                    def _():
                        for other in (1, 2):
                            half_copy(ogs, og_halves, other).wait_recv()
                            half_copy(hns, hn_halves, other).wait_recv()
                else:
                    @pl.when(o > 0)
                    def _():
                        hn_copy(o).wait_recv()
                        remote(og_ref, ogs.at[o], ps.at[0, o], ps.at[1, o], me.across(o)).wait_recv()
            else:
                spill_copy(o, True).start()

            hn, og = hns[o], ogs[o]
            at = pl.ds(pl.multiple_of(o * count, 128), count)
            if part == 0:
                hnt[:, at] = hn.T
                ogt[:, at] = og.T
            w_gate, w_up, w_down = (w[m].reshape(D, f) for m in range(3))
            gate = dot(hn, w_gate, NN)
            upper = dot(hn, w_up, NN)
            sigma = 1.0 / (1.0 + jnp.exp(-gate))
            active = gate * sigma
            middle = (active * upper).astype(BF)
            gmid = dot(og, w_down, NN)
            ggate = (gmid * upper * sigma * (1.0 + gate * (1.0 - sigma))).astype(BF)
            gupper = (gmid * active).astype(BF)
            mid[at, :f] = middle
            pair[0, at, :f] = ggate
            pair[1, at, :f] = gupper
            gn = dot(ggate, w_gate, NT) + dot(gupper, w_up, NT)
            out = dot(middle, w_down, NT)
            if part == 0:
                @pl.when(o > 0)
                def _():
                    spill_copy(o - 1, False).wait()

                proj[:, :D] = gn
                proj[:, D:] = out
                spill_copy(o, False).start()

                @pl.when(o == 0)
                def _():
                    if not square:
                        for other in far(planes):
                            hn_copy(other).start()
                    pass_second.step(2)

                @pl.when(o == planes // 2)
                def _():
                    pass_second.step(3)
            else:
                spill_copy(o, True).wait()
                gn = gn + proj[:, :D]
                out = out + proj[:, D:]

                @pl.when(i > 0)
                def _():
                    parts_copy(o + 1).wait()

                if square:
                    proj[:, :D] = gn

                    @pl.when(o == 3)
                    def _():
                        send_gn[2] = gn.astype(BF)
                        for other in (1, 2):
                            diagonal_copy(other).start()

                    for other in (1, 2):
                        @pl.when(o == other)
                        def _():
                            rows = diagonal_rows(3 - other)
                            diagonal_copy(3 - other).wait_recv()
                            proj[rows, :D] += recv_gn[2, rows].astype(F32)
                            send_gn[other - 1] = proj[:, :D].astype(BF)
                            gn_copy(other).start()
                else:
                    @pl.when(o > 0)
                    def _():
                        send_gn[o - 1] = gn.astype(BF)
                        gn_copy(o).start()

                @pl.when(o == 0)
                def _():
                    gn_out[...] = gn

                @pl.when(i == 0)
                def _():
                    fold.second()
                    fold.step(0)

                @pl.when(i == planes // 2)
                def _():
                    fold.step(1)

                part_s[...] = out.astype(BF)
                parts_copy(o).start()
            return carry

        lax.fori_loop(0, planes, block, 0)
        if part == 0:
            spill_copy(planes - 1, False).wait()
        else:
            parts_copy(0).wait()
        strip = D // planes
        grads = (grads_a, grads_b)[part]

        def out_copy(m, d):
            return pltpu.make_async_copy(stage.at[m, :, :, :f], grads.at[:, d, m], stsem.at[m])

        def weight_grads(d, carry):
            left = pl.ds(pl.multiple_of(d * strip, 128), strip)
            for m in (2, 0, 1):
                @pl.when(d > 0)
                def _():
                    out_copy(m, d - 1).wait()

                if m == 2:
                    total = dot(ogt[left, :], mid[:, :f], NN)
                else:
                    total = dot(hnt[left, :], pair[m, :, :f], NN)
                stage[m, :, :, :f] = total.astype(BF).reshape(depth * 2, rows, f)
                out_copy(m, d).start()
            return carry

        lax.fori_loop(0, planes, weight_grads, 0)
        for m in range(3):
            out_copy(m, planes - 1).wait()

    ffn_part(0)
    fold.first()
    for s in range(4, depth + 1):
        pass_second.step(s)
    pass_second.arrive()
    ffn_part(1)
    total = gn_out[...]
    for o in (1, 2) if square else range(1, planes):
        gn_copy(o).wait_recv()
        total = total + recv_gn[o - 1].astype(F32)
    gn_out[...] = total
    fold.settle(EARLY - 1)
    keep(mine, mine_any)
    pass_first.finish()
    pass_second.finish()
    fold.finish(True, range(EARLY))
    for o in (1, 2) if square else range(1, planes):
        gn_copy(o).wait_send()
        hn_copy(o).wait_send()
        if square:
            diagonal_copy(o).wait_send()
            half_copy(hns, hn_halves, o).wait_send()
            half_copy(ogs, og_halves, o).wait_send()

    for i in range(half):
        @pl.when(me.z - i - me.core >= 0)
        def _():
            c_copy(i).wait_send()

    for k in range(1, half + 1):
        @pl.when(z_sends(k))
        def _():
            z_copy(k).wait_send()

    for o in range(1, planes):
        a2a_copy(0, o).wait_send()
        a2a_copy(1, o).wait_send()
    for share in shares:
        share.wait_send()
    gains.finish()
    queries.finish()
    weights.finish()
    outputs.finish()
    for copy in kept:
        copy.wait()


def fore(tokens, places, gains, w_qkv, w_output, w_gate_up, w_down, cotangent, n_gains, planes, depth, turns, collective_id):
    half = turns // 2
    count = tokens.shape[0]
    rows = w_qkv.shape[0]
    first, second = split(w_down.shape[1] // planes)
    devices = planes * depth * 2
    everyone = (planes, depth, 2, rows)
    shapes = [
        ((HQ, count), BF),
        ((turns + 1, count, 2 * HK), BF),
        (everyone + (HQ,), BF),
        (everyone + (2 * HK,), BF),
        ((D, count), BF),
        ((HQ + HK, count), F32),
        (((HEADS + KV_HEADS) // 4, 4, count), F32),
        (everyone + (D,), BF),
        ((planes, count, D), BF),
        ((planes, count, 2 * D), F32),
        ((depth * 2, planes, 3, rows, first), BF),
        ((depth * 2, planes, 3, rows, second), BF),
        ((depth, planes, 3, rows, first), BF),
        ((1, devices * n_gains), F32),
        ((HQ, count), BF),
        ((GROUPS, 4, count), F32),
        ((count, D), F32),
        ((count, D), F32),
        ((HEAD_DIM // 2, count), F32),
        ((HEAD_DIM // 2, count), F32),
        ((1, count), jnp.int32),
    ]
    flops = 18 * planes * count * D * (first + second)
    return pl.pallas_call(
        functools.partial(fore_kernel, planes, depth, turns, n_gains),
        out_shape=tuple(jax.ShapeDtypeStruct(s, k) for s, k in shapes),
        in_specs=[VMEM] * 7 + [ANY],
        out_specs=(ANY,) * 13 + (VMEM,) * 8,
        scratch_shapes=[pltpu.VMEM(*shape) for shape in shapes[:8]]
        + [
            pltpu.VMEM((planes, 3, rows, first), BF),
            pltpu.VMEM((planes, 3, rows, second), BF),
            pltpu.VMEM((planes, depth, 2, 8, 128), F32),
            pltpu.VMEM((planes, count, D // planes), BF),
            pltpu.VMEM((count, 2 * HQ), F32),
            pltpu.VMEM((count, count), F32),
            pltpu.VMEM((HQ, count), F32),
            pltpu.VMEM((GROUPS, 4, count), F32),
            pltpu.VMEM((3, planes, depth * 2, rows, first), BF),
            pltpu.VMEM((3, planes, depth * 2, rows, second), BF),
            pltpu.VMEM((planes, count, D), BF),
            pltpu.VMEM((planes, count, D), BF),
            pltpu.VMEM((D, planes * count), BF),
            pltpu.VMEM((D, planes * count), BF),
            pltpu.VMEM((planes * count, max(first, second)), BF),
            pltpu.VMEM((2, planes * count, max(first, second)), BF),
            pltpu.VMEM((planes - 1, count, D), BF),
            pltpu.VMEM((planes - 1, count, D), BF),
            pltpu.VMEM((count, D), BF),
            pltpu.VMEM((3, depth * 2, rows, max(first, second)), BF),
            pltpu.VMEM((depth, planes, 3, rows, first), BF),
            DMA((2,)),
            DMA((9,)),
            DMA((2, half + 1)),
            DMA((2, half)),
            DMA((2, planes)),
            DMA((2, planes)),
            DMA((2, planes)),
            DMA((8, depth + 1)),
            DMA((8, depth + 1)),
            DMA((2, planes)),
            DMA((2, planes)),
            DMA((1,)),
            DMA((1,)),
            DMA((3,)),
            DMA((2, 3)),
            DMA((2, 3)),
            DMA((2, 3)),
        ]
        + spread_sems(planes, depth) * 4
        + fold_scratch(planes, depth, rows, first),
        compiler_params=params(collective_id),
        cost_estimate=pl.CostEstimate(flops=flops, bytes_accessed=30 << 20, transcendentals=0),
    )(tokens, places, gains, w_qkv, w_output, w_gate_up, w_down, cotangent)


class Fold:
    def __init__(self, me, g_any, mine, scratch):
        self.me, self.g, self.mine = me, g_any, mine
        self.other, self.from_line, self.sems = scratch

    def own_copy(self, z):
        return pltpu.make_async_copy(
            self.g.at[z * 2 + self.me.core], self.mine.at[z], self.sems.at[0, z]
        )

    def core_copy(self, z):
        me = self.me
        return remote(
            self.g.at[z * 2 + 1 - me.core], self.other.at[z], self.sems.at[1, z], self.sems.at[2, z], me.sibling()
        )

    def first(self):
        for z in range(self.me.depth):
            self.core_copy(z).start()
            self.own_copy(z).start()

    def add(self, total, term):
        def plane(d, carry):
            total[d] = (total[d].astype(F32) + term[d].astype(F32)).astype(BF)
            return carry

        lax.fori_loop(0, self.me.planes, plane, 0)

    def second(self):
        for z in range(self.me.depth):
            self.own_copy(z).wait()
            self.core_copy(z).wait_recv()
            self.add(self.mine.at[z], self.other.at[z])

    def target(self, z, k, down):
        return k - (self.me.depth - 1) + z if down else self.me.depth - 1 - k + z

    def sends(self, k, down):
        me = self.me
        return self.target(me.z, k, down) >= 0 if down else me.z <= k

    def slot(self, t, k, down):
        return self.me.depth if k == self.me.depth - 2 and not down else t

    def copy(self, k, down):
        me = self.me
        t = self.target(me.z, k, down)
        kind = 5 if down else 3
        return remote(
            self.mine.at[t], self.from_line.at[self.slot(t, k, down)], self.sems.at[kind, k], self.sems.at[kind + 1, k],
            me.along(me.z - 1 if down else me.z + 1),
        )

    def send(self, k):
        for down in (False, True):
            @pl.when(self.sends(k, down))
            def _():
                self.copy(k, down).start()

    def settle(self, k):
        me = self.me
        for down in (False, True):
            t = self.target(me.z + 1 if down else me.z - 1, k, down)
            comes = (me.z < me.depth - 1) & (t >= 0) if down else (me.z > 0) & (me.z - 1 <= k)

            @pl.when(comes)
            def _():
                block = self.from_line.at[self.slot(t, k, down)]
                kind = 5 if down else 3
                remote(
                    block, block, self.sems.at[kind, k], self.sems.at[kind + 1, k], me.sibling()
                ).wait_recv()
                self.add(self.mine.at[t], block)

    def step(self, k):
        if k > 0:
            self.settle(k - 1)
        self.send(k)

    def finish(self, first, steps):
        if first:
            for z in range(self.me.depth):
                self.core_copy(z).wait_send()
        for k in steps:
            for down in (False, True):
                @pl.when(self.sends(k, down))
                def _():
                    self.copy(k, down).wait_send()


class Swap:
    def __init__(self, me, ready, landed, sems):
        self.me, self.ready, self.landed, self.sems = me, ready, landed, sems

    def copy(self, o):
        me = self.me
        return remote(
            self.ready.at[me.dp ^ o], self.landed.at[me.dp], self.sems.at[0, o], self.sems.at[1, o], me.across(o)
        )

    def start(self, value):
        self.ready[...] = value
        for o in range(1, self.me.planes):
            self.copy(o).start()

    def last(self):
        me = self.me
        self.landed[me.dp] = self.ready[me.dp]
        for o in range(1, me.planes):
            block = self.landed.at[me.dp ^ o]
            remote(block, block, self.sems.at[0, o], self.sems.at[1, o], me.across(o)).wait_recv()

    def finish(self):
        for o in range(1, self.me.planes):
            self.copy(o).wait_send()


FOLD = 3


def fold_scratch(planes, depth, rows, full):
    block = (planes, 3, rows, full)
    return [
        pltpu.VMEM((depth,) + block, BF),
        pltpu.VMEM((depth + 1,) + block, BF),
        DMA((7, depth)),
    ]


def split(full):
    first = (full // 128 + 1) // 2 * 128
    return (first, full - first)


EARLY = 2


def home_kernel(
    planes, depth, turns, n_gains,
    gn_ref, mixed_ref, og_ref, gains_ref, o_ref, lse_ref, q_ref, lower_ref, cos_ref, sin_ref, tok_ref,
    wo_any, kv_any, parts_any, grads_b, mine_a, unit_any, recip_any, wq_any, wkv_any, xat_any,
    block_out, grad_out, shard_out, shard_qkv, gains_out, pair_out, down_out,
    wo, kv, unit_s, recip_s, wq_all, wkv_all, xat, own_part, gq, grad_kv, gmixed_s,
    bias, gob, delta, gkv, from_core, from_z, from_plane, partial, gproj, partial_q, partial_kv, gains_p, *rest,
):
    me = Place(planes, depth)
    collect = Collect(me, partial, rest[:COLLECT])
    collect_q = Collect(me, partial_q, rest[COLLECT : 2 * COLLECT])
    collect_kv = Collect(me, partial_kv, rest[2 * COLLECT : 3 * COLLECT])
    small = Collect(me, gains_p, rest[3 * COLLECT : 4 * COLLECT])
    rest = rest[4 * COLLECT :]
    mine_first, ready_first, landed_first, swap_first, mine_second, ready_second, landed_second, swap_second = rest[:8]
    folds = (
        Fold(me, None, mine_first, (None,) + rest[8:10]),
        Fold(me, grads_b, mine_second, rest[10 : 10 + FOLD]),
    )
    swaps = (
        Swap(me, ready_first, landed_first, swap_first),
        Swap(me, ready_second, landed_second, swap_second),
    )
    cs, zs, ps, load = rest[10 + FOLD :]
    half = turns // 2
    count = gn_ref.shape[0]
    sources = [wo_any, kv_any, unit_any, recip_any, xat_any, parts_any.at[0], wq_any, wkv_any, mine_a]
    places = [wo, kv, unit_s, recip_s, xat, own_part, wq_all, wkv_all, mine_first]
    loads = [pltpu.make_async_copy(a, b, load.at[i]) for i, (a, b) in enumerate(zip(sources, places))]
    for copy in loads[8:] + loads[:8]:
        copy.start()
    greet(me.plane() + me.line() + [me.sibling()])
    loads[8].wait()
    folds[0].send(EARLY)
    folds[1].first()

    def c_copy(i):
        return remote(gkv.at[2 * i + 1], from_core.at[i], cs.at[0, i], cs.at[1, i], me.sibling())

    def z_copy(k):
        return remote(gkv.at[2 * k], from_z.at[k - 1], zs.at[0, k], zs.at[1, k], me.along(me.behind(1)))

    def join(k):
        if k < half:
            @pl.when((me.z - k >= 0) & (me.z + 1 < depth))
            def _():
                z_copy(k + 1).wait_recv()
                gkv[2 * k] = (gkv[2 * k].astype(F32) + from_z[k].astype(F32)).astype(BF)

        @pl.when(me.z - k >= 0)
        def _():
            z_copy(k).start()

    def p_copy(o):
        return remote(parts_any.at[o], from_plane.at[o - 1], ps.at[0, o], ps.at[1, o], me.across(o))

    for o in range(1, planes):
        p_copy(o).start()
    unit, recip = unit_of(mixed_ref[...], 1)
    grad = gn_ref[...]
    scaled = grad * gains_ref[:, D : 2 * D]
    inner = jnp.mean(scaled * unit, axis=1, keepdims=True)
    gmixed = og_ref[...].astype(F32) + recip * (scaled - unit * inner)
    gmixed_s[...] = gmixed
    dgf = jnp.sum(grad * unit, axis=0, keepdims=True)
    gmixed_b = gmixed.astype(BF)
    loads[0].wait()
    gob[...] = dot(wo[...].reshape(HQ, D), gmixed_b, NT).astype(BF)
    for t in range(GROUPS):
        rows = []
        for h in range(4):
            at = pl.ds(t * 256 + h * 64, 64)
            rows.append(
                jnp.sum(gob[at, :].astype(F32) * o_ref[at, :].astype(F32), axis=0, keepdims=True)
            )
        delta[t] = jnp.concatenate(rows, axis=0)
    half_rows = D // planes
    order = list(range(1, planes)) + [0]
    gq[...] = jnp.zeros_like(gq)
    loads[1].wait()

    def visit(slot):
        fill_bias(bias, lower_ref[...], slot)

        def four_heads(t, carry):
            key_at = pl.ds(pl.multiple_of(t * 128, 128), 128)
            value_at = pl.ds(pl.multiple_of(HK + t * 128, 128), 128)
            keys, values = kv[slot, :, key_at], kv[slot, :, value_at]
            lse_t, delta_t = lse_ref[t], delta[t]
            grad_keys, grad_values = [], []
            for u in range(2):
                key = keys[:, u * 64 : u * 64 + 64]
                value = values[:, u * 64 : u * 64 + 64]
                grad_key, grad_value = 0.0, 0.0
                for g in range(2):
                    h = 2 * u + g
                    at = pl.ds(pl.multiple_of(t * 256 + h * 64, 64), 64)
                    query, gob_h = q_ref[at, :], gob[at, :]
                    probs = jnp.exp(dot(key, query, NN) + bias[...] - lse_t[h : h + 1, :])
                    grad_value = grad_value + dot(probs.astype(BF), gob_h, NT)
                    grad_scores = (probs * (dot(value, gob_h, NN) - delta_t[h : h + 1, :])).astype(BF)
                    grad_key = grad_key + dot(grad_scores, query, NT)
                    gq[at, :] += dot(key, grad_scores, TN)
                grad_keys.append(grad_key)
                grad_values.append(grad_value)
            gkv[slot, :, key_at] = jnp.concatenate(grad_keys, axis=1).astype(BF)
            gkv[slot, :, value_at] = jnp.concatenate(grad_values, axis=1).astype(BF)
            return carry

        lax.fori_loop(0, GROUPS, four_heads, 0)

    for i in range(half - 1, -1, -1):
        @pl.when(me.z - i - 1 + me.core >= 0)
        def _():
            visit(2 * i + 1)
            c_copy(i).start()

    for k in range(half, 0, -1):
        @pl.when(me.z - k >= 0)
        def _():
            visit(2 * k)

            @pl.when(me.core == 0)
            def _():
                if k < half:
                    c_copy(k).wait_recv()
                    gkv[2 * k] = (gkv[2 * k].astype(F32) + from_core[k].astype(F32)).astype(BF)

            @pl.when(me.core == 1)
            def _():
                c_copy(k - 1).wait_recv()
                gkv[2 * k] = (gkv[2 * k].astype(F32) + from_core[k - 1].astype(F32)).astype(BF)

        if k == half:
            join(k)

    folds[1].second()
    folds[1].step(0)
    visit(0)
    for k in range(half - 1, 0, -1):
        join(k)
    for o in order:
        d = me.dp ^ o
        rows = o_ref[pl.ds(pl.multiple_of(d * half_rows, 128), half_rows), :]
        partial[d] = dot(rows, gmixed_b, NN).astype(BF).reshape(partial.shape[1:])
        collect.first(o)
    for i in (2, 3, 4):
        loads[i].wait()
    tail_row = gains_ref[:, 2 * D : 2 * D + 128]
    gain_q, gain_k = column_of(tail_row, 0), column_of(tail_row, HEAD_DIM)
    cosine, sine = cos_ref[...], -sin_ref[...]
    gained = [0.0, 0.0]

    def four_grads(h):
        kind = 0 if h < HEADS else 1
        if kind == 0:
            four = gq[pl.ds(h * HEAD_DIM, 4 * HEAD_DIM), :] * HEAD_DIM ** (-0.5)
        else:
            four = grad_kv[:, pl.ds((h - HEADS) * HEAD_DIM, 4 * HEAD_DIM)].T
        recips = recip_s[h // 4]
        results = []
        for i in range(4):
            unit = unit_s[pl.ds((h + i) * HEAD_DIM, HEAD_DIM), :]
            grad = turned(four[i * HEAD_DIM : (i + 1) * HEAD_DIM], cosine, sine)
            scaled = grad * (gain_k if kind else gain_q)
            inner = jnp.mean(scaled * unit, axis=0, keepdims=True)
            results.append(recips[i : i + 1, :] * (scaled - unit * inner))
            gained[kind] = gained[kind] + grad * unit
        gproj[:, pl.ds(h * HEAD_DIM, 4 * HEAD_DIM)] = jnp.concatenate(results, axis=0).T.astype(BF)

    def gather_grads(columns, table, collected):
        for o in order:
            d = me.dp ^ o
            rows = xat[pl.ds(pl.multiple_of(d * half_rows, 128), half_rows), :]
            table[d] = dot(rows, gproj[:, columns], NN).astype(BF).reshape(table.shape[1:])
            collected.first(o)
            if o != order[0]:
                collected.second(order[order.index(o) - 1])
        collected.second(0)

    for o in order:
        collect.second(o)
    for h in range(0, HEADS, 4):
        four_grads(h)
    gather_grads(pl.ds(0, HQ), partial_q, collect_q)
    folds[1].step(1)
    for k in range(EARLY + 1, depth - 1):
        folds[0].step(k)
    grad_kv[...] = gkv[0].astype(F32)

    @pl.when(me.core == 0)
    def _():
        c_copy(0).wait_recv()
        grad_kv[...] += from_core[0].astype(F32)

    @pl.when(me.z + 1 < depth)
    def _():
        z_copy(1).wait_recv()
        grad_kv[...] += from_z[0].astype(F32)

    for h in range(HEADS, HEADS + KV_HEADS, 4):
        four_grads(h)
    gproj[:, pl.ds(HQ + HK, HK)] = grad_kv[:, pl.ds(HK, HK)].astype(BF)
    gather_grads(pl.ds(HQ, 2 * HK), partial_kv, collect_kv)
    value_o = collect.third()
    value_q = collect_q.third()
    for i in (6, 7):
        loads[i].wait()
    grad = dot(gproj[:, :HQ], wq_all[...].reshape(D, HQ), NT)
    grad = grad + dot(gproj[:, HQ:], wkv_all[...].reshape(D, 2 * HK), NT)
    unit, recip = unit_of(tok_ref[...].astype(F32), 1)
    scaled = grad * gains_ref[:, :D]
    inner = jnp.mean(scaled * unit, axis=1, keepdims=True)
    grad_out[...] = gmixed_s[...] + recip * (scaled - unit * inner)
    dga = jnp.sum(grad * unit, axis=0, keepdims=True)
    for k in range(2, depth - 1):
        folds[1].step(k)
    folds[0].settle(depth - 2)
    swaps[0].start(mine_first[me.z])
    lane = lax.broadcasted_iota(jnp.int32, (HEAD_DIM, 128), 1)
    entry = lax.broadcasted_iota(jnp.int32, (HEAD_DIM, 128), 0)
    sums = [jnp.sum(g, axis=1, keepdims=True) for g in gained]
    last = jnp.sum(
        jnp.where(lane == entry, sums[0], 0.0) + jnp.where(lane == entry + HEAD_DIM, sums[1], 0.0),
        axis=0,
        keepdims=True,
    )
    whole = jnp.concatenate([dga, dgf, last], axis=1)
    devices = planes * depth * 2
    entries = devices * n_gains
    index = lax.broadcasted_iota(jnp.int32, (devices, entries), 1)
    device = lax.broadcasted_iota(jnp.int32, (devices, entries), 0)
    apart = jnp.where(index // n_gains == device, whole, 0.0)
    pick = jnp.where(
        lax.broadcasted_iota(jnp.int32, (128, entries), 1) % n_gains
        == lax.broadcasted_iota(jnp.int32, (128, entries), 0),
        1.0,
        0.0,
    )
    table = lax.dot_general(
        apart, pick, NT, preferred_element_type=F32, precision=lax.Precision.HIGHEST
    )
    gains_p[...] = jnp.broadcast_to(table[:, None, :], (devices, 8, 128)).reshape(gains_p.shape)
    for o in order:
        small.first(o)
    for o in order:
        small.second(o)
    value_kv = collect_kv.third()
    little = small.third()
    total = mixed_ref[...]
    loads[5].wait()
    total = total + own_part[...].astype(F32)
    for o in range(1, planes):
        p_copy(o).wait_recv()
        total = total + from_plane[o - 1].astype(F32)
    block_out[...] = total.astype(BF)
    folds[1].settle(depth - 2)
    swaps[1].start(mine_second[me.z])
    shard_out[...] = collect.last(value_o)
    shard_qkv[:, :HQ] = collect_q.last(value_q)
    shard_qkv[:, HQ:] = collect_kv.last(value_kv)
    gains_out[...] = small.last(little)
    start = 0
    full = landed_first.shape[3] + landed_second.shape[3]
    for swap in swaps:
        swap.last()
        f = swap.landed.shape[3]
        for d in range(planes):
            for m in range(2):
                at = (m * planes + d) * full + start
                pair_out[:, at : at + f] = swap.landed[d, m]
            at = d * full + start
            down_out[:, at : at + f] = swap.landed[d, 2]
        start = f

    for o in range(1, planes):
        p_copy(o).wait_send()
    for i in range(half):
        @pl.when(me.z - i - 1 + me.core >= 0)
        def _():
            c_copy(i).wait_send()
    for k in range(1, half + 1):
        @pl.when(me.z - k >= 0)
        def _():
            z_copy(k).wait_send()
    collect.finish()
    collect_q.finish()
    collect_kv.finish()
    small.finish()
    folds[0].finish(False, range(EARLY, depth - 1))
    folds[1].finish(True, range(depth - 1))
    for swap in swaps:
        swap.finish()


def home(first, second, n_gains, planes, depth, turns, collective_id):
    half = turns // 2
    count = first[0].shape[0]
    wo_all, kv_all, _, grads, mine, unit, recip, wq_all, wkv_all, xat = second
    rows = wo_all.shape[3]
    parts = (mine.shape[4], grads.shape[4])
    full = sum(parts)
    return pl.pallas_call(
        functools.partial(home_kernel, planes, depth, turns, n_gains),
        out_shape=(
            jax.ShapeDtypeStruct((count, D), BF),
            jax.ShapeDtypeStruct((count, D), F32),
            jax.ShapeDtypeStruct((rows, D), F32),
            jax.ShapeDtypeStruct((rows, 2 * HQ), F32),
            jax.ShapeDtypeStruct((8, 128), F32),
            jax.ShapeDtypeStruct((rows, 2 * planes * full), BF),
            jax.ShapeDtypeStruct((rows, planes * full), BF),
        ),
        in_specs=[VMEM] * len(first) + [ANY] * len(second),
        out_specs=(VMEM,) * 7,
        scratch_shapes=[pltpu.VMEM(a.shape, a.dtype) for a in (wo_all, kv_all, unit, recip, wq_all, wkv_all, xat)]
        + [
            pltpu.VMEM((count, D), BF),
            pltpu.VMEM((HQ, count), F32),
            pltpu.VMEM((count, 2 * HK), F32),
            pltpu.VMEM((count, D), F32),
            pltpu.VMEM((count, count), F32),
            pltpu.VMEM((HQ, count), BF),
            pltpu.VMEM((GROUPS, 4, count), F32),
            pltpu.VMEM((turns + 1, count, 2 * HK), BF),
            pltpu.VMEM((half, count, 2 * HK), BF),
            pltpu.VMEM((half, count, 2 * HK), BF),
            pltpu.VMEM((planes - 1, count, D), BF),
            pltpu.VMEM((planes, depth, 2, rows, D), BF),
            pltpu.VMEM((count, 2 * HQ), BF),
            pltpu.VMEM((planes, depth, 2, rows, HQ), BF),
            pltpu.VMEM((planes, depth, 2, rows, 2 * HK), BF),
            pltpu.VMEM((planes, depth, 2, 8, 128), F32),
        ]
        + collect_scratch(planes, depth, rows, D, BF)
        + collect_scratch(planes, depth, rows, HQ, BF)
        + collect_scratch(planes, depth, rows, 2 * HK, BF)
        + collect_scratch(planes, depth, 8, 128, F32)
        + [
            scratch
            for part in parts
            for scratch in (
                pltpu.VMEM((depth, planes, 3, rows, part), BF),
                pltpu.VMEM((planes, 3, rows, part), BF),
                pltpu.VMEM((planes, 3, rows, part), BF),
                DMA((2, planes)),
            )
        ]
        + fold_scratch(planes, depth, rows, parts[0])[1:]
        + fold_scratch(planes, depth, rows, parts[1])
        + [DMA((2, half)), DMA((2, half + 1)), DMA((2, planes)), DMA((9,))],
        compiler_params=params(collective_id),
        cost_estimate=pl.CostEstimate(flops=60 << 30, bytes_accessed=8 << 20, transcendentals=0),
    )(*first, *second)


def adam_kernel(rates, *refs):
    n = len(rates)
    for i, rate in enumerate(rates):
        weight, grad, first, second = (r[...] for r in refs[4 * i : 4 * i + 4])
        grad = grad.astype(F32)
        outs = refs[4 * (n + i) : 4 * (n + i) + 4]
        for out, value in zip(outs, (grad,) + adam_step(weight, grad, first, second, rate, 0.1)):
            out[...] = value


def adam(groups, rates):
    rows = groups[0][0].shape[0]
    block = 16 if rows % 16 == 0 else rows
    specs, shapes = [], []
    for group in groups:
        columns = group[0].shape[1]
        specs += [pl.BlockSpec((block, columns), lambda i: (i, 0))] * 4
        shapes += [jax.ShapeDtypeStruct((rows, columns), F32)] * 4
    outs = pl.pallas_call(
        functools.partial(adam_kernel, rates),
        out_shape=tuple(shapes),
        grid=(rows // block,),
        in_specs=specs,
        out_specs=tuple(specs),
        compiler_params=pltpu.CompilerParams(vmem_limit_bytes=VMEM_BYTES),
    )(*[array for group in groups for array in group])
    return [outs[4 * i : 4 * i + 4] for i in range(len(groups))]


def per_device(
    tokens_in,
    positions,
    out_grad,
    w_qkv,
    w_output,
    w_gate_up,
    w_down,
    norm_gains,
    first_qkv,
    first_output,
    first_gate_up,
    first_down,
    first_gains,
    second_qkv,
    second_output,
    second_gate_up,
    second_down,
    second_gains,
):
    planes, ctxs = lax.axis_size("dp"), lax.axis_size("ctx")
    depth = ctxs // 2
    turns = ctxs // 2
    rows = w_qkv.shape[0]
    n_gains = norm_gains.shape[0]
    count = tokens_in.shape[0] * tokens_in.shape[1]
    tokens = tokens_in.reshape(count, D)
    places = positions.reshape(1, count)
    cotangent = out_grad.reshape(count, D)

    (
        query, kv_all, wq_all, wkv_all, xat, unit_heads, recip_heads, output_all, parts, _, _, grads, mine,
        gains_row, attn_t, lse, mixed, grad_normed, cosine, sine, lower,
    ) = fore(
        tokens, places, norm_gains[None, :], w_qkv, w_output, w_gate_up, w_down, cotangent,
        n_gains, planes, depth, turns, 0,
    )
    block_out, input_grad, shard_output, shard_qkv, gains_tile, pair_b, down_b = home(
        (grad_normed, mixed, cotangent, gains_row, attn_t, lse, query, lower, cosine, sine, tokens),
        (output_all, kv_all, parts, grads, mine, unit_heads, recip_heads, wq_all, wkv_all, xat),
        n_gains, planes, depth, turns, 1,
    )
    shard_gains = gains_tile[0, :n_gains]
    (
        (shard_qkv, new_qkv, new_first_qkv, new_second_qkv),
        (shard_output, new_output, new_first_output, new_second_output),
        (shard_gate_up, new_gate_up, new_first_gate_up, new_second_gate_up),
        (shard_down, new_down, new_first_down, new_second_down),
    ) = adam(
        (
            (w_qkv, shard_qkv, first_qkv, second_qkv),
            (w_output, shard_output, first_output, second_output),
            (w_gate_up, pair_b, first_gate_up, second_gate_up),
            (w_down, down_b, first_down, second_down),
        ),
        (0.02, 0.2, 0.02, 0.02),
    )
    new_gains, new_first_gains, new_second_gains = adam_step(
        norm_gains, shard_gains, first_gains, second_gains, 0.1, 0.0
    )
    return (
        block_out.reshape(tokens_in.shape),
        input_grad.reshape(tokens_in.shape),
        shard_qkv,
        shard_output,
        shard_gate_up,
        shard_down,
        shard_gains,
        new_qkv,
        new_output,
        new_gate_up,
        new_down,
        new_gains,
        new_first_qkv,
        new_first_output,
        new_first_gate_up,
        new_first_down,
        new_first_gains,
        new_second_qkv,
        new_second_output,
        new_second_gate_up,
        new_second_down,
        new_second_gains,
    )


def solution(mesh):
    in_specs = (
        P("dp", "ctx", None),
        P("dp", "ctx"),
        P("dp", "ctx", None),
        P(("dp", "ctx"), None),
        P(("dp", "ctx"), None),
        P(("dp", "ctx"), None),
        P(("dp", "ctx"), None),
        P(("dp", "ctx")),
        P(("dp", "ctx"), None),
        P(("dp", "ctx"), None),
        P(("dp", "ctx"), None),
        P(("dp", "ctx"), None),
        P(("dp", "ctx")),
        P(("dp", "ctx"), None),
        P(("dp", "ctx"), None),
        P(("dp", "ctx"), None),
        P(("dp", "ctx"), None),
        P(("dp", "ctx")),
    )
    out_specs = (
        P("dp", "ctx", None),
        P("dp", "ctx", None),
        P(("dp", "ctx"), None),
        P(("dp", "ctx"), None),
        P(("dp", "ctx"), None),
        P(("dp", "ctx"), None),
        P(("dp", "ctx")),
        P(("dp", "ctx"), None),
        P(("dp", "ctx"), None),
        P(("dp", "ctx"), None),
        P(("dp", "ctx"), None),
        P(("dp", "ctx")),
        P(("dp", "ctx"), None),
        P(("dp", "ctx"), None),
        P(("dp", "ctx"), None),
        P(("dp", "ctx"), None),
        P(("dp", "ctx")),
        P(("dp", "ctx"), None),
        P(("dp", "ctx"), None),
        P(("dp", "ctx"), None),
        P(("dp", "ctx"), None),
        P(("dp", "ctx")),
    )
    return jax.shard_map(
        per_device, mesh=mesh, in_specs=in_specs, out_specs=out_specs, check_vma=False
    )
```

```python
import functools
import math

import jax
import jax.numpy as jnp
from jax import lax
from jax.experimental import pallas as pl
from jax.experimental.pallas import tpu as pltpu
from jax.sharding import PartitionSpec as P

D = 1024
HEADS = 16
KV_HEADS = 8
HEAD_DIM = 64
STEP = 4
HQ = 1024
HK = 512


EPS = 1e-05
THETA = 1000000.0
NEG_BIG = -1e30
BETA_ONE = 0.9
BETA_TWO = 0.95
ADAM_EPS = 1e-08


def adam_step(weight, grad, first, second, rate, decay):
    first_new = BETA_ONE * first + (1.0 - BETA_ONE) * grad
    second_new = BETA_TWO * second + (1.0 - BETA_TWO) * grad * grad
    first_hat = first_new / (1.0 - BETA_ONE**STEP)
    second_hat = second_new / (1.0 - BETA_TWO**STEP)
    weight_new = weight - rate * (first_hat / (jnp.sqrt(second_hat) + ADAM_EPS) + decay * weight)
    return (weight_new, first_new, second_new)


BF = jnp.bfloat16
F32 = jnp.float32
MESH_ID = pl.DeviceIdType.MESH
ANY = pl.BlockSpec(memory_space=pl.ANY)
VMEM = pl.BlockSpec(memory_space=pltpu.VMEM)
DMA = pltpu.SemaphoreType.DMA
NN = (((1,), (0,)), ((), ()))
NT = (((1,), (1,)), ((), ()))
TN = (((0,), (0,)), ((), ()))
VMEM_BYTES = 121 << 19
GROUPS = HEADS // 4


def dot(a, b, dims):
    return lax.dot_general(a, b, dims, preferred_element_type=F32)


class Place:
    def __init__(self, planes, depth):
        self.planes, self.depth = planes, depth
        self.dp = lax.axis_index("dp")
        self.ctx = lax.axis_index("ctx")
        self.z = self.ctx // 2
        self.core = self.ctx % 2

    def sibling(self):
        return {"dp": self.dp, "ctx": self.z * 2 + 1 - self.core}

    def across(self, o):
        return {"dp": self.dp ^ o, "ctx": self.ctx}

    def behind(self, k):
        return lax.rem(self.z + self.depth - k, self.depth)

    def ahead(self, k):
        return lax.rem(self.z + k, self.depth)

    def along(self, z):
        return {"dp": self.dp, "ctx": z * 2 + self.core}

    def plane(self):
        return [self.across(o) for o in range(1, self.planes)]

    def line(self):
        return [self.along(self.ahead(k)) for k in range(1, self.depth)]


def near(planes):
    return [o for o in range(1, planes) if o & (o - 1) == 0]


def far(planes):
    return [o for o in range(1, planes) if o & (o - 1) != 0]


def greet(devices):
    barrier = pltpu.get_barrier_semaphore()
    for device in devices:
        pl.semaphore_signal(barrier, inc=1, device_id=device, device_id_type=MESH_ID)
    pl.semaphore_wait(barrier, len(devices))


def remote(src, dst, send, recv, device):
    return pltpu.make_async_remote_copy(
        src_ref=src, dst_ref=dst, send_sem=send, recv_sem=recv, device_id=device, device_id_type=MESH_ID
    )


def params(collective_id):
    return pltpu.CompilerParams(
        vmem_limit_bytes=VMEM_BYTES, collective_id=collective_id, has_side_effects=True
    )


class Spread:
    def __init__(self, me, g_ref, line_sems, sems, halves=True):
        self.me, self.g, self.line_sems, self.sems = me, g_ref, line_sems, sems
        self.by_halves = halves and me.planes == 4
        self.sent = []

    def push(self, src, dst, kind, o, device):
        copy = remote(src, dst, self.sems.at[kind, o], self.sems.at[kind + 1, o], device)
        copy.start()
        self.sent.append(copy)

    def mine(self, o, core):
        return self.g.at[self.me.dp ^ o, :, core]

    def line(self):
        me = self.me
        block = self.g.at[me.dp, me.z, me.core]
        for k in range(1, me.depth):
            copy = remote(
                block, block, self.line_sems.at[0, k], self.line_sems.at[1, k], me.along(me.ahead(k))
            )
            copy.start()
            self.sent.append(copy)

    def first(self):
        me = self.me
        for k in range(1, me.depth):
            block = self.g.at[me.dp, me.behind(k), me.core]
            remote(
                block, block, self.line_sems.at[0, k], self.line_sems.at[1, k], me.along(me.ahead(k))
            ).wait_recv()
        self.push(self.mine(0, me.core), self.mine(0, me.core), 2, 0, me.sibling())
        self.plane(near(me.planes))

    def plane(self, places):
        me = self.me
        for o in places:
            self.push(self.mine(0, me.core), self.mine(0, me.core), 0, o, me.across(o))

    def part(self, o, number):
        half = self.me.depth // 2
        return self.g.at[self.me.dp ^ o, pl.ds(number * half, half), self.me.core]

    def relay(self, o):
        block = self.mine(o, self.me.core)
        if self.by_halves and o == 3:
            for number in range(2):
                piece = self.part(o, number)
                kind = 4 + 2 * number
                remote(
                    piece, piece, self.sems.at[kind, o], self.sems.at[kind + 1, o], self.me.sibling()
                ).wait_recv()
        else:
            remote(block, block, self.sems.at[0, o], self.sems.at[1, o], self.me.sibling()).wait_recv()
        if self.by_halves and o < 3:
            piece = self.part(o, o - 1)
            self.push(piece, piece, 2 + 2 * o, 3, self.me.across(3 - o))
        self.push(block, block, 2, o, self.me.sibling())

    def arrive(self, o):
        block = self.mine(o, 1 - self.me.core)
        remote(block, block, self.sems.at[2, o], self.sems.at[3, o], self.me.sibling()).wait_recv()

    def finish(self):
        for copy in self.sent:
            copy.wait_send()


def spread_sems(planes, depth):
    return [DMA((2, depth)), DMA((8, planes))]


class Collect:
    def __init__(self, me, p_ref, scratch):
        self.me, self.p = me, p_ref
        self.sums, self.from_plane, self.total, self.from_z, self.cs, self.ps, self.zs = scratch

    def c_copy(self, o):
        me = self.me
        return remote(
            self.p.at[me.dp ^ o, :, 1 - me.core], self.sums.at[o], self.cs.at[0, o], self.cs.at[1, o], me.sibling()
        )

    def p_copy(self, o):
        return remote(
            self.sums.at[o], self.from_plane.at[o - 1], self.ps.at[0, o], self.ps.at[1, o], self.me.across(o)
        )

    def z_copy(self, k):
        me = self.me
        return remote(
            self.total.at[me.ahead(k)], self.from_z.at[k], self.zs.at[0, k], self.zs.at[1, k], me.along(me.ahead(k))
        )

    def first(self, o):
        self.c_copy(o).start()

    def second(self, o):
        me = self.me
        self.c_copy(o).wait_recv()
        own = self.p[me.dp ^ o, :, me.core].astype(F32)
        self.sums[o] = (own + self.sums[o].astype(F32)).astype(self.sums.dtype)
        if o > 0:
            self.p_copy(o).start()

    def third(self):
        me = self.me
        for o in range(1, me.planes):
            self.p_copy(o).wait_recv()
        for k in list(range(1, me.depth)) + [0]:
            z = me.ahead(k)
            value = self.sums[0, z].astype(F32)
            for o in range(1, me.planes):
                value = value + self.from_plane[o - 1, z].astype(F32)
            self.total[z] = value.astype(self.total.dtype)
            if k > 0:
                self.z_copy(k).start()
        return value

    def last(self, value):
        for k in range(1, self.me.depth):
            self.z_copy(k).wait_recv()
            value = value + self.from_z[k].astype(F32)
        return value

    def finish(self):
        for o in range(self.me.planes):
            self.c_copy(o).wait_send()
        for o in range(1, self.me.planes):
            self.p_copy(o).wait_send()
        for k in range(1, self.me.depth):
            self.z_copy(k).wait_send()


def collect_scratch(planes, depth, rows, columns, kind):
    return [
        pltpu.VMEM((planes, depth, rows, columns), kind),
        pltpu.VMEM((planes - 1, depth, rows, columns), kind),
        pltpu.VMEM((depth, rows, columns), kind),
        pltpu.VMEM((depth, rows, columns), kind),
        DMA((2, planes)),
        DMA((2, planes)),
        DMA((2, depth)),
    ]


COLLECT = 7


def unit_of(values, axis):
    recip = lax.rsqrt(jnp.mean(values * values, axis=axis, keepdims=True) + EPS)
    return values * recip, recip


def column_of(row, start):
    lane = lax.broadcasted_iota(jnp.int32, (HEAD_DIM, 128), 1)
    entry = lax.broadcasted_iota(jnp.int32, (HEAD_DIM, 128), 0)
    return jnp.sum(jnp.where(lane == entry + start, row, 0.0), axis=1, keepdims=True)


def turned(values, cosine, sine):
    half = HEAD_DIM // 2
    a, b = values[:half], values[half:]
    return jnp.concatenate([a * cosine - b * sine, b * cosine + a * sine], axis=0)


def paired(h, count):
    rows = slice(h // 2 * HEAD_DIM, (h // 2 + 1) * HEAD_DIM)
    return rows, slice(h % 2 * count, (h % 2 + 1) * count)


def fill_bias(bias, lower, slot):
    count = bias.shape[0]
    query = lax.broadcasted_iota(jnp.int32, (count, count), 1)
    key = lax.broadcasted_iota(jnp.int32, (count, count), 0) - slot * count
    allowed = jnp.where((key <= query) & (key >= lower), 0.0, NEG_BIG)
    bias[:, :count] = allowed
    bias[:, count:] = allowed


class Pass:
    def __init__(self, me, w_ref, sems):
        self.me, self.w, self.sems = me, w_ref, sems

    def copy(self, kind, s, down, core=None, device=None):
        me = self.me
        z = me.z + s - 1 if down else me.z - s + 1
        block = self.w.at[:, :, z * 2 + (me.core if core is None else core)]
        device = me.sibling() if device is None else device
        return remote(block, block, self.sems.at[kind, s], self.sems.at[kind + 1, s], device)

    def held(self, s, down):
        me = self.me
        return me.z + s - 1 < me.depth if down else me.z - s + 1 >= 0

    def on(self, s, down):
        me = self.me
        return self.held(s, down) & (me.z >= 1 if down else me.z + 1 < me.depth)

    def line_copy(self, s, down):
        me = self.me
        return self.copy(2 if down else 0, s, down, None, me.along(me.z - 1 if down else me.z + 1))

    def step(self, s):
        for down in (False, True):
            if s > 1:
                @pl.when(self.held(s, down))
                def _():
                    me = self.me
                    z = me.z + s - 1 if down else me.z - s + 1
                    block = self.w.at[:, :, z * 2 + me.core]
                    kind = 2 if down else 0
                    remote(
                        block, block, self.sems.at[kind, s - 1], self.sems.at[kind + 1, s - 1], me.sibling()
                    ).wait_recv()

            @pl.when(self.on(s, down))
            def _():
                self.line_copy(s, down).start()

            if s > 1 or not down:
                @pl.when(self.held(s, down))
                def _():
                    self.copy(6 if down else 4, s, down).start()

    def arrive(self):
        for s in range(1, self.me.depth + 1):
            for down in (False, True):
                if s > 1 or not down:
                    @pl.when(self.held(s, down))
                    def _():
                        self.copy(6 if down else 4, s, down, 1 - self.me.core).wait_recv()

    def finish(self):
        for s in range(1, self.me.depth + 1):
            for down in (False, True):
                @pl.when(self.on(s, down))
                def _():
                    self.line_copy(s, down).wait_send()

                if s > 1 or not down:
                    @pl.when(self.held(s, down))
                    def _():
                        self.copy(6 if down else 4, s, down).wait_send()


def fore_kernel(
    planes, depth, turns, n_gains,
    tok_ref, place_ref, gain_ref, wqkv_ref, wout_ref, wpair_ref, wdown_ref, og_ref,
    q_any, kv_any, wq_any, wkv_any, xat_any, unit_any, recip_any, wo_any, parts_any, spill_any, grads_a, grads_b, mine_any,
    gains_out, o_out, lse_out, mixed_out, gn_out, cos_ref, sin_ref, lower_ref,
    q_s, kv_all, wq_all, wkv_all, xat, unit_s, recip_s, wo_all, blocks_a, blocks_b, gains_g, xa, proj, bias, accum, sums,
    wa, wb, hns, ogs, hnt, ogt, mid, pair, send_gn, recv_gn, part_s, stage, mine,
    own_sem, keep_sem, zs, cs, ps, a2a_a, a2a_b, pass_a, pass_b, hsem, nsem, psem, ssem, stsem, og_halves, hn_halves, dsem,
    glsem, gsem, qlsem, qsem, wlsem, wsem, olsem, osem, *fold_rest,
):
    me = Place(planes, depth)
    half = turns // 2
    count = tok_ref.shape[0]
    width = D // planes
    rows = wqkv_ref.shape[0]
    halves = (blocks_a.shape[3], blocks_b.shape[3])
    full = sum(halves)
    gains = Spread(me, gains_g, glsem, gsem, False)
    queries = Spread(me, wq_all, qlsem, qsem)
    weights = Spread(me, wkv_all, wlsem, wsem)
    outputs = Spread(me, wo_all, olsem, osem)
    pass_first, pass_second = Pass(me, wa, pass_a), Pass(me, wb, pass_b)
    fold = Fold(me, grads_a, mine, fold_rest)
    kept = []

    def keep(source, into):
        copy = pltpu.make_async_copy(source, into, keep_sem.at[len(kept)])
        copy.start()
        kept.append(copy)

    here = gains_g.at[me.dp, me.z, me.core]
    here[...] = jnp.zeros((8, 128), F32)
    here[0:1, 0:n_gains] = gain_ref[...].astype(BF).astype(F32)
    wq_all[me.dp, me.z, me.core] = wqkv_ref[:, :HQ].astype(BF)
    wkv_all[me.dp, me.z, me.core] = wqkv_ref[:, HQ:].astype(BF)
    wo_all[me.dp, me.z, me.core] = wout_ref[...].astype(BF)
    for d in range(planes):
        for m in range(3):
            source = wdown_ref if m == 2 else wpair_ref
            at = d * full if m == 2 else (m * planes + d) * full
            blocks_a[d, m] = source[:, at : at + halves[0]].astype(BF)
            blocks_b[d, m] = source[:, at + halves[0] : at + full].astype(BF)
    wa[:, me.dp, me.ctx] = blocks_a[me.dp]
    wb[:, me.dp, me.ctx] = blocks_b[me.dp]
    own_og = pltpu.make_async_copy(og_ref, ogs.at[0], own_sem.at[1])
    own_og.start()
    greet(me.plane() + me.line() + [me.sibling()])
    gains.line()
    weights.line()

    def a2a_copy(part, o):
        source, into, sems = ((blocks_a, wa, a2a_a), (blocks_b, wb, a2a_b))[part]
        return remote(
            source.at[me.dp ^ o], into.at[:, me.dp, me.ctx], sems.at[0, o], sems.at[1, o], me.across(o)
        )

    def a2a_wait(part):
        into, sems = ((wa, a2a_a), (wb, a2a_b))[part]
        for o in range(1, planes):
            block = into.at[:, me.dp ^ o, me.ctx]
            remote(block, block, sems.at[0, o], sems.at[1, o], me.across(o)).wait_recv()

    for part in range(2):
        for o in range(1, planes):
            a2a_copy(part, o).start()
    unit, _ = unit_of(tok_ref[...].astype(F32), 1)
    proj[:, :D] = unit
    places = place_ref[...]
    lower_ref[...] = lax.broadcasted_iota(jnp.int32, (1, count), 1) - places
    steps = lax.broadcasted_iota(jnp.int32, (HEAD_DIM // 2, 1), 0).astype(F32)
    angles = jnp.exp(-math.log(THETA) * (2.0 * steps / HEAD_DIM)) * places.astype(F32)
    cos_ref[...] = jnp.cos(angles)
    sin_ref[...] = jnp.sin(angles)
    gains.first()
    gains.plane(far(planes))
    weights.first()
    queries.line()
    a2a_wait(0)
    pass_first.step(1)
    for o in range(1, planes):
        gains.relay(o)
    for o in range(planes):
        gains.arrive(o)
    devices = planes * depth * 2
    table = gains_g[...].reshape(devices, 8, 128)[:, 0, :].astype(BF)
    entries = devices * n_gains
    index = lax.broadcasted_iota(jnp.int32, (128, entries), 1)
    pick = jnp.where(
        index % n_gains == lax.broadcasted_iota(jnp.int32, (128, entries), 0), 1.0, 0.0
    ).astype(BF)
    spread = dot(table, pick, NN)
    owner = lax.broadcasted_iota(jnp.int32, (devices, entries), 1) // n_gains
    device = lax.broadcasted_iota(jnp.int32, (devices, entries), 0)
    gains_row = 1.0 + jnp.sum(jnp.where(owner == device, spread, 0.0), axis=0, keepdims=True)
    gains_out[...] = gains_row
    normed = (proj[:, :D] * gains_row[:, :D]).astype(BF)
    xat[...] = normed.T
    keep(xat, xat_any)
    for d in range(planes):
        xa[d] = normed[:, d * width : (d + 1) * width]

    def project(source, table, at):
        proj[:, at] = jnp.zeros((count, D), F32)
        places = [0] + near(planes) + far(planes)
        for o in places:
            if o > 0:
                source.relay(o)
            source.arrive(o)
            if o == near(planes)[-1] and planes != 4:
                source.plane(far(planes))
            proj[:, at] += dot(xa[me.dp ^ o], table[me.dp ^ o].reshape(width, D), NN)

    project(weights, wkv_all, pl.ds(HQ, 2 * HK))
    queries.first()
    outputs.line()
    tail_row = gains_row[:, 2 * D : 2 * D + 128]
    gain_q, gain_k = column_of(tail_row, 0), column_of(tail_row, HEAD_DIM)
    cosine, sine = cos_ref[...], sin_ref[...]

    def four_raw(h):
        four = proj[:, h * HEAD_DIM : (h + 4) * HEAD_DIM].T
        results, recips = [], []
        for i in range(4):
            value, recip = unit_of(four[i * HEAD_DIM : (i + 1) * HEAD_DIM], 0)
            unit_s[pl.ds((h + i) * HEAD_DIM, HEAD_DIM), :] = value
            recips.append(recip)
            results.append(turned(value * (gain_q if h < HEADS else gain_k), cosine, sine))
        recip_s[h // 4] = jnp.concatenate(recips, axis=0)
        return jnp.concatenate(results, axis=0)

    for h in range(HEADS, HEADS + KV_HEADS, 4):
        kv_all[0, :, pl.ds((h - HEADS) * HEAD_DIM, 4 * HEAD_DIM)] = four_raw(h).T.astype(BF)
    kv_all[0, :, pl.ds(HK, HK)] = proj[:, HQ + HK :].astype(BF)

    def half_copy(slots, sems, o):
        rows = pl.ds((o - 1) * (count // 2), count // 2)
        return remote(
            slots.at[o, rows], slots.at[3, rows], sems.at[0, o], sems.at[1, o], me.across(3 - o)
        )

    def z_copy(k):
        return remote(kv_all.at[2 * k - 2], kv_all.at[2 * k], zs.at[0, k], zs.at[1, k], me.along(me.ahead(1)))

    def z_sends(k):
        return (me.z + 1 < depth) & (me.z - k + 1 >= 0)

    def c_copy(i):
        return remote(
            kv_all.at[2 * i + 2 * me.core], kv_all.at[2 * i + 1], cs.at[0, i], cs.at[1, i], me.sibling()
        )

    @pl.when(z_sends(1))
    def _():
        z_copy(1).start()

    @pl.when(me.core == 0)
    def _():
        c_copy(0).start()

    project(queries, wq_all, pl.ds(0, HQ))
    outputs.first()
    for h in range(0, HEADS, 4):
        four = (four_raw(h) * HEAD_DIM ** (-0.5)).astype(BF)
        for i in range(4):
            q_s[paired(h + i, count)] = four[i * HEAD_DIM : (i + 1) * HEAD_DIM]
    keep(q_s, q_any)
    keep(unit_s, unit_any)
    keep(recip_s, recip_any)
    keep(wq_all, wq_any)
    keep(wkv_all, wkv_any)
    square = planes == 4
    if not square:
        outputs.plane(far(planes))
    shares = []
    for o in near(planes) if square else range(1, planes):
        share = remote(og_ref, ogs.at[o], ps.at[0, o], ps.at[1, o], me.across(o))
        share.start()
        shares.append(share)
    accum[...] = jnp.zeros_like(accum)
    sums[...] = jnp.zeros_like(sums)

    def visit(slot):
        fill_bias(bias, lower_ref[...], slot)

        def four_heads(t, carry):
            keys = kv_all[slot, :, pl.ds(pl.multiple_of(t * 128, 128), 128)]
            values = kv_all[slot, :, pl.ds(pl.multiple_of(HK + t * 128, 128), 128)]
            totals = []
            for u in range(2):
                key = keys[:, u * 64 : u * 64 + 64]
                value = values[:, u * 64 : u * 64 + 64]
                at = pl.ds(pl.multiple_of(t * 128 + u * 64, 64), 64)
                weight = jnp.exp(dot(key, q_s[at, :], NN) + bias[...])
                totals.append(jnp.sum(weight, axis=0, keepdims=True))
                accum[at, :] += dot(value, weight.astype(BF), TN)
            sums[t] += jnp.concatenate(totals, axis=0)
            return carry

        lax.fori_loop(0, GROUPS, four_heads, 0)

    visit(0)
    for k in range(1, half + 1):
        there = me.z - k >= 0

        @pl.when(there)
        def _():
            z_copy(k).wait_recv()

        if k < half:
            @pl.when(z_sends(k + 1))
            def _():
                z_copy(k + 1).start()

        @pl.when(there & (me.core == 1))
        def _():
            c_copy(k - 1).start()

        if k < half:
            @pl.when(there & (me.core == 0))
            def _():
                c_copy(k).start()

        @pl.when(there)
        def _():
            visit(2 * k)

    pass_first.step(2)
    for i in range(half):
        @pl.when(me.z - i - 1 + me.core >= 0)
        def _():
            c_copy(i).wait_recv()
            visit(2 * i + 1)

    pass_first.step(3)
    a2a_wait(1)
    pass_second.step(1)
    keep(kv_all, kv_any)
    for o in range(1, planes):
        outputs.relay(o)
    if square:
        for o in (1, 2):
            remote(og_ref, ogs.at[o], ps.at[0, o], ps.at[1, o], me.across(o)).wait_recv()
            half_copy(ogs, og_halves, o).start()
    for t in range(GROUPS):
        lse_out[t] = jnp.log(sums[t])
    for h in range(HEADS):
        at = paired(h, count)
        total = sums[h // 4, h // 2 % 2 : h // 2 % 2 + 1, at[1]]
        o_out[pl.ds(h * HEAD_DIM, HEAD_DIM), :] = (accum[at] / total).astype(BF)
    for o in range(planes):
        outputs.arrive(o)
    keep(wo_all, wo_any)
    mixed = tok_ref[...].astype(F32) + dot(o_out[...].T, wo_all[...].reshape(HQ, D), NN)
    mixed_out[...] = mixed
    unit, _ = unit_of(mixed, 1)
    hns[0] = (unit * gains_out[:, D : 2 * D]).astype(BF)

    def hn_copy(o):
        return remote(hns.at[0], hns.at[o], hsem.at[0, o], hsem.at[1, o], me.across(o))

    def gn_copy(o):
        return remote(send_gn.at[o - 1], recv_gn.at[o - 1], nsem.at[0, o], nsem.at[1, o], me.across(o))

    def diagonal_rows(other):
        return pl.ds((other - 1) * (count // 2), count // 2)

    def diagonal_copy(other):
        rows = diagonal_rows(other)
        return remote(
            send_gn.at[2, rows], recv_gn.at[2, rows], dsem.at[0, other], dsem.at[1, other], me.across(other)
        )

    def spill_copy(o, back):
        ends = (spill_any.at[o], proj) if back else (proj, spill_any.at[o])
        return pltpu.make_async_copy(*ends, ssem.at[0])

    def parts_copy(o):
        return pltpu.make_async_copy(part_s, parts_any.at[o], psem.at[0])

    for o in near(planes):
        hn_copy(o).start()
    for s in range(4, depth + 1):
        pass_first.step(s)
    pass_first.arrive()
    own_og.wait()

    def ffn_part(part):
        w, f = (wa, wb)[part], halves[part]

        def block(i, carry):
            o = i if part == 0 else planes - 1 - i
            if part == 0:
                if square:
                    @pl.when(o == 1)
                    def _():
                        for other in (1, 2):
                            hn_copy(other).wait_recv()
                            half_copy(hns, hn_halves, other).start()

                    @pl.when(o == 3)
                    def _():
                        for other in (1, 2):
                            half_copy(ogs, og_halves, other).wait_recv()
                            half_copy(hns, hn_halves, other).wait_recv()
                else:
                    @pl.when(o > 0)
                    def _():
                        hn_copy(o).wait_recv()
                        remote(og_ref, ogs.at[o], ps.at[0, o], ps.at[1, o], me.across(o)).wait_recv()
            else:
                spill_copy(o, True).start()

            hn, og = hns[o], ogs[o]
            at = pl.ds(pl.multiple_of(o * count, 128), count)
            if part == 0:
                hnt[:, at] = hn.T
                ogt[:, at] = og.T
            w_gate, w_up, w_down = (w[m].reshape(D, f) for m in range(3))
            gate = dot(hn, w_gate, NN)
            upper = dot(hn, w_up, NN)
            sigma = 1.0 / (1.0 + jnp.exp(-gate))
            active = gate * sigma
            middle = (active * upper).astype(BF)
            gmid = dot(og, w_down, NN)
            ggate = (gmid * upper * sigma * (1.0 + gate * (1.0 - sigma))).astype(BF)
            gupper = (gmid * active).astype(BF)
            mid[at, :f] = middle
            pair[0, at, :f] = ggate
            pair[1, at, :f] = gupper
            gn = dot(ggate, w_gate, NT) + dot(gupper, w_up, NT)
            out = dot(middle, w_down, NT)
            if part == 0:
                @pl.when(o > 0)
                def _():
                    spill_copy(o - 1, False).wait()

                proj[:, :D] = gn
                proj[:, D:] = out
                spill_copy(o, False).start()

                @pl.when(o == 0)
                def _():
                    if not square:
                        for other in far(planes):
                            hn_copy(other).start()
                    pass_second.step(2)

                @pl.when(o == planes // 2)
                def _():
                    pass_second.step(3)
            else:
                spill_copy(o, True).wait()
                gn = gn + proj[:, :D]
                out = out + proj[:, D:]

                @pl.when(i > 0)
                def _():
                    parts_copy(o + 1).wait()

                if square:
                    proj[:, :D] = gn

                    @pl.when(o == 3)
                    def _():
                        send_gn[2] = gn.astype(BF)
                        for other in (1, 2):
                            diagonal_copy(other).start()

                    for other in (1, 2):
                        @pl.when(o == other)
                        def _():
                            rows = diagonal_rows(3 - other)
                            diagonal_copy(3 - other).wait_recv()
                            proj[rows, :D] += recv_gn[2, rows].astype(F32)
                            send_gn[other - 1] = proj[:, :D].astype(BF)
                            gn_copy(other).start()
                else:
                    @pl.when(o > 0)
                    def _():
                        send_gn[o - 1] = gn.astype(BF)
                        gn_copy(o).start()

                @pl.when(o == 0)
                def _():
                    gn_out[...] = gn

                @pl.when(i == 0)
                def _():
                    fold.second()
                    fold.step(0)

                @pl.when(i == planes // 2)
                def _():
                    fold.step(1)

                part_s[...] = out.astype(BF)
                parts_copy(o).start()
            return carry

        lax.fori_loop(0, planes, block, 0)
        if part == 0:
            spill_copy(planes - 1, False).wait()
        else:
            parts_copy(0).wait()
        strip = D // planes
        grads = (grads_a, grads_b)[part]

        def out_copy(m, d):
            return pltpu.make_async_copy(stage.at[m, :, :, :f], grads.at[:, d, m], stsem.at[m])

        def weight_grads(d, carry):
            left = pl.ds(pl.multiple_of(d * strip, 128), strip)
            for m in (2, 0, 1):
                @pl.when(d > 0)
                def _():
                    out_copy(m, d - 1).wait()

                if m == 2:
                    total = dot(ogt[left, :], mid[:, :f], NN)
                else:
                    total = dot(hnt[left, :], pair[m, :, :f], NN)
                stage[m, :, :, :f] = total.astype(BF).reshape(depth * 2, rows, f)
                out_copy(m, d).start()
            return carry

        lax.fori_loop(0, planes, weight_grads, 0)
        for m in range(3):
            out_copy(m, planes - 1).wait()

    ffn_part(0)
    fold.first()
    for s in range(4, depth + 1):
        pass_second.step(s)
    pass_second.arrive()
    ffn_part(1)
    total = gn_out[...]
    for o in (1, 2) if square else range(1, planes):
        gn_copy(o).wait_recv()
        total = total + recv_gn[o - 1].astype(F32)
    gn_out[...] = total
    fold.settle(EARLY - 1)
    keep(mine, mine_any)
    pass_first.finish()
    pass_second.finish()
    fold.finish(True, range(EARLY))
    for o in (1, 2) if square else range(1, planes):
        gn_copy(o).wait_send()
        hn_copy(o).wait_send()
        if square:
            diagonal_copy(o).wait_send()
            half_copy(hns, hn_halves, o).wait_send()
            half_copy(ogs, og_halves, o).wait_send()

    for i in range(half):
        @pl.when(me.z - i - me.core >= 0)
        def _():
            c_copy(i).wait_send()

    for k in range(1, half + 1):
        @pl.when(z_sends(k))
        def _():
            z_copy(k).wait_send()

    for o in range(1, planes):
        a2a_copy(0, o).wait_send()
        a2a_copy(1, o).wait_send()
    for share in shares:
        share.wait_send()
    gains.finish()
    queries.finish()
    weights.finish()
    outputs.finish()
    for copy in kept:
        copy.wait()


def fore(tokens, places, gains, w_qkv, w_output, w_gate_up, w_down, cotangent, n_gains, planes, depth, turns, collective_id):
    half = turns // 2
    count = tokens.shape[0]
    rows = w_qkv.shape[0]
    first, second = split(w_down.shape[1] // planes)
    devices = planes * depth * 2
    everyone = (planes, depth, 2, rows)
    shapes = [
        ((HK, 2 * count), BF),
        ((turns + 1, count, 2 * HK), BF),
        (everyone + (HQ,), BF),
        (everyone + (2 * HK,), BF),
        ((D, count), BF),
        ((HQ + HK, count), F32),
        (((HEADS + KV_HEADS) // 4, 4, count), F32),
        (everyone + (D,), BF),
        ((planes, count, D), BF),
        ((planes, count, 2 * D), F32),
        ((depth * 2, planes, 3, rows, first), BF),
        ((depth * 2, planes, 3, rows, second), BF),
        ((depth, planes, 3, rows, first), BF),
        ((1, devices * n_gains), F32),
        ((HQ, count), BF),
        ((GROUPS, 2, 2 * count), F32),
        ((count, D), F32),
        ((count, D), F32),
        ((HEAD_DIM // 2, count), F32),
        ((HEAD_DIM // 2, count), F32),
        ((1, count), jnp.int32),
    ]
    flops = 18 * planes * count * D * (first + second)
    return pl.pallas_call(
        functools.partial(fore_kernel, planes, depth, turns, n_gains),
        out_shape=tuple(jax.ShapeDtypeStruct(s, k) for s, k in shapes),
        in_specs=[VMEM] * 7 + [ANY],
        out_specs=(ANY,) * 13 + (VMEM,) * 8,
        scratch_shapes=[pltpu.VMEM(*shape) for shape in shapes[:8]]
        + [
            pltpu.VMEM((planes, 3, rows, first), BF),
            pltpu.VMEM((planes, 3, rows, second), BF),
            pltpu.VMEM((planes, depth, 2, 8, 128), F32),
            pltpu.VMEM((planes, count, D // planes), BF),
            pltpu.VMEM((count, 2 * HQ), F32),
            pltpu.VMEM((count, 2 * count), F32),
            pltpu.VMEM((HK, 2 * count), F32),
            pltpu.VMEM((GROUPS, 2, 2 * count), F32),
            pltpu.VMEM((3, planes, depth * 2, rows, first), BF),
            pltpu.VMEM((3, planes, depth * 2, rows, second), BF),
            pltpu.VMEM((planes, count, D), BF),
            pltpu.VMEM((planes, count, D), BF),
            pltpu.VMEM((D, planes * count), BF),
            pltpu.VMEM((D, planes * count), BF),
            pltpu.VMEM((planes * count, max(first, second)), BF),
            pltpu.VMEM((2, planes * count, max(first, second)), BF),
            pltpu.VMEM((planes - 1, count, D), BF),
            pltpu.VMEM((planes - 1, count, D), BF),
            pltpu.VMEM((count, D), BF),
            pltpu.VMEM((3, depth * 2, rows, max(first, second)), BF),
            pltpu.VMEM((depth, planes, 3, rows, first), BF),
            DMA((2,)),
            DMA((9,)),
            DMA((2, half + 1)),
            DMA((2, half)),
            DMA((2, planes)),
            DMA((2, planes)),
            DMA((2, planes)),
            DMA((8, depth + 1)),
            DMA((8, depth + 1)),
            DMA((2, planes)),
            DMA((2, planes)),
            DMA((1,)),
            DMA((1,)),
            DMA((3,)),
            DMA((2, 3)),
            DMA((2, 3)),
            DMA((2, 3)),
        ]
        + spread_sems(planes, depth) * 4
        + fold_scratch(planes, depth, rows, first),
        compiler_params=params(collective_id),
        cost_estimate=pl.CostEstimate(flops=flops, bytes_accessed=30 << 20, transcendentals=0),
    )(tokens, places, gains, w_qkv, w_output, w_gate_up, w_down, cotangent)


class Fold:
    def __init__(self, me, g_any, mine, scratch):
        self.me, self.g, self.mine = me, g_any, mine
        self.other, self.from_line, self.sems = scratch

    def own_copy(self, z):
        return pltpu.make_async_copy(
            self.g.at[z * 2 + self.me.core], self.mine.at[z], self.sems.at[0, z]
        )

    def core_copy(self, z):
        me = self.me
        return remote(
            self.g.at[z * 2 + 1 - me.core], self.other.at[z], self.sems.at[1, z], self.sems.at[2, z], me.sibling()
        )

    def first(self):
        for z in range(self.me.depth):
            self.core_copy(z).start()
            self.own_copy(z).start()

    def add(self, total, term):
        def plane(d, carry):
            total[d] = (total[d].astype(F32) + term[d].astype(F32)).astype(BF)
            return carry

        lax.fori_loop(0, self.me.planes, plane, 0)

    def second(self):
        for z in range(self.me.depth):
            self.own_copy(z).wait()
            self.core_copy(z).wait_recv()
            self.add(self.mine.at[z], self.other.at[z])

    def target(self, z, k, down):
        return k - (self.me.depth - 1) + z if down else self.me.depth - 1 - k + z

    def sends(self, k, down):
        me = self.me
        return self.target(me.z, k, down) >= 0 if down else me.z <= k

    def slot(self, t, k, down):
        return self.me.depth if k == self.me.depth - 2 and not down else t

    def copy(self, k, down):
        me = self.me
        t = self.target(me.z, k, down)
        kind = 5 if down else 3
        return remote(
            self.mine.at[t], self.from_line.at[self.slot(t, k, down)], self.sems.at[kind, k], self.sems.at[kind + 1, k],
            me.along(me.z - 1 if down else me.z + 1),
        )

    def send(self, k):
        for down in (False, True):
            @pl.when(self.sends(k, down))
            def _():
                self.copy(k, down).start()

    def settle(self, k):
        me = self.me
        for down in (False, True):
            t = self.target(me.z + 1 if down else me.z - 1, k, down)
            comes = (me.z < me.depth - 1) & (t >= 0) if down else (me.z > 0) & (me.z - 1 <= k)

            @pl.when(comes)
            def _():
                block = self.from_line.at[self.slot(t, k, down)]
                kind = 5 if down else 3
                remote(
                    block, block, self.sems.at[kind, k], self.sems.at[kind + 1, k], me.sibling()
                ).wait_recv()
                self.add(self.mine.at[t], block)

    def step(self, k):
        if k > 0:
            self.settle(k - 1)
        self.send(k)

    def finish(self, first, steps):
        if first:
            for z in range(self.me.depth):
                self.core_copy(z).wait_send()
        for k in steps:
            for down in (False, True):
                @pl.when(self.sends(k, down))
                def _():
                    self.copy(k, down).wait_send()


class Swap:
    def __init__(self, me, ready, landed, sems):
        self.me, self.ready, self.landed, self.sems = me, ready, landed, sems

    def copy(self, o):
        me = self.me
        return remote(
            self.ready.at[me.dp ^ o], self.landed.at[me.dp], self.sems.at[0, o], self.sems.at[1, o], me.across(o)
        )

    def start(self, value):
        self.ready[...] = value
        for o in range(1, self.me.planes):
            self.copy(o).start()

    def last(self):
        me = self.me
        self.landed[me.dp] = self.ready[me.dp]
        for o in range(1, me.planes):
            block = self.landed.at[me.dp ^ o]
            remote(block, block, self.sems.at[0, o], self.sems.at[1, o], me.across(o)).wait_recv()

    def finish(self):
        for o in range(1, self.me.planes):
            self.copy(o).wait_send()


FOLD = 3


def fold_scratch(planes, depth, rows, full):
    block = (planes, 3, rows, full)
    return [
        pltpu.VMEM((depth,) + block, BF),
        pltpu.VMEM((depth + 1,) + block, BF),
        DMA((7, depth)),
    ]


def split(full):
    first = (full // 128 + 1) // 2 * 128
    return (first, full - first)


EARLY = 2


def home_kernel(
    planes, depth, turns, n_gains,
    gn_ref, mixed_ref, og_ref, gains_ref, o_ref, lse_ref, q_ref, lower_ref, cos_ref, sin_ref, tok_ref,
    wo_any, kv_any, parts_any, grads_b, mine_a, unit_any, recip_any, wq_any, wkv_any, xat_any,
    block_out, grad_out, shard_out, shard_qkv, gains_out, pair_out, down_out,
    wo, kv, unit_s, recip_s, wq_all, wkv_all, xat, own_part, gq, grad_kv, gmixed_s,
    bias, gob, delta, gkv, from_core, from_z, from_plane, partial, gproj, partial_q, partial_kv, gains_p, *rest,
):
    me = Place(planes, depth)
    collect = Collect(me, partial, rest[:COLLECT])
    collect_q = Collect(me, partial_q, rest[COLLECT : 2 * COLLECT])
    collect_kv = Collect(me, partial_kv, rest[2 * COLLECT : 3 * COLLECT])
    small = Collect(me, gains_p, rest[3 * COLLECT : 4 * COLLECT])
    rest = rest[4 * COLLECT :]
    mine_first, ready_first, landed_first, swap_first, mine_second, ready_second, landed_second, swap_second = rest[:8]
    folds = (
        Fold(me, None, mine_first, (None,) + rest[8:10]),
        Fold(me, grads_b, mine_second, rest[10 : 10 + FOLD]),
    )
    swaps = (
        Swap(me, ready_first, landed_first, swap_first),
        Swap(me, ready_second, landed_second, swap_second),
    )
    cs, zs, ps, load = rest[10 + FOLD :]
    half = turns // 2
    count = gn_ref.shape[0]
    sources = [wo_any, kv_any, unit_any, recip_any, xat_any, parts_any.at[0], wq_any, wkv_any, mine_a]
    places = [wo, kv, unit_s, recip_s, xat, own_part, wq_all, wkv_all, mine_first]
    loads = [pltpu.make_async_copy(a, b, load.at[i]) for i, (a, b) in enumerate(zip(sources, places))]
    for copy in loads[8:] + loads[:8]:
        copy.start()
    greet(me.plane() + me.line() + [me.sibling()])
    loads[8].wait()
    folds[0].send(EARLY)
    folds[1].first()

    def c_copy(i):
        return remote(gkv.at[2 * i + 1], from_core.at[i], cs.at[0, i], cs.at[1, i], me.sibling())

    def z_copy(k):
        return remote(gkv.at[2 * k], from_z.at[k - 1], zs.at[0, k], zs.at[1, k], me.along(me.behind(1)))

    def join(k):
        if k < half:
            @pl.when((me.z - k >= 0) & (me.z + 1 < depth))
            def _():
                z_copy(k + 1).wait_recv()
                gkv[2 * k] = (gkv[2 * k].astype(F32) + from_z[k].astype(F32)).astype(BF)

        @pl.when(me.z - k >= 0)
        def _():
            z_copy(k).start()

    def p_copy(o):
        return remote(parts_any.at[o], from_plane.at[o - 1], ps.at[0, o], ps.at[1, o], me.across(o))

    for o in range(1, planes):
        p_copy(o).start()
    unit, recip = unit_of(mixed_ref[...], 1)
    grad = gn_ref[...]
    scaled = grad * gains_ref[:, D : 2 * D]
    inner = jnp.mean(scaled * unit, axis=1, keepdims=True)
    gmixed = og_ref[...].astype(F32) + recip * (scaled - unit * inner)
    gmixed_s[...] = gmixed
    dgf = jnp.sum(grad * unit, axis=0, keepdims=True)
    gmixed_b = gmixed.astype(BF)
    loads[0].wait()
    gob_all = dot(wo[...].reshape(HQ, D), gmixed_b, NT).astype(BF)
    for h in range(HEADS):
        gob_h = gob_all[h * HEAD_DIM : (h + 1) * HEAD_DIM]
        gob[paired(h, count)] = gob_h
        out = o_ref[pl.ds(h * HEAD_DIM, HEAD_DIM), :].astype(F32)
        delta[h // 4, h // 2 % 2 : h // 2 % 2 + 1, paired(h, count)[1]] = jnp.sum(
            gob_h.astype(F32) * out, axis=0, keepdims=True
        )
    half_rows = D // planes
    order = list(range(1, planes)) + [0]
    gq[...] = jnp.zeros_like(gq)
    loads[1].wait()

    def visit(slot):
        fill_bias(bias, lower_ref[...], slot)

        def four_heads(t, carry):
            key_at = pl.ds(pl.multiple_of(t * 128, 128), 128)
            value_at = pl.ds(pl.multiple_of(HK + t * 128, 128), 128)
            keys, values = kv[slot, :, key_at], kv[slot, :, value_at]
            lse_t, delta_t = lse_ref[t], delta[t]
            grad_keys, grad_values = [], []
            for u in range(2):
                key = keys[:, u * 64 : u * 64 + 64]
                value = values[:, u * 64 : u * 64 + 64]
                at = pl.ds(pl.multiple_of(t * 128 + u * 64, 64), 64)
                query, gob_h = q_ref[at, :], gob[at, :]
                probs = jnp.exp(dot(key, query, NN) + bias[...] - lse_t[u : u + 1, :])
                grad_value = dot(probs.astype(BF), gob_h, NT)
                grad_scores = (probs * (dot(value, gob_h, NN) - delta_t[u : u + 1, :])).astype(BF)
                grad_key = dot(grad_scores, query, NT)
                gq[at, :] += dot(key, grad_scores, TN)
                grad_keys.append(grad_key)
                grad_values.append(grad_value)
            gkv[slot, :, key_at] = jnp.concatenate(grad_keys, axis=1).astype(BF)
            gkv[slot, :, value_at] = jnp.concatenate(grad_values, axis=1).astype(BF)
            return carry

        lax.fori_loop(0, GROUPS, four_heads, 0)

    for i in range(half - 1, -1, -1):
        @pl.when(me.z - i - 1 + me.core >= 0)
        def _():
            visit(2 * i + 1)
            c_copy(i).start()

    for k in range(half, 0, -1):
        @pl.when(me.z - k >= 0)
        def _():
            visit(2 * k)

            @pl.when(me.core == 0)
            def _():
                if k < half:
                    c_copy(k).wait_recv()
                    gkv[2 * k] = (gkv[2 * k].astype(F32) + from_core[k].astype(F32)).astype(BF)

            @pl.when(me.core == 1)
            def _():
                c_copy(k - 1).wait_recv()
                gkv[2 * k] = (gkv[2 * k].astype(F32) + from_core[k - 1].astype(F32)).astype(BF)

        if k == half:
            join(k)

    folds[1].second()
    folds[1].step(0)
    visit(0)
    for k in range(half - 1, 0, -1):
        join(k)
    for o in order:
        d = me.dp ^ o
        rows = o_ref[pl.ds(pl.multiple_of(d * half_rows, 128), half_rows), :]
        partial[d] = dot(rows, gmixed_b, NN).astype(BF).reshape(partial.shape[1:])
        collect.first(o)
    for i in (2, 3, 4):
        loads[i].wait()
    tail_row = gains_ref[:, 2 * D : 2 * D + 128]
    gain_q, gain_k = column_of(tail_row, 0), column_of(tail_row, HEAD_DIM)
    cosine, sine = cos_ref[...], -sin_ref[...]
    gained = [0.0, 0.0]

    def four_grads(h):
        kind = 0 if h < HEADS else 1
        if kind == 0:
            heads = [gq[paired(h + i, count)] * HEAD_DIM ** (-0.5) for i in range(4)]
        else:
            four = grad_kv[:, pl.ds((h - HEADS) * HEAD_DIM, 4 * HEAD_DIM)].T
            heads = [four[i * HEAD_DIM : (i + 1) * HEAD_DIM] for i in range(4)]
        recips = recip_s[h // 4]
        results = []
        for i in range(4):
            unit = unit_s[pl.ds((h + i) * HEAD_DIM, HEAD_DIM), :]
            grad = turned(heads[i], cosine, sine)
            scaled = grad * (gain_k if kind else gain_q)
            inner = jnp.mean(scaled * unit, axis=0, keepdims=True)
            results.append(recips[i : i + 1, :] * (scaled - unit * inner))
            gained[kind] = gained[kind] + grad * unit
        gproj[:, pl.ds(h * HEAD_DIM, 4 * HEAD_DIM)] = jnp.concatenate(results, axis=0).T.astype(BF)

    def gather_grads(columns, table, collected):
        for o in order:
            d = me.dp ^ o
            rows = xat[pl.ds(pl.multiple_of(d * half_rows, 128), half_rows), :]
            table[d] = dot(rows, gproj[:, columns], NN).astype(BF).reshape(table.shape[1:])
            collected.first(o)
            if o != order[0]:
                collected.second(order[order.index(o) - 1])
        collected.second(0)

    for o in order:
        collect.second(o)
    for h in range(0, HEADS, 4):
        four_grads(h)
    gather_grads(pl.ds(0, HQ), partial_q, collect_q)
    folds[1].step(1)
    for k in range(EARLY + 1, depth - 1):
        folds[0].step(k)
    grad_kv[...] = gkv[0].astype(F32)

    @pl.when(me.core == 0)
    def _():
        c_copy(0).wait_recv()
        grad_kv[...] += from_core[0].astype(F32)

    @pl.when(me.z + 1 < depth)
    def _():
        z_copy(1).wait_recv()
        grad_kv[...] += from_z[0].astype(F32)

    for h in range(HEADS, HEADS + KV_HEADS, 4):
        four_grads(h)
    gproj[:, pl.ds(HQ + HK, HK)] = grad_kv[:, pl.ds(HK, HK)].astype(BF)
    gather_grads(pl.ds(HQ, 2 * HK), partial_kv, collect_kv)
    value_o = collect.third()
    value_q = collect_q.third()
    for i in (6, 7):
        loads[i].wait()
    grad = dot(gproj[:, :HQ], wq_all[...].reshape(D, HQ), NT)
    grad = grad + dot(gproj[:, HQ:], wkv_all[...].reshape(D, 2 * HK), NT)
    unit, recip = unit_of(tok_ref[...].astype(F32), 1)
    scaled = grad * gains_ref[:, :D]
    inner = jnp.mean(scaled * unit, axis=1, keepdims=True)
    grad_out[...] = gmixed_s[...] + recip * (scaled - unit * inner)
    dga = jnp.sum(grad * unit, axis=0, keepdims=True)
    for k in range(2, depth - 1):
        folds[1].step(k)
    folds[0].settle(depth - 2)
    swaps[0].start(mine_first[me.z])
    lane = lax.broadcasted_iota(jnp.int32, (HEAD_DIM, 128), 1)
    entry = lax.broadcasted_iota(jnp.int32, (HEAD_DIM, 128), 0)
    sums = [jnp.sum(g, axis=1, keepdims=True) for g in gained]
    last = jnp.sum(
        jnp.where(lane == entry, sums[0], 0.0) + jnp.where(lane == entry + HEAD_DIM, sums[1], 0.0),
        axis=0,
        keepdims=True,
    )
    whole = jnp.concatenate([dga, dgf, last], axis=1)
    devices = planes * depth * 2
    entries = devices * n_gains
    index = lax.broadcasted_iota(jnp.int32, (devices, entries), 1)
    device = lax.broadcasted_iota(jnp.int32, (devices, entries), 0)
    apart = jnp.where(index // n_gains == device, whole, 0.0)
    pick = jnp.where(
        lax.broadcasted_iota(jnp.int32, (128, entries), 1) % n_gains
        == lax.broadcasted_iota(jnp.int32, (128, entries), 0),
        1.0,
        0.0,
    )
    table = lax.dot_general(
        apart, pick, NT, preferred_element_type=F32, precision=lax.Precision.HIGHEST
    )
    gains_p[...] = jnp.broadcast_to(table[:, None, :], (devices, 8, 128)).reshape(gains_p.shape)
    for o in order:
        small.first(o)
    for o in order:
        small.second(o)
    value_kv = collect_kv.third()
    little = small.third()
    total = mixed_ref[...]
    loads[5].wait()
    total = total + own_part[...].astype(F32)
    for o in range(1, planes):
        p_copy(o).wait_recv()
        total = total + from_plane[o - 1].astype(F32)
    block_out[...] = total.astype(BF)
    folds[1].settle(depth - 2)
    swaps[1].start(mine_second[me.z])
    shard_out[...] = collect.last(value_o)
    shard_qkv[:, :HQ] = collect_q.last(value_q)
    shard_qkv[:, HQ:] = collect_kv.last(value_kv)
    gains_out[...] = small.last(little)
    start = 0
    full = landed_first.shape[3] + landed_second.shape[3]
    for swap in swaps:
        swap.last()
        f = swap.landed.shape[3]
        for d in range(planes):
            for m in range(2):
                at = (m * planes + d) * full + start
                pair_out[:, at : at + f] = swap.landed[d, m]
            at = d * full + start
            down_out[:, at : at + f] = swap.landed[d, 2]
        start = f

    for o in range(1, planes):
        p_copy(o).wait_send()
    for i in range(half):
        @pl.when(me.z - i - 1 + me.core >= 0)
        def _():
            c_copy(i).wait_send()
    for k in range(1, half + 1):
        @pl.when(me.z - k >= 0)
        def _():
            z_copy(k).wait_send()
    collect.finish()
    collect_q.finish()
    collect_kv.finish()
    small.finish()
    folds[0].finish(False, range(EARLY, depth - 1))
    folds[1].finish(True, range(depth - 1))
    for swap in swaps:
        swap.finish()


def home(first, second, n_gains, planes, depth, turns, collective_id):
    half = turns // 2
    count = first[0].shape[0]
    wo_all, kv_all, _, grads, mine, unit, recip, wq_all, wkv_all, xat = second
    rows = wo_all.shape[3]
    parts = (mine.shape[4], grads.shape[4])
    full = sum(parts)
    return pl.pallas_call(
        functools.partial(home_kernel, planes, depth, turns, n_gains),
        out_shape=(
            jax.ShapeDtypeStruct((count, D), BF),
            jax.ShapeDtypeStruct((count, D), F32),
            jax.ShapeDtypeStruct((rows, D), F32),
            jax.ShapeDtypeStruct((rows, 2 * HQ), F32),
            jax.ShapeDtypeStruct((8, 128), F32),
            jax.ShapeDtypeStruct((rows, 2 * planes * full), BF),
            jax.ShapeDtypeStruct((rows, planes * full), BF),
        ),
        in_specs=[VMEM] * len(first) + [ANY] * len(second),
        out_specs=(VMEM,) * 7,
        scratch_shapes=[pltpu.VMEM(a.shape, a.dtype) for a in (wo_all, kv_all, unit, recip, wq_all, wkv_all, xat)]
        + [
            pltpu.VMEM((count, D), BF),
            pltpu.VMEM((HK, 2 * count), F32),
            pltpu.VMEM((count, 2 * HK), F32),
            pltpu.VMEM((count, D), F32),
            pltpu.VMEM((count, 2 * count), F32),
            pltpu.VMEM((HK, 2 * count), BF),
            pltpu.VMEM((GROUPS, 2, 2 * count), F32),
            pltpu.VMEM((turns + 1, count, 2 * HK), BF),
            pltpu.VMEM((half, count, 2 * HK), BF),
            pltpu.VMEM((half, count, 2 * HK), BF),
            pltpu.VMEM((planes - 1, count, D), BF),
            pltpu.VMEM((planes, depth, 2, rows, D), BF),
            pltpu.VMEM((count, 2 * HQ), BF),
            pltpu.VMEM((planes, depth, 2, rows, HQ), BF),
            pltpu.VMEM((planes, depth, 2, rows, 2 * HK), BF),
            pltpu.VMEM((planes, depth, 2, 8, 128), F32),
        ]
        + collect_scratch(planes, depth, rows, D, BF)
        + collect_scratch(planes, depth, rows, HQ, BF)
        + collect_scratch(planes, depth, rows, 2 * HK, BF)
        + collect_scratch(planes, depth, 8, 128, F32)
        + [
            scratch
            for part in parts
            for scratch in (
                pltpu.VMEM((depth, planes, 3, rows, part), BF),
                pltpu.VMEM((planes, 3, rows, part), BF),
                pltpu.VMEM((planes, 3, rows, part), BF),
                DMA((2, planes)),
            )
        ]
        + fold_scratch(planes, depth, rows, parts[0])[1:]
        + fold_scratch(planes, depth, rows, parts[1])
        + [DMA((2, half)), DMA((2, half + 1)), DMA((2, planes)), DMA((9,))],
        compiler_params=params(collective_id),
        cost_estimate=pl.CostEstimate(flops=60 << 30, bytes_accessed=8 << 20, transcendentals=0),
    )(*first, *second)


def adam_kernel(rates, *refs):
    n = len(rates)
    for i, rate in enumerate(rates):
        weight, grad, first, second = (r[...] for r in refs[4 * i : 4 * i + 4])
        grad = grad.astype(F32)
        outs = refs[4 * (n + i) : 4 * (n + i) + 4]
        for out, value in zip(outs, (grad,) + adam_step(weight, grad, first, second, rate, 0.1)):
            out[...] = value


def adam(groups, rates):
    rows = groups[0][0].shape[0]
    block = 16 if rows % 16 == 0 else rows
    specs, shapes = [], []
    for group in groups:
        columns = group[0].shape[1]
        specs += [pl.BlockSpec((block, columns), lambda i: (i, 0))] * 4
        shapes += [jax.ShapeDtypeStruct((rows, columns), F32)] * 4
    outs = pl.pallas_call(
        functools.partial(adam_kernel, rates),
        out_shape=tuple(shapes),
        grid=(rows // block,),
        in_specs=specs,
        out_specs=tuple(specs),
        compiler_params=pltpu.CompilerParams(vmem_limit_bytes=VMEM_BYTES),
    )(*[array for group in groups for array in group])
    return [outs[4 * i : 4 * i + 4] for i in range(len(groups))]


def per_device(
    tokens_in,
    positions,
    out_grad,
    w_qkv,
    w_output,
    w_gate_up,
    w_down,
    norm_gains,
    first_qkv,
    first_output,
    first_gate_up,
    first_down,
    first_gains,
    second_qkv,
    second_output,
    second_gate_up,
    second_down,
    second_gains,
):
    planes, ctxs = lax.axis_size("dp"), lax.axis_size("ctx")
    depth = ctxs // 2
    turns = ctxs // 2
    rows = w_qkv.shape[0]
    n_gains = norm_gains.shape[0]
    count = tokens_in.shape[0] * tokens_in.shape[1]
    tokens = tokens_in.reshape(count, D)
    places = positions.reshape(1, count)
    cotangent = out_grad.reshape(count, D)

    (
        query, kv_all, wq_all, wkv_all, xat, unit_heads, recip_heads, output_all, parts, _, _, grads, mine,
        gains_row, attn_t, lse, mixed, grad_normed, cosine, sine, lower,
    ) = fore(
        tokens, places, norm_gains[None, :], w_qkv, w_output, w_gate_up, w_down, cotangent,
        n_gains, planes, depth, turns, 0,
    )
    block_out, input_grad, shard_output, shard_qkv, gains_tile, pair_b, down_b = home(
        (grad_normed, mixed, cotangent, gains_row, attn_t, lse, query, lower, cosine, sine, tokens),
        (output_all, kv_all, parts, grads, mine, unit_heads, recip_heads, wq_all, wkv_all, xat),
        n_gains, planes, depth, turns, 1,
    )
    shard_gains = gains_tile[0, :n_gains]
    (
        (shard_qkv, new_qkv, new_first_qkv, new_second_qkv),
        (shard_output, new_output, new_first_output, new_second_output),
        (shard_gate_up, new_gate_up, new_first_gate_up, new_second_gate_up),
        (shard_down, new_down, new_first_down, new_second_down),
    ) = adam(
        (
            (w_qkv, shard_qkv, first_qkv, second_qkv),
            (w_output, shard_output, first_output, second_output),
            (w_gate_up, pair_b, first_gate_up, second_gate_up),
            (w_down, down_b, first_down, second_down),
        ),
        (0.02, 0.2, 0.02, 0.02),
    )
    new_gains, new_first_gains, new_second_gains = adam_step(
        norm_gains, shard_gains, first_gains, second_gains, 0.1, 0.0
    )
    return (
        block_out.reshape(tokens_in.shape),
        input_grad.reshape(tokens_in.shape),
        shard_qkv,
        shard_output,
        shard_gate_up,
        shard_down,
        shard_gains,
        new_qkv,
        new_output,
        new_gate_up,
        new_down,
        new_gains,
        new_first_qkv,
        new_first_output,
        new_first_gate_up,
        new_first_down,
        new_first_gains,
        new_second_qkv,
        new_second_output,
        new_second_gate_up,
        new_second_down,
        new_second_gains,
    )


def solution(mesh):
    in_specs = (
        P("dp", "ctx", None),
        P("dp", "ctx"),
        P("dp", "ctx", None),
        P(("dp", "ctx"), None),
        P(("dp", "ctx"), None),
        P(("dp", "ctx"), None),
        P(("dp", "ctx"), None),
        P(("dp", "ctx")),
        P(("dp", "ctx"), None),
        P(("dp", "ctx"), None),
        P(("dp", "ctx"), None),
        P(("dp", "ctx"), None),
        P(("dp", "ctx")),
        P(("dp", "ctx"), None),
        P(("dp", "ctx"), None),
        P(("dp", "ctx"), None),
        P(("dp", "ctx"), None),
        P(("dp", "ctx")),
    )
    out_specs = (
        P("dp", "ctx", None),
        P("dp", "ctx", None),
        P(("dp", "ctx"), None),
        P(("dp", "ctx"), None),
        P(("dp", "ctx"), None),
        P(("dp", "ctx"), None),
        P(("dp", "ctx")),
        P(("dp", "ctx"), None),
        P(("dp", "ctx"), None),
        P(("dp", "ctx"), None),
        P(("dp", "ctx"), None),
        P(("dp", "ctx")),
        P(("dp", "ctx"), None),
        P(("dp", "ctx"), None),
        P(("dp", "ctx"), None),
        P(("dp", "ctx"), None),
        P(("dp", "ctx")),
        P(("dp", "ctx"), None),
        P(("dp", "ctx"), None),
        P(("dp", "ctx"), None),
        P(("dp", "ctx"), None),
        P(("dp", "ctx")),
    )
    return jax.shard_map(
        per_device, mesh=mesh, in_specs=in_specs, out_specs=out_specs, check_vma=False
    )
```

```python
import functools
import math

import jax
import jax.numpy as jnp
from jax import lax
from jax.experimental import pallas as pl
from jax.experimental.pallas import tpu as pltpu
from jax.sharding import PartitionSpec as P

D = 1024
HEADS = 16
KV_HEADS = 8
HEAD_DIM = 64
STEP = 4
HQ = 1024
HK = 512


EPS = 1e-05
THETA = 1000000.0
NEG_BIG = -1e30
BETA_ONE = 0.9
BETA_TWO = 0.95
ADAM_EPS = 1e-08


def adam_step(weight, grad, first, second, rate, decay):
    first_new = BETA_ONE * first + (1.0 - BETA_ONE) * grad
    second_new = BETA_TWO * second + (1.0 - BETA_TWO) * grad * grad
    first_hat = first_new / (1.0 - BETA_ONE**STEP)
    second_hat = second_new / (1.0 - BETA_TWO**STEP)
    weight_new = weight - rate * (first_hat / (jnp.sqrt(second_hat) + ADAM_EPS) + decay * weight)
    return (weight_new, first_new, second_new)


BF = jnp.bfloat16
F32 = jnp.float32
MESH_ID = pl.DeviceIdType.MESH
ANY = pl.BlockSpec(memory_space=pl.ANY)
VMEM = pl.BlockSpec(memory_space=pltpu.VMEM)
DMA = pltpu.SemaphoreType.DMA
NN = (((1,), (0,)), ((), ()))
NT = (((1,), (1,)), ((), ()))
TN = (((0,), (0,)), ((), ()))
VMEM_BYTES = 121 << 19
GROUPS = HEADS // 4


def dot(a, b, dims):
    return lax.dot_general(a, b, dims, preferred_element_type=F32)


class Place:
    def __init__(self, planes, depth):
        self.planes, self.depth = planes, depth
        self.dp = lax.axis_index("dp")
        self.ctx = lax.axis_index("ctx")
        self.z = self.ctx // 2
        self.core = self.ctx % 2

    def sibling(self):
        return {"dp": self.dp, "ctx": self.z * 2 + 1 - self.core}

    def across(self, o):
        return {"dp": self.dp ^ o, "ctx": self.ctx}

    def behind(self, k):
        return lax.rem(self.z + self.depth - k, self.depth)

    def ahead(self, k):
        return lax.rem(self.z + k, self.depth)

    def along(self, z):
        return {"dp": self.dp, "ctx": z * 2 + self.core}

    def plane(self):
        return [self.across(o) for o in range(1, self.planes)]

    def line(self):
        return [self.along(self.ahead(k)) for k in range(1, self.depth)]


def near(planes):
    return [o for o in range(1, planes) if o & (o - 1) == 0]


def far(planes):
    return [o for o in range(1, planes) if o & (o - 1) != 0]


def greet(devices):
    barrier = pltpu.get_barrier_semaphore()
    for device in devices:
        pl.semaphore_signal(barrier, inc=1, device_id=device, device_id_type=MESH_ID)
    pl.semaphore_wait(barrier, len(devices))


def remote(src, dst, send, recv, device):
    return pltpu.make_async_remote_copy(
        src_ref=src, dst_ref=dst, send_sem=send, recv_sem=recv, device_id=device, device_id_type=MESH_ID
    )


def params(collective_id):
    return pltpu.CompilerParams(
        vmem_limit_bytes=VMEM_BYTES, collective_id=collective_id, has_side_effects=True
    )


class Spread:
    def __init__(self, me, g_ref, line_sems, sems, halves=True):
        self.me, self.g, self.line_sems, self.sems = me, g_ref, line_sems, sems
        self.by_halves = halves and me.planes == 4
        self.sent = []

    def push(self, src, dst, kind, o, device):
        copy = remote(src, dst, self.sems.at[kind, o], self.sems.at[kind + 1, o], device)
        copy.start()
        self.sent.append(copy)

    def mine(self, o, core):
        return self.g.at[self.me.dp ^ o, :, core]

    def line(self):
        me = self.me
        block = self.g.at[me.dp, me.z, me.core]
        for k in range(1, me.depth):
            copy = remote(
                block, block, self.line_sems.at[0, k], self.line_sems.at[1, k], me.along(me.ahead(k))
            )
            copy.start()
            self.sent.append(copy)

    def first(self):
        me = self.me
        for k in range(1, me.depth):
            block = self.g.at[me.dp, me.behind(k), me.core]
            remote(
                block, block, self.line_sems.at[0, k], self.line_sems.at[1, k], me.along(me.ahead(k))
            ).wait_recv()
        self.push(self.mine(0, me.core), self.mine(0, me.core), 2, 0, me.sibling())
        self.plane(near(me.planes))

    def plane(self, places):
        me = self.me
        for o in places:
            self.push(self.mine(0, me.core), self.mine(0, me.core), 0, o, me.across(o))

    def part(self, o, number):
        half = self.me.depth // 2
        return self.g.at[self.me.dp ^ o, pl.ds(number * half, half), self.me.core]

    def relay(self, o):
        block = self.mine(o, self.me.core)
        if self.by_halves and o == 3:
            for number in range(2):
                piece = self.part(o, number)
                kind = 4 + 2 * number
                remote(
                    piece, piece, self.sems.at[kind, o], self.sems.at[kind + 1, o], self.me.sibling()
                ).wait_recv()
        else:
            remote(block, block, self.sems.at[0, o], self.sems.at[1, o], self.me.sibling()).wait_recv()
        if self.by_halves and o < 3:
            piece = self.part(o, o - 1)
            self.push(piece, piece, 2 + 2 * o, 3, self.me.across(3 - o))
        self.push(block, block, 2, o, self.me.sibling())

    def arrive(self, o):
        block = self.mine(o, 1 - self.me.core)
        remote(block, block, self.sems.at[2, o], self.sems.at[3, o], self.me.sibling()).wait_recv()

    def finish(self):
        for copy in self.sent:
            copy.wait_send()


def spread_sems(planes, depth):
    return [DMA((2, depth)), DMA((8, planes))]


class Collect:
    def __init__(self, me, p_ref, scratch):
        self.me, self.p = me, p_ref
        self.sums, self.from_plane, self.total, self.from_z, self.cs, self.ps, self.zs = scratch

    def c_copy(self, o):
        me = self.me
        return remote(
            self.p.at[me.dp ^ o, :, 1 - me.core], self.sums.at[o], self.cs.at[0, o], self.cs.at[1, o], me.sibling()
        )

    def p_copy(self, o):
        return remote(
            self.sums.at[o], self.from_plane.at[o - 1], self.ps.at[0, o], self.ps.at[1, o], self.me.across(o)
        )

    def z_copy(self, k):
        me = self.me
        return remote(
            self.total.at[me.ahead(k)], self.from_z.at[k], self.zs.at[0, k], self.zs.at[1, k], me.along(me.ahead(k))
        )

    def first(self, o):
        self.c_copy(o).start()

    def second(self, o):
        me = self.me
        self.c_copy(o).wait_recv()
        own = self.p[me.dp ^ o, :, me.core].astype(F32)
        self.sums[o] = (own + self.sums[o].astype(F32)).astype(self.sums.dtype)
        if o > 0:
            self.p_copy(o).start()

    def third(self):
        me = self.me
        for o in range(1, me.planes):
            self.p_copy(o).wait_recv()
        for k in list(range(1, me.depth)) + [0]:
            z = me.ahead(k)
            value = self.sums[0, z].astype(F32)
            for o in range(1, me.planes):
                value = value + self.from_plane[o - 1, z].astype(F32)
            self.total[z] = value.astype(self.total.dtype)
            if k > 0:
                self.z_copy(k).start()
        return value

    def last(self, value):
        for k in range(1, self.me.depth):
            self.z_copy(k).wait_recv()
            value = value + self.from_z[k].astype(F32)
        return value

    def finish(self):
        for o in range(self.me.planes):
            self.c_copy(o).wait_send()
        for o in range(1, self.me.planes):
            self.p_copy(o).wait_send()
        for k in range(1, self.me.depth):
            self.z_copy(k).wait_send()


def collect_scratch(planes, depth, rows, columns, kind):
    return [
        pltpu.VMEM((planes, depth, rows, columns), kind),
        pltpu.VMEM((planes - 1, depth, rows, columns), kind),
        pltpu.VMEM((depth, rows, columns), kind),
        pltpu.VMEM((depth, rows, columns), kind),
        DMA((2, planes)),
        DMA((2, planes)),
        DMA((2, depth)),
    ]


COLLECT = 7


def unit_of(values, axis):
    recip = lax.rsqrt(jnp.mean(values * values, axis=axis, keepdims=True) + EPS)
    return values * recip, recip


def column_of(row, start):
    lane = lax.broadcasted_iota(jnp.int32, (HEAD_DIM, 128), 1)
    entry = lax.broadcasted_iota(jnp.int32, (HEAD_DIM, 128), 0)
    return jnp.sum(jnp.where(lane == entry + start, row, 0.0), axis=1, keepdims=True)


def turned(values, cosine, sine):
    half = HEAD_DIM // 2
    a, b = values[:half], values[half:]
    return jnp.concatenate([a * cosine - b * sine, b * cosine + a * sine], axis=0)


def paired(h, count):
    rows = slice(h // 2 * HEAD_DIM, (h // 2 + 1) * HEAD_DIM)
    return rows, slice(h % 2 * count, (h % 2 + 1) * count)


def fill_bias(bias, lower, slot):
    count = bias.shape[0]
    query = lax.broadcasted_iota(jnp.int32, (count, count), 1)
    key = lax.broadcasted_iota(jnp.int32, (count, count), 0) - slot * count
    allowed = jnp.where((key <= query) & (key >= lower), 0.0, NEG_BIG)
    bias[:, :count] = allowed
    bias[:, count:] = allowed


class Pass:
    def __init__(self, me, w_ref, sems):
        self.me, self.w, self.sems = me, w_ref, sems

    def copy(self, kind, s, down, core=None, device=None):
        me = self.me
        z = me.z + s - 1 if down else me.z - s + 1
        block = self.w.at[:, :, z * 2 + (me.core if core is None else core)]
        device = me.sibling() if device is None else device
        return remote(block, block, self.sems.at[kind, s], self.sems.at[kind + 1, s], device)

    def held(self, s, down):
        me = self.me
        return me.z + s - 1 < me.depth if down else me.z - s + 1 >= 0

    def on(self, s, down):
        me = self.me
        return self.held(s, down) & (me.z >= 1 if down else me.z + 1 < me.depth)

    def line_copy(self, s, down):
        me = self.me
        return self.copy(2 if down else 0, s, down, None, me.along(me.z - 1 if down else me.z + 1))

    def step(self, s):
        for down in (False, True):
            if s > 1:
                @pl.when(self.held(s, down))
                def _():
                    me = self.me
                    z = me.z + s - 1 if down else me.z - s + 1
                    block = self.w.at[:, :, z * 2 + me.core]
                    kind = 2 if down else 0
                    remote(
                        block, block, self.sems.at[kind, s - 1], self.sems.at[kind + 1, s - 1], me.sibling()
                    ).wait_recv()

            @pl.when(self.on(s, down))
            def _():
                self.line_copy(s, down).start()

            if s > 1 or not down:
                @pl.when(self.held(s, down))
                def _():
                    self.copy(6 if down else 4, s, down).start()

    def arrive(self):
        for s in range(1, self.me.depth + 1):
            for down in (False, True):
                if s > 1 or not down:
                    @pl.when(self.held(s, down))
                    def _():
                        self.copy(6 if down else 4, s, down, 1 - self.me.core).wait_recv()

    def finish(self):
        for s in range(1, self.me.depth + 1):
            for down in (False, True):
                @pl.when(self.on(s, down))
                def _():
                    self.line_copy(s, down).wait_send()

                if s > 1 or not down:
                    @pl.when(self.held(s, down))
                    def _():
                        self.copy(6 if down else 4, s, down).wait_send()


def fore_kernel(
    planes, depth, turns, n_gains,
    tok_ref, place_ref, gain_ref, wqkv_ref, wout_ref, wpair_ref, wdown_ref, og_ref,
    q_any, kv_any, wq_any, wkv_any, xat_any, unit_any, recip_any, wo_any, parts_any, spill_any, grads_a, grads_b, mine_any,
    gains_out, o_out, lse_out, mixed_out, gn_out, cos_ref, sin_ref, lower_ref,
    q_s, kv_all, wq_all, wkv_all, xat, unit_s, recip_s, wo_all, blocks_a, blocks_b, gains_g, xa, proj, bias, accum, sums,
    wa, wb, hns, ogs, hnt, ogt, mid, pair, send_gn, recv_gn, part_s, stage, mine,
    own_sem, keep_sem, zs, cs, ps, a2a_a, a2a_b, pass_a, pass_b, hsem, nsem, psem, ssem, stsem, og_halves, hn_halves, dsem,
    glsem, gsem, qlsem, qsem, wlsem, wsem, olsem, osem, *fold_rest,
):
    me = Place(planes, depth)
    half = turns // 2
    count = tok_ref.shape[0]
    width = D // planes
    rows = wqkv_ref.shape[0]
    halves = (blocks_a.shape[3], blocks_b.shape[3])
    full = sum(halves)
    gains = Spread(me, gains_g, glsem, gsem, False)
    queries = Spread(me, wq_all, qlsem, qsem)
    weights = Spread(me, wkv_all, wlsem, wsem)
    outputs = Spread(me, wo_all, olsem, osem)
    pass_first, pass_second = Pass(me, wa, pass_a), Pass(me, wb, pass_b)
    fold = Fold(me, grads_a, mine, fold_rest)
    kept = []

    def keep(source, into):
        copy = pltpu.make_async_copy(source, into, keep_sem.at[len(kept)])
        copy.start()
        kept.append(copy)

    here = gains_g.at[me.dp, me.z, me.core]
    here[...] = jnp.zeros((8, 128), F32)
    here[0:1, 0:n_gains] = gain_ref[...].astype(BF).astype(F32)
    wq_all[me.dp, me.z, me.core] = wqkv_ref[:, :HQ].astype(BF)
    wkv_all[me.dp, me.z, me.core] = wqkv_ref[:, HQ:].astype(BF)
    wo_all[me.dp, me.z, me.core] = wout_ref[...].astype(BF)
    for d in range(planes):
        for m in range(3):
            source = wdown_ref if m == 2 else wpair_ref
            at = d * full if m == 2 else (m * planes + d) * full
            blocks_a[d, m] = source[:, at : at + halves[0]].astype(BF)
            blocks_b[d, m] = source[:, at + halves[0] : at + full].astype(BF)
    wa[:, me.dp, me.ctx] = blocks_a[me.dp]
    wb[:, me.dp, me.ctx] = blocks_b[me.dp]
    own_og = pltpu.make_async_copy(og_ref, ogs.at[0], own_sem.at[1])
    own_og.start()
    greet(me.plane() + me.line() + [me.sibling()])
    gains.line()
    weights.line()

    def a2a_copy(part, o):
        source, into, sems = ((blocks_a, wa, a2a_a), (blocks_b, wb, a2a_b))[part]
        return remote(
            source.at[me.dp ^ o], into.at[:, me.dp, me.ctx], sems.at[0, o], sems.at[1, o], me.across(o)
        )

    def a2a_wait(part):
        into, sems = ((wa, a2a_a), (wb, a2a_b))[part]
        for o in range(1, planes):
            block = into.at[:, me.dp ^ o, me.ctx]
            remote(block, block, sems.at[0, o], sems.at[1, o], me.across(o)).wait_recv()

    for part in range(2):
        for o in range(1, planes):
            a2a_copy(part, o).start()
    unit, _ = unit_of(tok_ref[...].astype(F32), 1)
    proj[:, :D] = unit
    places = place_ref[...]
    lower_ref[...] = lax.broadcasted_iota(jnp.int32, (1, count), 1) - places
    steps = lax.broadcasted_iota(jnp.int32, (HEAD_DIM // 2, 1), 0).astype(F32)
    angles = jnp.exp(-math.log(THETA) * (2.0 * steps / HEAD_DIM)) * places.astype(F32)
    cos_ref[...] = jnp.cos(angles)
    sin_ref[...] = jnp.sin(angles)
    gains.first()
    gains.plane(far(planes))
    weights.first()
    queries.line()
    a2a_wait(0)
    pass_first.step(1)
    for o in range(1, planes):
        gains.relay(o)
    for o in range(planes):
        gains.arrive(o)
    devices = planes * depth * 2
    table = gains_g[...].reshape(devices, 8, 128)[:, 0, :].astype(BF)
    entries = devices * n_gains
    index = lax.broadcasted_iota(jnp.int32, (128, entries), 1)
    pick = jnp.where(
        index % n_gains == lax.broadcasted_iota(jnp.int32, (128, entries), 0), 1.0, 0.0
    ).astype(BF)
    spread = dot(table, pick, NN)
    owner = lax.broadcasted_iota(jnp.int32, (devices, entries), 1) // n_gains
    device = lax.broadcasted_iota(jnp.int32, (devices, entries), 0)
    gains_row = 1.0 + jnp.sum(jnp.where(owner == device, spread, 0.0), axis=0, keepdims=True)
    gains_out[...] = gains_row
    normed = (proj[:, :D] * gains_row[:, :D]).astype(BF)
    xat[...] = normed.T
    keep(xat, xat_any)
    for d in range(planes):
        xa[d] = normed[:, d * width : (d + 1) * width]

    def project(source, table, at):
        proj[:, at] = jnp.zeros((count, D), F32)
        places = [0] + near(planes) + far(planes)
        for o in places:
            if o > 0:
                source.relay(o)
            source.arrive(o)
            if o == near(planes)[-1] and planes != 4:
                source.plane(far(planes))
            proj[:, at] += dot(xa[me.dp ^ o], table[me.dp ^ o].reshape(width, D), NN)

    project(weights, wkv_all, pl.ds(HQ, 2 * HK))
    queries.first()
    outputs.line()
    tail_row = gains_row[:, 2 * D : 2 * D + 128]
    gain_q, gain_k = column_of(tail_row, 0), column_of(tail_row, HEAD_DIM)
    cosine, sine = cos_ref[...], sin_ref[...]

    def four_raw(h):
        four = proj[:, h * HEAD_DIM : (h + 4) * HEAD_DIM].T
        results, recips = [], []
        for i in range(4):
            value, recip = unit_of(four[i * HEAD_DIM : (i + 1) * HEAD_DIM], 0)
            unit_s[pl.ds((h + i) * HEAD_DIM, HEAD_DIM), :] = value
            recips.append(recip)
            results.append(turned(value * (gain_q if h < HEADS else gain_k), cosine, sine))
        recip_s[h // 4] = jnp.concatenate(recips, axis=0)
        return jnp.concatenate(results, axis=0)

    for h in range(HEADS, HEADS + KV_HEADS, 4):
        kv_all[0, :, pl.ds((h - HEADS) * HEAD_DIM, 4 * HEAD_DIM)] = four_raw(h).T.astype(BF)
    kv_all[0, :, pl.ds(HK, HK)] = proj[:, HQ + HK :].astype(BF)

    def half_copy(slots, sems, o):
        rows = pl.ds((o - 1) * (count // 2), count // 2)
        return remote(
            slots.at[o, rows], slots.at[3, rows], sems.at[0, o], sems.at[1, o], me.across(3 - o)
        )

    def z_copy(k):
        return remote(kv_all.at[2 * k - 2], kv_all.at[2 * k], zs.at[0, k], zs.at[1, k], me.along(me.ahead(1)))

    def z_sends(k):
        return (me.z + 1 < depth) & (me.z - k + 1 >= 0)

    def c_copy(i):
        return remote(
            kv_all.at[2 * i + 2 * me.core], kv_all.at[2 * i + 1], cs.at[0, i], cs.at[1, i], me.sibling()
        )

    @pl.when(z_sends(1))
    def _():
        z_copy(1).start()

    @pl.when(me.core == 0)
    def _():
        c_copy(0).start()

    project(queries, wq_all, pl.ds(0, HQ))
    outputs.first()
    for h in range(0, HEADS, 4):
        four = (four_raw(h) * HEAD_DIM ** (-0.5)).astype(BF)
        for i in range(4):
            q_s[paired(h + i, count)] = four[i * HEAD_DIM : (i + 1) * HEAD_DIM]
    keep(q_s, q_any)
    keep(unit_s, unit_any)
    keep(recip_s, recip_any)
    keep(wq_all, wq_any)
    keep(wkv_all, wkv_any)
    square = planes == 4
    if not square:
        outputs.plane(far(planes))
    shares = []
    for o in near(planes) if square else range(1, planes):
        share = remote(og_ref, ogs.at[o], ps.at[0, o], ps.at[1, o], me.across(o))
        share.start()
        shares.append(share)
    accum[...] = jnp.zeros_like(accum)
    sums[...] = jnp.zeros_like(sums)

    def visit(slot):
        fill_bias(bias, lower_ref[...], slot)

        def four_heads(t, carry):
            keys = kv_all[slot, :, pl.ds(pl.multiple_of(t * 128, 128), 128)]
            values = kv_all[slot, :, pl.ds(pl.multiple_of(HK + t * 128, 128), 128)]
            totals = []
            for u in range(2):
                key = keys[:, u * 64 : u * 64 + 64]
                value = values[:, u * 64 : u * 64 + 64]
                at = pl.ds(pl.multiple_of(t * 128 + u * 64, 64), 64)
                weight = jnp.exp(dot(key, q_s[at, :], NN) + bias[...])
                totals.append(jnp.sum(weight, axis=0, keepdims=True))
                accum[at, :] += dot(value, weight.astype(BF), TN)
            sums[t] += jnp.concatenate(totals, axis=0)
            return carry

        lax.fori_loop(0, GROUPS, four_heads, 0)

    visit(0)
    for k in range(1, half + 1):
        there = me.z - k >= 0

        @pl.when(there)
        def _():
            z_copy(k).wait_recv()

        if k < half:
            @pl.when(z_sends(k + 1))
            def _():
                z_copy(k + 1).start()

        @pl.when(there & (me.core == 1))
        def _():
            c_copy(k - 1).start()

        if k < half:
            @pl.when(there & (me.core == 0))
            def _():
                c_copy(k).start()

        @pl.when(there)
        def _():
            visit(2 * k)

    pass_first.step(2)
    for i in range(half):
        @pl.when(me.z - i - 1 + me.core >= 0)
        def _():
            c_copy(i).wait_recv()
            visit(2 * i + 1)

    pass_first.step(3)
    a2a_wait(1)
    pass_second.step(1)
    keep(kv_all, kv_any)
    for o in range(1, planes):
        outputs.relay(o)
    if square:
        for o in (1, 2):
            remote(og_ref, ogs.at[o], ps.at[0, o], ps.at[1, o], me.across(o)).wait_recv()
            half_copy(ogs, og_halves, o).start()
    for t in range(GROUPS):
        lse_out[t] = jnp.log(sums[t])
    for h in range(HEADS):
        at = paired(h, count)
        total = sums[h // 4, h // 2 % 2 : h // 2 % 2 + 1, at[1]]
        o_out[pl.ds(h * HEAD_DIM, HEAD_DIM), :] = (accum[at] / total).astype(BF)
    for o in range(planes):
        outputs.arrive(o)
    keep(wo_all, wo_any)
    mixed = tok_ref[...].astype(F32) + dot(o_out[...].T, wo_all[...].reshape(HQ, D), NN)
    mixed_out[...] = mixed
    unit, _ = unit_of(mixed, 1)
    hns[0] = (unit * gains_out[:, D : 2 * D]).astype(BF)

    def hn_copy(o):
        return remote(hns.at[0], hns.at[o], hsem.at[0, o], hsem.at[1, o], me.across(o))

    def gn_copy(o):
        return remote(send_gn.at[o - 1], recv_gn.at[o - 1], nsem.at[0, o], nsem.at[1, o], me.across(o))

    def diagonal_rows(other):
        return pl.ds((other - 1) * (count // 2), count // 2)

    def diagonal_copy(other):
        rows = diagonal_rows(other)
        return remote(
            send_gn.at[2, rows], recv_gn.at[2, rows], dsem.at[0, other], dsem.at[1, other], me.across(other)
        )

    def spill_copy(o, back):
        ends = (spill_any.at[o], proj) if back else (proj, spill_any.at[o])
        return pltpu.make_async_copy(*ends, ssem.at[0])

    def parts_copy(o):
        return pltpu.make_async_copy(part_s, parts_any.at[o], psem.at[0])

    for o in near(planes):
        hn_copy(o).start()
    for s in range(4, depth + 1):
        pass_first.step(s)
    pass_first.arrive()
    own_og.wait()

    def ffn_part(part):
        w, f = (wa, wb)[part], halves[part]

        def block(i, carry):
            o = i if part == 0 else planes - 1 - i
            if part == 0:
                if square:
                    @pl.when(o == 1)
                    def _():
                        for other in (1, 2):
                            hn_copy(other).wait_recv()
                            half_copy(hns, hn_halves, other).start()

                    @pl.when(o == 3)
                    def _():
                        for other in (1, 2):
                            half_copy(ogs, og_halves, other).wait_recv()
                            half_copy(hns, hn_halves, other).wait_recv()
                else:
                    @pl.when(o > 0)
                    def _():
                        hn_copy(o).wait_recv()
                        remote(og_ref, ogs.at[o], ps.at[0, o], ps.at[1, o], me.across(o)).wait_recv()
            else:
                spill_copy(o, True).start()

            hn, og = hns[o], ogs[o]
            at = pl.ds(pl.multiple_of(o * count, 128), count)
            if part == 0:
                hnt[:, at] = hn.T
                ogt[:, at] = og.T
            w_gate, w_up, w_down = (w[m].reshape(D, f) for m in range(3))
            gate = dot(hn, w_gate, NN)
            upper = dot(hn, w_up, NN)
            sigma = 1.0 / (1.0 + jnp.exp(-gate))
            active = gate * sigma
            middle = (active * upper).astype(BF)
            gmid = dot(og, w_down, NN)
            ggate = (gmid * upper * sigma * (1.0 + gate * (1.0 - sigma))).astype(BF)
            gupper = (gmid * active).astype(BF)
            mid[at, :f] = middle
            pair[0, at, :f] = ggate
            pair[1, at, :f] = gupper
            gn = dot(ggate, w_gate, NT) + dot(gupper, w_up, NT)
            out = dot(middle, w_down, NT)
            if part == 0:
                @pl.when(o > 0)
                def _():
                    spill_copy(o - 1, False).wait()

                proj[:, :D] = gn
                proj[:, D:] = out
                spill_copy(o, False).start()

                @pl.when(o == 0)
                def _():
                    if not square:
                        for other in far(planes):
                            hn_copy(other).start()
                    pass_second.step(2)

                @pl.when(o == planes // 2)
                def _():
                    pass_second.step(3)
            else:
                spill_copy(o, True).wait()
                gn = gn + proj[:, :D]
                out = out + proj[:, D:]

                @pl.when(i > 0)
                def _():
                    parts_copy(o + 1).wait()

                if square:
                    proj[:, :D] = gn

                    @pl.when(o == 3)
                    def _():
                        send_gn[2] = gn.astype(BF)
                        for other in (1, 2):
                            diagonal_copy(other).start()

                    for other in (1, 2):
                        @pl.when(o == other)
                        def _():
                            rows = diagonal_rows(3 - other)
                            diagonal_copy(3 - other).wait_recv()
                            proj[rows, :D] += recv_gn[2, rows].astype(F32)
                            send_gn[other - 1] = proj[:, :D].astype(BF)
                            gn_copy(other).start()
                else:
                    @pl.when(o > 0)
                    def _():
                        send_gn[o - 1] = gn.astype(BF)
                        gn_copy(o).start()

                @pl.when(o == 0)
                def _():
                    gn_out[...] = gn

                @pl.when(i == 0)
                def _():
                    fold.second()
                    fold.step(0)

                @pl.when(i == planes // 2)
                def _():
                    fold.step(1)

                part_s[...] = out.astype(BF)
                parts_copy(o).start()
            return carry

        lax.fori_loop(0, planes, block, 0)
        if part == 0:
            spill_copy(planes - 1, False).wait()
        else:
            parts_copy(0).wait()
        strip = D // planes
        grads = (grads_a, grads_b)[part]

        def out_copy(m, d):
            return pltpu.make_async_copy(stage.at[m, :, :, :f], grads.at[:, d, m], stsem.at[m])

        def weight_grads(d, carry):
            left = pl.ds(pl.multiple_of(d * strip, 128), strip)
            for m in (2, 0, 1):
                @pl.when(d > 0)
                def _():
                    out_copy(m, d - 1).wait()

                if m == 2:
                    total = dot(ogt[left, :], mid[:, :f], NN)
                else:
                    total = dot(hnt[left, :], pair[m, :, :f], NN)
                stage[m, :, :, :f] = total.astype(BF).reshape(depth * 2, rows, f)
                out_copy(m, d).start()
            return carry

        lax.fori_loop(0, planes, weight_grads, 0)
        for m in range(3):
            out_copy(m, planes - 1).wait()

    ffn_part(0)
    fold.first()
    for s in range(4, depth + 1):
        pass_second.step(s)
    pass_second.arrive()
    ffn_part(1)
    for k in range(2, EARLY):
        fold.step(k)
    total = gn_out[...]
    for o in (1, 2) if square else range(1, planes):
        gn_copy(o).wait_recv()
        total = total + recv_gn[o - 1].astype(F32)
    gn_out[...] = total
    fold.settle(EARLY - 1)
    keep(mine, mine_any)
    pass_first.finish()
    pass_second.finish()
    fold.finish(True, range(EARLY))
    for o in (1, 2) if square else range(1, planes):
        gn_copy(o).wait_send()
        hn_copy(o).wait_send()
        if square:
            diagonal_copy(o).wait_send()
            half_copy(hns, hn_halves, o).wait_send()
            half_copy(ogs, og_halves, o).wait_send()

    for i in range(half):
        @pl.when(me.z - i - me.core >= 0)
        def _():
            c_copy(i).wait_send()

    for k in range(1, half + 1):
        @pl.when(z_sends(k))
        def _():
            z_copy(k).wait_send()

    for o in range(1, planes):
        a2a_copy(0, o).wait_send()
        a2a_copy(1, o).wait_send()
    for share in shares:
        share.wait_send()
    gains.finish()
    queries.finish()
    weights.finish()
    outputs.finish()
    for copy in kept:
        copy.wait()


def fore(tokens, places, gains, w_qkv, w_output, w_gate_up, w_down, cotangent, n_gains, planes, depth, turns, collective_id):
    half = turns // 2
    count = tokens.shape[0]
    rows = w_qkv.shape[0]
    first, second = split(w_down.shape[1] // planes)
    devices = planes * depth * 2
    everyone = (planes, depth, 2, rows)
    shapes = [
        ((HK, 2 * count), BF),
        ((turns + 1, count, 2 * HK), BF),
        (everyone + (HQ,), BF),
        (everyone + (2 * HK,), BF),
        ((D, count), BF),
        ((HQ + HK, count), F32),
        (((HEADS + KV_HEADS) // 4, 4, count), F32),
        (everyone + (D,), BF),
        ((planes, count, D), BF),
        ((planes, count, 2 * D), F32),
        ((depth * 2, planes, 3, rows, first), BF),
        ((depth * 2, planes, 3, rows, second), BF),
        ((depth, planes, 3, rows, first), BF),
        ((1, devices * n_gains), F32),
        ((HQ, count), BF),
        ((GROUPS, 2, 2 * count), F32),
        ((count, D), F32),
        ((count, D), F32),
        ((HEAD_DIM // 2, count), F32),
        ((HEAD_DIM // 2, count), F32),
        ((1, count), jnp.int32),
    ]
    flops = 18 * planes * count * D * (first + second)
    return pl.pallas_call(
        functools.partial(fore_kernel, planes, depth, turns, n_gains),
        out_shape=tuple(jax.ShapeDtypeStruct(s, k) for s, k in shapes),
        in_specs=[VMEM] * 7 + [ANY],
        out_specs=(ANY,) * 13 + (VMEM,) * 8,
        scratch_shapes=[pltpu.VMEM(*shape) for shape in shapes[:8]]
        + [
            pltpu.VMEM((planes, 3, rows, first), BF),
            pltpu.VMEM((planes, 3, rows, second), BF),
            pltpu.VMEM((planes, depth, 2, 8, 128), F32),
            pltpu.VMEM((planes, count, D // planes), BF),
            pltpu.VMEM((count, 2 * HQ), F32),
            pltpu.VMEM((count, 2 * count), F32),
            pltpu.VMEM((HK, 2 * count), F32),
            pltpu.VMEM((GROUPS, 2, 2 * count), F32),
            pltpu.VMEM((3, planes, depth * 2, rows, first), BF),
            pltpu.VMEM((3, planes, depth * 2, rows, second), BF),
            pltpu.VMEM((planes, count, D), BF),
            pltpu.VMEM((planes, count, D), BF),
            pltpu.VMEM((D, planes * count), BF),
            pltpu.VMEM((D, planes * count), BF),
            pltpu.VMEM((planes * count, max(first, second)), BF),
            pltpu.VMEM((2, planes * count, max(first, second)), BF),
            pltpu.VMEM((planes - 1, count, D), BF),
            pltpu.VMEM((planes - 1, count, D), BF),
            pltpu.VMEM((count, D), BF),
            pltpu.VMEM((3, depth * 2, rows, max(first, second)), BF),
            pltpu.VMEM((depth, planes, 3, rows, first), BF),
            DMA((2,)),
            DMA((9,)),
            DMA((2, half + 1)),
            DMA((2, half)),
            DMA((2, planes)),
            DMA((2, planes)),
            DMA((2, planes)),
            DMA((8, depth + 1)),
            DMA((8, depth + 1)),
            DMA((2, planes)),
            DMA((2, planes)),
            DMA((1,)),
            DMA((1,)),
            DMA((3,)),
            DMA((2, 3)),
            DMA((2, 3)),
            DMA((2, 3)),
        ]
        + spread_sems(planes, depth) * 4
        + fold_scratch(planes, depth, rows, first),
        compiler_params=params(collective_id),
        cost_estimate=pl.CostEstimate(flops=flops, bytes_accessed=30 << 20, transcendentals=0),
    )(tokens, places, gains, w_qkv, w_output, w_gate_up, w_down, cotangent)


class Fold:
    def __init__(self, me, g_any, mine, scratch):
        self.me, self.g, self.mine = me, g_any, mine
        self.other, self.from_line, self.sems = scratch

    def own_copy(self, z):
        return pltpu.make_async_copy(
            self.g.at[z * 2 + self.me.core], self.mine.at[z], self.sems.at[0, z]
        )

    def core_copy(self, z):
        me = self.me
        return remote(
            self.g.at[z * 2 + 1 - me.core], self.other.at[z], self.sems.at[1, z], self.sems.at[2, z], me.sibling()
        )

    def first(self):
        for z in range(self.me.depth):
            self.core_copy(z).start()
            self.own_copy(z).start()

    def add(self, total, term):
        def plane(d, carry):
            total[d] = (total[d].astype(F32) + term[d].astype(F32)).astype(BF)
            return carry

        lax.fori_loop(0, self.me.planes, plane, 0)

    def second(self):
        for z in range(self.me.depth):
            self.own_copy(z).wait()
            self.core_copy(z).wait_recv()
            self.add(self.mine.at[z], self.other.at[z])

    def target(self, z, k, down):
        return k - (self.me.depth - 1) + z if down else self.me.depth - 1 - k + z

    def sends(self, k, down):
        me = self.me
        return self.target(me.z, k, down) >= 0 if down else me.z <= k

    def slot(self, t, k, down):
        return self.me.depth if k == self.me.depth - 2 and not down else t

    def copy(self, k, down):
        me = self.me
        t = self.target(me.z, k, down)
        kind = 5 if down else 3
        return remote(
            self.mine.at[t], self.from_line.at[self.slot(t, k, down)], self.sems.at[kind, k], self.sems.at[kind + 1, k],
            me.along(me.z - 1 if down else me.z + 1),
        )

    def send(self, k):
        for down in (False, True):
            @pl.when(self.sends(k, down))
            def _():
                self.copy(k, down).start()

    def settle(self, k):
        me = self.me
        for down in (False, True):
            t = self.target(me.z + 1 if down else me.z - 1, k, down)
            comes = (me.z < me.depth - 1) & (t >= 0) if down else (me.z > 0) & (me.z - 1 <= k)

            @pl.when(comes)
            def _():
                block = self.from_line.at[self.slot(t, k, down)]
                kind = 5 if down else 3
                remote(
                    block, block, self.sems.at[kind, k], self.sems.at[kind + 1, k], me.sibling()
                ).wait_recv()
                self.add(self.mine.at[t], block)

    def step(self, k):
        if k > 0:
            self.settle(k - 1)
        self.send(k)

    def finish(self, first, steps):
        if first:
            for z in range(self.me.depth):
                self.core_copy(z).wait_send()
        for k in steps:
            for down in (False, True):
                @pl.when(self.sends(k, down))
                def _():
                    self.copy(k, down).wait_send()


class Swap:
    def __init__(self, me, ready, landed, sems):
        self.me, self.ready, self.landed, self.sems = me, ready, landed, sems

    def copy(self, o):
        me = self.me
        return remote(
            self.ready.at[me.dp ^ o], self.landed.at[me.dp], self.sems.at[0, o], self.sems.at[1, o], me.across(o)
        )

    def start(self, value):
        self.ready[...] = value
        for o in range(1, self.me.planes):
            self.copy(o).start()

    def last(self):
        me = self.me
        self.landed[me.dp] = self.ready[me.dp]
        for o in range(1, me.planes):
            block = self.landed.at[me.dp ^ o]
            remote(block, block, self.sems.at[0, o], self.sems.at[1, o], me.across(o)).wait_recv()

    def finish(self):
        for o in range(1, self.me.planes):
            self.copy(o).wait_send()


FOLD = 3


def fold_scratch(planes, depth, rows, full):
    block = (planes, 3, rows, full)
    return [
        pltpu.VMEM((depth,) + block, BF),
        pltpu.VMEM((depth + 1,) + block, BF),
        DMA((7, depth)),
    ]


def split(full):
    first = (full // 128 + 1) // 2 * 128
    return (first, full - first)


EARLY = 2


def home_kernel(
    planes, depth, turns, n_gains,
    gn_ref, mixed_ref, og_ref, gains_ref, o_ref, lse_ref, q_ref, lower_ref, cos_ref, sin_ref, tok_ref,
    wo_any, kv_any, parts_any, grads_b, mine_a, unit_any, recip_any, wq_any, wkv_any, xat_any,
    block_out, grad_out, shard_out, shard_qkv, gains_out, pair_out, down_out,
    wo, kv, unit_s, recip_s, wq_all, wkv_all, xat, own_part, gq, grad_kv, gmixed_s,
    bias, gob, delta, gkv, from_core, from_z, from_plane, partial, gproj, partial_q, partial_kv, gains_p, *rest,
):
    me = Place(planes, depth)
    collect = Collect(me, partial, rest[:COLLECT])
    collect_q = Collect(me, partial_q, rest[COLLECT : 2 * COLLECT])
    collect_kv = Collect(me, partial_kv, rest[2 * COLLECT : 3 * COLLECT])
    small = Collect(me, gains_p, rest[3 * COLLECT : 4 * COLLECT])
    rest = rest[4 * COLLECT :]
    mine_first, ready_first, landed_first, swap_first, mine_second, ready_second, landed_second, swap_second = rest[:8]
    folds = (
        Fold(me, None, mine_first, (None,) + rest[8:10]),
        Fold(me, grads_b, mine_second, rest[10 : 10 + FOLD]),
    )
    swaps = (
        Swap(me, ready_first, landed_first, swap_first),
        Swap(me, ready_second, landed_second, swap_second),
    )
    cs, zs, ps, load = rest[10 + FOLD :]
    half = turns // 2
    count = gn_ref.shape[0]
    sources = [wo_any, kv_any, unit_any, recip_any, xat_any, parts_any.at[0], wq_any, wkv_any, mine_a]
    places = [wo, kv, unit_s, recip_s, xat, own_part, wq_all, wkv_all, mine_first]
    loads = [pltpu.make_async_copy(a, b, load.at[i]) for i, (a, b) in enumerate(zip(sources, places))]
    for copy in loads[8:] + loads[:8]:
        copy.start()
    greet(me.plane() + me.line() + [me.sibling()])
    loads[8].wait()
    if depth - 1 > EARLY:
        folds[0].send(EARLY)
    folds[1].first()

    def c_copy(i):
        return remote(gkv.at[2 * i + 1], from_core.at[i], cs.at[0, i], cs.at[1, i], me.sibling())

    def z_copy(k):
        return remote(gkv.at[2 * k], from_z.at[k - 1], zs.at[0, k], zs.at[1, k], me.along(me.behind(1)))

    def join(k):
        if k < half:
            @pl.when((me.z - k >= 0) & (me.z + 1 < depth))
            def _():
                z_copy(k + 1).wait_recv()
                gkv[2 * k] = (gkv[2 * k].astype(F32) + from_z[k].astype(F32)).astype(BF)

        @pl.when(me.z - k >= 0)
        def _():
            z_copy(k).start()

    def p_copy(o):
        return remote(parts_any.at[o], from_plane.at[o - 1], ps.at[0, o], ps.at[1, o], me.across(o))

    for o in range(1, planes):
        p_copy(o).start()
    unit, recip = unit_of(mixed_ref[...], 1)
    grad = gn_ref[...]
    scaled = grad * gains_ref[:, D : 2 * D]
    inner = jnp.mean(scaled * unit, axis=1, keepdims=True)
    gmixed = og_ref[...].astype(F32) + recip * (scaled - unit * inner)
    gmixed_s[...] = gmixed
    dgf = jnp.sum(grad * unit, axis=0, keepdims=True)
    gmixed_b = gmixed.astype(BF)
    loads[0].wait()
    gob_all = dot(wo[...].reshape(HQ, D), gmixed_b, NT).astype(BF)
    for h in range(HEADS):
        gob_h = gob_all[h * HEAD_DIM : (h + 1) * HEAD_DIM]
        gob[paired(h, count)] = gob_h
        out = o_ref[pl.ds(h * HEAD_DIM, HEAD_DIM), :].astype(F32)
        delta[h // 4, h // 2 % 2 : h // 2 % 2 + 1, paired(h, count)[1]] = jnp.sum(
            gob_h.astype(F32) * out, axis=0, keepdims=True
        )
    half_rows = D // planes
    order = list(range(1, planes)) + [0]
    gq[...] = jnp.zeros_like(gq)
    loads[1].wait()

    def visit(slot):
        fill_bias(bias, lower_ref[...], slot)

        def four_heads(t, carry):
            key_at = pl.ds(pl.multiple_of(t * 128, 128), 128)
            value_at = pl.ds(pl.multiple_of(HK + t * 128, 128), 128)
            keys, values = kv[slot, :, key_at], kv[slot, :, value_at]
            lse_t, delta_t = lse_ref[t], delta[t]
            grad_keys, grad_values = [], []
            for u in range(2):
                key = keys[:, u * 64 : u * 64 + 64]
                value = values[:, u * 64 : u * 64 + 64]
                at = pl.ds(pl.multiple_of(t * 128 + u * 64, 64), 64)
                query, gob_h = q_ref[at, :], gob[at, :]
                probs = jnp.exp(dot(key, query, NN) + bias[...] - lse_t[u : u + 1, :])
                grad_value = dot(probs.astype(BF), gob_h, NT)
                grad_scores = (probs * (dot(value, gob_h, NN) - delta_t[u : u + 1, :])).astype(BF)
                grad_key = dot(grad_scores, query, NT)
                gq[at, :] += dot(key, grad_scores, TN)
                grad_keys.append(grad_key)
                grad_values.append(grad_value)
            gkv[slot, :, key_at] = jnp.concatenate(grad_keys, axis=1).astype(BF)
            gkv[slot, :, value_at] = jnp.concatenate(grad_values, axis=1).astype(BF)
            return carry

        lax.fori_loop(0, GROUPS, four_heads, 0)

    for i in range(half - 1, -1, -1):
        @pl.when(me.z - i - 1 + me.core >= 0)
        def _():
            visit(2 * i + 1)
            c_copy(i).start()

    for k in range(half, 0, -1):
        @pl.when(me.z - k >= 0)
        def _():
            visit(2 * k)

            @pl.when(me.core == 0)
            def _():
                if k < half:
                    c_copy(k).wait_recv()
                    gkv[2 * k] = (gkv[2 * k].astype(F32) + from_core[k].astype(F32)).astype(BF)

            @pl.when(me.core == 1)
            def _():
                c_copy(k - 1).wait_recv()
                gkv[2 * k] = (gkv[2 * k].astype(F32) + from_core[k - 1].astype(F32)).astype(BF)

        if k == half:
            join(k)

    folds[1].second()
    folds[1].step(0)
    visit(0)
    for k in range(half - 1, 0, -1):
        join(k)
    for o in order:
        d = me.dp ^ o
        rows = o_ref[pl.ds(pl.multiple_of(d * half_rows, 128), half_rows), :]
        partial[d] = dot(rows, gmixed_b, NN).astype(BF).reshape(partial.shape[1:])
        collect.first(o)
    for i in (2, 3, 4):
        loads[i].wait()
    tail_row = gains_ref[:, 2 * D : 2 * D + 128]
    gain_q, gain_k = column_of(tail_row, 0), column_of(tail_row, HEAD_DIM)
    cosine, sine = cos_ref[...], -sin_ref[...]
    gained = [0.0, 0.0]

    def four_grads(h):
        kind = 0 if h < HEADS else 1
        if kind == 0:
            heads = [gq[paired(h + i, count)] * HEAD_DIM ** (-0.5) for i in range(4)]
        else:
            four = grad_kv[:, pl.ds((h - HEADS) * HEAD_DIM, 4 * HEAD_DIM)].T
            heads = [four[i * HEAD_DIM : (i + 1) * HEAD_DIM] for i in range(4)]
        recips = recip_s[h // 4]
        results = []
        for i in range(4):
            unit = unit_s[pl.ds((h + i) * HEAD_DIM, HEAD_DIM), :]
            grad = turned(heads[i], cosine, sine)
            scaled = grad * (gain_k if kind else gain_q)
            inner = jnp.mean(scaled * unit, axis=0, keepdims=True)
            results.append(recips[i : i + 1, :] * (scaled - unit * inner))
            gained[kind] = gained[kind] + grad * unit
        gproj[:, pl.ds(h * HEAD_DIM, 4 * HEAD_DIM)] = jnp.concatenate(results, axis=0).T.astype(BF)

    def gather_grads(columns, table, collected):
        for o in order:
            d = me.dp ^ o
            rows = xat[pl.ds(pl.multiple_of(d * half_rows, 128), half_rows), :]
            table[d] = dot(rows, gproj[:, columns], NN).astype(BF).reshape(table.shape[1:])
            collected.first(o)
            if o != order[0]:
                collected.second(order[order.index(o) - 1])
        collected.second(0)

    for o in order:
        collect.second(o)
    for h in range(0, HEADS, 4):
        four_grads(h)
    gather_grads(pl.ds(0, HQ), partial_q, collect_q)
    folds[1].step(1)
    for k in range(EARLY + 1, depth - 1):
        folds[0].step(k)
    grad_kv[...] = gkv[0].astype(F32)

    @pl.when(me.core == 0)
    def _():
        c_copy(0).wait_recv()
        grad_kv[...] += from_core[0].astype(F32)

    @pl.when(me.z + 1 < depth)
    def _():
        z_copy(1).wait_recv()
        grad_kv[...] += from_z[0].astype(F32)

    for h in range(HEADS, HEADS + KV_HEADS, 4):
        four_grads(h)
    gproj[:, pl.ds(HQ + HK, HK)] = grad_kv[:, pl.ds(HK, HK)].astype(BF)
    value_o = collect.third()
    gather_grads(pl.ds(HQ, 2 * HK), partial_kv, collect_kv)
    value_q = collect_q.third()
    for i in (6, 7):
        loads[i].wait()
    grad = dot(gproj[:, :HQ], wq_all[...].reshape(D, HQ), NT)
    grad = grad + dot(gproj[:, HQ:], wkv_all[...].reshape(D, 2 * HK), NT)
    unit, recip = unit_of(tok_ref[...].astype(F32), 1)
    scaled = grad * gains_ref[:, :D]
    inner = jnp.mean(scaled * unit, axis=1, keepdims=True)
    grad_out[...] = gmixed_s[...] + recip * (scaled - unit * inner)
    dga = jnp.sum(grad * unit, axis=0, keepdims=True)
    for k in range(2, depth - 1):
        folds[1].step(k)
    if depth - 1 > EARLY:
        folds[0].settle(depth - 2)
    swaps[0].start(mine_first[me.z])
    lane = lax.broadcasted_iota(jnp.int32, (HEAD_DIM, 128), 1)
    entry = lax.broadcasted_iota(jnp.int32, (HEAD_DIM, 128), 0)
    sums = [jnp.sum(g, axis=1, keepdims=True) for g in gained]
    last = jnp.sum(
        jnp.where(lane == entry, sums[0], 0.0) + jnp.where(lane == entry + HEAD_DIM, sums[1], 0.0),
        axis=0,
        keepdims=True,
    )
    whole = jnp.concatenate([dga, dgf, last], axis=1)
    devices = planes * depth * 2
    entries = devices * n_gains
    index = lax.broadcasted_iota(jnp.int32, (devices, entries), 1)
    device = lax.broadcasted_iota(jnp.int32, (devices, entries), 0)
    apart = jnp.where(index // n_gains == device, whole, 0.0)
    pick = jnp.where(
        lax.broadcasted_iota(jnp.int32, (128, entries), 1) % n_gains
        == lax.broadcasted_iota(jnp.int32, (128, entries), 0),
        1.0,
        0.0,
    )
    table = lax.dot_general(
        apart, pick, NT, preferred_element_type=F32, precision=lax.Precision.HIGHEST
    )
    gains_p[...] = jnp.broadcast_to(table[:, None, :], (devices, 8, 128)).reshape(gains_p.shape)
    for o in order:
        small.first(o)
    value_kv = collect_kv.third()
    for o in order:
        small.second(o)
    folds[1].settle(depth - 2)
    swaps[1].start(mine_second[me.z])
    total = mixed_ref[...]
    loads[5].wait()
    total = total + own_part[...].astype(F32)
    for o in range(1, planes):
        p_copy(o).wait_recv()
        total = total + from_plane[o - 1].astype(F32)
    block_out[...] = total.astype(BF)
    little = small.third()
    shard_out[...] = collect.last(value_o)
    shard_qkv[:, :HQ] = collect_q.last(value_q)
    shard_qkv[:, HQ:] = collect_kv.last(value_kv)
    gains_out[...] = small.last(little)
    start = 0
    full = landed_first.shape[3] + landed_second.shape[3]
    for swap in swaps:
        swap.last()
        f = swap.landed.shape[3]
        for d in range(planes):
            for m in range(2):
                at = (m * planes + d) * full + start
                pair_out[:, at : at + f] = swap.landed[d, m]
            at = d * full + start
            down_out[:, at : at + f] = swap.landed[d, 2]
        start = f

    for o in range(1, planes):
        p_copy(o).wait_send()
    for i in range(half):
        @pl.when(me.z - i - 1 + me.core >= 0)
        def _():
            c_copy(i).wait_send()
    for k in range(1, half + 1):
        @pl.when(me.z - k >= 0)
        def _():
            z_copy(k).wait_send()
    collect.finish()
    collect_q.finish()
    collect_kv.finish()
    small.finish()
    folds[0].finish(False, range(EARLY, depth - 1))
    folds[1].finish(True, range(depth - 1))
    for swap in swaps:
        swap.finish()


def home(first, second, n_gains, planes, depth, turns, collective_id):
    half = turns // 2
    count = first[0].shape[0]
    wo_all, kv_all, _, grads, mine, unit, recip, wq_all, wkv_all, xat = second
    rows = wo_all.shape[3]
    parts = (mine.shape[4], grads.shape[4])
    full = sum(parts)
    return pl.pallas_call(
        functools.partial(home_kernel, planes, depth, turns, n_gains),
        out_shape=(
            jax.ShapeDtypeStruct((count, D), BF),
            jax.ShapeDtypeStruct((count, D), F32),
            jax.ShapeDtypeStruct((rows, D), F32),
            jax.ShapeDtypeStruct((rows, 2 * HQ), F32),
            jax.ShapeDtypeStruct((8, 128), F32),
            jax.ShapeDtypeStruct((rows, 2 * planes * full), BF),
            jax.ShapeDtypeStruct((rows, planes * full), BF),
        ),
        in_specs=[VMEM] * len(first) + [ANY] * len(second),
        out_specs=(VMEM,) * 7,
        scratch_shapes=[pltpu.VMEM(a.shape, a.dtype) for a in (wo_all, kv_all, unit, recip, wq_all, wkv_all, xat)]
        + [
            pltpu.VMEM((count, D), BF),
            pltpu.VMEM((HK, 2 * count), F32),
            pltpu.VMEM((count, 2 * HK), F32),
            pltpu.VMEM((count, D), F32),
            pltpu.VMEM((count, 2 * count), F32),
            pltpu.VMEM((HK, 2 * count), BF),
            pltpu.VMEM((GROUPS, 2, 2 * count), F32),
            pltpu.VMEM((turns + 1, count, 2 * HK), BF),
            pltpu.VMEM((half, count, 2 * HK), BF),
            pltpu.VMEM((half, count, 2 * HK), BF),
            pltpu.VMEM((planes - 1, count, D), BF),
            pltpu.VMEM((planes, depth, 2, rows, D), BF),
            pltpu.VMEM((count, 2 * HQ), BF),
            pltpu.VMEM((planes, depth, 2, rows, HQ), BF),
            pltpu.VMEM((planes, depth, 2, rows, 2 * HK), BF),
            pltpu.VMEM((planes, depth, 2, 8, 128), F32),
        ]
        + collect_scratch(planes, depth, rows, D, BF)
        + collect_scratch(planes, depth, rows, HQ, BF)
        + collect_scratch(planes, depth, rows, 2 * HK, BF)
        + collect_scratch(planes, depth, 8, 128, F32)
        + [
            scratch
            for part in parts
            for scratch in (
                pltpu.VMEM((depth, planes, 3, rows, part), BF),
                pltpu.VMEM((planes, 3, rows, part), BF),
                pltpu.VMEM((planes, 3, rows, part), BF),
                DMA((2, planes)),
            )
        ]
        + fold_scratch(planes, depth, rows, parts[0])[1:]
        + fold_scratch(planes, depth, rows, parts[1])
        + [DMA((2, half)), DMA((2, half + 1)), DMA((2, planes)), DMA((9,))],
        compiler_params=params(collective_id),
        cost_estimate=pl.CostEstimate(flops=60 << 30, bytes_accessed=8 << 20, transcendentals=0),
    )(*first, *second)


def adam_kernel(rates, *refs):
    n = len(rates)
    for i, rate in enumerate(rates):
        weight, grad, first, second = (r[...] for r in refs[4 * i : 4 * i + 4])
        grad = grad.astype(F32)
        outs = refs[4 * (n + i) : 4 * (n + i) + 4]
        for out, value in zip(outs, (grad,) + adam_step(weight, grad, first, second, rate, 0.1)):
            out[...] = value


def adam(groups, rates):
    rows = groups[0][0].shape[0]
    block = 16 if rows % 16 == 0 else rows
    specs, shapes = [], []
    for group in groups:
        columns = group[0].shape[1]
        specs += [pl.BlockSpec((block, columns), lambda i: (i, 0))] * 4
        shapes += [jax.ShapeDtypeStruct((rows, columns), F32)] * 4
    outs = pl.pallas_call(
        functools.partial(adam_kernel, rates),
        out_shape=tuple(shapes),
        grid=(rows // block,),
        in_specs=specs,
        out_specs=tuple(specs),
        compiler_params=pltpu.CompilerParams(vmem_limit_bytes=VMEM_BYTES),
    )(*[array for group in groups for array in group])
    return [outs[4 * i : 4 * i + 4] for i in range(len(groups))]


def per_device(
    tokens_in,
    positions,
    out_grad,
    w_qkv,
    w_output,
    w_gate_up,
    w_down,
    norm_gains,
    first_qkv,
    first_output,
    first_gate_up,
    first_down,
    first_gains,
    second_qkv,
    second_output,
    second_gate_up,
    second_down,
    second_gains,
):
    planes, ctxs = lax.axis_size("dp"), lax.axis_size("ctx")
    depth = ctxs // 2
    turns = ctxs // 2
    rows = w_qkv.shape[0]
    n_gains = norm_gains.shape[0]
    count = tokens_in.shape[0] * tokens_in.shape[1]
    tokens = tokens_in.reshape(count, D)
    places = positions.reshape(1, count)
    cotangent = out_grad.reshape(count, D)

    (
        query, kv_all, wq_all, wkv_all, xat, unit_heads, recip_heads, output_all, parts, _, _, grads, mine,
        gains_row, attn_t, lse, mixed, grad_normed, cosine, sine, lower,
    ) = fore(
        tokens, places, norm_gains[None, :], w_qkv, w_output, w_gate_up, w_down, cotangent,
        n_gains, planes, depth, turns, 0,
    )
    block_out, input_grad, shard_output, shard_qkv, gains_tile, pair_b, down_b = home(
        (grad_normed, mixed, cotangent, gains_row, attn_t, lse, query, lower, cosine, sine, tokens),
        (output_all, kv_all, parts, grads, mine, unit_heads, recip_heads, wq_all, wkv_all, xat),
        n_gains, planes, depth, turns, 1,
    )
    shard_gains = gains_tile[0, :n_gains]
    (
        (shard_qkv, new_qkv, new_first_qkv, new_second_qkv),
        (shard_output, new_output, new_first_output, new_second_output),
        (shard_gate_up, new_gate_up, new_first_gate_up, new_second_gate_up),
        (shard_down, new_down, new_first_down, new_second_down),
    ) = adam(
        (
            (w_qkv, shard_qkv, first_qkv, second_qkv),
            (w_output, shard_output, first_output, second_output),
            (w_gate_up, pair_b, first_gate_up, second_gate_up),
            (w_down, down_b, first_down, second_down),
        ),
        (0.02, 0.2, 0.02, 0.02),
    )
    new_gains, new_first_gains, new_second_gains = adam_step(
        norm_gains, shard_gains, first_gains, second_gains, 0.1, 0.0
    )
    return (
        block_out.reshape(tokens_in.shape),
        input_grad.reshape(tokens_in.shape),
        shard_qkv,
        shard_output,
        shard_gate_up,
        shard_down,
        shard_gains,
        new_qkv,
        new_output,
        new_gate_up,
        new_down,
        new_gains,
        new_first_qkv,
        new_first_output,
        new_first_gate_up,
        new_first_down,
        new_first_gains,
        new_second_qkv,
        new_second_output,
        new_second_gate_up,
        new_second_down,
        new_second_gains,
    )


def solution(mesh):
    in_specs = (
        P("dp", "ctx", None),
        P("dp", "ctx"),
        P("dp", "ctx", None),
        P(("dp", "ctx"), None),
        P(("dp", "ctx"), None),
        P(("dp", "ctx"), None),
        P(("dp", "ctx"), None),
        P(("dp", "ctx")),
        P(("dp", "ctx"), None),
        P(("dp", "ctx"), None),
        P(("dp", "ctx"), None),
        P(("dp", "ctx"), None),
        P(("dp", "ctx")),
        P(("dp", "ctx"), None),
        P(("dp", "ctx"), None),
        P(("dp", "ctx"), None),
        P(("dp", "ctx"), None),
        P(("dp", "ctx")),
    )
    out_specs = (
        P("dp", "ctx", None),
        P("dp", "ctx", None),
        P(("dp", "ctx"), None),
        P(("dp", "ctx"), None),
        P(("dp", "ctx"), None),
        P(("dp", "ctx"), None),
        P(("dp", "ctx")),
        P(("dp", "ctx"), None),
        P(("dp", "ctx"), None),
        P(("dp", "ctx"), None),
        P(("dp", "ctx"), None),
        P(("dp", "ctx")),
        P(("dp", "ctx"), None),
        P(("dp", "ctx"), None),
        P(("dp", "ctx"), None),
        P(("dp", "ctx"), None),
        P(("dp", "ctx")),
        P(("dp", "ctx"), None),
        P(("dp", "ctx"), None),
        P(("dp", "ctx"), None),
        P(("dp", "ctx"), None),
        P(("dp", "ctx")),
    )
    return jax.shard_map(
        per_device, mesh=mesh, in_specs=in_specs, out_specs=out_specs, check_vma=False
    )
```
